32 devices in a mesh: dp: 8 (over z, y), ctx: 4 (over x, core).
Axes of the slice: x: 2, y: 2, z: 4, core: 2. Of those that a mesh axis runs over, the one named last changes fastest.
Arguments:
- hidden_in: bfloat16 [24, 1024, 768], P('dp', 'ctx'), may hold values from -6 to 6
- seg_ids: int32 [24, 1024], P('dp', 'ctx'), may hold values from 0 to 15, as said below
- valid: int32 [24, 1024], P('dp', 'ctx'), may hold values from 0 to 1, as said below
- w_query: bfloat16 [768, 768], replicated, may hold values from -0.21875 to 0.21875
- b_query: bfloat16 [768], replicated, may hold values from -3 to 3
- w_key: bfloat16 [768, 768], replicated, may hold values from -0.21875 to 0.21875
- w_value: bfloat16 [768, 768], replicated, may hold values from -0.21875 to 0.21875
- b_value: bfloat16 [768], replicated, may hold values from -1.1953125 to 1.1953125
- w_out: bfloat16 [768, 768], replicated, may hold values from -0.875 to 0.875
- b_out: bfloat16 [768], replicated, may hold values from -3 to 3
- gain_attn: bfloat16 [768], replicated, may hold values from 0.099609375 to 1.8984375
- shift_attn: bfloat16 [768], replicated, may hold values from -1.796875 to 1.796875
- w_up: bfloat16 [768, 3072], replicated, may hold values from -0.21875 to 0.21875
- b_up: bfloat16 [3072], replicated, may hold values from -3 to 3
- w_down: bfloat16 [3072, 768], replicated, may hold values from -0.109375 to 0.109375
- b_down: bfloat16 [768], replicated, may hold values from -3 to 3
- gain_ffn: bfloat16 [768], replicated, may hold values from 0.099609375 to 1.8984375
- shift_ffn: bfloat16 [768], replicated, may hold values from -1.796875 to 1.796875
- pooled_text_gradient: float32 [24, 16, 768], P('dp'), may hold values from -384 to 384
Outputs:
- layer_out: bfloat16 [24, 1024, 768], P('dp', 'ctx')
- pooled: float32 [24, 16, 768], P('dp')
- grad_in: bfloat16 [24, 1024, 768], P('dp', 'ctx')
- grad_w_query: float32 [768, 768], P('dp')
- grad_b_query: float32 [768], P('dp')
- grad_w_key: float32 [768, 768], P('dp')
- grad_w_value: float32 [768, 768], P('dp')
- grad_b_value: float32 [768], P('dp')
- grad_w_out: float32 [768, 768], P('dp')
- grad_b_out: float32 [768], P('dp')
- grad_gain_attn: float32 [768], P('dp')
- attention_shift_gradient: float32 [768], P('dp')
- grad_w_up: float32 [768, 3072], P('dp')
- grad_b_up: float32 [3072], P('dp')
- grad_w_down: float32 [3072, 768], P('dp')
- grad_b_down: float32 [768], P('dp')
- grad_gain_ffn: float32 [768], P('dp')
- grad_shift_ffn: float32 [768], P('dp')
The draws below stay inside these ranges and needn't reach their ends.
Inputs may be any that keep to these rules, and one draw needn't show every extreme that they name: seg_ids never fall along a row and the row's last position holds text 16 - 1. In each block of 3 rows on one index of dp one row holds a text that begins in the first 128 positions and ends in the last 128. `valid`: the real tokens of a row are a prefix of at least 820 positions.
All inputs are finite; a program needn't handle non-finite values.
Results may differ from the reference program's by a relative error of at most 0.012.
Values may be sent and summed in bfloat16 or wider, within the bound.
A program may use at most 256 MiB of HBM per device.

```python
import jax
import jax.numpy as jnp
from jax import lax

D = 768
HEADS = 12
HEAD_DIM = 64
FF = 3072
GROUP = 256
SEQ_DEV = 3
NSEG = 16
ROW_LEN = 1024
SEQS = 24


def draw_seg_ids(key, part):
    key = jax.random.fold_in(key, 11)
    key_drawn, key_near, key_far, key_slot = jax.random.split(key, 4)

    def drawn_row(row_key):
        return jax.random.permutation(row_key, ROW_LEN - 1)[:NSEG - 1] + 1
    breaks_drawn = jax.vmap(drawn_row)(jax.random.split(key_drawn, SEQS))
    near_count = (NSEG - 1) // 2
    breaks_near = jax.random.randint(key_near, (SEQS, near_count), 1, GROUP // 2)
    breaks_far = jax.random.randint(key_far, (SEQS, NSEG - 1 - near_count), ROW_LEN - GROUP // 2, ROW_LEN)
    breaks_wide = jnp.concatenate([breaks_near, breaks_far], axis=1)
    chosen_slot = jax.random.randint(key_slot, (SEQS // SEQ_DEV,), 0, SEQ_DEV)
    row_index = jnp.arange(SEQS)
    chosen = row_index % SEQ_DEV == jnp.repeat(chosen_slot, SEQ_DEV)
    breaks = jnp.where(chosen[:, None], breaks_wide, breaks_drawn)
    positions = jnp.arange(ROW_LEN)
    return jnp.sum((positions[None, :, None] >= breaks[:, None, :]).astype(jnp.int32), axis=2).astype(jnp.int32)


def draw_valid(key, part):
    key = jax.random.fold_in(key, 23)
    fill_length = jax.random.randint(key, (SEQS, 1), ROW_LEN - ROW_LEN // 5, ROW_LEN + 1)
    return (jnp.arange(ROW_LEN)[None, :] < fill_length).astype(jnp.int32)


def block_scale(rng, extent, cuts, low, high):
    loudness = 1.0
    for position, blocks in cuts:
        draws = jax.random.uniform(jax.random.fold_in(jax.random.fold_in(rng, 6), position), (blocks,), jnp.float32, low / len(cuts), high / len(cuts))
        loudness = loudness * jnp.repeat(jnp.exp(draws), extent[position] // blocks).reshape((-1,) + (1,) * (len(extent) - 1 - position))
    return loudness


def noise(own_key, extent, scale, most, cuts=(), dtype=jnp.bfloat16):
    gain = block_scale(own_key, extent, cuts, -0.22, 0.18) if cuts else 1.0
    result = jax.random.normal(own_key, extent, jnp.float32) * scale * gain
    return jnp.minimum(jnp.maximum(result, -most), most).astype(dtype)


def setup_inputs(seed: int = 0) -> dict:
    streams_of = jax.random.split(jax.random.key(seed), 20)
    hidden_in = noise(streams_of[0], (SEQS, ROW_LEN, D), 1.0, 6.0, ((0, 8), (1, 4)))
    seg_ids = draw_seg_ids(jax.random.fold_in(streams_of[19], 71), 0)
    valid = draw_valid(jax.random.fold_in(streams_of[19], 71), 0)
    w_query = noise(streams_of[3], (D, D), D ** -0.5, 0.21875)
    b_query = noise(streams_of[4], (D,), 0.5, 3.0)
    w_key = noise(streams_of[5], (D, D), D ** -0.5, 0.21875)
    w_value = noise(streams_of[6], (D, D), D ** -0.5, 0.21875)
    b_value = noise(streams_of[7], (D,), 0.2, 1.1953125)
    w_out = noise(streams_of[8], (D, D), (D // 16) ** -0.5, 0.875)
    b_out = noise(streams_of[9], (D,), 0.5, 3.0)
    gain_attn = jnp.clip(1.0 + 0.18 * jax.random.normal(streams_of[10], (D,), jnp.float32), 0.099609375, 1.8984375).astype(jnp.bfloat16)
    shift_attn = noise(streams_of[11], (D,), 0.3, 1.796875)
    w_up = noise(streams_of[12], (D, FF), D ** -0.5, 0.21875)
    b_up = noise(streams_of[13], (FF,), 0.5, 3.0)
    w_down = noise(streams_of[14], (FF, D), FF ** -0.5, 0.109375)
    b_down = noise(streams_of[15], (D,), 0.5, 3.0)
    gain_ffn = jnp.clip(1.0 + 0.18 * jax.random.normal(streams_of[16], (D,), jnp.float32), 0.099609375, 1.8984375).astype(jnp.bfloat16)
    shift_ffn = noise(streams_of[17], (D,), 0.3, 1.796875)
    pooled_text_gradient = noise(streams_of[18], (SEQS, NSEG, D), (ROW_LEN // NSEG), 384.0, ((0, 8),), jnp.float32)
    return {"hidden_in": hidden_in, "seg_ids": seg_ids, "valid": valid, "w_query": w_query, "b_query": b_query, "w_key": w_key, "w_value": w_value, "b_value": b_value, "w_out": w_out, "b_out": b_out, "gain_attn": gain_attn, "shift_attn": shift_attn, "w_up": w_up, "b_up": b_up, "w_down": w_down, "b_down": b_down, "gain_ffn": gain_ffn, "shift_ffn": shift_ffn, "pooled_text_gradient": pooled_text_gradient}


@jax.custom_vjp
def low(v):
    return lax.optimization_barrier(v.astype(jnp.bfloat16)).astype(jnp.float32)

@jax.custom_vjp
def low_back(v):
    return v

def low_keep(v):
    return (low(v), None)

def low_pass(kept, grad):
    return (grad,)

def back_keep(v):
    return (v, None)

def back_low(kept, grad):
    return (low(grad),)
low.defvjp(low_keep, low_pass)
low_back.defvjp(back_keep, back_low)
eps = 1e-12

def layer_norm(values_in, gain_vec, shift_vec):
    centre = lax.optimization_barrier(jnp.mean(values_in, axis=-1, keepdims=True))
    centred = values_in - centre
    spread = lax.optimization_barrier(jnp.mean(centred * centred, axis=-1, keepdims=True))
    return centred * lax.rsqrt(spread + eps) * gain_vec + shift_vec

def product(left_side, right_side):
    return jnp.dot(left_side, right_side, precision=lax.Precision.HIGHEST)

def attend_row(item_tuple):
    queries, key_rows, values, seg_row = item_tuple
    row_length = queries.shape[0]
    queries = queries.reshape(row_length, HEADS, HEAD_DIM)
    key_rows = key_rows.reshape(row_length, HEADS, HEAD_DIM)
    values = values.reshape(row_length, HEADS, HEAD_DIM)
    scores = jnp.einsum('qhe,khe->hqk', queries, key_rows, precision=lax.Precision.HIGHEST) * HEAD_DIM ** (-0.5)
    scores = low_back(scores)
    same_text = seg_row[:, None] == seg_row[None, :]
    scores = jnp.where(same_text[None], scores, -1e+30)
    row_max = lax.optimization_barrier(jnp.max(scores, axis=-1, keepdims=True))
    exponent = jnp.exp(scores - row_max)
    probs = low(exponent / lax.optimization_barrier(jnp.sum(exponent, axis=-1, keepdims=True)))
    context = jnp.einsum('hqk,khe->qhe', probs, values, precision=lax.Precision.HIGHEST)
    return context.reshape(row_length, HEADS * HEAD_DIM)

def layer_forward(hidden, seg_ids, w_query, b_query, w_key, w_value, b_value, w_out, b_out, gain_attn, shift_attn, w_up, b_up, w_down, b_down, gain_ffn, shift_ffn):
    row_count = hidden.shape[0]
    row_length = hidden.shape[1]
    tokens_flat = hidden.reshape(row_count * row_length, D)
    queries = low_back(low(product(tokens_flat, w_query) + b_query))
    key_rows = low_back(low(product(tokens_flat, w_key)))
    values = low_back(low(product(tokens_flat, w_value) + b_value))
    context = lax.map(jax.checkpoint(attend_row), (queries.reshape(row_count, row_length, D), key_rows.reshape(row_count, row_length, D), values.reshape(row_count, row_length, D), seg_ids))
    context = low_back(low(context.reshape(row_count * row_length, D)))
    attn_out = low_back(product(context, w_out) + b_out)
    normed = layer_norm(tokens_flat + attn_out, gain_attn, shift_attn)
    pre_act = low_back(product(low(normed), w_up) + b_up)
    activation = low(jax.nn.gelu(pre_act, approximate=False))
    ffn_out = low_back(product(activation, w_down) + b_down)
    final_out = layer_norm(normed + ffn_out, gain_ffn, shift_ffn)
    return final_out.reshape(row_count, row_length, D)

def reference(hidden_in, seg_ids, valid, w_query, b_query, w_key, w_value, b_value, w_out, b_out, gain_attn, shift_attn, w_up, b_up, w_down, b_down, gain_ffn, shift_ffn, pooled_text_gradient):
    weights_f32 = tuple((member.astype(jnp.float32) for member in (w_query, b_query, w_key, w_value, b_value, w_out, b_out, gain_attn, shift_attn, w_up, b_up, w_down, b_down, gain_ffn, shift_ffn)))
    hidden = hidden_in.astype(jnp.float32)

    def run_layer(hidden_f32, *weight_list):
        return layer_forward(hidden_f32, seg_ids, *weight_list)
    final_out, layer_back = jax.vjp(run_layer, hidden, *weights_f32)
    text_membership = ((seg_ids[:, :, None] == jnp.arange(NSEG)[None, None, :]) & (valid[:, :, None] == 1)).astype(jnp.float32)

    def pool_texts(layer_results):
        token_totals = jnp.einsum('ofr,ofy->ory', text_membership, layer_results, precision=lax.Precision.HIGHEST)
        counts = lax.optimization_barrier(jnp.sum(text_membership, axis=1))
        return token_totals / jnp.maximum(counts, 1.0)[:, :, None]
    pooled, pool_back = jax.vjp(pool_texts, final_out)
    grad_final = pool_back(pooled_text_gradient.astype(jnp.float32))[0]
    gradients = layer_back(grad_final)
    return (final_out.astype(jnp.bfloat16), pooled, gradients[0].astype(jnp.bfloat16), gradients[1], gradients[2], gradients[3], gradients[4], gradients[5], gradients[6], gradients[7], gradients[8], gradients[9], gradients[10], gradients[11], gradients[12], gradients[13], gradients[14], gradients[15])
```

```python
import jax
import jax.numpy as jnp
from jax import lax
from jax.sharding import PartitionSpec as P

HEADS = 12
HEAD_DIM = 64
NSEG = 16


eps = 1e-12


def layer_norm(values_in, gain_vec, shift_vec):
    centre = jnp.mean(values_in, axis=-1, keepdims=True)
    centred = values_in - centre
    spread = jnp.mean(centred * centred, axis=-1, keepdims=True)
    return centred * lax.rsqrt(spread + eps) * gain_vec + shift_vec


def gelu_exact(values_in):
    return jax.nn.gelu(values_in, approximate=False)


def matmul(left_side, right_side):
    return jnp.dot(left_side, right_side, preferred_element_type=jnp.float32)


def matmul_left(left_side, right_side):
    return lax.dot_general(
        left_side, right_side, (((0,), (0,)), ((), ())), preferred_element_type=jnp.float32
    )


def matmul_right(left_side, right_side):
    return lax.dot_general(
        left_side, right_side, (((1,), (1,)), ((), ())), preferred_element_type=jnp.float32
    )


def masked_scores(queries, key_rows, seg_query, seg_key):
    scores = jnp.einsum(
        "sqhe,skhe->shqk", queries, key_rows, preferred_element_type=jnp.float32
    ) * HEAD_DIM ** (-0.5)
    same_text = seg_query[:, None, :, None] == seg_key[:, None, None, :]
    return jnp.where(same_text, scores, -1e30)

def radices_of(count):
    if count == 8:
        return ((1, 2), (2, 4))
    digits = []
    stride = 1
    while stride < count:
        digits.append((stride, 2))
        stride *= 2
    return tuple(digits)


def exchange(piece, axis_name, stride, offset):
    count = lax.axis_size(axis_name)
    pairs = [(i, i ^ (offset * stride)) for i in range(count)]
    return lax.ppermute(piece, axis_name, pairs)


def scatter_digit(pieces, place, axis_name, stride, radix):
    here = (lax.axis_index(axis_name) // stride) % radix
    received = [
        exchange(
            lax.dynamic_index_in_dim(pieces, here ^ offset, place, keepdims=False),
            axis_name, stride, offset,
        )
        for offset in range(1, radix)
    ]
    total = lax.dynamic_index_in_dim(pieces, here, place, keepdims=False).astype(jnp.float32)
    for item in received:
        total = total + item.astype(jnp.float32)
    return total.astype(jnp.bfloat16)


def gather_digit(piece, axis_name, stride):
    here = (lax.axis_index(axis_name) // stride) % 2
    other = exchange(piece, axis_name, stride, 1)
    first = jnp.where(here == 0, piece, other)
    second = jnp.where(here == 0, other, piece)
    return jnp.stack([first, second])


def reduce_group(group, ctx_first):
    dp_size, ctx_size = lax.axis_size("dp"), lax.axis_size("ctx")
    dp_digits, ctx_digits = radices_of(dp_size), radices_of(ctx_size)
    tail = group.shape[2:]
    shape = [r for _, r in reversed(dp_digits)] + [r for _, r in reversed(ctx_digits)]
    group = group.reshape(tuple(shape) + tail)
    group = scatter_digit(group, len(shape) - 1, "ctx", 1, 2)
    place = len(shape) - 2
    if ctx_first:
        group = scatter_digit(group, place, "ctx", 2, 2)
        for stride, radix in dp_digits:
            place -= 1
            group = scatter_digit(group, place, "dp", stride, radix)
        group = gather_digit(group, "ctx", 2)
    else:
        for stride, radix in dp_digits:
            place -= 1
            group = scatter_digit(group, place, "dp", stride, radix)
        other = exchange(group, "ctx", 2, 1)
        group = group.astype(jnp.float32) + other.astype(jnp.float32)
        group = group.astype(jnp.bfloat16)
    both = gather_digit(group, "ctx", 1)
    return both.swapaxes(0, 1).reshape((ctx_size,) + tail)


def per_device(
    hidden_in,
    seg_ids,
    valid,
    w_query,
    b_query,
    w_key,
    w_value,
    b_value,
    w_out,
    b_out,
    gain_attn,
    shift_attn,
    w_up,
    b_up,
    w_down,
    b_down,
    gain_ffn,
    shift_ffn,
    pooled_text_gradient,
):
    row_count, group_size, model_width = hidden_in.shape
    token_count = row_count * group_size
    tokens_flat = hidden_in.reshape(token_count, model_width)
    residual = tokens_flat.astype(jnp.float32)
    seg_here = seg_ids.astype(jnp.bfloat16)
    gain_one = gain_attn.astype(jnp.float32)
    shift_one = shift_attn.astype(jnp.float32)
    gain_two = gain_ffn.astype(jnp.float32)
    shift_two = shift_ffn.astype(jnp.float32)
    scale_value = HEAD_DIM ** (-0.5)
    queries = (
        (matmul(tokens_flat, w_query) + b_query.astype(jnp.float32))
        .astype(jnp.bfloat16)
        .reshape(row_count, group_size, HEADS, HEAD_DIM)
    )
    key_rows = (
        matmul(tokens_flat, w_key).astype(jnp.bfloat16).reshape(row_count, group_size, model_width)
    )
    values = (
        (matmul(tokens_flat, w_value) + b_value.astype(jnp.float32))
        .astype(jnp.bfloat16)
        .reshape(row_count, group_size, model_width)
    )
    keys_all, values_all, seg_all = (
        lax.all_gather(key_rows, "ctx", axis=1, tiled=True),
        lax.all_gather(values, "ctx", axis=1, tiled=True),
        lax.all_gather(seg_here, "ctx", axis=1, tiled=True),
    )
    keys_heads = keys_all.reshape(row_count, -1, HEADS, HEAD_DIM)
    values_heads = values_all.reshape(row_count, -1, HEADS, HEAD_DIM)
    scores = masked_scores(queries, keys_heads, seg_here, seg_all)
    row_max = jnp.max(scores, axis=-1, keepdims=True)
    exponent = jnp.exp(scores - row_max)
    row_total = jnp.sum(exponent, axis=-1, keepdims=True)
    probs_bf = (exponent / row_total).astype(jnp.bfloat16)
    context = jnp.einsum(
        "shqk,skhe->sqhe", probs_bf, values_heads, preferred_element_type=jnp.float32
    )
    context = context.reshape(token_count, model_width).astype(jnp.bfloat16)
    attn_out = matmul(context, w_out) + b_out.astype(jnp.float32)
    mixed_sum = residual + attn_out
    normed = layer_norm(mixed_sum, gain_one, shift_one)
    normed_bf = normed.astype(jnp.bfloat16)
    act_bf = gelu_exact(matmul(normed_bf, w_up) + b_up.astype(jnp.float32)).astype(jnp.bfloat16)
    ffn_out = matmul(act_bf, w_down) + b_down.astype(jnp.float32)
    summed = normed + ffn_out
    final_out = layer_norm(summed, gain_two, shift_two)
    text_membership = (
        (seg_ids[:, :, None] == jnp.arange(NSEG)[None, None, :]) & (valid[:, :, None] == 1)
    ).astype(jnp.float32)
    part_sums = jnp.einsum(
        "ofr,ofy->ory",
        text_membership,
        final_out.reshape(row_count, group_size, model_width),
        precision=lax.Precision.HIGHEST,
    )
    part_counts = jnp.sum(text_membership, axis=1)
    text_totals, text_counts = (
        lax.psum(part_sums.astype(jnp.bfloat16), "ctx").astype(jnp.float32),
        lax.psum(part_counts.astype(jnp.bfloat16), "ctx").astype(jnp.float32),
    )
    clamped_text_counts = jnp.maximum(text_counts, 1.0)[:, :, None]
    pooled = text_totals / clamped_text_counts
    grad_final = jnp.einsum(
        "heb,hbj->hej",
        text_membership,
        pooled_text_gradient / clamped_text_counts,
        precision=lax.Precision.HIGHEST,
    ).reshape(token_count, model_width)
    _, norm_two_back = jax.vjp(layer_norm, summed, gain_two, shift_two)
    grad_summed, grad_gain_two, grad_shift_two = norm_two_back(grad_final)
    grad_ffn = grad_summed.astype(jnp.bfloat16)
    grad_w_down = matmul_left(act_bf, grad_ffn)
    grad_b_down = jnp.sum(grad_ffn.astype(jnp.float32), axis=0)
    grad_act = matmul_right(grad_ffn, w_down)
    pre_again = matmul(normed_bf, w_up) + b_up.astype(jnp.float32)
    _, gelu_back = jax.vjp(gelu_exact, pre_again)
    grad_pre = gelu_back(grad_act)[0].astype(jnp.bfloat16)
    grad_w_up = matmul_left(normed_bf, grad_pre)
    grad_b_up = jnp.sum(grad_pre.astype(jnp.float32), axis=0)
    grad_normed = grad_summed + matmul_right(grad_pre, w_up)
    _, norm_one_back = jax.vjp(layer_norm, mixed_sum, gain_one, shift_one)
    grad_mixed, grad_gain_one, grad_shift_one = norm_one_back(grad_normed)
    grad_attn = grad_mixed.astype(jnp.bfloat16)
    grad_w_out = matmul_left(context, grad_attn)
    grad_b_out = jnp.sum(grad_attn.astype(jnp.float32), axis=0)
    grad_context = (
        matmul_right(grad_attn, w_out)
        .astype(jnp.bfloat16)
        .reshape(row_count, group_size, HEADS, HEAD_DIM)
    )
    probs = jnp.exp(masked_scores(queries, keys_heads, seg_here, seg_all) - row_max) / row_total
    grad_probs = jnp.einsum(
        "sqhe,skhe->shqk", grad_context, values_heads, preferred_element_type=jnp.float32
    )
    row_delta = jnp.sum(probs * grad_probs, axis=-1, keepdims=True)
    grad_scores = (probs * (grad_probs - row_delta)).astype(jnp.bfloat16)
    query_gradient = (
        jnp.einsum("shqk,skhe->sqhe", grad_scores, keys_heads, preferred_element_type=jnp.float32)
        * scale_value
    )
    grad_keys_all = (
        jnp.einsum("shqk,sqhe->skhe", grad_scores, queries, preferred_element_type=jnp.float32)
        * scale_value
    )
    grad_values_all = jnp.einsum(
        "shqk,sqhe->skhe",
        probs.astype(jnp.bfloat16),
        grad_context,
        preferred_element_type=jnp.float32,
    )
    grad_keys, grad_values = (
        lax.psum_scatter(
            grad_keys_all.astype(jnp.bfloat16), "ctx", scatter_dimension=1, tiled=True
        ).astype(jnp.float32),
        lax.psum_scatter(
            grad_values_all.astype(jnp.bfloat16), "ctx", scatter_dimension=1, tiled=True
        ).astype(jnp.float32),
    )
    grad_q = query_gradient.reshape(token_count, model_width).astype(jnp.bfloat16)
    grad_k = grad_keys.reshape(token_count, model_width).astype(jnp.bfloat16)
    grad_v = grad_values.reshape(token_count, model_width).astype(jnp.bfloat16)
    grad_w_query = matmul_left(tokens_flat, grad_q)
    grad_b_query = jnp.sum(grad_q.astype(jnp.float32), axis=0)
    grad_w_key = matmul_left(tokens_flat, grad_k)
    grad_w_value = matmul_left(tokens_flat, grad_v)
    grad_b_value = jnp.sum(grad_v.astype(jnp.float32), axis=0)
    grad_input = (
        grad_mixed
        + matmul_right(grad_q, w_query)
        + matmul_right(grad_k, w_key)
        + matmul_right(grad_v, w_value)
    )
    dp_size, ctx_size = lax.axis_size("dp"), lax.axis_size("ctx")
    ff_width = w_up.shape[1]
    rows_here, ff_here = model_width // dp_size, ff_width // dp_size
    low = jnp.bfloat16
    up_group = (
        grad_w_up.astype(low)
        .reshape(dp_size, rows_here, ctx_size, ff_width // ctx_size)
        .transpose(0, 2, 1, 3)
    )
    down_group = grad_w_down.astype(low).reshape(
        dp_size, ctx_size, ff_here // ctx_size, model_width
    )
    squares = [
        piece.astype(low).reshape(dp_size, rows_here, ctx_size, model_width // ctx_size)
        .transpose(0, 2, 1, 3)
        for piece in (grad_w_query, grad_w_key, grad_w_value, grad_w_out)
    ]
    square_group = jnp.concatenate(squares, axis=2)
    vectors = [
        piece.astype(low).reshape(dp_size, rows_here)
        for piece in (
            grad_b_query, grad_b_value, grad_b_out, grad_gain_one, grad_shift_one,
            grad_b_down, grad_gain_two, grad_shift_two,
        )
    ] + [grad_b_up.astype(low).reshape(dp_size, ff_here)]
    vector_group = jnp.concatenate(vectors, axis=1)
    vector_size = vector_group.shape[1]
    lanes = model_width // ctx_size
    vector_rows = -(-vector_size // (ctx_size * lanes))
    vector_group = jnp.pad(
        vector_group, ((0, 0), (0, vector_rows * ctx_size * lanes - vector_size))
    ).reshape(dp_size, ctx_size, vector_rows, lanes)
    rest_group = jnp.concatenate([square_group, vector_group], axis=2)
    up_sum = reduce_group(up_group, True)
    down_sum = reduce_group(down_group, False)
    rest_sum = reduce_group(rest_group, True).astype(jnp.float32)
    sum_up = up_sum.astype(jnp.float32).transpose(1, 0, 2).reshape(rows_here, ff_width)
    sum_down = down_sum.astype(jnp.float32).reshape(ff_here, model_width)
    sum_squares = [
        rest_sum[:, i * rows_here : (i + 1) * rows_here].transpose(1, 0, 2).reshape(
            rows_here, model_width
        )
        for i in range(4)
    ]
    sum_vector = rest_sum[:, 4 * rows_here :].reshape(-1)
    sums = [sum_vector[i * rows_here : (i + 1) * rows_here] for i in range(8)]
    sum_bu = sum_vector[8 * rows_here : 8 * rows_here + ff_here]
    results = (
        sum_squares[0], sums[0], sum_squares[1], sum_squares[2], sums[1], sum_squares[3],
        sums[2], sums[3], sums[4], sum_up, sum_bu, sum_down, sums[5], sums[6], sums[7],
    )
    return (
        final_out.reshape(row_count, group_size, model_width).astype(jnp.bfloat16),
        pooled,
        grad_input.reshape(row_count, group_size, model_width).astype(jnp.bfloat16),
    ) + tuple(results)


def solution(mesh):
    placed = (
        P("dp", "ctx", None),
        P("dp", "ctx"),
        P("dp", "ctx"),
        P(),
        P(),
        P(),
        P(),
        P(),
        P(),
        P(),
        P(),
        P(),
        P(),
        P(),
        P(),
        P(),
        P(),
        P(),
        P("dp", None, None),
    )
    return jax.shard_map(
        per_device,
        mesh=mesh,
        in_specs=placed,
        out_specs=(
            P("dp", "ctx", None),
            P("dp", None, None),
            P("dp", "ctx", None),
            P("dp", None),
            P("dp"),
            P("dp", None),
            P("dp", None),
            P("dp"),
            P("dp", None),
            P("dp"),
            P("dp"),
            P("dp"),
            P("dp", None),
            P("dp"),
            P("dp", None),
            P("dp"),
            P("dp"),
            P("dp"),
        ),
        check_vma=False,
    )
```

```python
import jax
import jax.numpy as jnp
from jax import lax
from jax.experimental import pallas as pl
from jax.experimental.pallas import tpu as pltpu
from jax.sharding import PartitionSpec as P

HEADS = 12
HEAD_DIM = 64
NSEG = 16


eps = 1e-12


def layer_norm(values_in, gain_vec, shift_vec):
    centre = jnp.mean(values_in, axis=-1, keepdims=True)
    centred = values_in - centre
    spread = jnp.mean(centred * centred, axis=-1, keepdims=True)
    return centred * lax.rsqrt(spread + eps) * gain_vec + shift_vec


def gelu_exact(values_in):
    return jax.nn.gelu(values_in, approximate=False)


def matmul(left_side, right_side):
    return jnp.dot(left_side, right_side, preferred_element_type=jnp.float32)


def matmul_left(left_side, right_side):
    return lax.dot_general(
        left_side, right_side, (((0,), (0,)), ((), ())), preferred_element_type=jnp.float32
    )


def matmul_right(left_side, right_side):
    return lax.dot_general(
        left_side, right_side, (((1,), (1,)), ((), ())), preferred_element_type=jnp.float32
    )


PAIR = 2 * HEAD_DIM
MASKED = -1e30


def dot_nt(left_side, right_side):
    return lax.dot_general(
        left_side, right_side, (((1,), (1,)), ((), ())), preferred_element_type=jnp.float32
    )


def dot_tn(left_side, right_side):
    return lax.dot_general(
        left_side, right_side, (((0,), (0,)), ((), ())), preferred_element_type=jnp.float32
    )


def split_heads(pair):
    lane = lax.broadcasted_iota(jnp.int32, pair.shape, 1)
    zero = jnp.zeros_like(pair)
    return jnp.concatenate(
        [jnp.where(lane < HEAD_DIM, pair, zero), jnp.where(lane < HEAD_DIM, zero, pair)], axis=0
    )


def attend_kernel(
    x_own, x_one, x_two, x_three, seg_query, seg_key, w_query, w_key, w_value, b_query, b_value,
    q_out, k_out, v_out, context_out, lse_out, bias_ref, stat_ref,
):
    size = x_own.shape[0]
    q = matmul(x_own[...], w_query[...]) + b_query[...]
    q_out[...] = (q.astype(jnp.bfloat16) * HEAD_DIM ** (-0.5)).astype(jnp.bfloat16)
    for j, x_ref in enumerate((x_own, x_one, x_two, x_three)):
        rows = slice(j * size, (j + 1) * size)
        k_out[rows] = matmul(x_ref[...], w_key[...]).astype(jnp.bfloat16)
        v_out[rows] = (matmul(x_ref[...], w_value[...]) + b_value[...]).astype(jnp.bfloat16)
    bias_ref[...] = jnp.where(seg_query[...] == seg_key[...], 0.0, MASKED)
    stat_ref[...] = jnp.zeros_like(stat_ref)
    lane = lax.broadcasted_iota(jnp.int32, (size, PAIR), 1)

    def one_pair(pair, carry):
        columns = pl.ds(pl.multiple_of(pair * PAIR, PAIR), PAIR)
        both = split_heads(q_out[:, columns])
        scores = dot_nt(both, k_out[:, columns])
        scores = scores.reshape(2, size, scores.shape[1]) + bias_ref[...][None]
        top = jnp.max(scores, axis=-1, keepdims=True)
        weight = jnp.exp(scores - top)
        total = jnp.sum(weight, axis=-1, keepdims=True)
        mixed = matmul(
            weight.astype(jnp.bfloat16).reshape(2 * size, -1), v_out[:, columns]
        ).reshape(2, size, PAIR) / total
        context_out[:, columns] = jnp.where(lane < HEAD_DIM, mixed[0], mixed[1]).astype(jnp.bfloat16)
        lse = top + jnp.log(total)
        stat = stat_ref[...]
        stat = jnp.where(lane == 2 * pair, lse[0], stat)
        stat_ref[...] = jnp.where(lane == 2 * pair + 1, lse[1], stat)
        return carry

    lax.fori_loop(0, HEADS // 2, one_pair, 0)
    lse_out[...] = stat_ref[...].T[: lse_out.shape[0]]


def attend(blocks, seg_query, seg_key, w_query, w_key, w_value, b_query, b_value):
    size, width = blocks[0].shape
    keys = size * len(blocks)
    low = jnp.bfloat16
    return pl.pallas_call(
        attend_kernel,
        out_shape=(
            jax.ShapeDtypeStruct((size, width), low),
            jax.ShapeDtypeStruct((keys, width), low),
            jax.ShapeDtypeStruct((keys, width), low),
            jax.ShapeDtypeStruct((size, width), low),
            jax.ShapeDtypeStruct((16, size), jnp.float32),
        ),
        scratch_shapes=[
            pltpu.VMEM((size, keys), jnp.float32),
            pltpu.VMEM((size, PAIR), jnp.float32),
        ],
        compiler_params=pltpu.CompilerParams(vmem_limit_bytes=48 * 2**20),
        cost_estimate=pl.CostEstimate(
            flops=2 * (size + 2 * keys) * width * width + 16 * size * keys * width,
            bytes_accessed=2 * (3 * width * width + 5 * keys * width),
            transcendentals=HEADS * size * keys,
        ),
    )(*blocks, seg_query, seg_key, w_query, w_key, w_value, b_query, b_value)


def attend_back_kernel(
    x_own, x_one, x_two, x_three, q_ref, k_ref, v_ref, context_ref, grad_ref, lse_ref,
    seg_query, seg_key, w_query, w_key, w_value,
    dx_own, dx_one, dx_two, dx_three, dwq_out, dwk_out, dwv_out, bias_out,
    bias_ref, dq_ref, dk_ref, dv_ref,
):
    size, width = x_own.shape
    low = jnp.bfloat16
    blocks = k_ref.shape[0] // size
    bias_ref[...] = jnp.where(seg_key[...] == seg_query[...], 0.0, MASKED)
    row = lax.broadcasted_iota(jnp.int32, (PAIR, size), 0)

    def one_pair(pair, carry):
        columns = pl.ds(pl.multiple_of(pair * PAIR, PAIR), PAIR)
        grad = grad_ref[:, columns]
        q_both = split_heads(q_ref[:, columns])
        g_both = split_heads(grad)
        product = (grad.astype(jnp.float32) * context_ref[:, columns].astype(jnp.float32)).T
        delta = jnp.concatenate(
            [
                jnp.sum(product[:HEAD_DIM], axis=0, keepdims=True),
                jnp.sum(product[HEAD_DIM:], axis=0, keepdims=True),
            ],
            axis=1,
        )
        lse = jnp.concatenate(
            [lse_ref[pl.ds(2 * pair, 1), :], lse_ref[pl.ds(2 * pair + 1, 1), :]], axis=1
        )
        dq = jnp.zeros((PAIR, 2 * size), jnp.float32)
        for j in range(blocks):
            rows = pl.ds(j * size, size)
            keys = k_ref[rows, columns]
            bias = bias_ref[rows, :]
            bias = jnp.concatenate([bias, bias], axis=1)
            probs = jnp.exp(dot_nt(keys, q_both) + bias - lse)
            grad_s = probs * (dot_nt(v_ref[rows, columns], g_both) - delta)
            grad_s = grad_s.astype(low)
            dv_ref[rows, columns] = matmul(probs.astype(low), g_both).astype(low)
            dk_ref[rows, columns] = matmul(grad_s, q_both).astype(low)
            dq = dq + matmul(keys.T, grad_s)
        dq = jnp.where(row < HEAD_DIM, dq[:, :size], dq[:, size:]) * HEAD_DIM ** (-0.5)
        dq_ref[:, columns] = dq.T.astype(low)
        return carry

    lax.fori_loop(0, HEADS // 2, one_pair, 0)
    for j, out in enumerate((dx_own, dx_one, dx_two, dx_three)):
        rows = pl.ds(j * size, size)
        part = dot_nt(dk_ref[rows, :], w_key[...]) + dot_nt(dv_ref[rows, :], w_value[...])
        if j == 0:
            part = part + dot_nt(dq_ref[...], w_query[...])
        out[...] = part.astype(out.dtype)
    dwq_out[...] = dot_tn(x_own[...], dq_ref[...]).astype(low)
    for source, out in ((dk_ref, dwk_out), (dv_ref, dwv_out)):
        total = jnp.zeros((width, width), jnp.float32)
        for j, x_ref in enumerate((x_own, x_one, x_two, x_three)):
            total = total + dot_tn(x_ref[...], source[pl.ds(j * size, size), :])
        out[...] = total.astype(low)
    bias_out[0:1, :] = jnp.sum(dq_ref[...].astype(jnp.float32), axis=0, keepdims=True)
    bias_out[1:2, :] = jnp.sum(dv_ref[...].astype(jnp.float32), axis=0, keepdims=True)


def attend_back(blocks, q, k, v, context, grad, lse, seg_query, seg_key, w_query, w_key, w_value):
    size, width = blocks[0].shape
    keys = size * len(blocks)
    low = jnp.bfloat16
    token_block = jax.ShapeDtypeStruct((size, width), low)
    square = jax.ShapeDtypeStruct((width, width), low)
    return pl.pallas_call(
        attend_back_kernel,
        out_shape=(
            jax.ShapeDtypeStruct((size, width), jnp.float32),
            token_block, token_block, token_block, square, square, square,
            jax.ShapeDtypeStruct((2, width), jnp.float32),
        ),
        scratch_shapes=[
            pltpu.VMEM((keys, size), jnp.float32),
            pltpu.VMEM((size, width), low),
            pltpu.VMEM((keys, width), low),
            pltpu.VMEM((keys, width), low),
        ],
        compiler_params=pltpu.CompilerParams(vmem_limit_bytes=56 * 2**20),
        cost_estimate=pl.CostEstimate(
            flops=4 * (size + 2 * keys) * width * width + 40 * size * keys * width,
            bytes_accessed=2 * (6 * width * width + 5 * keys * width),
            transcendentals=HEADS * size * keys,
        ),
    )(*blocks, q, k, v, context, grad, lse, seg_query, seg_key, w_query, w_key, w_value)


def radices_of(count):
    if count == 8:
        return ((1, 2), (2, 4))
    digits = []
    stride = 1
    while stride < count:
        digits.append((stride, 2))
        stride *= 2
    return tuple(digits)


def exchange(piece, axis_name, stride, offset):
    count = lax.axis_size(axis_name)
    pairs = [(i, i ^ (offset * stride)) for i in range(count)]
    return lax.ppermute(piece, axis_name, pairs)


def digit_of(axis_name, stride, radix):
    return (lax.axis_index(axis_name) // stride) % radix


def scatter_digit(pieces, place, axis_name, stride, radix):
    here = digit_of(axis_name, stride, radix)
    received = [
        exchange(
            lax.dynamic_index_in_dim(pieces, here ^ offset, place, keepdims=False).astype(
                jnp.bfloat16
            ),
            axis_name, stride, offset,
        )
        for offset in range(1, radix)
    ]
    total = lax.dynamic_index_in_dim(pieces, here, place, keepdims=False).astype(jnp.float32)
    for item in received:
        total = total + item.astype(jnp.float32)
    return total.astype(jnp.bfloat16)


def halve(piece, place, axis_name, stride):
    half = piece.shape[place] // 2
    here = digit_of(axis_name, stride, 2)
    sent = lax.dynamic_slice_in_dim(piece, (1 - here) * half, half, place).astype(jnp.bfloat16)
    kept = lax.dynamic_slice_in_dim(piece, here * half, half, place).astype(jnp.float32)
    return (kept + exchange(sent, axis_name, stride, 1).astype(jnp.float32)).astype(jnp.bfloat16)


def join(piece, place, axis_name, stride):
    here = digit_of(axis_name, stride, 2)
    other = exchange(piece, axis_name, stride, 1)
    first = jnp.where(here == 0, piece, other)
    second = jnp.where(here == 0, other, piece)
    return jnp.concatenate([first, second], axis=place)


def scatter_rows(group, dp_size):
    digits = radices_of(dp_size)
    shape = tuple(r for _, r in reversed(digits))
    group = group.reshape(shape + (group.shape[0] // dp_size, group.shape[1]))
    for place, (stride, radix) in zip(range(len(digits) - 1, -1, -1), digits):
        group = scatter_digit(group, place, "dp", stride, radix)
    return group


def reduce_weight(gradient, dp_size, ctx_first, side):
    rows = gradient.shape[0] // dp_size
    if side == 0:
        gradient = gradient.reshape(dp_size, rows, -1)
    place = 1
    gradient = halve(gradient, place, "ctx", 1)
    if ctx_first:
        gradient = halve(gradient, place, "ctx", 2)
    flat = gradient.reshape(-1, gradient.shape[-1])
    flat = scatter_rows(flat, dp_size)
    if ctx_first:
        flat = join(flat, side, "ctx", 2)
    else:
        flat = flat.astype(jnp.float32) + exchange(flat, "ctx", 2, 1).astype(jnp.float32)
        flat = flat.astype(jnp.bfloat16)
    return join(flat, side, "ctx", 1).astype(jnp.float32)


def reduce_vector(group):
    for stride in (1, 2):
        group = group + exchange(group, "ctx", stride, 1)
    dp_size = group.shape[0]
    digits = radices_of(dp_size)
    group = group.reshape(tuple(r for _, r in reversed(digits)) + (-1,))
    for place, (stride, radix) in zip(range(len(digits) - 1, -1, -1), digits):
        here = digit_of("dp", stride, radix)
        total = lax.dynamic_index_in_dim(group, here, place, keepdims=False)
        for offset in range(1, radix):
            piece = lax.dynamic_index_in_dim(group, here ^ offset, place, keepdims=False)
            total = total + exchange(piece, "dp", stride, offset)
        group = total
    return group


def per_device(
    hidden_in,
    seg_ids,
    valid,
    w_query,
    b_query,
    w_key,
    w_value,
    b_value,
    w_out,
    b_out,
    gain_attn,
    shift_attn,
    w_up,
    b_up,
    w_down,
    b_down,
    gain_ffn,
    shift_ffn,
    pooled_text_gradient,
):
    row_count, group_size, model_width = hidden_in.shape
    token_count = row_count * group_size
    tokens_flat = hidden_in.reshape(token_count, model_width)
    residual = tokens_flat.astype(jnp.float32)
    gain_one = gain_attn.astype(jnp.float32)
    shift_one = shift_attn.astype(jnp.float32)
    gain_two = gain_ffn.astype(jnp.float32)
    shift_two = shift_ffn.astype(jnp.float32)
    ids_all = [seg_ids] + [exchange(seg_ids, "ctx", 1, o) for o in (1, 2, 3)]
    ids_all = jnp.stack(ids_all, axis=1).reshape(row_count, -1)
    x_one = exchange(hidden_in, "ctx", 1, 1)
    blocks, saved = [], []
    far = [exchange(hidden_in[r], "ctx", 2, 1) for r in range(row_count)]
    for r in range(row_count):
        blocks.append((hidden_in[r], x_one[r], far[r], exchange(far[r], "ctx", 1, 1)))
    wide = lambda vector: vector.astype(jnp.float32)[None]
    for r in range(row_count):
        saved.append(
            attend(
                blocks[r], seg_ids[r][:, None], ids_all[r][None], w_query, w_key, w_value,
                wide(b_query), wide(b_value),
            )
        )
    context = jnp.concatenate([item[3] for item in saved], axis=0)
    attn_out = matmul(context, w_out) + b_out.astype(jnp.float32)
    mixed_sum = residual + attn_out
    normed = layer_norm(mixed_sum, gain_one, shift_one)
    normed_bf = normed.astype(jnp.bfloat16)
    act_bf = gelu_exact(matmul(normed_bf, w_up) + b_up.astype(jnp.float32)).astype(jnp.bfloat16)
    ffn_out = matmul(act_bf, w_down) + b_down.astype(jnp.float32)
    summed = normed + ffn_out
    final_out = layer_norm(summed, gain_two, shift_two)
    text_membership = (
        (seg_ids[:, :, None] == jnp.arange(NSEG)[None, None, :]) & (valid[:, :, None] == 1)
    ).astype(jnp.float32)
    part_sums = jnp.einsum(
        "ofr,ofy->ory",
        text_membership,
        final_out.reshape(row_count, group_size, model_width),
        precision=lax.Precision.HIGHEST,
    )
    text_totals = part_sums
    for stride in (1, 2):
        part = text_totals.astype(jnp.bfloat16)
        other = exchange(part, "ctx", stride, 1)
        text_totals = part.astype(jnp.float32) + other.astype(jnp.float32)
    valid_all = [valid] + [exchange(valid, "ctx", 1, o) for o in (1, 2, 3)]
    valid_all = jnp.stack(valid_all, axis=1).reshape(row_count, -1)
    text_counts = jnp.sum(
        (
            (ids_all[:, :, None] == jnp.arange(NSEG)[None, None, :])
            & (valid_all[:, :, None] == 1)
        ).astype(jnp.float32),
        axis=1,
    )
    clamped_text_counts = jnp.maximum(text_counts, 1.0)[:, :, None]
    pooled = text_totals / clamped_text_counts
    grad_final = jnp.einsum(
        "heb,hbj->hej",
        text_membership,
        pooled_text_gradient / clamped_text_counts,
        precision=lax.Precision.HIGHEST,
    ).reshape(token_count, model_width)
    _, norm_two_back = jax.vjp(layer_norm, summed, gain_two, shift_two)
    grad_summed, grad_gain_two, grad_shift_two = norm_two_back(grad_final)
    grad_ffn = grad_summed.astype(jnp.bfloat16)
    grad_w_down = matmul_left(act_bf, grad_ffn)
    grad_b_down = jnp.sum(grad_ffn.astype(jnp.float32), axis=0)
    grad_act = matmul_right(grad_ffn, w_down)
    pre_again = matmul(normed_bf, w_up) + b_up.astype(jnp.float32)
    _, gelu_back = jax.vjp(gelu_exact, pre_again)
    grad_pre = gelu_back(grad_act)[0].astype(jnp.bfloat16)
    grad_w_up = matmul_left(normed_bf, grad_pre)
    grad_b_up = jnp.sum(grad_pre.astype(jnp.float32), axis=0)
    grad_normed = grad_summed + matmul_right(grad_pre, w_up)
    _, norm_one_back = jax.vjp(layer_norm, mixed_sum, gain_one, shift_one)
    grad_mixed, grad_gain_one, grad_shift_one = norm_one_back(grad_normed)
    grad_attn = grad_mixed.astype(jnp.bfloat16)
    grad_w_out = matmul_left(context, grad_attn)
    grad_b_out = jnp.sum(grad_attn.astype(jnp.float32), axis=0)
    grad_context = matmul_right(grad_attn, w_out).astype(jnp.bfloat16)
    grad_input, square_parts, bias_parts = [], [], []
    for r in range(row_count):
        tokens = slice(r * group_size, (r + 1) * group_size)
        q, k, v, context_row, lse = saved[r]
        dx_own, dx_one, dx_two, dx_three, dwq, dwk, dwv, biases = attend_back(
            blocks[r], q, k, v, context_row, grad_context[tokens], lse,
            seg_ids[r][None], ids_all[r][:, None], w_query, w_key, w_value,
        )
        from_one = exchange(jnp.stack([dx_one, dx_three]), "ctx", 1, 1).astype(jnp.float32)
        far_sum = (dx_two.astype(jnp.float32) + from_one[1]).astype(jnp.bfloat16)
        from_far = exchange(far_sum, "ctx", 2, 1).astype(jnp.float32)
        grad_input.append(grad_mixed[tokens] + dx_own + from_one[0] + from_far)
        square_parts.append((dwq, dwk, dwv))
        bias_parts.append(biases)
    add_up = lambda parts: sum(part.astype(jnp.float32) for part in parts)
    grad_w_query, grad_w_key, grad_w_value = (add_up(parts) for parts in zip(*square_parts))
    grad_b_query, grad_b_value = sum(bias_parts)
    grad_input = jnp.stack(grad_input)
    dp_size, ctx_size = lax.axis_size("dp"), lax.axis_size("ctx")
    ff_width = w_up.shape[1]
    rows_here, ff_here = model_width // dp_size, ff_width // dp_size
    up_sum = reduce_weight(grad_w_up, dp_size, True, 1)
    down_sum = reduce_weight(grad_w_down, dp_size, False, 0)
    square_sums = [
        reduce_weight(piece, dp_size, first, 1)
        for piece, first in (
            (grad_w_query, True), (grad_w_key, False), (grad_w_value, True), (grad_w_out, False)
        )
    ]
    vectors = [
        piece.reshape(dp_size, rows_here)
        for piece in (
            grad_b_query, grad_b_value, grad_b_out, grad_gain_one, grad_shift_one,
            grad_b_down, grad_gain_two, grad_shift_two,
        )
    ] + [grad_b_up.reshape(dp_size, ff_here)]
    sum_vector = reduce_vector(jnp.concatenate(vectors, axis=1))
    sums = [sum_vector[i * rows_here : (i + 1) * rows_here] for i in range(8)]
    sum_bu = sum_vector[8 * rows_here :]
    results = (
        square_sums[0], sums[0], square_sums[1], square_sums[2], sums[1], square_sums[3],
        sums[2], sums[3], sums[4], up_sum, sum_bu, down_sum, sums[5], sums[6], sums[7],
    )
    return (
        final_out.reshape(row_count, group_size, model_width).astype(jnp.bfloat16),
        pooled,
        grad_input.reshape(row_count, group_size, model_width).astype(jnp.bfloat16),
    ) + tuple(results)


def solution(mesh):
    placed = (
        P("dp", "ctx", None),
        P("dp", "ctx"),
        P("dp", "ctx"),
        P(),
        P(),
        P(),
        P(),
        P(),
        P(),
        P(),
        P(),
        P(),
        P(),
        P(),
        P(),
        P(),
        P(),
        P(),
        P("dp", None, None),
    )
    return jax.shard_map(
        per_device,
        mesh=mesh,
        in_specs=placed,
        out_specs=(
            P("dp", "ctx", None),
            P("dp", None, None),
            P("dp", "ctx", None),
            P("dp", None),
            P("dp"),
            P("dp", None),
            P("dp", None),
            P("dp"),
            P("dp", None),
            P("dp"),
            P("dp"),
            P("dp"),
            P("dp", None),
            P("dp"),
            P("dp", None),
            P("dp"),
            P("dp"),
            P("dp"),
        ),
        check_vma=False,
    )
```

```python
import jax
import jax.numpy as jnp
from jax import lax
from jax.experimental import pallas as pl
from jax.experimental.pallas import tpu as pltpu
from jax.sharding import PartitionSpec as P

HEADS = 12
HEAD_DIM = 64
NSEG = 16


eps = 1e-12


def layer_norm(values_in, gain_vec, shift_vec):
    centre = jnp.mean(values_in, axis=-1, keepdims=True)
    centred = values_in - centre
    spread = jnp.mean(centred * centred, axis=-1, keepdims=True)
    return centred * lax.rsqrt(spread + eps) * gain_vec + shift_vec


def gelu_exact(values_in):
    return jax.nn.gelu(values_in, approximate=False)


def matmul(left_side, right_side):
    return jnp.dot(left_side, right_side, preferred_element_type=jnp.float32)


def matmul_left(left_side, right_side):
    return lax.dot_general(
        left_side, right_side, (((0,), (0,)), ((), ())), preferred_element_type=jnp.float32
    )


def matmul_right(left_side, right_side):
    return lax.dot_general(
        left_side, right_side, (((1,), (1,)), ((), ())), preferred_element_type=jnp.float32
    )


PAIR = 2 * HEAD_DIM
MESH = pl.DeviceIdType.MESH
MASKED = -1e30


def dot_nt(left_side, right_side):
    return lax.dot_general(
        left_side, right_side, (((1,), (1,)), ((), ())), preferred_element_type=jnp.float32
    )


def dot_tn(left_side, right_side):
    return lax.dot_general(
        left_side, right_side, (((0,), (0,)), ((), ())), preferred_element_type=jnp.float32
    )


def split_heads(pair):
    lane = lax.broadcasted_iota(jnp.int32, pair.shape, 1)
    zero = jnp.zeros_like(pair)
    return jnp.concatenate(
        [jnp.where(lane < HEAD_DIM, pair, zero), jnp.where(lane < HEAD_DIM, zero, pair)], axis=0
    )


def attend_kernel(
    x_ref, ids_ref, w_query, w_key, w_value, b_query, b_value,
    q_out, context_out, lse_out, ids_out, x_hbm, k_hbm, v_hbm,
    x_got, k_ref, v_ref, bias_ref, stat_ref, send_sem, recv_sem, local_sem,
):
    rows_here, size, width = x_ref.shape
    me = lax.axis_index("ctx")
    one = me + 1 - 2 * (me % 2)
    two = (me + 2) % 4
    three = (one + 2) % 4
    low = jnp.bfloat16

    barrier = pltpu.get_barrier_semaphore()
    for peer in (one, two, three):
        pl.semaphore_signal(barrier, inc=1, device_id={"ctx": peer}, device_id_type=MESH)
    pl.semaphore_wait(barrier, 3)

    def send(source, target, slot, peer):
        return pltpu.make_async_remote_copy(
            src_ref=source, dst_ref=target, send_sem=send_sem.at[slot],
            recv_sem=recv_sem.at[slot], device_id={"ctx": peer}, device_id_type=MESH,
        )

    ids_out[0] = ids_ref[...]
    ids_sends = [send(ids_ref, ids_out.at[j + 1], j, peer) for j, peer in enumerate((one, two, three))]
    near = send(x_ref, x_got.at[0], 3, one)

    def far(r):
        return send(x_ref.at[r], x_got.at[1, r], 4 + r, two)

    def passed(r):
        return send(x_got.at[1, r], x_got.at[2, r], 4 + rows_here + r, one)

    far(0).start()
    near.start()
    for item in ids_sends:
        item.start()
    for r in range(1, rows_here):
        far(r).start()

    def project(r, x, j):
        rows = pl.ds(j * size, size)
        k_ref[r, rows, :] = matmul(x, w_key[...]).astype(low)
        v_ref[r, rows, :] = (matmul(x, w_value[...]) + b_value[...]).astype(low)

    def own_row(r, carry):
        x = x_ref[r]
        q = (matmul(x, w_query[...]) + b_query[...]).astype(low)
        q_out[r] = (q * HEAD_DIM ** (-0.5)).astype(low)
        project(r, x, 0)
        return carry

    lax.fori_loop(0, rows_here, own_row, 0)
    near.wait_recv()

    def near_row(r, carry):
        project(r, x_got[0, r], 1)
        return carry

    lax.fori_loop(0, rows_here, near_row, 0)
    for item in ids_sends:
        item.wait_recv()
    lane = lax.broadcasted_iota(jnp.int32, (size, PAIR), 1)
    far(0).wait_recv()
    passed(0).start()

    def keep(r):
        return (
            pltpu.make_async_copy(k_ref.at[r], k_hbm.at[r], local_sem.at[0, r]),
            pltpu.make_async_copy(v_ref.at[r], v_hbm.at[r], local_sem.at[1, r]),
        )

    for r in range(rows_here):
        project(r, x_got[1, r], 2)
        passed(r).wait_recv()
        project(r, x_got[2, r], 3)
        for item in keep(r):
            item.start()
        seg_query = jnp.broadcast_to(
            ids_ref[r : r + 1, :].astype(jnp.float32), (PAIR, size)
        ).T[:, :1]
        for j in range(4):
            seg_key = ids_out[j, r : r + 1, :].astype(jnp.float32)
            bias_ref[:, j * size : (j + 1) * size] = jnp.where(seg_query == seg_key, 0.0, MASKED)
        stat_ref[...] = jnp.zeros_like(stat_ref)

        def one_pair(pair, carry, r=r):
            columns = pl.ds(pl.multiple_of(pair * PAIR, PAIR), PAIR)
            both = split_heads(q_out[r, :, columns])
            scores = dot_nt(both, k_ref[r, :, columns])
            scores = scores.reshape(2, size, scores.shape[1]) + bias_ref[...][None]
            top = jnp.max(scores, axis=-1, keepdims=True)
            weight = jnp.exp(scores - top)
            total = jnp.sum(weight, axis=-1, keepdims=True)
            mixed = matmul(
                weight.astype(low).reshape(2 * size, -1), v_ref[r, :, columns]
            ).reshape(2, size, PAIR) / total
            context_out[r, :, columns] = jnp.where(lane < HEAD_DIM, mixed[0], mixed[1]).astype(low)
            lse = top + jnp.log(total)
            stat = stat_ref[...]
            stat = jnp.where(lane == 2 * pair, lse[0], stat)
            stat_ref[...] = jnp.where(lane == 2 * pair + 1, lse[1], stat)
            return carry

        lax.fori_loop(0, HEADS // 2, one_pair, 0)
        lse_out[r] = stat_ref[...].T[: lse_out.shape[1]]
        if r + 1 < rows_here:
            far(r + 1).wait_recv()
            passed(r + 1).start()
    keep_x = pltpu.make_async_copy(x_got, x_hbm, local_sem.at[2, 0])
    keep_x.start()
    for r in range(rows_here):
        for item in keep(r):
            item.wait()
        far(r).wait_send()
        passed(r).wait_send()
    near.wait_send()
    for item in ids_sends:
        item.wait_send()
    keep_x.wait()


def attend(x, ids, w_query, w_key, w_value, b_query, b_value):
    rows_here, size, width = x.shape
    keys = size * 4
    low = jnp.bfloat16
    whole = pl.BlockSpec(memory_space=pltpu.VMEM)
    outside = pl.BlockSpec(memory_space=pl.ANY)
    slots = 4 + 2 * rows_here
    return pl.pallas_call(
        attend_kernel,
        out_shape=(
            jax.ShapeDtypeStruct((rows_here, size, width), low),
            jax.ShapeDtypeStruct((rows_here, size, width), low),
            jax.ShapeDtypeStruct((rows_here, 16, size), jnp.float32),
            jax.ShapeDtypeStruct((4,) + ids.shape, jnp.int32),
            jax.ShapeDtypeStruct((3,) + x.shape, low),
            jax.ShapeDtypeStruct((rows_here, keys, width), low),
            jax.ShapeDtypeStruct((rows_here, keys, width), low),
        ),
        in_specs=[whole] * 7,
        out_specs=(whole, whole, whole, whole, outside, outside, outside),
        scratch_shapes=[
            pltpu.VMEM((3,) + x.shape, low),
            pltpu.VMEM((rows_here, keys, width), low),
            pltpu.VMEM((rows_here, keys, width), low),
            pltpu.VMEM((size, keys), jnp.float32),
            pltpu.VMEM((size, PAIR), jnp.float32),
            pltpu.SemaphoreType.DMA((slots,)),
            pltpu.SemaphoreType.DMA((slots,)),
            pltpu.SemaphoreType.DMA((3, rows_here)),
        ],
        compiler_params=pltpu.CompilerParams(
            vmem_limit_bytes=56 * 2**20, collective_id=0, has_side_effects=True
        ),
        cost_estimate=pl.CostEstimate(
            flops=rows_here * (2 * (size + 2 * keys) * width * width + 16 * size * keys * width),
            bytes_accessed=2 * (3 * width * width + 9 * keys * width),
            transcendentals=rows_here * HEADS * size * keys,
        ),
    )(x, ids, w_query, w_key, w_value, b_query, b_value)


def attend_back_kernel(
    x_own, x_one, x_two, x_three, q_ref, k_ref, v_ref, context_ref, grad_ref, lse_ref,
    seg_query, seg_key, w_query, w_key, w_value,
    dx_own, dx_one, dx_two, dx_three, dwq_out, dwk_out, dwv_out, bias_out,
    bias_ref, dq_ref, dk_ref, dv_ref,
):
    size, width = x_own.shape
    low = jnp.bfloat16
    blocks = k_ref.shape[0] // size
    bias_ref[...] = jnp.where(seg_key[...] == seg_query[...], 0.0, MASKED)
    row = lax.broadcasted_iota(jnp.int32, (PAIR, size), 0)

    def one_pair(pair, carry):
        columns = pl.ds(pl.multiple_of(pair * PAIR, PAIR), PAIR)
        grad = grad_ref[:, columns]
        q_both = split_heads(q_ref[:, columns])
        g_both = split_heads(grad)
        product = (grad.astype(jnp.float32) * context_ref[:, columns].astype(jnp.float32)).T
        delta = jnp.concatenate(
            [
                jnp.sum(product[:HEAD_DIM], axis=0, keepdims=True),
                jnp.sum(product[HEAD_DIM:], axis=0, keepdims=True),
            ],
            axis=1,
        )
        lse = jnp.concatenate(
            [lse_ref[pl.ds(2 * pair, 1), :], lse_ref[pl.ds(2 * pair + 1, 1), :]], axis=1
        )
        dq = jnp.zeros((PAIR, 2 * size), jnp.float32)
        for j in range(blocks):
            rows = pl.ds(j * size, size)
            keys = k_ref[rows, columns]
            bias = bias_ref[rows, :]
            bias = jnp.concatenate([bias, bias], axis=1)
            probs = jnp.exp(dot_nt(keys, q_both) + bias - lse)
            grad_s = probs * (dot_nt(v_ref[rows, columns], g_both) - delta)
            grad_s = grad_s.astype(low)
            dv_ref[rows, columns] = matmul(probs.astype(low), g_both).astype(low)
            dk_ref[rows, columns] = matmul(grad_s, q_both).astype(low)
            dq = dq + matmul(keys.T, grad_s)
        dq = jnp.where(row < HEAD_DIM, dq[:, :size], dq[:, size:]) * HEAD_DIM ** (-0.5)
        dq_ref[:, columns] = dq.T.astype(low)
        return carry

    lax.fori_loop(0, HEADS // 2, one_pair, 0)
    for j, out in enumerate((dx_own, dx_one, dx_two, dx_three)):
        rows = pl.ds(j * size, size)
        part = dot_nt(dk_ref[rows, :], w_key[...]) + dot_nt(dv_ref[rows, :], w_value[...])
        if j == 0:
            part = part + dot_nt(dq_ref[...], w_query[...])
        out[...] = part.astype(out.dtype)
    dwq_out[...] = dot_tn(x_own[...], dq_ref[...]).astype(low)
    for source, out in ((dk_ref, dwk_out), (dv_ref, dwv_out)):
        total = jnp.zeros((width, width), jnp.float32)
        for j, x_ref in enumerate((x_own, x_one, x_two, x_three)):
            total = total + dot_tn(x_ref[...], source[pl.ds(j * size, size), :])
        out[...] = total.astype(low)
    bias_out[0:1, :] = jnp.sum(dq_ref[...].astype(jnp.float32), axis=0, keepdims=True)
    bias_out[1:2, :] = jnp.sum(dv_ref[...].astype(jnp.float32), axis=0, keepdims=True)


def attend_back(blocks, q, k, v, context, grad, lse, seg_query, seg_key, w_query, w_key, w_value):
    size, width = blocks[0].shape
    keys = size * len(blocks)
    low = jnp.bfloat16
    token_block = jax.ShapeDtypeStruct((size, width), low)
    square = jax.ShapeDtypeStruct((width, width), low)
    return pl.pallas_call(
        attend_back_kernel,
        out_shape=(
            jax.ShapeDtypeStruct((size, width), jnp.float32),
            token_block, token_block, token_block, square, square, square,
            jax.ShapeDtypeStruct((2, width), jnp.float32),
        ),
        scratch_shapes=[
            pltpu.VMEM((keys, size), jnp.float32),
            pltpu.VMEM((size, width), low),
            pltpu.VMEM((keys, width), low),
            pltpu.VMEM((keys, width), low),
        ],
        compiler_params=pltpu.CompilerParams(vmem_limit_bytes=56 * 2**20),
        cost_estimate=pl.CostEstimate(
            flops=4 * (size + 2 * keys) * width * width + 40 * size * keys * width,
            bytes_accessed=2 * (6 * width * width + 5 * keys * width),
            transcendentals=HEADS * size * keys,
        ),
    )(*blocks, q, k, v, context, grad, lse, seg_query, seg_key, w_query, w_key, w_value)


def radices_of(count):
    if count == 8:
        return ((1, 2), (2, 4))
    digits = []
    stride = 1
    while stride < count:
        digits.append((stride, 2))
        stride *= 2
    return tuple(digits)


def exchange(piece, axis_name, stride, offset):
    count = lax.axis_size(axis_name)
    pairs = [(i, i ^ (offset * stride)) for i in range(count)]
    return lax.ppermute(piece, axis_name, pairs)


def digit_of(axis_name, stride, radix):
    return (lax.axis_index(axis_name) // stride) % radix


def scatter_digit(pieces, place, axis_name, stride, radix):
    here = digit_of(axis_name, stride, radix)
    received = [
        exchange(
            lax.dynamic_index_in_dim(pieces, here ^ offset, place, keepdims=False).astype(
                jnp.bfloat16
            ),
            axis_name, stride, offset,
        )
        for offset in range(1, radix)
    ]
    total = lax.dynamic_index_in_dim(pieces, here, place, keepdims=False).astype(jnp.float32)
    for item in received:
        total = total + item.astype(jnp.float32)
    return total.astype(jnp.bfloat16)


def halve(piece, place, axis_name, stride):
    half = piece.shape[place] // 2
    here = digit_of(axis_name, stride, 2)
    sent = lax.dynamic_slice_in_dim(piece, (1 - here) * half, half, place).astype(jnp.bfloat16)
    kept = lax.dynamic_slice_in_dim(piece, here * half, half, place).astype(jnp.float32)
    return (kept + exchange(sent, axis_name, stride, 1).astype(jnp.float32)).astype(jnp.bfloat16)


def join(piece, place, axis_name, stride):
    here = digit_of(axis_name, stride, 2)
    other = exchange(piece, axis_name, stride, 1)
    first = jnp.where(here == 0, piece, other)
    second = jnp.where(here == 0, other, piece)
    return jnp.concatenate([first, second], axis=place)


def scatter_rows(group, dp_size):
    digits = radices_of(dp_size)
    shape = tuple(r for _, r in reversed(digits))
    group = group.reshape(shape + (group.shape[0] // dp_size, group.shape[1]))
    for place, (stride, radix) in zip(range(len(digits) - 1, -1, -1), digits):
        group = scatter_digit(group, place, "dp", stride, radix)
    return group


def reduce_weight(gradient, dp_size, ctx_first, side):
    rows = gradient.shape[0] // dp_size
    if side == 0:
        gradient = gradient.reshape(dp_size, rows, -1)
    place = 1
    gradient = halve(gradient, place, "ctx", 1)
    if ctx_first:
        gradient = halve(gradient, place, "ctx", 2)
    flat = gradient.reshape(-1, gradient.shape[-1])
    flat = scatter_rows(flat, dp_size)
    if ctx_first:
        flat = join(flat, side, "ctx", 2)
    else:
        flat = flat.astype(jnp.float32) + exchange(flat, "ctx", 2, 1).astype(jnp.float32)
        flat = flat.astype(jnp.bfloat16)
    return join(flat, side, "ctx", 1).astype(jnp.float32)


def reduce_vector(group):
    for stride in (1, 2):
        group = group + exchange(group, "ctx", stride, 1)
    dp_size = group.shape[0]
    digits = radices_of(dp_size)
    group = group.reshape(tuple(r for _, r in reversed(digits)) + (-1,))
    for place, (stride, radix) in zip(range(len(digits) - 1, -1, -1), digits):
        here = digit_of("dp", stride, radix)
        total = lax.dynamic_index_in_dim(group, here, place, keepdims=False)
        for offset in range(1, radix):
            piece = lax.dynamic_index_in_dim(group, here ^ offset, place, keepdims=False)
            total = total + exchange(piece, "dp", stride, offset)
        group = total
    return group


def per_device(
    hidden_in,
    seg_ids,
    valid,
    w_query,
    b_query,
    w_key,
    w_value,
    b_value,
    w_out,
    b_out,
    gain_attn,
    shift_attn,
    w_up,
    b_up,
    w_down,
    b_down,
    gain_ffn,
    shift_ffn,
    pooled_text_gradient,
):
    row_count, group_size, model_width = hidden_in.shape
    token_count = row_count * group_size
    tokens_flat = hidden_in.reshape(token_count, model_width)
    residual = tokens_flat.astype(jnp.float32)
    gain_one = gain_attn.astype(jnp.float32)
    shift_one = shift_attn.astype(jnp.float32)
    gain_two = gain_ffn.astype(jnp.float32)
    shift_two = shift_ffn.astype(jnp.float32)
    wide = lambda vector: vector.astype(jnp.float32)[None]
    ids = jnp.concatenate([seg_ids, valid], axis=0)
    ids = jnp.pad(ids, ((0, 8 - ids.shape[0]), (0, 0)))
    q_all, context, lse_all, ids_got, x_got, k_all, v_all = attend(
        hidden_in, ids, w_query, w_key, w_value, wide(b_query), wide(b_value)
    )
    blocks = [
        (hidden_in[r], x_got[0, r], x_got[1, r], x_got[2, r]) for r in range(row_count)
    ]
    ids_all = ids_got[:, :row_count].transpose(1, 0, 2).reshape(row_count, -1)
    valid_all = ids_got[:, row_count : 2 * row_count].transpose(1, 0, 2).reshape(row_count, -1)
    context = context.reshape(token_count, model_width)
    attn_out = matmul(context, w_out) + b_out.astype(jnp.float32)
    mixed_sum = residual + attn_out
    normed = layer_norm(mixed_sum, gain_one, shift_one)
    normed_bf = normed.astype(jnp.bfloat16)
    act_bf = gelu_exact(matmul(normed_bf, w_up) + b_up.astype(jnp.float32)).astype(jnp.bfloat16)
    ffn_out = matmul(act_bf, w_down) + b_down.astype(jnp.float32)
    summed = normed + ffn_out
    final_out = layer_norm(summed, gain_two, shift_two)
    text_membership = (
        (seg_ids[:, :, None] == jnp.arange(NSEG)[None, None, :]) & (valid[:, :, None] == 1)
    ).astype(jnp.float32)
    part_sums = jnp.einsum(
        "ofr,ofy->ory",
        text_membership,
        final_out.reshape(row_count, group_size, model_width),
        precision=lax.Precision.HIGHEST,
    )
    text_totals = part_sums
    for stride in (1, 2):
        part = text_totals.astype(jnp.bfloat16)
        other = exchange(part, "ctx", stride, 1)
        text_totals = part.astype(jnp.float32) + other.astype(jnp.float32)
    text_counts = jnp.sum(
        (
            (ids_all[:, :, None] == jnp.arange(NSEG)[None, None, :])
            & (valid_all[:, :, None] == 1)
        ).astype(jnp.float32),
        axis=1,
    )
    clamped_text_counts = jnp.maximum(text_counts, 1.0)[:, :, None]
    pooled = text_totals / clamped_text_counts
    grad_final = jnp.einsum(
        "heb,hbj->hej",
        text_membership,
        pooled_text_gradient / clamped_text_counts,
        precision=lax.Precision.HIGHEST,
    ).reshape(token_count, model_width)
    _, norm_two_back = jax.vjp(layer_norm, summed, gain_two, shift_two)
    grad_summed, grad_gain_two, grad_shift_two = norm_two_back(grad_final)
    grad_ffn = grad_summed.astype(jnp.bfloat16)
    grad_w_down = matmul_left(act_bf, grad_ffn)
    grad_b_down = jnp.sum(grad_ffn.astype(jnp.float32), axis=0)
    grad_act = matmul_right(grad_ffn, w_down)
    pre_again = matmul(normed_bf, w_up) + b_up.astype(jnp.float32)
    _, gelu_back = jax.vjp(gelu_exact, pre_again)
    grad_pre = gelu_back(grad_act)[0].astype(jnp.bfloat16)
    grad_w_up = matmul_left(normed_bf, grad_pre)
    grad_b_up = jnp.sum(grad_pre.astype(jnp.float32), axis=0)
    grad_normed = grad_summed + matmul_right(grad_pre, w_up)
    _, norm_one_back = jax.vjp(layer_norm, mixed_sum, gain_one, shift_one)
    grad_mixed, grad_gain_one, grad_shift_one = norm_one_back(grad_normed)
    grad_attn = grad_mixed.astype(jnp.bfloat16)
    grad_w_out = matmul_left(context, grad_attn)
    grad_b_out = jnp.sum(grad_attn.astype(jnp.float32), axis=0)
    grad_context = matmul_right(grad_attn, w_out).astype(jnp.bfloat16)
    grad_input, square_parts, bias_parts = [], [], []
    for r in range(row_count):
        tokens = slice(r * group_size, (r + 1) * group_size)
        q, k, v, lse = q_all[r], k_all[r], v_all[r], lse_all[r]
        dx_own, dx_one, dx_two, dx_three, dwq, dwk, dwv, biases = attend_back(
            blocks[r], q, k, v, context[tokens], grad_context[tokens], lse,
            seg_ids[r][None], ids_all[r][:, None], w_query, w_key, w_value,
        )
        from_one = exchange(jnp.stack([dx_one, dx_three]), "ctx", 1, 1).astype(jnp.float32)
        far_sum = (dx_two.astype(jnp.float32) + from_one[1]).astype(jnp.bfloat16)
        from_far = exchange(far_sum, "ctx", 2, 1).astype(jnp.float32)
        grad_input.append(grad_mixed[tokens] + dx_own + from_one[0] + from_far)
        square_parts.append((dwq, dwk, dwv))
        bias_parts.append(biases)
    add_up = lambda parts: sum(part.astype(jnp.float32) for part in parts)
    grad_w_query, grad_w_key, grad_w_value = (add_up(parts) for parts in zip(*square_parts))
    grad_b_query, grad_b_value = sum(bias_parts)
    grad_input = jnp.stack(grad_input)
    dp_size, ctx_size = lax.axis_size("dp"), lax.axis_size("ctx")
    ff_width = w_up.shape[1]
    rows_here, ff_here = model_width // dp_size, ff_width // dp_size
    up_sum = reduce_weight(grad_w_up, dp_size, True, 1)
    down_sum = reduce_weight(grad_w_down, dp_size, False, 0)
    square_sums = [
        reduce_weight(piece, dp_size, first, 1)
        for piece, first in (
            (grad_w_query, True), (grad_w_key, False), (grad_w_value, True), (grad_w_out, False)
        )
    ]
    vectors = [
        piece.reshape(dp_size, rows_here)
        for piece in (
            grad_b_query, grad_b_value, grad_b_out, grad_gain_one, grad_shift_one,
            grad_b_down, grad_gain_two, grad_shift_two,
        )
    ] + [grad_b_up.reshape(dp_size, ff_here)]
    sum_vector = reduce_vector(jnp.concatenate(vectors, axis=1))
    sums = [sum_vector[i * rows_here : (i + 1) * rows_here] for i in range(8)]
    sum_bu = sum_vector[8 * rows_here :]
    results = (
        square_sums[0], sums[0], square_sums[1], square_sums[2], sums[1], square_sums[3],
        sums[2], sums[3], sums[4], up_sum, sum_bu, down_sum, sums[5], sums[6], sums[7],
    )
    return (
        final_out.reshape(row_count, group_size, model_width).astype(jnp.bfloat16),
        pooled,
        grad_input.reshape(row_count, group_size, model_width).astype(jnp.bfloat16),
    ) + tuple(results)


def solution(mesh):
    placed = (
        P("dp", "ctx", None),
        P("dp", "ctx"),
        P("dp", "ctx"),
        P(),
        P(),
        P(),
        P(),
        P(),
        P(),
        P(),
        P(),
        P(),
        P(),
        P(),
        P(),
        P(),
        P(),
        P(),
        P("dp", None, None),
    )
    return jax.shard_map(
        per_device,
        mesh=mesh,
        in_specs=placed,
        out_specs=(
            P("dp", "ctx", None),
            P("dp", None, None),
            P("dp", "ctx", None),
            P("dp", None),
            P("dp"),
            P("dp", None),
            P("dp", None),
            P("dp"),
            P("dp", None),
            P("dp"),
            P("dp"),
            P("dp"),
            P("dp", None),
            P("dp"),
            P("dp", None),
            P("dp"),
            P("dp"),
            P("dp"),
        ),
        check_vma=False,
    )
```

```python
import functools

import jax
import jax.numpy as jnp
from jax import lax
from jax.experimental import pallas as pl
from jax.experimental.pallas import tpu as pltpu
from jax.sharding import PartitionSpec as P

HEADS = 12
HEAD_DIM = 64
NSEG = 16


eps = 1e-12


def layer_norm(values_in, gain_vec, shift_vec):
    centre = jnp.mean(values_in, axis=-1, keepdims=True)
    centred = values_in - centre
    spread = jnp.mean(centred * centred, axis=-1, keepdims=True)
    return centred * lax.rsqrt(spread + eps) * gain_vec + shift_vec


def gelu_exact(values_in):
    return jax.nn.gelu(values_in, approximate=False)


def matmul(left_side, right_side):
    return jnp.dot(left_side, right_side, preferred_element_type=jnp.float32)


def matmul_left(left_side, right_side):
    return lax.dot_general(
        left_side, right_side, (((0,), (0,)), ((), ())), preferred_element_type=jnp.float32
    )


def matmul_right(left_side, right_side):
    return lax.dot_general(
        left_side, right_side, (((1,), (1,)), ((), ())), preferred_element_type=jnp.float32
    )


PAIR = 2 * HEAD_DIM
MESH = pl.DeviceIdType.MESH
MASKED = -1e30


def dot_nt(left_side, right_side):
    return lax.dot_general(
        left_side, right_side, (((1,), (1,)), ((), ())), preferred_element_type=jnp.float32
    )


def dot_tn(left_side, right_side):
    return lax.dot_general(
        left_side, right_side, (((0,), (0,)), ((), ())), preferred_element_type=jnp.float32
    )


def split_heads(pair):
    lane = lax.broadcasted_iota(jnp.int32, pair.shape, 1)
    zero = jnp.zeros_like(pair)
    return jnp.concatenate(
        [jnp.where(lane < HEAD_DIM, pair, zero), jnp.where(lane < HEAD_DIM, zero, pair)], axis=0
    )


def attend_kernel(
    x_ref, ids_ref, w_query, w_key, w_value, b_query, b_value,
    q_out, context_out, lse_out, ids_out, x_hbm, k_hbm, v_hbm,
    x_got, k_ref, v_ref, bias_ref, stat_ref, send_sem, recv_sem, local_sem,
):
    rows_here, size, width = x_ref.shape
    me = lax.axis_index("ctx")
    one = me + 1 - 2 * (me % 2)
    two = (me + 2) % 4
    three = (one + 2) % 4
    low = jnp.bfloat16

    barrier = pltpu.get_barrier_semaphore()
    for peer in (one, two, three):
        pl.semaphore_signal(barrier, inc=1, device_id={"ctx": peer}, device_id_type=MESH)
    pl.semaphore_wait(barrier, 3)

    def send(source, target, slot, peer):
        return pltpu.make_async_remote_copy(
            src_ref=source, dst_ref=target, send_sem=send_sem.at[slot],
            recv_sem=recv_sem.at[slot], device_id={"ctx": peer}, device_id_type=MESH,
        )

    ids_out[0] = ids_ref[...]
    ids_sends = [send(ids_ref, ids_out.at[j + 1], j, peer) for j, peer in enumerate((one, two, three))]
    near = send(x_ref, x_got.at[0], 3, one)

    def far(r):
        return send(x_ref.at[r], x_got.at[1, r], 4 + r, two)

    def passed(r):
        return send(x_got.at[1, r], x_got.at[2, r], 4 + rows_here + r, one)

    far(0).start()
    near.start()
    for item in ids_sends:
        item.start()
    for r in range(1, rows_here):
        far(r).start()

    def project(r, x, j):
        rows = pl.ds(j * size, size)
        k_ref[r, rows, :] = matmul(x, w_key[...]).astype(low)
        v_ref[r, rows, :] = (matmul(x, w_value[...]) + b_value[...]).astype(low)

    def own_row(r, carry):
        x = x_ref[r]
        q = (matmul(x, w_query[...]) + b_query[...]).astype(low)
        q_out[r] = (q * HEAD_DIM ** (-0.5)).astype(low)
        project(r, x, 0)
        return carry

    lax.fori_loop(0, rows_here, own_row, 0)
    near.wait_recv()

    def near_row(r, carry):
        project(r, x_got[0, r], 1)
        return carry

    lax.fori_loop(0, rows_here, near_row, 0)
    for item in ids_sends:
        item.wait_recv()
    lane = lax.broadcasted_iota(jnp.int32, (size, PAIR), 1)
    far(0).wait_recv()
    passed(0).start()

    def keep(r):
        return (
            pltpu.make_async_copy(k_ref.at[r], k_hbm.at[r], local_sem.at[0, r]),
            pltpu.make_async_copy(v_ref.at[r], v_hbm.at[r], local_sem.at[1, r]),
        )

    for r in range(rows_here):
        project(r, x_got[1, r], 2)
        passed(r).wait_recv()
        project(r, x_got[2, r], 3)
        for item in keep(r):
            item.start()
        seg_query = jnp.broadcast_to(
            ids_ref[r : r + 1, :].astype(jnp.float32), (PAIR, size)
        ).T[:, :1]
        for j in range(4):
            seg_key = ids_out[j, r : r + 1, :].astype(jnp.float32)
            bias_ref[:, j * size : (j + 1) * size] = jnp.where(seg_query == seg_key, 0.0, MASKED)
        stat_ref[...] = jnp.zeros_like(stat_ref)

        def one_pair(pair, carry, r=r):
            columns = pl.ds(pl.multiple_of(pair * PAIR, PAIR), PAIR)
            both = split_heads(q_out[r, :, columns])
            scores = dot_nt(both, k_ref[r, :, columns])
            scores = scores.reshape(2, size, scores.shape[1]) + bias_ref[...][None]
            top = jnp.max(scores, axis=-1, keepdims=True)
            weight = jnp.exp(scores - top)
            total = jnp.sum(weight, axis=-1, keepdims=True)
            mixed = matmul(
                weight.astype(low).reshape(2 * size, -1), v_ref[r, :, columns]
            ).reshape(2, size, PAIR) / total
            context_out[r, :, columns] = jnp.where(lane < HEAD_DIM, mixed[0], mixed[1]).astype(low)
            lse = top + jnp.log(total)
            stat = stat_ref[...]
            stat = jnp.where(lane == 2 * pair, lse[0], stat)
            stat_ref[...] = jnp.where(lane == 2 * pair + 1, lse[1], stat)
            return carry

        lax.fori_loop(0, HEADS // 2, one_pair, 0)
        lse_out[r] = stat_ref[...].T[: lse_out.shape[1]]
        if r + 1 < rows_here:
            far(r + 1).wait_recv()
            passed(r + 1).start()
    keep_x = pltpu.make_async_copy(x_got, x_hbm, local_sem.at[2, 0])
    keep_x.start()
    for r in range(rows_here):
        for item in keep(r):
            item.wait()
        far(r).wait_send()
        passed(r).wait_send()
    near.wait_send()
    for item in ids_sends:
        item.wait_send()
    keep_x.wait()


def attend(x, ids, w_query, w_key, w_value, b_query, b_value):
    rows_here, size, width = x.shape
    keys = size * 4
    low = jnp.bfloat16
    whole = pl.BlockSpec(memory_space=pltpu.VMEM)
    outside = pl.BlockSpec(memory_space=pl.ANY)
    slots = 4 + 2 * rows_here
    return pl.pallas_call(
        attend_kernel,
        out_shape=(
            jax.ShapeDtypeStruct((rows_here, size, width), low),
            jax.ShapeDtypeStruct((rows_here, size, width), low),
            jax.ShapeDtypeStruct((rows_here, 16, size), jnp.float32),
            jax.ShapeDtypeStruct((4,) + ids.shape, jnp.int32),
            jax.ShapeDtypeStruct((3,) + x.shape, low),
            jax.ShapeDtypeStruct((rows_here, keys, width), low),
            jax.ShapeDtypeStruct((rows_here, keys, width), low),
        ),
        in_specs=[whole] * 7,
        out_specs=(whole, whole, whole, whole, outside, outside, outside),
        scratch_shapes=[
            pltpu.VMEM((3,) + x.shape, low),
            pltpu.VMEM((rows_here, keys, width), low),
            pltpu.VMEM((rows_here, keys, width), low),
            pltpu.VMEM((size, keys), jnp.float32),
            pltpu.VMEM((size, PAIR), jnp.float32),
            pltpu.SemaphoreType.DMA((slots,)),
            pltpu.SemaphoreType.DMA((slots,)),
            pltpu.SemaphoreType.DMA((3, rows_here)),
        ],
        compiler_params=pltpu.CompilerParams(
            vmem_limit_bytes=56 * 2**20, collective_id=0, has_side_effects=True
        ),
        cost_estimate=pl.CostEstimate(
            flops=rows_here * (2 * (size + 2 * keys) * width * width + 16 * size * keys * width),
            bytes_accessed=2 * (3 * width * width + 9 * keys * width),
            transcendentals=rows_here * HEADS * size * keys,
        ),
    )(x, ids, w_query, w_key, w_value, b_query, b_value)


class Links:
    def __init__(self, send_sem, recv_sem):
        self.send_sem, self.recv_sem = send_sem, recv_sem
        self.slots, self.copies = {}, {}

    def start(self, name, source, target, device):
        slot = self.slots.setdefault(name, len(self.slots))
        copy = pltpu.make_async_remote_copy(
            src_ref=source, dst_ref=target, send_sem=self.send_sem.at[slot],
            recv_sem=self.recv_sem.at[slot], device_id=device, device_id_type=MESH,
        )
        copy.start()
        self.copies[name] = copy

    def arrived(self, *names):
        for name in names:
            self.copies[name].wait_recv()

    def finish(self):
        for copy in self.copies.values():
            copy.wait_send()


def add_into(target, others, count):
    def one(i, carry):
        total = target[i].astype(jnp.float32)
        for other in others:
            total = total + other[i].astype(jnp.float32)
        target[i] = total.astype(target.dtype)
        return carry

    lax.fori_loop(0, count, one, 0)


def add_up(parts):
    total = parts[0].astype(jnp.float32)
    for part in parts[1:]:
        total = total + part.astype(jnp.float32)
    return total


def attend_back_kernel(
    fused,
    x_ref, ids_ref, lse_ref, w_query, w_key, w_value, pool_ref, count_ref, vector_ref,
    x_hbm, q_hbm, k_hbm, v_hbm, context_hbm, grad_hbm, mixed_hbm, up_hbm, down_hbm, out_hbm,
    dx_out, pool_out, vector_out, square_out, up_out, down_out, wo_out,
    x_got, q_ref, k_ref, v_ref, context_ref, grad_ref, bias_ref, dq_ref, dk_ref, dv_ref, dw_ref,
    dx_acc, dx_sent, dx_far, dx_near_got, dx_far_got, pool_parts, pool_got, vec_parts, vec_got,
    gb_ref, gb_got, s1_x, s1_y, s1_z, s2_y, s2_z, s2_s, s2_x,
    u_ref, u_x, u_y, u_z, d_ref, d_y, d_z, d_s, d_x, o_ref, o_y, o_z, o_s, o_x,
    send_sem, recv_sem, row_sem, local_sem,
):
    rows_here, size, width = x_ref.shape
    half = width // 2
    low = jnp.bfloat16
    me, place = lax.axis_index("ctx"), lax.axis_index("dp")
    core, side = me % 2, me // 2
    near, across = me + 1 - 2 * core, (me + 2) % 4
    near_dev, across_dev = {"ctx": near}, {"ctx": across}
    y, z = place % 2, place // 2
    y_dev = {"dp": place + 1 - 2 * y}
    z_at = (z + 1 - 2 * (z % 2), (z + 2) % 4, 3 - z)
    z_dev = [{"dp": other * 2 + y} for other in z_at]
    peers = [near_dev, across_dev] + ([y_dev] + z_dev if fused else [])

    barrier = pltpu.get_barrier_semaphore()
    for peer in peers:
        pl.semaphore_signal(barrier, inc=1, device_id=peer, device_id_type=MESH)
    pl.semaphore_wait(barrier, len(peers))
    links = Links(send_sem, recv_sem)

    def load_row(r):
        slot = r % 2
        pairs = (
            (k_hbm, k_ref), (v_hbm, v_ref), (q_hbm, q_ref), (context_hbm, context_ref),
            (grad_hbm, grad_ref),
        )
        copies = [
            pltpu.make_async_copy(source.at[r], target.at[slot], row_sem.at[slot, i])
            for i, (source, target) in enumerate(pairs)
        ]
        return copies + [
            pltpu.make_async_copy(x_hbm.at[:, r], x_got.at[slot], row_sem.at[slot, 5])
        ]

    for item in load_row(0):
        item.start()
    load_mixed = pltpu.make_async_copy(mixed_hbm, dx_acc, local_sem.at[0])
    load_mixed.start()
    links.start("pool0", pool_ref, pool_got.at[0], near_dev)
    if fused:
        mine = pl.ds(pl.multiple_of(side * width, 128), width)
        other = pl.ds(pl.multiple_of((1 - side) * width, 128), width)
        links.start("up_x", up_hbm.at[:, :, :, other], u_x, across_dev)
        links.start("down_y", down_hbm.at[:, 1 - y], d_y, y_dev)
        links.start("out_y", out_hbm.at[:, 1 - y], o_y, y_dev)
        load_parts = [
            pltpu.make_async_copy(up_hbm.at[:, :, :, mine], u_ref, local_sem.at[1]),
            pltpu.make_async_copy(down_hbm.at[:, y], d_ref, local_sem.at[2]),
            pltpu.make_async_copy(out_hbm.at[:, y], o_ref, local_sem.at[3]),
        ]
        for item in load_parts:
            item.start()

    def step_one():
        links.arrived("pool0")
        pool_parts[...] = add_up([pool_ref[...], pool_got[0]]).astype(low)
        links.start("pool1", pool_parts, pool_got.at[1], across_dev)
        if not fused:
            return
        for item in load_parts:
            item.wait()
        links.arrived("down_y", "out_y")
        add_into(d_ref, [d_y], 4)
        add_into(o_ref, [o_y], 4)
        for o in range(3):
            links.start(f"down_z{o}", d_ref.at[z_at[o]], d_z.at[o], z_dev[o])
            links.start(f"out_z{o}", o_ref.at[z_at[o]], o_z.at[o], z_dev[o])

    def step_two():
        links.arrived("pool1")
        pool_out[...] = add_up([pool_parts[...], pool_got[1]]) / count_ref[...]
        if not fused:
            return
        links.arrived("up_x")
        for i in range(4):
            add_into(u_ref.at[i], [u_x.at[i]], 2)
        links.start("up_y", u_ref.at[:, 1 - y], u_y, y_dev)

    def step_three():
        if not fused:
            return
        links.arrived("up_y")

        def one(i, carry):
            u_ref[i, y] = add_up([u_ref[i, y], u_y[i]]).astype(low)
            return carry

        lax.fori_loop(0, 4, one, 0)
        for o in range(3):
            links.start(f"up_z{o}", u_ref.at[z_at[o], y], u_z.at[o], z_dev[o])

    def step_four():
        if not fused:
            return
        links.arrived("down_z0", "down_z1", "down_z2", "out_z0", "out_z1", "out_z2")
        d_s[...] = add_up([d_ref[z]] + [d_z[o] for o in range(3)]).astype(low)
        o_s[...] = add_up([o_ref[z]] + [o_z[o] for o in range(3)]).astype(low)
        links.start("down_x", d_s, d_x, across_dev)
        links.start("out_x", o_s, o_x, across_dev)

    def step_five():
        if not fused:
            return
        links.arrived("up_z0", "up_z1", "up_z2")
        up_out[me] = add_up([u_ref[z, y]] + [u_z[o] for o in range(3)]).astype(low)
        links.start("up_gather", up_out.at[me], up_out.at[me], across_dev)

    def step_six():
        if not fused:
            return
        links.arrived("down_x", "out_x")
        down_out[core] = add_up([d_s[...], d_x[...]]).astype(low)
        wo_out[core] = add_up([o_s[...], o_x[...]]).astype(low)
        links.start("down_gather", down_out.at[core], down_out.at[core], near_dev)
        links.start("out_gather", wo_out.at[core], wo_out.at[core], near_dev)
        links.arrived("up_gather")
        links.start("up_near0", up_out.at[me], up_out.at[me], near_dev)
        links.start("up_near1", up_out.at[across], up_out.at[across], near_dev)

    row = lax.broadcasted_iota(jnp.int32, (PAIR, size), 0)

    def attend_pairs(r, first, last):
        slot = r % 2

        def one_pair(pair, carry):
            columns = pl.ds(pl.multiple_of(pair * PAIR, PAIR), PAIR)
            grad = grad_ref[slot, :, columns]
            q_both = split_heads(q_ref[slot, :, columns])
            g_both = split_heads(grad)
            product = grad.astype(jnp.float32) * context_ref[slot, :, columns].astype(jnp.float32)
            product = product.T
            delta = jnp.concatenate(
                [
                    jnp.sum(product[:HEAD_DIM], axis=0, keepdims=True),
                    jnp.sum(product[HEAD_DIM:], axis=0, keepdims=True),
                ],
                axis=1,
            )
            lse = jnp.concatenate(
                [lse_ref[r, pl.ds(2 * pair, 1), :], lse_ref[r, pl.ds(2 * pair + 1, 1), :]], axis=1
            )
            dq = jnp.zeros((PAIR, 2 * size), jnp.float32)
            for j in range(4):
                rows = pl.ds(j * size, size)
                keys = k_ref[slot, rows, columns]
                bias = bias_ref[rows, :]
                bias = jnp.concatenate([bias, bias], axis=1)
                probs = jnp.exp(dot_nt(keys, q_both) + bias - lse)
                grad_s = probs * (dot_nt(v_ref[slot, rows, columns], g_both) - delta)
                grad_s = grad_s.astype(low)
                dv_ref[rows, columns] = matmul(probs.astype(low), g_both).astype(low)
                dk_ref[rows, columns] = matmul(grad_s, q_both).astype(low)
                dq = dq + matmul(keys.T, grad_s)
            dq = jnp.where(row < HEAD_DIM, dq[:, :size], dq[:, size:]) * HEAD_DIM ** (-0.5)
            dq_ref[:, columns] = dq.T.astype(low)
            return carry

        lax.fori_loop(first, last, one_pair, 0)

    def weight_parts(r):
        slot = r % 2

        def x_block(j):
            return x_ref[r] if j == 0 else x_got[slot, j - 1]

        def one_part(i, carry):
            columns = pl.ds(pl.multiple_of(i * (width // 3), 128), width // 3)
            parts = (
                dot_tn(x_ref[r], dq_ref[:, columns]),
                sum(dot_tn(x_block(j), dk_ref[pl.ds(j * size, size), columns]) for j in range(4)),
                sum(dot_tn(x_block(j), dv_ref[pl.ds(j * size, size), columns]) for j in range(4)),
            )
            for n, part in enumerate(parts):
                dw_ref[n, :, columns] = part if r == 0 else dw_ref[n, :, columns] + part
            return carry

        lax.fori_loop(0, 3, one_part, 0)
        biases = jnp.concatenate(
            [
                jnp.sum(source[...].astype(jnp.float32), axis=0, keepdims=True)
                for source in (dq_ref, dv_ref)
            ],
            axis=0,
        )
        vec_parts[0, 0:2, :] = biases if r == 0 else vec_parts[0, 0:2, :] + biases

    def input_parts(r):
        for j in range(4):
            rows = pl.ds(j * size, size)
            part = dot_nt(dk_ref[rows, :], w_key[...]) + dot_nt(dv_ref[rows, :], w_value[...])
            if j == 0:
                dx_acc[r] = dx_acc[r] + part + dot_nt(dq_ref[...], w_query[...])
            elif j == 2:
                dx_far[r] = part.astype(low)
            else:
                dx_sent[r, j // 2] = part.astype(low)
        links.start(f"dx_near{r}", dx_sent.at[r], dx_near_got.at[r], near_dev)

    def input_near(r):
        links.arrived(f"dx_near{r}")
        dx_far[r] = add_up([dx_far[r], dx_near_got[r, 1]]).astype(low)
        links.start(f"dx_far{r}", dx_far.at[r], dx_far_got.at[r], across_dev)
        dx_acc[r] = dx_acc[r] + dx_near_got[r, 0].astype(jnp.float32)

    def input_done(r):
        links.arrived(f"dx_far{r}")
        dx_out[r] = add_up([dx_acc[r], dx_far_got[r]]).astype(low)

    vec_parts[0] = vector_ref[...]
    for r in range(rows_here):
        slot = r % 2
        for item in load_row(r):
            item.wait()
        if r + 1 < rows_here:
            for item in load_row(r + 1):
                item.start()
        for j in range(4):
            seg_key = jnp.broadcast_to(
                ids_ref[j, r : r + 1, :].astype(jnp.float32), (PAIR, size)
            ).T[:, :1]
            seg_query = ids_ref[0, r : r + 1, :].astype(jnp.float32)
            bias_ref[j * size : (j + 1) * size, :] = jnp.where(seg_key == seg_query, 0.0, MASKED)
        attend_pairs(r, 0, HEADS // 4)
        if r == 1:
            step_one()
            input_near(0)
        if r == 2:
            step_three()
            input_near(1)
        attend_pairs(r, HEADS // 4, HEADS // 2)
        if r == 0:
            load_mixed.wait()
        if r == 1:
            step_two()
            input_done(0)
        if r == 2:
            step_four()
            input_done(1)
        weight_parts(r)
        if r + 1 < rows_here:
            input_parts(r)

    r = rows_here - 1
    if not fused:
        input_parts(r)
        for n in range(3):
            square_out[n] = dw_ref[n].astype(low)
        vector_out[...] = vec_parts[0]
        input_near(r)
        input_done(r)
        links.finish()
        return

    depth = gb_ref.shape[3]
    for n in range(3):
        for h in range(2):
            part = dw_ref[n, :, h * half : (h + 1) * half].astype(low)
            gb_ref[h, :, :, :, n * half : (n + 1) * half] = part.reshape(4, 2, depth, half)
    links.start("square_core", gb_ref.at[1 - core], gb_got, near_dev)
    links.start("vector0", vec_parts.at[0], vec_got.at[0], near_dev)
    input_parts(r)
    step_five()
    cut = s1_x.shape[3]
    own = pl.ds(pl.multiple_of(side * cut, 128), cut)
    its = pl.ds(pl.multiple_of((1 - side) * cut, 128), cut)
    rest = pl.ds(2 * cut, 3 * half - 2 * cut)
    links.arrived("square_core")
    for i in range(4):
        add_into(gb_ref.at[core, i], [gb_got.at[i]], 2)
    g = gb_ref.at[core]
    links.start("s2_y", g.at[:, 1 - y, :, rest], s2_y, y_dev)
    links.start("s1_x", g.at[:, :, :, its], s1_x, across_dev)
    links.arrived("vector0")
    vec_parts[1] = vec_parts[0] + vec_got[0]
    links.start("vector1", vec_parts.at[1], vec_got.at[1], across_dev)
    input_near(r)
    step_six()
    links.arrived("vector1")
    vec_parts[2] = vec_parts[1] + vec_got[1]
    links.start("vector2", vec_parts.at[2], vec_got.at[2], y_dev)

    links.arrived("s1_x")
    for i in range(4):
        for j in range(2):
            g[i, j, :, own] = add_up([g[i, j, :, own], s1_x[i, j]]).astype(low)
    links.start("s1_y", g.at[:, 1 - y, :, own], s1_y, y_dev)
    links.arrived("s2_y")
    for i in range(4):
        g[i, y, :, rest] = add_up([g[i, y, :, rest], s2_y[i]]).astype(low)
    for o in range(3):
        links.start(f"s2_z{o}", g.at[z_at[o], y, :, rest], s2_z.at[o], z_dev[o])
    links.arrived("vector2")
    vec_parts[3] = vec_parts[2] + vec_got[2]
    for o in range(3):
        links.start(f"vector_z{o}", vec_parts.at[3], vec_got.at[3 + o], z_dev[o])
    links.arrived("s1_y")
    for i in range(4):
        g[i, y, :, own] = add_up([g[i, y, :, own], s1_y[i]]).astype(low)
    for o in range(3):
        links.start(f"s1_z{o}", g.at[z_at[o], y, :, own], s1_z.at[o], z_dev[o])
    input_done(r)
    links.arrived("s2_z0", "s2_z1", "s2_z2")
    s2_s[...] = add_up([g[z, y, :, rest]] + [s2_z[o] for o in range(3)]).astype(low)
    links.start("s2_x", s2_s, s2_x, across_dev)
    links.arrived("s1_z0", "s1_z1", "s1_z2")
    square_out[core, :, own] = add_up([g[z, y, :, own]] + [s1_z[o] for o in range(3)]).astype(low)
    links.start(
        "s1_gather", square_out.at[core, :, own], square_out.at[core, :, own], across_dev
    )
    links.arrived("vector_z0", "vector_z1", "vector_z2")
    vector_out[...] = vec_parts[3] + (vec_got[3] + (vec_got[4] + vec_got[5]))
    links.arrived("s2_x")
    square_out[core, :, rest] = add_up([s2_s[...], s2_x[...]]).astype(low)
    links.arrived("s1_gather")
    links.start("square_gather", square_out.at[core], square_out.at[core], near_dev)
    links.arrived("down_gather", "out_gather", "up_near0", "up_near1", "square_gather")
    links.finish()


def attend_back(
    fused, x, ids, lse, w_query, w_key, w_value, pool, counts, vectors,
    x_got, q, k, v, context, grad, mixed, up, down, out,
):
    rows_here, size, width = x.shape
    keys = size * 4
    half = width // 2
    low = jnp.bfloat16
    f32 = jnp.float32
    whole = pl.BlockSpec(memory_space=pltpu.VMEM)
    outside = pl.BlockSpec(memory_space=pl.ANY)
    shape = jax.ShapeDtypeStruct
    up_rows, down_rows = (up.shape[2], down.shape[2]) if fused else (16, 16)
    cut = 2 * 128 if fused else 128
    rest = 3 * half - 2 * cut
    w = width if fused else 128
    h = half if fused else 128
    c3 = 3 * half if fused else 128
    rest = rest if fused else 128
    square_shape = (2, up_rows, 3 * half) if fused else (3, width, width)
    vec = vectors.shape
    scratch = [
        pltpu.VMEM((2, 3, size, width), low),
        pltpu.VMEM((2, size, width), low),
        pltpu.VMEM((2, keys, width), low),
        pltpu.VMEM((2, keys, width), low),
        pltpu.VMEM((2, size, width), low),
        pltpu.VMEM((2, size, width), low),
        pltpu.VMEM((keys, size), f32),
        pltpu.VMEM((size, width), low),
        pltpu.VMEM((keys, width), low),
        pltpu.VMEM((keys, width), low),
        pltpu.VMEM((3, width, width), f32),
        pltpu.VMEM((rows_here, size, width), f32),
        pltpu.VMEM((rows_here, 2, size, width), low),
        pltpu.VMEM((rows_here, size, width), low),
        pltpu.VMEM((rows_here, 2, size, width), low),
        pltpu.VMEM((rows_here, size, width), low),
        pltpu.VMEM(pool.shape, low),
        pltpu.VMEM((2,) + pool.shape, low),
        pltpu.VMEM((4,) + vec, f32),
        pltpu.VMEM((6,) + vec, f32),
        pltpu.VMEM((2, 4, 2, up_rows, c3), low),
        pltpu.VMEM((4, 2, up_rows, c3), low),
        pltpu.VMEM((4, 2, up_rows, cut), low),
        pltpu.VMEM((4, up_rows, cut), low),
        pltpu.VMEM((3, up_rows, cut), low),
        pltpu.VMEM((4, up_rows, rest), low),
        pltpu.VMEM((3, up_rows, rest), low),
        pltpu.VMEM((up_rows, rest), low),
        pltpu.VMEM((up_rows, rest), low),
        pltpu.VMEM((4, 2, up_rows, w), low),
        pltpu.VMEM((4, 2, up_rows, w), low),
        pltpu.VMEM((4, up_rows, w), low),
        pltpu.VMEM((3, up_rows, w), low),
        pltpu.VMEM((4, down_rows, w), low),
        pltpu.VMEM((4, down_rows, w), low),
        pltpu.VMEM((3, down_rows, w), low),
        pltpu.VMEM((down_rows, w), low),
        pltpu.VMEM((down_rows, w), low),
        pltpu.VMEM((4, up_rows, h), low),
        pltpu.VMEM((4, up_rows, h), low),
        pltpu.VMEM((3, up_rows, h), low),
        pltpu.VMEM((up_rows, h), low),
        pltpu.VMEM((up_rows, h), low),
        pltpu.SemaphoreType.DMA((56,)),
        pltpu.SemaphoreType.DMA((56,)),
        pltpu.SemaphoreType.DMA((2, 6)),
        pltpu.SemaphoreType.DMA((4,)),
    ]
    return pl.pallas_call(
        functools.partial(attend_back_kernel, fused),
        out_shape=(
            shape((rows_here, size, width), low),
            shape(pool.shape, f32),
            shape(vec, f32),
            shape(square_shape, low),
            shape((4, up_rows, w), low),
            shape((2, down_rows, w), low),
            shape((2, up_rows, h), low),
        ),
        in_specs=[whole] * 9 + [outside] * 10,
        out_specs=(whole,) * 7,
        scratch_shapes=scratch,
        compiler_params=pltpu.CompilerParams(
            vmem_limit_bytes=63 * 2**20, collective_id=1, has_side_effects=True
        ),
        cost_estimate=pl.CostEstimate(
            flops=rows_here
            * (4 * (size + 2 * keys) * width * width + 40 * size * keys * width),
            bytes_accessed=2 * (16 * width * width + 9 * keys * width),
            transcendentals=rows_here * HEADS * size * keys,
        ),
    )(
        x, ids, lse, w_query, w_key, w_value, pool, counts, vectors,
        x_got, q, k, v, context, grad, mixed, up, down, out,
    )


def radices_of(count):
    if count == 8:
        return ((1, 2), (2, 4))
    digits = []
    stride = 1
    while stride < count:
        digits.append((stride, 2))
        stride *= 2
    return tuple(digits)


def exchange(piece, axis_name, stride, offset):
    count = lax.axis_size(axis_name)
    pairs = [(i, i ^ (offset * stride)) for i in range(count)]
    return lax.ppermute(piece, axis_name, pairs)


def digit_of(axis_name, stride, radix):
    return (lax.axis_index(axis_name) // stride) % radix


def scatter_digit(pieces, place, axis_name, stride, radix):
    here = digit_of(axis_name, stride, radix)
    received = [
        exchange(
            lax.dynamic_index_in_dim(pieces, here ^ offset, place, keepdims=False).astype(
                jnp.bfloat16
            ),
            axis_name, stride, offset,
        )
        for offset in range(1, radix)
    ]
    total = lax.dynamic_index_in_dim(pieces, here, place, keepdims=False).astype(jnp.float32)
    for item in received:
        total = total + item.astype(jnp.float32)
    return total.astype(jnp.bfloat16)


def halve(piece, place, axis_name, stride):
    half = piece.shape[place] // 2
    here = digit_of(axis_name, stride, 2)
    sent = lax.dynamic_slice_in_dim(piece, (1 - here) * half, half, place).astype(jnp.bfloat16)
    kept = lax.dynamic_slice_in_dim(piece, here * half, half, place).astype(jnp.float32)
    return (kept + exchange(sent, axis_name, stride, 1).astype(jnp.float32)).astype(jnp.bfloat16)


def join(piece, place, axis_name, stride):
    here = digit_of(axis_name, stride, 2)
    other = exchange(piece, axis_name, stride, 1)
    first = jnp.where(here == 0, piece, other)
    second = jnp.where(here == 0, other, piece)
    return jnp.concatenate([first, second], axis=place)


def scatter_rows(group, dp_size):
    digits = radices_of(dp_size)
    shape = tuple(r for _, r in reversed(digits))
    group = group.reshape(shape + (group.shape[0] // dp_size, group.shape[1]))
    for place, (stride, radix) in zip(range(len(digits) - 1, -1, -1), digits):
        group = scatter_digit(group, place, "dp", stride, radix)
    return group


def reduce_weight(gradient, dp_size, ctx_first, side):
    rows = gradient.shape[0] // dp_size
    if side == 0:
        gradient = gradient.reshape(dp_size, rows, -1)
    place = 1
    gradient = halve(gradient, place, "ctx", 1)
    if ctx_first:
        gradient = halve(gradient, place, "ctx", 2)
    flat = gradient.reshape(-1, gradient.shape[-1])
    flat = scatter_rows(flat, dp_size)
    if ctx_first:
        flat = join(flat, side, "ctx", 2)
    else:
        flat = flat.astype(jnp.float32) + exchange(flat, "ctx", 2, 1).astype(jnp.float32)
        flat = flat.astype(jnp.bfloat16)
    return join(flat, side, "ctx", 1).astype(jnp.float32)


def per_device(
    hidden_in,
    seg_ids,
    valid,
    w_query,
    b_query,
    w_key,
    w_value,
    b_value,
    w_out,
    b_out,
    gain_attn,
    shift_attn,
    w_up,
    b_up,
    w_down,
    b_down,
    gain_ffn,
    shift_ffn,
    pooled_text_gradient,
):
    row_count, group_size, model_width = hidden_in.shape
    token_count = row_count * group_size
    tokens_flat = hidden_in.reshape(token_count, model_width)
    residual = tokens_flat.astype(jnp.float32)
    gain_one = gain_attn.astype(jnp.float32)
    shift_one = shift_attn.astype(jnp.float32)
    gain_two = gain_ffn.astype(jnp.float32)
    shift_two = shift_ffn.astype(jnp.float32)
    wide = lambda vector: vector.astype(jnp.float32)[None]
    ids = jnp.concatenate([seg_ids, valid], axis=0)
    ids = jnp.pad(ids, ((0, 8 - ids.shape[0]), (0, 0)))
    q_all, context, lse_all, ids_got, x_got, k_all, v_all = attend(
        hidden_in, ids, w_query, w_key, w_value, wide(b_query), wide(b_value)
    )
    ids_all = ids_got[:, :row_count].transpose(1, 0, 2).reshape(row_count, -1)
    valid_all = ids_got[:, row_count : 2 * row_count].transpose(1, 0, 2).reshape(row_count, -1)
    context_rows = context
    context = context.reshape(token_count, model_width)
    attn_out = matmul(context, w_out) + b_out.astype(jnp.float32)
    mixed_sum = residual + attn_out
    normed = layer_norm(mixed_sum, gain_one, shift_one)
    normed_bf = normed.astype(jnp.bfloat16)
    act_bf = gelu_exact(matmul(normed_bf, w_up) + b_up.astype(jnp.float32)).astype(jnp.bfloat16)
    ffn_out = matmul(act_bf, w_down) + b_down.astype(jnp.float32)
    summed = normed + ffn_out
    final_out = layer_norm(summed, gain_two, shift_two)
    text_membership = (
        (seg_ids[:, :, None] == jnp.arange(NSEG)[None, None, :]) & (valid[:, :, None] == 1)
    ).astype(jnp.float32)
    part_sums = jnp.einsum(
        "ofr,ofy->ory",
        text_membership,
        final_out.reshape(row_count, group_size, model_width),
        precision=lax.Precision.HIGHEST,
    )
    text_counts = jnp.sum(
        (
            (ids_all[:, :, None] == jnp.arange(NSEG)[None, None, :])
            & (valid_all[:, :, None] == 1)
        ).astype(jnp.float32),
        axis=1,
    )
    clamped_text_counts = jnp.maximum(text_counts, 1.0)[:, :, None]
    grad_final = jnp.einsum(
        "heb,hbj->hej",
        text_membership,
        pooled_text_gradient / clamped_text_counts,
        precision=lax.Precision.HIGHEST,
    ).reshape(token_count, model_width)
    _, norm_two_back = jax.vjp(layer_norm, summed, gain_two, shift_two)
    grad_summed, grad_gain_two, grad_shift_two = norm_two_back(grad_final)
    grad_ffn = grad_summed.astype(jnp.bfloat16)
    grad_w_down = matmul_left(act_bf, grad_ffn)
    grad_b_down = jnp.sum(grad_ffn.astype(jnp.float32), axis=0)
    grad_act = matmul_right(grad_ffn, w_down)
    pre_again = matmul(normed_bf, w_up) + b_up.astype(jnp.float32)
    _, gelu_back = jax.vjp(gelu_exact, pre_again)
    grad_pre = gelu_back(grad_act)[0].astype(jnp.bfloat16)
    grad_w_up = matmul_left(normed_bf, grad_pre)
    grad_b_up = jnp.sum(grad_pre.astype(jnp.float32), axis=0)
    grad_normed = grad_summed + matmul_right(grad_pre, w_up)
    _, norm_one_back = jax.vjp(layer_norm, mixed_sum, gain_one, shift_one)
    grad_mixed, grad_gain_one, grad_shift_one = norm_one_back(grad_normed)
    grad_attn = grad_mixed.astype(jnp.bfloat16)
    grad_w_out = matmul_left(context, grad_attn)
    grad_b_out = jnp.sum(grad_attn.astype(jnp.float32), axis=0)
    grad_context = matmul_right(grad_attn, w_out).astype(jnp.bfloat16)
    dp_size, ctx_size = lax.axis_size("dp"), lax.axis_size("ctx")
    ff_width = w_up.shape[1]
    rows_here, ff_here = model_width // dp_size, ff_width // dp_size
    low = jnp.bfloat16
    fused = dp_size == 8 and rows_here % 16 == 0 and model_width % 768 == 0
    vectors = jnp.concatenate(
        [
            jnp.zeros((2, model_width), jnp.float32),
            grad_b_out[None], grad_gain_one[None], grad_shift_one[None],
            grad_b_down[None], grad_gain_two[None], grad_shift_two[None],
            grad_b_up.reshape(-1, model_width),
        ],
        axis=0,
    )
    vectors = jnp.pad(vectors, ((0, -vectors.shape[0] % 8), (0, 0)))
    if fused:
        up = halve(grad_w_up, 1, "ctx", 1).reshape(4, 2, rows_here, -1)
        down = halve(grad_w_down.reshape(dp_size, ff_here, -1), 1, "ctx", 1)
        down = down.reshape(4, 2, ff_here // 2, -1)
        out = halve(grad_w_out, 1, "ctx", 1).reshape(4, 2, rows_here, -1)
    else:
        up = down = out = jnp.zeros((16, 128), low)
    grad_input, pooled, vector_sum, squares, up_sum, down_sum, out_sum = attend_back(
        fused, hidden_in, ids_got, lse_all, w_query, w_key, w_value,
        part_sums.astype(low).reshape(-1, model_width), clamped_text_counts.reshape(-1, 1), vectors,
        x_got, q_all, k_all, v_all, context_rows,
        grad_context.reshape(row_count, group_size, model_width),
        grad_mixed.reshape(row_count, group_size, model_width), up, down, out,
    )
    pooled = pooled.reshape(row_count, NSEG, model_width)
    wide_out = lambda piece: piece.astype(jnp.float32)
    if fused:
        half = model_width // 2
        square_sums = [
            wide_out(squares[:, :, n * half : (n + 1) * half])
            .transpose(1, 0, 2)
            .reshape(rows_here, model_width)
            for n in range(3)
        ]
        square_sums.append(wide_out(out_sum).transpose(1, 0, 2).reshape(rows_here, model_width))
        up_sum = (
            wide_out(up_sum).reshape(2, 2, rows_here, -1).transpose(2, 1, 0, 3)
            .reshape(rows_here, ff_width)
        )
        down_sum = wide_out(down_sum).reshape(ff_here, model_width)
    else:
        square_sums = [
            reduce_weight(piece, dp_size, True, 1)
            for piece in (squares[0], squares[1], squares[2], grad_w_out)
        ]
        up_sum = reduce_weight(grad_w_up, dp_size, True, 1)
        down_sum = reduce_weight(grad_w_down, dp_size, False, 0)
        vector_sum = lax.psum(vector_sum, ("dp", "ctx"))
    place = lax.axis_index("dp")
    sums = lax.dynamic_slice_in_dim(vector_sum[:8], place * rows_here, rows_here, 1)
    sum_bu = lax.dynamic_slice_in_dim(
        vector_sum[8 : 8 + ff_width // model_width].reshape(-1), place * ff_here, ff_here
    )
    results = (
        square_sums[0], sums[0], square_sums[1], square_sums[2], sums[1], square_sums[3],
        sums[2], sums[3], sums[4], up_sum, sum_bu, down_sum, sums[5], sums[6], sums[7],
    )
    return (
        final_out.reshape(row_count, group_size, model_width).astype(jnp.bfloat16),
        pooled,
        grad_input.reshape(row_count, group_size, model_width).astype(jnp.bfloat16),
    ) + tuple(results)


def solution(mesh):
    placed = (
        P("dp", "ctx", None),
        P("dp", "ctx"),
        P("dp", "ctx"),
        P(),
        P(),
        P(),
        P(),
        P(),
        P(),
        P(),
        P(),
        P(),
        P(),
        P(),
        P(),
        P(),
        P(),
        P(),
        P("dp", None, None),
    )
    return jax.shard_map(
        per_device,
        mesh=mesh,
        in_specs=placed,
        out_specs=(
            P("dp", "ctx", None),
            P("dp", None, None),
            P("dp", "ctx", None),
            P("dp", None),
            P("dp"),
            P("dp", None),
            P("dp", None),
            P("dp"),
            P("dp", None),
            P("dp"),
            P("dp"),
            P("dp"),
            P("dp", None),
            P("dp"),
            P("dp", None),
            P("dp"),
            P("dp"),
            P("dp"),
        ),
        check_vma=False,
    )
```

```python
import functools

import jax
import jax.numpy as jnp
from jax import lax
from jax.experimental import pallas as pl
from jax.experimental.pallas import tpu as pltpu
from jax.sharding import PartitionSpec as P

HEADS = 12
HEAD_DIM = 64
NSEG = 16


eps = 1e-12


def matmul(left_side, right_side):
    return jnp.dot(left_side, right_side, preferred_element_type=jnp.float32)


PAIR = 2 * HEAD_DIM
MESH = pl.DeviceIdType.MESH
MASKED = -1e30


def dot_nt(left_side, right_side):
    return lax.dot_general(
        left_side, right_side, (((1,), (1,)), ((), ())), preferred_element_type=jnp.float32
    )


def dot_tn(left_side, right_side):
    return lax.dot_general(
        left_side, right_side, (((0,), (0,)), ((), ())), preferred_element_type=jnp.float32
    )


def split_heads(pair):
    lane = lax.broadcasted_iota(jnp.int32, pair.shape, 1)
    zero = jnp.zeros_like(pair)
    return jnp.concatenate(
        [jnp.where(lane < HEAD_DIM, pair, zero), jnp.where(lane < HEAD_DIM, zero, pair)], axis=0
    )


def attend_kernel(
    x_ref, ids_ref, vec_ref, w_query, w_key, w_value,
    q_out, context_out, lse_out, ids_out, x_hbm, k_hbm, v_hbm,
    x_got, k_ref, v_ref, bias_ref, stat_ref, send_sem, recv_sem, local_sem,
):
    rows_here, size, width = x_ref.shape
    me = lax.axis_index("ctx")
    one = me + 1 - 2 * (me % 2)
    two = (me + 2) % 4
    three = (one + 2) % 4
    low = jnp.bfloat16

    barrier = pltpu.get_barrier_semaphore()
    for peer in (one, two, three):
        pl.semaphore_signal(barrier, inc=1, device_id={"ctx": peer}, device_id_type=MESH)
    pl.semaphore_wait(barrier, 3)

    def send(source, target, slot, peer):
        return pltpu.make_async_remote_copy(
            src_ref=source, dst_ref=target, send_sem=send_sem.at[slot],
            recv_sem=recv_sem.at[slot], device_id={"ctx": peer}, device_id_type=MESH,
        )

    ids_out[0] = ids_ref[...]
    ids_sends = [send(ids_ref, ids_out.at[j + 1], j, peer) for j, peer in enumerate((one, two, three))]
    near = send(x_ref, x_got.at[0], 3, one)

    def far(r):
        return send(x_ref.at[r], x_got.at[1, r], 4 + r, two)

    def passed(r):
        return send(x_got.at[1, r], x_got.at[2, r], 4 + rows_here + r, one)

    far(0).start()
    near.start()
    for item in ids_sends:
        item.start()
    for r in range(1, rows_here):
        far(r).start()

    def project(r, x, j):
        rows = pl.ds(j * size, size)
        k_ref[r, rows, :] = matmul(x, w_key[...]).astype(low)
        v_ref[r, rows, :] = (matmul(x, w_value[...]) + vec_ref[B_VALUE : B_VALUE + 1, :]).astype(low)

    def own_row(r, carry):
        x = x_ref[r]
        q = (matmul(x, w_query[...]) + vec_ref[B_QUERY : B_QUERY + 1, :]).astype(low)
        q_out[r] = (q * HEAD_DIM ** (-0.5)).astype(low)
        project(r, x, 0)
        return carry

    lax.fori_loop(0, rows_here, own_row, 0)
    near.wait_recv()

    def near_row(r, carry):
        project(r, x_got[0, r], 1)
        return carry

    lax.fori_loop(0, rows_here, near_row, 0)
    for item in ids_sends:
        item.wait_recv()
    lane = lax.broadcasted_iota(jnp.int32, (size, PAIR), 1)
    far(0).wait_recv()
    passed(0).start()

    def keep(r):
        return (
            pltpu.make_async_copy(k_ref.at[r], k_hbm.at[r], local_sem.at[0, r]),
            pltpu.make_async_copy(v_ref.at[r], v_hbm.at[r], local_sem.at[1, r]),
        )

    for r in range(rows_here):
        project(r, x_got[1, r], 2)
        passed(r).wait_recv()
        project(r, x_got[2, r], 3)
        for item in keep(r):
            item.start()
        seg_query = jnp.broadcast_to(
            ids_ref[r : r + 1, :].astype(jnp.float32), (PAIR, size)
        ).T[:, :1]
        for j in range(4):
            seg_key = ids_out[j, r : r + 1, :].astype(jnp.float32)
            bias_ref[:, j * size : (j + 1) * size] = jnp.where(seg_query == seg_key, 0.0, MASKED)
        stat_ref[...] = jnp.zeros_like(stat_ref)

        def one_pair(pair, carry, r=r):
            columns = pl.ds(pl.multiple_of(pair * PAIR, PAIR), PAIR)
            both = split_heads(q_out[r, :, columns])
            scores = dot_nt(both, k_ref[r, :, columns])
            scores = scores.reshape(2, size, scores.shape[1]) + bias_ref[...][None]
            top = jnp.max(scores, axis=-1, keepdims=True)
            weight = jnp.exp(scores - top)
            total = jnp.sum(weight, axis=-1, keepdims=True)
            mixed = matmul(
                weight.astype(low).reshape(2 * size, -1), v_ref[r, :, columns]
            ).reshape(2, size, PAIR) / total
            context_out[r, :, columns] = jnp.where(lane < HEAD_DIM, mixed[0], mixed[1]).astype(low)
            lse = top + jnp.log(total)
            stat = stat_ref[...]
            stat = jnp.where(lane == 2 * pair, lse[0], stat)
            stat_ref[...] = jnp.where(lane == 2 * pair + 1, lse[1], stat)
            return carry

        lax.fori_loop(0, HEADS // 2, one_pair, 0)
        lse_out[r] = stat_ref[...].T[: lse_out.shape[1]]
        if r + 1 < rows_here:
            far(r + 1).wait_recv()
            passed(r + 1).start()
    keep_x = pltpu.make_async_copy(x_got, x_hbm, local_sem.at[2, 0])
    keep_x.start()
    for r in range(rows_here):
        for item in keep(r):
            item.wait()
        far(r).wait_send()
        passed(r).wait_send()
    near.wait_send()
    for item in ids_sends:
        item.wait_send()
    keep_x.wait()


def attend(x, ids, vectors, w_query, w_key, w_value):
    rows_here, size, width = x.shape
    keys = size * 4
    low = jnp.bfloat16
    whole = pl.BlockSpec(memory_space=pltpu.VMEM)
    outside = pl.BlockSpec(memory_space=pl.ANY)
    slots = 4 + 2 * rows_here
    return pl.pallas_call(
        attend_kernel,
        out_shape=(
            jax.ShapeDtypeStruct((rows_here, size, width), low),
            jax.ShapeDtypeStruct((rows_here, size, width), low),
            jax.ShapeDtypeStruct((rows_here, 16, size), jnp.float32),
            jax.ShapeDtypeStruct((4,) + ids.shape, jnp.int32),
            jax.ShapeDtypeStruct((3,) + x.shape, low),
            jax.ShapeDtypeStruct((rows_here, keys, width), low),
            jax.ShapeDtypeStruct((rows_here, keys, width), low),
        ),
        in_specs=[whole] * 6,
        out_specs=(whole, whole, whole, whole, outside, outside, outside),
        scratch_shapes=[
            pltpu.VMEM((3,) + x.shape, low),
            pltpu.VMEM((rows_here, keys, width), low),
            pltpu.VMEM((rows_here, keys, width), low),
            pltpu.VMEM((size, keys), jnp.float32),
            pltpu.VMEM((size, PAIR), jnp.float32),
            pltpu.SemaphoreType.DMA((slots,)),
            pltpu.SemaphoreType.DMA((slots,)),
            pltpu.SemaphoreType.DMA((3, rows_here)),
        ],
        compiler_params=pltpu.CompilerParams(
            vmem_limit_bytes=56 * 2**20, collective_id=0, has_side_effects=True
        ),
        cost_estimate=pl.CostEstimate(
            flops=rows_here * (2 * (size + 2 * keys) * width * width + 16 * size * keys * width),
            bytes_accessed=2 * (3 * width * width + 9 * keys * width),
            transcendentals=rows_here * HEADS * size * keys,
        ),
    )(x, ids, vectors, w_query, w_key, w_value)


def gelu_both(u):
    size = jnp.abs(u)
    t = 1.0 / (1.0 + (0.3275911 * 0.5**0.5) * size)
    bell = jnp.exp(-0.5 * u * u)
    poly = t * (
        0.127414796 + t * (-0.142248368 + t * (0.7107068705 + t * (-0.7265760135 + t * 0.5307027145)))
    )
    tail = poly * bell
    cdf = jnp.where(u >= 0.0, 1.0 - tail, tail)
    return u * cdf, cdf + u * bell * 0.3989422804014327


def normalize(values_in):
    centre = jnp.mean(values_in, axis=-1, keepdims=True)
    centred = values_in - centre
    spread = jnp.mean(centred * centred, axis=-1, keepdims=True)
    scale = lax.rsqrt(spread + eps)
    return centred * scale, scale


def normalize_back(grad, unit, scale):
    mean_one = jnp.mean(grad, axis=-1, keepdims=True)
    mean_two = jnp.mean(grad * unit, axis=-1, keepdims=True)
    return (grad - mean_one - unit * mean_two) * scale


def column_sum(values_in):
    return jnp.sum(values_in, axis=0, keepdims=True)


B_QUERY, B_VALUE, B_OUT, GAIN_ONE, SHIFT_ONE, B_DOWN, GAIN_TWO, SHIFT_TWO, B_UP = range(9)


def middle_kernel(
    x_ref, context_ref, ids_ref, vec_ref, text_ref, w_out,
    up_hbm, down_hbm,
    pool_out, count_out, vector_out, grad_out, mixed_out, wo_out, final_hbm, up_out, down_out,
    w_up, w_down, unit_ref, scale_ref, normed_ref, normed_t, act_ref, slope_ref, acc_ref,
    g_ref, final_ref, upg_ref, up_got, downg_ref, down_got, wo_sent, wo_got,
    send_sem, recv_sem, load_sem, store_sem,
):
    rows_here, size, width = x_ref.shape
    tokens = rows_here * size
    parts = w_up.shape[0]
    half = width // 2
    low = jnp.bfloat16
    f32 = jnp.float32
    me = lax.axis_index("ctx")
    core = me % 2
    near = {"ctx": me + 1 - 2 * core}
    barrier = pltpu.get_barrier_semaphore()
    pl.semaphore_signal(barrier, inc=1, device_id=near, device_id_type=MESH)

    def vec(row):
        return vec_ref[row : row + 1, :]

    loads = []
    for i in range(parts):
        loads.append(
            (
                pltpu.make_async_copy(
                    up_hbm.at[:, pl.ds(i * width, width)], w_up.at[i], load_sem.at[0, i]
                ),
                pltpu.make_async_copy(
                    down_hbm.at[pl.ds(i * width, width)], w_down.at[i], load_sem.at[1, i]
                ),
            )
        )
    for pair in loads:
        for item in pair:
            item.start()

    def rows_of(r):
        return pl.ds(pl.multiple_of(r * size, size), size)

    text = lax.broadcasted_iota(jnp.int32, (NSEG, size), 0)

    def members(j, r):
        seg = ids_ref[j, r : r + 1, :]
        real = ids_ref[j, rows_here + r : rows_here + r + 1, :]
        return jnp.where((text == seg) & (real == 1), 1.0, 0.0)

    for r in range(rows_here):
        number = sum(jnp.sum(members(j, r), axis=1, keepdims=True) for j in range(4))
        count_out[r * NSEG : (r + 1) * NSEG, :] = jnp.maximum(number, 1.0)

    def first_norm(r, carry):
        rows = rows_of(r)
        mixed = x_ref[r].astype(f32) + (matmul(context_ref[r], w_out[...]) + vec(B_OUT))
        unit, scale = normalize(mixed)
        unit_ref[rows, :] = unit
        scale_ref[rows, :] = scale
        normed_ref[rows, :] = (unit * vec(GAIN_ONE) + vec(SHIFT_ONE)).astype(low)
        return carry

    lax.fori_loop(0, rows_here, first_norm, 0)
    for pair in loads:
        for item in pair:
            item.wait()

    def forward_part(i, carry):
        pre = matmul(normed_ref[...], w_up[i]) + vec_ref[pl.ds(B_UP + i, 1), :]
        act, slope = gelu_both(pre)
        act = act.astype(low)
        act_ref[i] = act
        slope_ref[i] = slope.astype(low)
        part = matmul(act, w_down[i])

        @pl.when(i == 0)
        def _():
            acc_ref[...] = part

        @pl.when(i > 0)
        def _():
            acc_ref[...] += part

        return carry

    lax.fori_loop(0, parts, forward_part, 0)
    normed_t[...] = normed_ref[...].T

    store_final = []
    vector_out[...] = jnp.zeros_like(vector_out)
    for r in range(rows_here):
        rows = pl.ds(r * size, size)
        normed = unit_ref[rows, :] * vec(GAIN_ONE) + vec(SHIFT_ONE)
        summed = normed + (acc_ref[rows, :] + vec(B_DOWN))
        unit, scale = normalize(summed)
        final = unit * vec(GAIN_TWO) + vec(SHIFT_TWO)
        high = final.astype(low)
        final_ref[r] = high
        item = pltpu.make_async_copy(final_ref.at[r], final_hbm.at[r], store_sem.at[r])
        item.start()
        store_final.append(item)
        own = members(0, r)
        own_low = own.astype(low)
        rest = (final - high.astype(f32)).astype(low)
        pool = matmul(own_low, high) + matmul(own_low, rest)
        pool_out[r * NSEG : (r + 1) * NSEG, :] = pool.astype(low)
        share = text_ref[r] / count_out[r * NSEG : (r + 1) * NSEG, :]
        grad = lax.dot_general(
            own, share, (((0,), (0,)), ((), ())), preferred_element_type=f32,
            precision=lax.Precision.HIGHEST,
        )
        back = normalize_back(grad * vec(GAIN_TWO), unit, scale)
        back_low = back.astype(low)
        acc_ref[rows, :] = back
        g_ref[rows, :] = back_low
        vector_out[GAIN_TWO : GAIN_TWO + 1, :] += column_sum(grad * unit)
        vector_out[SHIFT_TWO : SHIFT_TWO + 1, :] += column_sum(grad)
        vector_out[B_DOWN : B_DOWN + 1, :] += column_sum(back_low.astype(f32))

    pl.semaphore_wait(barrier, 1)

    def remote(source, target, slot):
        return pltpu.make_async_remote_copy(
            src_ref=source, dst_ref=target, send_sem=send_sem.at[slot],
            recv_sem=recv_sem.at[slot], device_id=near, device_id_type=MESH,
        )

    per_part = downg_ref.shape[0] // parts
    mine = parts // 2

    def up_send(i):
        return remote(upg_ref.at[i], up_got.at[i], i)

    def down_send(i):
        chunk = pl.ds(i * per_part, per_part)
        return remote(downg_ref.at[chunk, 1 - core], down_got.at[chunk], parts + i)

    def backward_part(step, carry):
        i = (step + mine * (1 - core)) % parts
        back = dot_nt(g_ref[...], w_down[i])
        back = (back * slope_ref[i].astype(f32)).astype(low)
        vector_out[pl.ds(B_UP + i, 1), :] = column_sum(back.astype(f32))
        acc_ref[...] += dot_nt(back, w_up[i])
        upg_ref[step] = matmul(normed_t[...], back).astype(low)

        @pl.when(step < mine)
        def _():
            up_send(step).start()

        part = dot_tn(act_ref[i], g_ref[...]).astype(low)
        downg_ref[pl.ds(i * per_part, per_part)] = part.reshape((per_part,) + downg_ref.shape[1:])
        down_send(i).start()
        return carry

    lax.fori_loop(0, parts, backward_part, 0)

    def first_back(r, carry):
        rows = rows_of(r)
        unit = unit_ref[rows, :]
        grad = acc_ref[rows, :]
        back = normalize_back(grad * vec(GAIN_ONE), unit, scale_ref[rows, :])
        back_low = back.astype(low)
        mixed_out[r] = back
        g_ref[rows, :] = back_low
        grad_out[r] = dot_nt(back_low, w_out[...]).astype(low)
        vector_out[GAIN_ONE : GAIN_ONE + 1, :] += column_sum(grad * unit)
        vector_out[SHIFT_ONE : SHIFT_ONE + 1, :] += column_sum(grad)
        vector_out[B_OUT : B_OUT + 1, :] += column_sum(back_low.astype(f32))
        return carry

    lax.fori_loop(0, rows_here, first_back, 0)

    def out_part(h):
        columns = pl.ds(pl.multiple_of(h * half, 128), half)
        total = jnp.zeros((width, half), f32)
        for r in range(rows_here):
            total = total + dot_tn(context_ref[r], g_ref[pl.ds(r * size, size), columns])
        return total

    wo_sent[...] = out_part(1 - core).astype(low)
    wo_send = remote(wo_sent, wo_got, 2 * parts)
    wo_send.start()
    own_part = out_part(core)

    def down_sum(i, carry):
        downg_ref[i, core] = (
            downg_ref[i, core].astype(f32) + down_got[i].astype(f32)
        ).astype(low)
        return carry

    for i in range(parts):
        down_send(i).wait_recv()
    lax.fori_loop(0, downg_ref.shape[0], down_sum, 0)
    store_down = pltpu.make_async_copy(downg_ref.at[:, core], down_out, store_sem.at[rows_here])
    store_down.start()
    for i in range(mine):
        up_send(i).wait_recv()

    def up_sum(n, carry):
        rows = pl.ds(pl.multiple_of(n * 128, 128), 128)
        for i in range(mine):
            upg_ref[mine + i, rows, :] = (
                upg_ref[mine + i, rows, :].astype(f32) + up_got[i, rows, :].astype(f32)
            ).astype(low)
        return carry

    lax.fori_loop(0, width // 128, up_sum, 0)
    store_up = pltpu.make_async_copy(
        upg_ref.at[pl.ds(mine, mine)], up_out, store_sem.at[rows_here + 1]
    )
    store_up.start()
    wo_send.wait_recv()
    wo_out[...] = (own_part + wo_got[...].astype(f32)).astype(low)
    for i in range(parts):
        down_send(i).wait_send()
    for i in range(mine):
        up_send(i).wait_send()
    wo_send.wait_send()
    for item in store_final + [store_down, store_up]:
        item.wait()


def middle(x, context, ids, vectors, text_gradient, w_out, w_up, w_down, dp_size):
    rows_here, size, width = x.shape
    ff = w_up.shape[1]
    parts = ff // width
    tokens = rows_here * size
    low = jnp.bfloat16
    f32 = jnp.float32
    shape = jax.ShapeDtypeStruct
    whole = pl.BlockSpec(memory_space=pltpu.VMEM)
    outside = pl.BlockSpec(memory_space=pl.ANY)
    chunks = max(dp_size, parts)
    chunk = ff // chunks // 2
    return pl.pallas_call(
        middle_kernel,
        out_shape=(
            shape((rows_here * NSEG, width), low),
            shape((rows_here * NSEG, 1), f32),
            shape(vectors.shape, f32),
            shape((rows_here, size, width), low),
            shape((rows_here, size, width), f32),
            shape((width, width // 2), low),
            shape((rows_here, size, width), low),
            shape((parts // 2, width, width), low),
            shape((chunks, chunk, width), low),
        ),
        in_specs=[whole] * 6 + [outside] * 2,
        out_specs=(whole,) * 6 + (outside,) * 3,
        scratch_shapes=[
            pltpu.VMEM((parts, width, width), low),
            pltpu.VMEM((parts, width, width), low),
            pltpu.VMEM((tokens, width), f32),
            pltpu.VMEM((tokens, 1), f32),
            pltpu.VMEM((tokens, width), low),
            pltpu.VMEM((width, tokens), low),
            pltpu.VMEM((parts, tokens, width), low),
            pltpu.VMEM((parts, tokens, width), low),
            pltpu.VMEM((tokens, width), f32),
            pltpu.VMEM((tokens, width), low),
            pltpu.VMEM((rows_here, size, width), low),
            pltpu.VMEM((parts, width, width), low),
            pltpu.VMEM((parts // 2, width, width), low),
            pltpu.VMEM((chunks, 2, chunk, width), low),
            pltpu.VMEM((chunks, chunk, width), low),
            pltpu.VMEM((width, width // 2), low),
            pltpu.VMEM((width, width // 2), low),
            pltpu.SemaphoreType.DMA((2 * parts + 1,)),
            pltpu.SemaphoreType.DMA((2 * parts + 1,)),
            pltpu.SemaphoreType.DMA((2, parts)),
            pltpu.SemaphoreType.DMA((rows_here + 2,)),
        ],
        compiler_params=pltpu.CompilerParams(
            vmem_limit_bytes=63 * 2**20, collective_id=2, has_side_effects=True
        ),
        cost_estimate=pl.CostEstimate(
            flops=2 * tokens * width * (6 * ff + 3 * width),
            bytes_accessed=2 * (5 * ff * width + 8 * tokens * width),
            transcendentals=2 * tokens * ff,
        ),
    )(x, context, ids, vectors, text_gradient, w_out, w_up, w_down)


class Links:
    def __init__(self, send_sem, recv_sem):
        self.send_sem, self.recv_sem = send_sem, recv_sem
        self.slots, self.copies = {}, {}

    def start(self, name, source, target, device):
        slot = self.slots.setdefault(name, len(self.slots))
        copy = pltpu.make_async_remote_copy(
            src_ref=source, dst_ref=target, send_sem=self.send_sem.at[slot],
            recv_sem=self.recv_sem.at[slot], device_id=device, device_id_type=MESH,
        )
        copy.start()
        self.copies[name] = copy

    def arrived(self, *names):
        for name in names:
            self.copies[name].wait_recv()

    def finish(self):
        for copy in self.copies.values():
            copy.wait_send()


def add_into(target, others, count):
    def one(i, carry):
        total = target[i].astype(jnp.float32)
        for other in others:
            total = total + other[i].astype(jnp.float32)
        target[i] = total.astype(target.dtype)
        return carry

    lax.fori_loop(0, count, one, 0)


def add_up(parts):
    total = parts[0].astype(jnp.float32)
    for part in parts[1:]:
        total = total + part.astype(jnp.float32)
    return total


def attend_back_kernel(
    fused,
    x_ref, ids_ref, lse_ref, w_query, w_key, w_value, pool_ref, count_ref, vector_ref,
    x_hbm, q_hbm, k_hbm, v_hbm, context_hbm, grad_hbm, mixed_hbm, up_hbm, down_hbm, out_hbm,
    dx_out, pool_out, vector_out, square_out, up_out, down_out, wo_out,
    x_got, q_ref, k_ref, v_ref, context_ref, grad_ref, bias_ref, dq_ref, dk_ref, dv_ref, dw_ref,
    dx_acc, dx_sent, dx_far, dx_near_got, dx_far_got, pool_parts, pool_got, vec_parts, vec_got,
    gb_ref, gb_got, s1_x, s1_y, s1_z, s2_y, s2_z, s2_s, s2_x,
    u_ref, u_x, u_y, u_z, d_ref, d_y, d_z, d_s, d_x, o_ref, o_y, o_z, o_s, o_x,
    send_sem, recv_sem, row_sem, local_sem,
):
    rows_here, size, width = x_ref.shape
    half = width // 2
    low = jnp.bfloat16
    me, place = lax.axis_index("ctx"), lax.axis_index("dp")
    core, side = me % 2, me // 2
    near, across = me + 1 - 2 * core, (me + 2) % 4
    near_dev, across_dev = {"ctx": near}, {"ctx": across}
    y, z = place % 2, place // 2
    y_dev = {"dp": place + 1 - 2 * y}
    z_at = (z + 1 - 2 * (z % 2), (z + 2) % 4, 3 - z)
    z_dev = [{"dp": other * 2 + y} for other in z_at]
    peers = [near_dev, across_dev] + ([y_dev] + z_dev if fused else [])

    barrier = pltpu.get_barrier_semaphore()
    for peer in peers:
        pl.semaphore_signal(barrier, inc=1, device_id=peer, device_id_type=MESH)
    pl.semaphore_wait(barrier, len(peers))
    links = Links(send_sem, recv_sem)

    def load_row(r):
        slot = r % 2
        pairs = (
            (k_hbm, k_ref), (v_hbm, v_ref), (q_hbm, q_ref), (context_hbm, context_ref),
            (grad_hbm, grad_ref),
        )
        copies = [
            pltpu.make_async_copy(source.at[r], target.at[slot], row_sem.at[slot, i])
            for i, (source, target) in enumerate(pairs)
        ]
        return copies + [
            pltpu.make_async_copy(x_hbm.at[:, r], x_got.at[slot], row_sem.at[slot, 5])
        ]

    for item in load_row(0):
        item.start()
    load_mixed = pltpu.make_async_copy(mixed_hbm, dx_acc, local_sem.at[0])
    load_mixed.start()
    links.start("pool0", pool_ref, pool_got.at[0], near_dev)
    if fused:
        links.start("up_x", up_hbm.at[1 - side], u_x, across_dev)
        links.start("down_y", down_hbm.at[:, 1 - y], d_y, y_dev)
        links.start("out_y", out_hbm.at[:, 1 - y], o_y, y_dev)
        load_parts = [
            pltpu.make_async_copy(up_hbm.at[side], u_ref, local_sem.at[1]),
            pltpu.make_async_copy(down_hbm.at[:, y], d_ref, local_sem.at[2]),
            pltpu.make_async_copy(out_hbm.at[:, y], o_ref, local_sem.at[3]),
        ]
        for item in load_parts:
            item.start()

    def step_one():
        links.arrived("pool0")
        pool_parts[...] = add_up([pool_ref[...], pool_got[0]]).astype(low)
        links.start("pool1", pool_parts, pool_got.at[1], across_dev)
        if not fused:
            return
        for item in load_parts:
            item.wait()
        links.arrived("down_y", "out_y")
        add_into(d_ref, [d_y], 4)
        add_into(o_ref, [o_y], 4)
        for o in range(3):
            links.start(f"down_z{o}", d_ref.at[z_at[o]], d_z.at[o], z_dev[o])
            links.start(f"out_z{o}", o_ref.at[z_at[o]], o_z.at[o], z_dev[o])

    def step_two():
        links.arrived("pool1")
        pool_out[...] = add_up([pool_parts[...], pool_got[1]]) / count_ref[...]
        if not fused:
            return
        links.arrived("up_x")
        for i in range(4):
            add_into(u_ref.at[i], [u_x.at[i]], 2)
        links.start("up_y", u_ref.at[:, 1 - y], u_y, y_dev)

    def step_three():
        if not fused:
            return
        links.arrived("up_y")

        def one(i, carry):
            u_ref[i, y] = add_up([u_ref[i, y], u_y[i]]).astype(low)
            return carry

        lax.fori_loop(0, 4, one, 0)
        for o in range(3):
            links.start(f"up_z{o}", u_ref.at[z_at[o], y], u_z.at[o], z_dev[o])

    def step_four():
        if not fused:
            return
        links.arrived("down_z0", "down_z1", "down_z2", "out_z0", "out_z1", "out_z2")
        d_s[...] = add_up([d_ref[z]] + [d_z[o] for o in range(3)]).astype(low)
        o_s[...] = add_up([o_ref[z]] + [o_z[o] for o in range(3)]).astype(low)
        links.start("down_x", d_s, d_x, across_dev)
        links.start("out_x", o_s, o_x, across_dev)

    def step_five():
        if not fused:
            return
        links.arrived("up_z0", "up_z1", "up_z2")
        up_out[me] = add_up([u_ref[z, y]] + [u_z[o] for o in range(3)]).astype(low)
        links.start("up_gather", up_out.at[me], up_out.at[me], across_dev)

    def step_six():
        if not fused:
            return
        links.arrived("down_x", "out_x")
        down_out[core] = add_up([d_s[...], d_x[...]]).astype(low)
        wo_out[core] = add_up([o_s[...], o_x[...]]).astype(low)
        links.start("down_gather", down_out.at[core], down_out.at[core], near_dev)
        links.start("out_gather", wo_out.at[core], wo_out.at[core], near_dev)
        links.arrived("up_gather")
        links.start("up_near0", up_out.at[me], up_out.at[me], near_dev)
        links.start("up_near1", up_out.at[across], up_out.at[across], near_dev)

    row = lax.broadcasted_iota(jnp.int32, (PAIR, size), 0)

    def attend_pairs(r, first, last):
        slot = r % 2

        def one_pair(pair, carry):
            columns = pl.ds(pl.multiple_of(pair * PAIR, PAIR), PAIR)
            grad = grad_ref[slot, :, columns]
            q_both = split_heads(q_ref[slot, :, columns])
            g_both = split_heads(grad)
            product = grad.astype(jnp.float32) * context_ref[slot, :, columns].astype(jnp.float32)
            product = product.T
            delta = jnp.concatenate(
                [
                    jnp.sum(product[:HEAD_DIM], axis=0, keepdims=True),
                    jnp.sum(product[HEAD_DIM:], axis=0, keepdims=True),
                ],
                axis=1,
            )
            lse = jnp.concatenate(
                [lse_ref[r, pl.ds(2 * pair, 1), :], lse_ref[r, pl.ds(2 * pair + 1, 1), :]], axis=1
            )
            dq = jnp.zeros((PAIR, 2 * size), jnp.float32)
            for j in range(4):
                rows = pl.ds(j * size, size)
                keys = k_ref[slot, rows, columns]
                bias = bias_ref[rows, :]
                bias = jnp.concatenate([bias, bias], axis=1)
                probs = jnp.exp(dot_nt(keys, q_both) + bias - lse)
                grad_s = probs * (dot_nt(v_ref[slot, rows, columns], g_both) - delta)
                grad_s = grad_s.astype(low)
                dv_ref[rows, columns] = matmul(probs.astype(low), g_both).astype(low)
                dk_ref[rows, columns] = matmul(grad_s, q_both).astype(low)
                dq = dq + matmul(keys.T, grad_s)
            dq = jnp.where(row < HEAD_DIM, dq[:, :size], dq[:, size:]) * HEAD_DIM ** (-0.5)
            dq_ref[:, columns] = dq.T.astype(low)
            return carry

        lax.fori_loop(first, last, one_pair, 0)

    def weight_parts(r):
        slot = r % 2

        def x_block(j):
            return x_ref[r] if j == 0 else x_got[slot, j - 1]

        def one_part(i, carry):
            columns = pl.ds(pl.multiple_of(i * (width // 3), 128), width // 3)
            parts = (
                dot_tn(x_ref[r], dq_ref[:, columns]),
                sum(dot_tn(x_block(j), dk_ref[pl.ds(j * size, size), columns]) for j in range(4)),
                sum(dot_tn(x_block(j), dv_ref[pl.ds(j * size, size), columns]) for j in range(4)),
            )
            for n, part in enumerate(parts):
                dw_ref[n, :, columns] = part if r == 0 else dw_ref[n, :, columns] + part
            return carry

        lax.fori_loop(0, 3, one_part, 0)
        biases = jnp.concatenate(
            [
                jnp.sum(source[...].astype(jnp.float32), axis=0, keepdims=True)
                for source in (dq_ref, dv_ref)
            ],
            axis=0,
        )
        vec_parts[0, 0:2, :] = biases if r == 0 else vec_parts[0, 0:2, :] + biases

    def input_parts(r):
        for j in range(4):
            rows = pl.ds(j * size, size)
            part = dot_nt(dk_ref[rows, :], w_key[...]) + dot_nt(dv_ref[rows, :], w_value[...])
            if j == 0:
                dx_acc[r] = dx_acc[r] + part + dot_nt(dq_ref[...], w_query[...])
            elif j == 2:
                dx_far[r] = part.astype(low)
            else:
                dx_sent[r, j // 2] = part.astype(low)
        links.start(f"dx_near{r}", dx_sent.at[r], dx_near_got.at[r], near_dev)

    def input_near(r):
        links.arrived(f"dx_near{r}")
        dx_far[r] = add_up([dx_far[r], dx_near_got[r, 1]]).astype(low)
        links.start(f"dx_far{r}", dx_far.at[r], dx_far_got.at[r], across_dev)
        dx_acc[r] = dx_acc[r] + dx_near_got[r, 0].astype(jnp.float32)

    def input_done(r):
        links.arrived(f"dx_far{r}")
        dx_out[r] = add_up([dx_acc[r], dx_far_got[r]]).astype(low)

    vec_parts[0] = vector_ref[...]
    for r in range(rows_here):
        slot = r % 2
        for item in load_row(r):
            item.wait()
        if r + 1 < rows_here:
            for item in load_row(r + 1):
                item.start()
        for j in range(4):
            seg_key = jnp.broadcast_to(
                ids_ref[j, r : r + 1, :].astype(jnp.float32), (PAIR, size)
            ).T[:, :1]
            seg_query = ids_ref[0, r : r + 1, :].astype(jnp.float32)
            bias_ref[j * size : (j + 1) * size, :] = jnp.where(seg_key == seg_query, 0.0, MASKED)
        attend_pairs(r, 0, HEADS // 4)
        if r == 1:
            step_one()
            input_near(0)
        if r == 2:
            step_three()
            input_near(1)
        attend_pairs(r, HEADS // 4, HEADS // 2)
        if r == 0:
            load_mixed.wait()
        if r == 1:
            step_two()
            input_done(0)
        if r == 2:
            step_four()
            input_done(1)
        weight_parts(r)
        if r + 1 < rows_here:
            input_parts(r)

    r = rows_here - 1
    if not fused:
        input_parts(r)
        for n in range(3):
            square_out[n] = dw_ref[n].astype(low)
        vector_out[...] = vec_parts[0]
        input_near(r)
        input_done(r)
        links.finish()
        return

    depth = gb_ref.shape[3]
    for n in range(3):
        for h in range(2):
            part = dw_ref[n, :, h * half : (h + 1) * half].astype(low)
            gb_ref[h, :, :, :, n * half : (n + 1) * half] = part.reshape(4, 2, depth, half)
    links.start("square_core", gb_ref.at[1 - core], gb_got, near_dev)
    links.start("vector0", vec_parts.at[0], vec_got.at[0], near_dev)
    input_parts(r)
    step_five()
    cut = s1_x.shape[3]
    own = pl.ds(pl.multiple_of(side * cut, 128), cut)
    its = pl.ds(pl.multiple_of((1 - side) * cut, 128), cut)
    rest = pl.ds(2 * cut, 3 * half - 2 * cut)
    links.arrived("square_core")
    for i in range(4):
        add_into(gb_ref.at[core, i], [gb_got.at[i]], 2)
    g = gb_ref.at[core]
    links.start("s2_y", g.at[:, 1 - y, :, rest], s2_y, y_dev)
    links.start("s1_x", g.at[:, :, :, its], s1_x, across_dev)
    links.arrived("vector0")
    vec_parts[1] = vec_parts[0] + vec_got[0]
    links.start("vector1", vec_parts.at[1], vec_got.at[1], across_dev)
    input_near(r)
    step_six()
    links.arrived("vector1")
    vec_parts[2] = vec_parts[1] + vec_got[1]
    links.start("vector2", vec_parts.at[2], vec_got.at[2], y_dev)

    links.arrived("s1_x")
    for i in range(4):
        for j in range(2):
            g[i, j, :, own] = add_up([g[i, j, :, own], s1_x[i, j]]).astype(low)
    links.start("s1_y", g.at[:, 1 - y, :, own], s1_y, y_dev)
    links.arrived("s2_y")
    for i in range(4):
        g[i, y, :, rest] = add_up([g[i, y, :, rest], s2_y[i]]).astype(low)
    for o in range(3):
        links.start(f"s2_z{o}", g.at[z_at[o], y, :, rest], s2_z.at[o], z_dev[o])
    links.arrived("vector2")
    vec_parts[3] = vec_parts[2] + vec_got[2]
    for o in range(3):
        links.start(f"vector_z{o}", vec_parts.at[3], vec_got.at[3 + o], z_dev[o])
    links.arrived("s1_y")
    for i in range(4):
        g[i, y, :, own] = add_up([g[i, y, :, own], s1_y[i]]).astype(low)
    for o in range(3):
        links.start(f"s1_z{o}", g.at[z_at[o], y, :, own], s1_z.at[o], z_dev[o])
    input_done(r)
    links.arrived("s2_z0", "s2_z1", "s2_z2")
    s2_s[...] = add_up([g[z, y, :, rest]] + [s2_z[o] for o in range(3)]).astype(low)
    links.start("s2_x", s2_s, s2_x, across_dev)
    links.arrived("s1_z0", "s1_z1", "s1_z2")
    square_out[core, :, own] = add_up([g[z, y, :, own]] + [s1_z[o] for o in range(3)]).astype(low)
    links.start(
        "s1_gather", square_out.at[core, :, own], square_out.at[core, :, own], across_dev
    )
    links.arrived("vector_z0", "vector_z1", "vector_z2")
    vector_out[...] = vec_parts[3] + (vec_got[3] + (vec_got[4] + vec_got[5]))
    links.arrived("s2_x")
    square_out[core, :, rest] = add_up([s2_s[...], s2_x[...]]).astype(low)
    links.arrived("s1_gather")
    links.start("square_gather", square_out.at[core], square_out.at[core], near_dev)
    links.arrived("down_gather", "out_gather", "up_near0", "up_near1", "square_gather")
    links.finish()


def attend_back(
    fused, x, ids, lse, w_query, w_key, w_value, pool, counts, vectors,
    x_got, q, k, v, context, grad, mixed, up, down, out,
):
    rows_here, size, width = x.shape
    keys = size * 4
    half = width // 2
    low = jnp.bfloat16
    f32 = jnp.float32
    whole = pl.BlockSpec(memory_space=pltpu.VMEM)
    outside = pl.BlockSpec(memory_space=pl.ANY)
    shape = jax.ShapeDtypeStruct
    up_rows, down_rows = (up.shape[3], down.shape[2]) if fused else (16, 16)
    cut = 2 * 128 if fused else 128
    rest = 3 * half - 2 * cut
    w = width if fused else 128
    h = half if fused else 128
    c3 = 3 * half if fused else 128
    rest = rest if fused else 128
    square_shape = (2, up_rows, 3 * half) if fused else (3, width, width)
    vec = vectors.shape
    scratch = [
        pltpu.VMEM((2, 3, size, width), low),
        pltpu.VMEM((2, size, width), low),
        pltpu.VMEM((2, keys, width), low),
        pltpu.VMEM((2, keys, width), low),
        pltpu.VMEM((2, size, width), low),
        pltpu.VMEM((2, size, width), low),
        pltpu.VMEM((keys, size), f32),
        pltpu.VMEM((size, width), low),
        pltpu.VMEM((keys, width), low),
        pltpu.VMEM((keys, width), low),
        pltpu.VMEM((3, width, width), f32),
        pltpu.VMEM((rows_here, size, width), f32),
        pltpu.VMEM((rows_here, 2, size, width), low),
        pltpu.VMEM((rows_here, size, width), low),
        pltpu.VMEM((rows_here, 2, size, width), low),
        pltpu.VMEM((rows_here, size, width), low),
        pltpu.VMEM(pool.shape, low),
        pltpu.VMEM((2,) + pool.shape, low),
        pltpu.VMEM((4,) + vec, f32),
        pltpu.VMEM((6,) + vec, f32),
        pltpu.VMEM((2, 4, 2, up_rows, c3), low),
        pltpu.VMEM((4, 2, up_rows, c3), low),
        pltpu.VMEM((4, 2, up_rows, cut), low),
        pltpu.VMEM((4, up_rows, cut), low),
        pltpu.VMEM((3, up_rows, cut), low),
        pltpu.VMEM((4, up_rows, rest), low),
        pltpu.VMEM((3, up_rows, rest), low),
        pltpu.VMEM((up_rows, rest), low),
        pltpu.VMEM((up_rows, rest), low),
        pltpu.VMEM((4, 2, up_rows, w), low),
        pltpu.VMEM((4, 2, up_rows, w), low),
        pltpu.VMEM((4, up_rows, w), low),
        pltpu.VMEM((3, up_rows, w), low),
        pltpu.VMEM((4, down_rows, w), low),
        pltpu.VMEM((4, down_rows, w), low),
        pltpu.VMEM((3, down_rows, w), low),
        pltpu.VMEM((down_rows, w), low),
        pltpu.VMEM((down_rows, w), low),
        pltpu.VMEM((4, up_rows, h), low),
        pltpu.VMEM((4, up_rows, h), low),
        pltpu.VMEM((3, up_rows, h), low),
        pltpu.VMEM((up_rows, h), low),
        pltpu.VMEM((up_rows, h), low),
        pltpu.SemaphoreType.DMA((56,)),
        pltpu.SemaphoreType.DMA((56,)),
        pltpu.SemaphoreType.DMA((2, 6)),
        pltpu.SemaphoreType.DMA((4,)),
    ]
    return pl.pallas_call(
        functools.partial(attend_back_kernel, fused),
        out_shape=(
            shape((rows_here, size, width), low),
            shape(pool.shape, f32),
            shape(vec, f32),
            shape(square_shape, low),
            shape((4, up_rows, w), low),
            shape((2, down_rows, w), low),
            shape((2, up_rows, h), low),
        ),
        in_specs=[whole] * 9 + [outside] * 10,
        out_specs=(whole,) * 7,
        scratch_shapes=scratch,
        compiler_params=pltpu.CompilerParams(
            vmem_limit_bytes=63 * 2**20, collective_id=1, has_side_effects=True
        ),
        cost_estimate=pl.CostEstimate(
            flops=rows_here
            * (4 * (size + 2 * keys) * width * width + 40 * size * keys * width),
            bytes_accessed=2 * (16 * width * width + 9 * keys * width),
            transcendentals=rows_here * HEADS * size * keys,
        ),
    )(
        x, ids, lse, w_query, w_key, w_value, pool, counts, vectors,
        x_got, q, k, v, context, grad, mixed, up, down, out,
    )


def radices_of(count):
    if count == 8:
        return ((1, 2), (2, 4))
    digits = []
    stride = 1
    while stride < count:
        digits.append((stride, 2))
        stride *= 2
    return tuple(digits)


def exchange(piece, axis_name, stride, offset):
    count = lax.axis_size(axis_name)
    pairs = [(i, i ^ (offset * stride)) for i in range(count)]
    return lax.ppermute(piece, axis_name, pairs)


def digit_of(axis_name, stride, radix):
    return (lax.axis_index(axis_name) // stride) % radix


def scatter_digit(pieces, place, axis_name, stride, radix):
    here = digit_of(axis_name, stride, radix)
    received = [
        exchange(
            lax.dynamic_index_in_dim(pieces, here ^ offset, place, keepdims=False).astype(
                jnp.bfloat16
            ),
            axis_name, stride, offset,
        )
        for offset in range(1, radix)
    ]
    total = lax.dynamic_index_in_dim(pieces, here, place, keepdims=False).astype(jnp.float32)
    for item in received:
        total = total + item.astype(jnp.float32)
    return total.astype(jnp.bfloat16)


def halve(piece, place, axis_name, stride):
    half = piece.shape[place] // 2
    here = digit_of(axis_name, stride, 2)
    sent = lax.dynamic_slice_in_dim(piece, (1 - here) * half, half, place).astype(jnp.bfloat16)
    kept = lax.dynamic_slice_in_dim(piece, here * half, half, place).astype(jnp.float32)
    return (kept + exchange(sent, axis_name, stride, 1).astype(jnp.float32)).astype(jnp.bfloat16)


def join(piece, place, axis_name, stride):
    here = digit_of(axis_name, stride, 2)
    other = exchange(piece, axis_name, stride, 1)
    first = jnp.where(here == 0, piece, other)
    second = jnp.where(here == 0, other, piece)
    return jnp.concatenate([first, second], axis=place)


def scatter_rows(group, dp_size):
    digits = radices_of(dp_size)
    shape = tuple(r for _, r in reversed(digits))
    group = group.reshape(shape + (group.shape[0] // dp_size, group.shape[1]))
    for place, (stride, radix) in zip(range(len(digits) - 1, -1, -1), digits):
        group = scatter_digit(group, place, "dp", stride, radix)
    return group


def finish_weight(flat, dp_size, side):
    flat = scatter_rows(flat, dp_size)
    flat = flat.astype(jnp.float32) + exchange(flat, "ctx", 2, 1).astype(jnp.float32)
    return join(flat.astype(jnp.bfloat16), side, "ctx", 1).astype(jnp.float32)


def reduce_weight(gradient, dp_size, side):
    return finish_weight(halve(gradient, side, "ctx", 1), dp_size, side)


def per_device(
    hidden_in,
    seg_ids,
    valid,
    w_query,
    b_query,
    w_key,
    w_value,
    b_value,
    w_out,
    b_out,
    gain_attn,
    shift_attn,
    w_up,
    b_up,
    w_down,
    b_down,
    gain_ffn,
    shift_ffn,
    pooled_text_gradient,
):
    row_count, group_size, model_width = hidden_in.shape
    dp_size, ctx_size = lax.axis_size("dp"), lax.axis_size("ctx")
    vectors = jnp.concatenate(
        [b_query, b_value, b_out, gain_attn, shift_attn, b_down, gain_ffn, shift_ffn, b_up]
    )
    vectors = jnp.pad(vectors, (0, -vectors.shape[0] % (8 * model_width)))
    vectors = vectors.astype(jnp.float32).reshape(-1, model_width)
    ids = jnp.concatenate([seg_ids, valid], axis=0)
    ids = jnp.pad(ids, ((0, 8 - ids.shape[0]), (0, 0)))
    q_all, context, lse_all, ids_got, x_got, k_all, v_all = attend(
        hidden_in, ids, vectors, w_query, w_key, w_value
    )
    pool, counts, vector_parts, grad_context, grad_mixed, out, final_out, up, down = middle(
        hidden_in, context, ids_got, vectors, pooled_text_gradient, w_out, w_up, w_down, dp_size
    )
    ff_width = w_up.shape[1]
    rows_here, ff_here = model_width // dp_size, ff_width // dp_size
    fused = dp_size == 8 and rows_here % 16 == 0 and model_width % 768 == 0
    if fused:
        up_part = up.reshape(2, 4, 2, rows_here, -1)
        down_part = down.reshape(4, 2, ff_here // 2, -1)
        out_part = out.reshape(4, 2, rows_here, -1)
    else:
        up_part = down_part = out_part = jnp.zeros((16, 128), jnp.bfloat16)
    grad_input, pooled, vector_sum, squares, up_sum, down_sum, out_sum = attend_back(
        fused, hidden_in, ids_got, lse_all, w_query, w_key, w_value,
        pool, counts, vector_parts, x_got, q_all, k_all, v_all, context, grad_context, grad_mixed,
        up_part, down_part, out_part,
    )
    pooled = pooled.reshape(row_count, NSEG, model_width)
    wide_out = lambda piece: piece.astype(jnp.float32)
    if fused:
        half = model_width // 2
        square_sums = [
            wide_out(squares[:, :, n * half : (n + 1) * half])
            .transpose(1, 0, 2)
            .reshape(rows_here, model_width)
            for n in range(3)
        ]
        square_sums.append(wide_out(out_sum).transpose(1, 0, 2).reshape(rows_here, model_width))
        up_sum = (
            wide_out(up_sum).reshape(2, 2, rows_here, -1).transpose(2, 1, 0, 3)
            .reshape(rows_here, ff_width)
        )
        down_sum = wide_out(down_sum).reshape(ff_here, model_width)
    else:
        square_sums = [reduce_weight(squares[n], dp_size, 1) for n in range(3)]
        square_sums.append(finish_weight(out, dp_size, 1))
        up_sum = finish_weight(up.transpose(1, 0, 2).reshape(model_width, -1), dp_size, 1)
        down_sum = finish_weight(down.reshape(-1, model_width), dp_size, 0)
        vector_sum = lax.psum(vector_sum, ("dp", "ctx"))
    place = lax.axis_index("dp")
    sums = lax.dynamic_slice_in_dim(vector_sum[:8], place * rows_here, rows_here, 1)
    sum_bu = lax.dynamic_slice_in_dim(
        vector_sum[8 : 8 + ff_width // model_width].reshape(-1), place * ff_here, ff_here
    )
    results = (
        square_sums[0], sums[0], square_sums[1], square_sums[2], sums[1], square_sums[3],
        sums[2], sums[3], sums[4], up_sum, sum_bu, down_sum, sums[5], sums[6], sums[7],
    )
    return (
        final_out,
        pooled,
        grad_input,
    ) + tuple(results)


def solution(mesh):
    placed = (
        P("dp", "ctx", None),
        P("dp", "ctx"),
        P("dp", "ctx"),
        P(),
        P(),
        P(),
        P(),
        P(),
        P(),
        P(),
        P(),
        P(),
        P(),
        P(),
        P(),
        P(),
        P(),
        P(),
        P("dp", None, None),
    )
    return jax.shard_map(
        per_device,
        mesh=mesh,
        in_specs=placed,
        out_specs=(
            P("dp", "ctx", None),
            P("dp", None, None),
            P("dp", "ctx", None),
            P("dp", None),
            P("dp"),
            P("dp", None),
            P("dp", None),
            P("dp"),
            P("dp", None),
            P("dp"),
            P("dp"),
            P("dp"),
            P("dp", None),
            P("dp"),
            P("dp", None),
            P("dp"),
            P("dp"),
            P("dp"),
        ),
        check_vma=False,
    )
```

```python
import functools

import jax
import jax.numpy as jnp
from jax import lax
from jax.experimental import pallas as pl
from jax.experimental.pallas import tpu as pltpu
from jax.sharding import PartitionSpec as P

HEADS = 12
HEAD_DIM = 64
NSEG = 16


eps = 1e-12


def matmul(left_side, right_side):
    return jnp.dot(left_side, right_side, preferred_element_type=jnp.float32)


PAIR = 2 * HEAD_DIM
MESH = pl.DeviceIdType.MESH
MASKED = -1e30


def dot_nt(left_side, right_side):
    return lax.dot_general(
        left_side, right_side, (((1,), (1,)), ((), ())), preferred_element_type=jnp.float32
    )


def dot_tn(left_side, right_side):
    return lax.dot_general(
        left_side, right_side, (((0,), (0,)), ((), ())), preferred_element_type=jnp.float32
    )


def split_heads(pair):
    lane = lax.broadcasted_iota(jnp.int32, pair.shape, 1)
    zero = jnp.zeros_like(pair)
    return jnp.concatenate(
        [jnp.where(lane < HEAD_DIM, pair, zero), jnp.where(lane < HEAD_DIM, zero, pair)], axis=0
    )


def attend_kernel(
    x_ref, ids_ref, vec_ref, w_query, w_key, w_value,
    q_out, context_out, lse_out, ids_out, x_hbm, k_hbm, v_hbm,
    x_got, k_ref, v_ref, bias_ref, stat_ref, send_sem, recv_sem, local_sem,
):
    rows_here, size, width = x_ref.shape
    me = lax.axis_index("ctx")
    one = me + 1 - 2 * (me % 2)
    two = (me + 2) % 4
    three = (one + 2) % 4
    low = jnp.bfloat16

    barrier = pltpu.get_barrier_semaphore()
    for peer in (one, two, three):
        pl.semaphore_signal(barrier, inc=1, device_id={"ctx": peer}, device_id_type=MESH)
    pl.semaphore_wait(barrier, 3)

    def send(source, target, slot, peer):
        return pltpu.make_async_remote_copy(
            src_ref=source, dst_ref=target, send_sem=send_sem.at[slot],
            recv_sem=recv_sem.at[slot], device_id={"ctx": peer}, device_id_type=MESH,
        )

    ids_out[0] = ids_ref[...]
    ids_sends = [send(ids_ref, ids_out.at[j + 1], j, peer) for j, peer in enumerate((one, two, three))]
    near = send(x_ref, x_got.at[0], 3, one)

    def far(r):
        return send(x_ref.at[r], x_got.at[1, r], 4 + r, two)

    def passed(r):
        return send(x_got.at[1, r], x_got.at[2, r], 4 + rows_here + r, one)

    far(0).start()
    near.start()
    for item in ids_sends:
        item.start()
    for r in range(1, rows_here):
        far(r).start()

    def project(r, x, j):
        rows = pl.ds(j * size, size)
        k_ref[r, rows, :] = matmul(x, w_key[...]).astype(low)
        v_ref[r, rows, :] = (matmul(x, w_value[...]) + vec_ref[B_VALUE : B_VALUE + 1, :]).astype(low)

    def own_row(r, carry):
        x = x_ref[r]
        q = (matmul(x, w_query[...]) + vec_ref[B_QUERY : B_QUERY + 1, :]).astype(low)
        q_out[r] = (q * HEAD_DIM ** (-0.5)).astype(low)
        project(r, x, 0)
        return carry

    lax.fori_loop(0, rows_here, own_row, 0)
    near.wait_recv()

    def near_row(r, carry):
        project(r, x_got[0, r], 1)
        return carry

    lax.fori_loop(0, rows_here, near_row, 0)
    for item in ids_sends:
        item.wait_recv()
    lane = lax.broadcasted_iota(jnp.int32, (size, PAIR), 1)
    far(0).wait_recv()
    passed(0).start()

    def keep(r):
        return (
            pltpu.make_async_copy(k_ref.at[r], k_hbm.at[r], local_sem.at[0, r]),
            pltpu.make_async_copy(v_ref.at[r], v_hbm.at[r], local_sem.at[1, r]),
        )

    for r in range(rows_here):
        project(r, x_got[1, r], 2)
        passed(r).wait_recv()
        project(r, x_got[2, r], 3)
        for item in keep(r):
            item.start()
        seg_query = jnp.broadcast_to(
            ids_ref[r : r + 1, :].astype(jnp.float32), (PAIR, size)
        ).T[:, :1]
        for j in range(4):
            seg_key = ids_out[j, r : r + 1, :].astype(jnp.float32)
            bias_ref[:, j * size : (j + 1) * size] = jnp.where(seg_query == seg_key, 0.0, MASKED)
        stat_ref[...] = jnp.zeros_like(stat_ref)

        def one_pair(pair, carry, r=r):
            columns = pl.ds(pl.multiple_of(pair * PAIR, PAIR), PAIR)
            both = split_heads(q_out[r, :, columns])
            scores = dot_nt(both, k_ref[r, :, columns])
            scores = scores.reshape(2, size, scores.shape[1]) + bias_ref[...][None]
            top = jnp.max(scores, axis=-1, keepdims=True)
            weight = jnp.exp(scores - top)
            total = jnp.sum(weight, axis=-1, keepdims=True)
            mixed = matmul(
                weight.astype(low).reshape(2 * size, -1), v_ref[r, :, columns]
            ).reshape(2, size, PAIR) / total
            context_out[r, :, columns] = jnp.where(lane < HEAD_DIM, mixed[0], mixed[1]).astype(low)
            lse = top + jnp.log(total)
            stat = stat_ref[...]
            stat = jnp.where(lane == 2 * pair, lse[0], stat)
            stat_ref[...] = jnp.where(lane == 2 * pair + 1, lse[1], stat)
            return carry

        lax.fori_loop(0, HEADS // 2, one_pair, 0)
        lse_out[r] = stat_ref[...].T[: lse_out.shape[1]]
        if r + 1 < rows_here:
            far(r + 1).wait_recv()
            passed(r + 1).start()
    keep_x = pltpu.make_async_copy(x_got, x_hbm, local_sem.at[2, 0])
    keep_x.start()
    for r in range(rows_here):
        for item in keep(r):
            item.wait()
        far(r).wait_send()
        passed(r).wait_send()
    near.wait_send()
    for item in ids_sends:
        item.wait_send()
    keep_x.wait()


def attend(x, ids, vectors, w_query, w_key, w_value):
    rows_here, size, width = x.shape
    keys = size * 4
    low = jnp.bfloat16
    whole = pl.BlockSpec(memory_space=pltpu.VMEM)
    outside = pl.BlockSpec(memory_space=pl.ANY)
    slots = 4 + 2 * rows_here
    return pl.pallas_call(
        attend_kernel,
        out_shape=(
            jax.ShapeDtypeStruct((rows_here, size, width), low),
            jax.ShapeDtypeStruct((rows_here, size, width), low),
            jax.ShapeDtypeStruct((rows_here, 16, size), jnp.float32),
            jax.ShapeDtypeStruct((4,) + ids.shape, jnp.int32),
            jax.ShapeDtypeStruct((3,) + x.shape, low),
            jax.ShapeDtypeStruct((rows_here, keys, width), low),
            jax.ShapeDtypeStruct((rows_here, keys, width), low),
        ),
        in_specs=[whole] * 6,
        out_specs=(whole, whole, whole, whole, outside, outside, outside),
        scratch_shapes=[
            pltpu.VMEM((3,) + x.shape, low),
            pltpu.VMEM((rows_here, keys, width), low),
            pltpu.VMEM((rows_here, keys, width), low),
            pltpu.VMEM((size, keys), jnp.float32),
            pltpu.VMEM((size, PAIR), jnp.float32),
            pltpu.SemaphoreType.DMA((slots,)),
            pltpu.SemaphoreType.DMA((slots,)),
            pltpu.SemaphoreType.DMA((3, rows_here)),
        ],
        compiler_params=pltpu.CompilerParams(
            vmem_limit_bytes=56 * 2**20, collective_id=0, has_side_effects=True
        ),
        cost_estimate=pl.CostEstimate(
            flops=rows_here * (2 * (size + 2 * keys) * width * width + 16 * size * keys * width),
            bytes_accessed=2 * (3 * width * width + 9 * keys * width),
            transcendentals=rows_here * HEADS * size * keys,
        ),
    )(x, ids, vectors, w_query, w_key, w_value)


def gelu_both(u):
    size = jnp.abs(u)
    t = 1.0 / (1.0 + (0.3275911 * 0.5**0.5) * size)
    bell = jnp.exp(-0.5 * u * u)
    poly = t * (
        0.127414796 + t * (-0.142248368 + t * (0.7107068705 + t * (-0.7265760135 + t * 0.5307027145)))
    )
    tail = poly * bell
    cdf = jnp.where(u >= 0.0, 1.0 - tail, tail)
    return u * cdf, cdf + u * bell * 0.3989422804014327


def normalize(values_in):
    centre = jnp.mean(values_in, axis=-1, keepdims=True)
    centred = values_in - centre
    spread = jnp.mean(centred * centred, axis=-1, keepdims=True)
    scale = lax.rsqrt(spread + eps)
    return centred * scale, scale


def normalize_back(grad, unit, scale):
    mean_one = jnp.mean(grad, axis=-1, keepdims=True)
    mean_two = jnp.mean(grad * unit, axis=-1, keepdims=True)
    return (grad - mean_one - unit * mean_two) * scale


def column_sum(values_in):
    return jnp.sum(values_in, axis=0, keepdims=True)


B_QUERY, B_VALUE, B_OUT, GAIN_ONE, SHIFT_ONE, B_DOWN, GAIN_TWO, SHIFT_TWO, B_UP = range(9)


def middle_kernel(
    x_ref, context_ref, ids_ref, vec_ref, text_ref, w_out,
    up_hbm, down_hbm,
    pool_out, count_out, vector_out, grad_out, mixed_out, wo_out, final_hbm, up_out, down_out,
    w_up, w_down, unit_ref, scale_ref, normed_ref, normed_t, act_ref, slope_ref, acc_ref,
    g_ref, final_ref, upg_ref, up_got, downg_ref, down_got, wo_sent, wo_got,
    send_sem, recv_sem, load_sem, store_sem,
):
    rows_here, size, width = x_ref.shape
    tokens = rows_here * size
    parts = w_up.shape[0]
    half = width // 2
    low = jnp.bfloat16
    f32 = jnp.float32
    me = lax.axis_index("ctx")
    core = me % 2
    near = {"ctx": me + 1 - 2 * core}
    barrier = pltpu.get_barrier_semaphore()
    pl.semaphore_signal(barrier, inc=1, device_id=near, device_id_type=MESH)

    def vec(row):
        return vec_ref[row : row + 1, :]

    loads = []
    for i in range(parts):
        loads.append(
            (
                pltpu.make_async_copy(
                    up_hbm.at[:, pl.ds(i * width, width)], w_up.at[i], load_sem.at[0, i]
                ),
                pltpu.make_async_copy(
                    down_hbm.at[pl.ds(i * width, width)], w_down.at[i], load_sem.at[1, i]
                ),
            )
        )
    for pair in loads:
        for item in pair:
            item.start()

    def rows_of(r):
        return pl.ds(pl.multiple_of(r * size, size), size)

    text = lax.broadcasted_iota(jnp.int32, (NSEG, size), 0)

    def members(j, r):
        seg = ids_ref[j, r : r + 1, :]
        real = ids_ref[j, rows_here + r : rows_here + r + 1, :]
        return jnp.where((text == seg) & (real == 1), 1.0, 0.0)

    for r in range(rows_here):
        number = sum(jnp.sum(members(j, r), axis=1, keepdims=True) for j in range(4))
        count_out[r * NSEG : (r + 1) * NSEG, :] = jnp.maximum(number, 1.0)

    def first_norm(r, carry):
        rows = rows_of(r)
        mixed = x_ref[r].astype(f32) + (matmul(context_ref[r], w_out[...]) + vec(B_OUT))
        unit, scale = normalize(mixed)
        unit_ref[rows, :] = unit
        scale_ref[rows, :] = scale
        normed_ref[rows, :] = (unit * vec(GAIN_ONE) + vec(SHIFT_ONE)).astype(low)
        return carry

    lax.fori_loop(0, rows_here, first_norm, 0)
    for pair in loads:
        for item in pair:
            item.wait()

    def forward_part(i, carry):
        pre = matmul(normed_ref[...], w_up[i]) + vec_ref[pl.ds(B_UP + i, 1), :]
        act, slope = gelu_both(pre)
        act = act.astype(low)
        act_ref[i] = act
        slope_ref[i] = slope.astype(low)
        part = matmul(act, w_down[i])

        @pl.when(i == 0)
        def _():
            acc_ref[...] = part

        @pl.when(i > 0)
        def _():
            acc_ref[...] += part

        return carry

    lax.fori_loop(0, parts, forward_part, 0)
    normed_t[...] = normed_ref[...].T

    store_final = []
    vector_out[...] = jnp.zeros_like(vector_out)
    for r in range(rows_here):
        rows = pl.ds(r * size, size)
        normed = unit_ref[rows, :] * vec(GAIN_ONE) + vec(SHIFT_ONE)
        summed = normed + (acc_ref[rows, :] + vec(B_DOWN))
        unit, scale = normalize(summed)
        final = unit * vec(GAIN_TWO) + vec(SHIFT_TWO)
        high = final.astype(low)
        final_ref[r] = high
        item = pltpu.make_async_copy(final_ref.at[r], final_hbm.at[r], store_sem.at[r])
        item.start()
        store_final.append(item)
        own = members(0, r)
        own_low = own.astype(low)
        rest = (final - high.astype(f32)).astype(low)
        pool = matmul(own_low, high) + matmul(own_low, rest)
        pool_out[r * NSEG : (r + 1) * NSEG, :] = pool.astype(low)
        share = text_ref[r] / count_out[r * NSEG : (r + 1) * NSEG, :]
        grad = lax.dot_general(
            own, share, (((0,), (0,)), ((), ())), preferred_element_type=f32,
            precision=lax.Precision.HIGHEST,
        )
        back = normalize_back(grad * vec(GAIN_TWO), unit, scale)
        back_low = back.astype(low)
        acc_ref[rows, :] = back
        g_ref[rows, :] = back_low
        vector_out[GAIN_TWO : GAIN_TWO + 1, :] += column_sum(grad * unit)
        vector_out[SHIFT_TWO : SHIFT_TWO + 1, :] += column_sum(grad)
        vector_out[B_DOWN : B_DOWN + 1, :] += column_sum(back_low.astype(f32))

    pl.semaphore_wait(barrier, 1)

    def remote(source, target, slot):
        return pltpu.make_async_remote_copy(
            src_ref=source, dst_ref=target, send_sem=send_sem.at[slot],
            recv_sem=recv_sem.at[slot], device_id=near, device_id_type=MESH,
        )

    per_part = downg_ref.shape[0] // parts
    mine = parts // 2

    def up_send(i):
        return remote(upg_ref.at[i], up_got.at[i], i)

    def down_send(i):
        chunk = pl.ds(i * per_part, per_part)
        return remote(downg_ref.at[chunk, 1 - core], down_got.at[chunk], parts + i)

    def backward_part(step, carry):
        i = (step + mine * (1 - core)) % parts
        back = dot_nt(g_ref[...], w_down[i])
        back = (back * slope_ref[i].astype(f32)).astype(low)
        vector_out[pl.ds(B_UP + i, 1), :] = column_sum(back.astype(f32))
        acc_ref[...] += dot_nt(back, w_up[i])
        upg_ref[step] = matmul(normed_t[...], back).astype(low)

        @pl.when(step < mine)
        def _():
            up_send(step).start()

        part = dot_tn(act_ref[i], g_ref[...]).astype(low)
        downg_ref[pl.ds(i * per_part, per_part)] = part.reshape((per_part,) + downg_ref.shape[1:])
        down_send(i).start()
        return carry

    lax.fori_loop(0, parts, backward_part, 0)

    def first_back(r, carry):
        rows = rows_of(r)
        unit = unit_ref[rows, :]
        grad = acc_ref[rows, :]
        back = normalize_back(grad * vec(GAIN_ONE), unit, scale_ref[rows, :])
        back_low = back.astype(low)
        mixed_out[r] = back
        g_ref[rows, :] = back_low
        grad_out[r] = dot_nt(back_low, w_out[...]).astype(low)
        vector_out[GAIN_ONE : GAIN_ONE + 1, :] += column_sum(grad * unit)
        vector_out[SHIFT_ONE : SHIFT_ONE + 1, :] += column_sum(grad)
        vector_out[B_OUT : B_OUT + 1, :] += column_sum(back_low.astype(f32))
        return carry

    lax.fori_loop(0, rows_here, first_back, 0)

    def out_part(h):
        columns = pl.ds(pl.multiple_of(h * half, 128), half)
        total = jnp.zeros((width, half), f32)
        for r in range(rows_here):
            total = total + dot_tn(context_ref[r], g_ref[pl.ds(r * size, size), columns])
        return total

    wo_sent[...] = out_part(1 - core).astype(low)
    wo_send = remote(wo_sent, wo_got, 2 * parts)
    wo_send.start()
    own_part = out_part(core)

    def down_sum(i, carry):
        downg_ref[i, core] = (
            downg_ref[i, core].astype(f32) + down_got[i].astype(f32)
        ).astype(low)
        return carry

    for i in range(parts):
        down_send(i).wait_recv()
    lax.fori_loop(0, downg_ref.shape[0], down_sum, 0)
    store_down = pltpu.make_async_copy(downg_ref.at[:, core], down_out, store_sem.at[rows_here])
    store_down.start()
    for i in range(mine):
        up_send(i).wait_recv()

    def up_sum(n, carry):
        rows = pl.ds(pl.multiple_of(n * 128, 128), 128)
        for i in range(mine):
            upg_ref[mine + i, rows, :] = (
                upg_ref[mine + i, rows, :].astype(f32) + up_got[i, rows, :].astype(f32)
            ).astype(low)
        return carry

    lax.fori_loop(0, width // 128, up_sum, 0)
    store_up = pltpu.make_async_copy(
        upg_ref.at[pl.ds(mine, mine)], up_out, store_sem.at[rows_here + 1]
    )
    store_up.start()
    wo_send.wait_recv()
    wo_out[...] = (own_part + wo_got[...].astype(f32)).astype(low)
    for i in range(parts):
        down_send(i).wait_send()
    for i in range(mine):
        up_send(i).wait_send()
    wo_send.wait_send()
    for item in store_final + [store_down, store_up]:
        item.wait()


def middle(x, context, ids, vectors, text_gradient, w_out, w_up, w_down, dp_size):
    rows_here, size, width = x.shape
    ff = w_up.shape[1]
    parts = ff // width
    tokens = rows_here * size
    low = jnp.bfloat16
    f32 = jnp.float32
    shape = jax.ShapeDtypeStruct
    whole = pl.BlockSpec(memory_space=pltpu.VMEM)
    outside = pl.BlockSpec(memory_space=pl.ANY)
    chunks = max(dp_size, parts)
    chunk = ff // chunks // 2
    return pl.pallas_call(
        middle_kernel,
        out_shape=(
            shape((rows_here * NSEG, width), low),
            shape((rows_here * NSEG, 1), f32),
            shape(vectors.shape, f32),
            shape((rows_here, size, width), low),
            shape((rows_here, size, width), f32),
            shape((width, width // 2), low),
            shape((rows_here, size, width), low),
            shape((parts // 2, width, width), low),
            shape((chunks, chunk, width), low),
        ),
        in_specs=[whole] * 6 + [outside] * 2,
        out_specs=(whole,) * 6 + (outside,) * 3,
        scratch_shapes=[
            pltpu.VMEM((parts, width, width), low),
            pltpu.VMEM((parts, width, width), low),
            pltpu.VMEM((tokens, width), f32),
            pltpu.VMEM((tokens, 1), f32),
            pltpu.VMEM((tokens, width), low),
            pltpu.VMEM((width, tokens), low),
            pltpu.VMEM((parts, tokens, width), low),
            pltpu.VMEM((parts, tokens, width), low),
            pltpu.VMEM((tokens, width), f32),
            pltpu.VMEM((tokens, width), low),
            pltpu.VMEM((rows_here, size, width), low),
            pltpu.VMEM((parts, width, width), low),
            pltpu.VMEM((parts // 2, width, width), low),
            pltpu.VMEM((chunks, 2, chunk, width), low),
            pltpu.VMEM((chunks, chunk, width), low),
            pltpu.VMEM((width, width // 2), low),
            pltpu.VMEM((width, width // 2), low),
            pltpu.SemaphoreType.DMA((2 * parts + 1,)),
            pltpu.SemaphoreType.DMA((2 * parts + 1,)),
            pltpu.SemaphoreType.DMA((2, parts)),
            pltpu.SemaphoreType.DMA((rows_here + 2,)),
        ],
        compiler_params=pltpu.CompilerParams(
            vmem_limit_bytes=63 * 2**20, collective_id=2, has_side_effects=True
        ),
        cost_estimate=pl.CostEstimate(
            flops=2 * tokens * width * (6 * ff + 3 * width),
            bytes_accessed=2 * (5 * ff * width + 8 * tokens * width),
            transcendentals=2 * tokens * ff,
        ),
    )(x, context, ids, vectors, text_gradient, w_out, w_up, w_down)


class Links:
    def __init__(self, send_sem, recv_sem):
        self.send_sem, self.recv_sem = send_sem, recv_sem
        self.slots, self.copies = {}, {}

    def start(self, name, source, target, device):
        slot = self.slots.setdefault(name, len(self.slots))
        copy = pltpu.make_async_remote_copy(
            src_ref=source, dst_ref=target, send_sem=self.send_sem.at[slot],
            recv_sem=self.recv_sem.at[slot], device_id=device, device_id_type=MESH,
        )
        copy.start()
        self.copies[name] = copy

    def arrived(self, *names):
        for name in names:
            self.copies[name].wait_recv()

    def finish(self):
        for copy in self.copies.values():
            copy.wait_send()


def add_into(target, others, count):
    def one(i, carry):
        total = target[i].astype(jnp.float32)
        for other in others:
            total = total + other[i].astype(jnp.float32)
        target[i] = total.astype(target.dtype)
        return carry

    lax.fori_loop(0, count, one, 0)


def add_up(parts):
    total = parts[0].astype(jnp.float32)
    for part in parts[1:]:
        total = total + part.astype(jnp.float32)
    return total


def attend_back_kernel(
    fused,
    x_ref, ids_ref, lse_ref, w_query, w_key, w_value, pool_ref, count_ref, vector_ref,
    x_hbm, q_hbm, k_hbm, v_hbm, context_hbm, grad_hbm, mixed_hbm, up_hbm, down_hbm, out_hbm,
    dx_out, pool_out, vector_out, square_out, up_out, down_out, wo_out,
    x_got, x_t, q_ref, k_ref, v_ref, context_ref, grad_ref, bias_ref, dq_ref, dk_ref, dv_ref,
    dx_acc, dx_sent, dx_far, dx_near_got, dx_far_got, pool_parts, pool_got, vec_parts, vec_got,
    gb_ref, gb_got, g_y, g_z, g_s, g_x,
    u_ref, u_x, u_y, u_z, d_ref, d_y, d_z, d_s, d_x, o_ref, o_y, o_z, o_s, o_x,
    send_sem, recv_sem, row_sem, local_sem,
):
    rows_here, size, width = x_ref.shape
    per_group = q_ref.shape[2]
    groups = width // per_group
    cut = per_group // 2
    low = jnp.bfloat16
    me, place = lax.axis_index("ctx"), lax.axis_index("dp")
    core, side = me % 2, me // 2
    near, across = me + 1 - 2 * core, (me + 2) % 4
    near_dev, across_dev = {"ctx": near}, {"ctx": across}
    y, z = place % 2, place // 2
    y_dev = {"dp": place + 1 - 2 * y}
    z_at = (z + 1 - 2 * (z % 2), (z + 2) % 4, 3 - z)
    z_dev = [{"dp": other * 2 + y} for other in z_at]
    peers = [near_dev, across_dev] + ([y_dev] + z_dev if fused else [])

    barrier = pltpu.get_barrier_semaphore()
    for peer in peers:
        pl.semaphore_signal(barrier, inc=1, device_id=peer, device_id_type=MESH)
    pl.semaphore_wait(barrier, len(peers))
    links = Links(send_sem, recv_sem)

    def load_step(step):
        slot = step % 2
        group, r = divmod(step, rows_here)
        columns = pl.ds(group * per_group, per_group)
        pairs = (
            (k_hbm, k_ref), (v_hbm, v_ref), (q_hbm, q_ref), (context_hbm, context_ref),
            (grad_hbm, grad_ref),
        )
        copies = [
            pltpu.make_async_copy(source.at[r, :, columns], target.at[slot], row_sem.at[slot, i])
            for i, (source, target) in enumerate(pairs)
        ]
        if group == 0:
            copies.append(pltpu.make_async_copy(x_hbm.at[:, r], x_got.at[slot], row_sem.at[slot, 5]))
        return copies

    for item in load_step(0):
        item.start()
    load_mixed = pltpu.make_async_copy(mixed_hbm, dx_acc, local_sem.at[0])
    links.start("pool0", pool_ref, pool_got.at[0], near_dev)
    piece = d_ref.shape[1] // 2
    if fused:
        links.start("up_x", up_hbm.at[1 - side], u_x, across_dev)
        links.start("out_y", out_hbm.at[:, 1 - y], o_y, y_dev)
        for h in range(2):
            rows = pl.ds(h * piece, piece)
            links.start(f"down_y{h}", down_hbm.at[:, 1 - y, rows], d_y.at[:, rows], y_dev)
        load_parts = [
            pltpu.make_async_copy(out_hbm.at[:, y], o_ref, local_sem.at[1]),
            pltpu.make_async_copy(down_hbm.at[:, y], d_ref, local_sem.at[2]),
            pltpu.make_async_copy(up_hbm.at[side], u_ref, local_sem.at[3]),
        ]
        for item in load_parts:
            item.start()
    load_mixed.start()
    vec_parts[0] = vector_ref[...]

    def pool_one():
        links.arrived("pool0")
        pool_parts[...] = add_up([pool_ref[...], pool_got[0]]).astype(low)
        links.start("pool1", pool_parts, pool_got.at[1], across_dev)

    def pool_two():
        links.arrived("pool1")
        pool_out[...] = add_up([pool_parts[...], pool_got[1]]) / count_ref[...]

    def out_z():
        load_parts[0].wait()
        links.arrived("out_y")
        add_into(o_ref, [o_y], 4)
        for o in range(3):
            links.start(f"out_z{o}", o_ref.at[z_at[o]], o_z.at[o], z_dev[o])

    def out_far():
        links.arrived("out_z0", "out_z1", "out_z2")
        o_s[...] = add_up([o_ref[z]] + [o_z[o] for o in range(3)]).astype(low)
        links.start("out_x", o_s, o_x, across_dev)

    def out_end():
        links.arrived("out_x")
        wo_out[core] = add_up([o_s[...], o_x[...]]).astype(low)
        links.start("out_gather", wo_out.at[core], wo_out.at[core], near_dev)

    def down_z(h):
        if h == 0:
            load_parts[1].wait()
        rows = pl.ds(h * piece, piece)
        links.arrived(f"down_y{h}")
        add_into(d_ref.at[:, rows], [d_y.at[:, rows]], 4)
        for o in range(3):
            links.start(f"down_z{h}{o}", d_ref.at[z_at[o], rows], d_z.at[o, rows], z_dev[o])

    def down_far(h):
        rows = pl.ds(h * piece, piece)
        links.arrived(f"down_z{h}0", f"down_z{h}1", f"down_z{h}2")
        d_s[rows] = add_up([d_ref[z, rows]] + [d_z[o, rows] for o in range(3)]).astype(low)
        links.start(f"down_x{h}", d_s.at[rows], d_x.at[rows], across_dev)

    def down_end():
        links.arrived("down_x0", "down_x1")
        down_out[core] = add_up([d_s[...], d_x[...]]).astype(low)
        links.start("down_gather", down_out.at[core], down_out.at[core], near_dev)

    def up_y():
        load_parts[2].wait()
        links.arrived("up_x")
        for i in range(4):
            add_into(u_ref.at[i], [u_x.at[i]], 2)
        links.start("up_y", u_ref.at[:, 1 - y], u_y, y_dev)

    def up_z():
        links.arrived("up_y")
        for i in range(4):
            u_ref[i, y] = add_up([u_ref[i, y], u_y[i]]).astype(low)
        for o in range(3):
            links.start(f"up_z{o}", u_ref.at[z_at[o], y], u_z.at[o], z_dev[o])

    def up_far():
        links.arrived("up_z0", "up_z1", "up_z2")
        up_out[me] = add_up([u_ref[z, y]] + [u_z[o] for o in range(3)]).astype(low)
        links.start("up_gather", up_out.at[me], up_out.at[me], across_dev)

    def up_end():
        links.arrived("up_gather")
        links.start("up_near0", up_out.at[me], up_out.at[me], near_dev)
        links.start("up_near1", up_out.at[across], up_out.at[across], near_dev)

    def group_core(g):
        links.start(f"group_core{g}", gb_ref.at[g, 1 - core], gb_got.at[g], near_dev)

    def group_y(g):
        links.arrived(f"group_core{g}")
        for i in range(4):
            add_into(gb_ref.at[g, core, i], [gb_got.at[g, i]], 2)
        links.start(f"group_y{g}", gb_ref.at[g, core, :, 1 - y], g_y.at[g], y_dev)

    def group_z(g):
        links.arrived(f"group_y{g}")
        for i in range(4):
            gb_ref[g, core, i, y] = add_up([gb_ref[g, core, i, y], g_y[g, i]]).astype(low)
        for o in range(3):
            links.start(
                f"group_z{g}{o}", gb_ref.at[g, core, z_at[o], y], g_z.at[g, o], z_dev[o]
            )

    def group_far(g):
        links.arrived(f"group_z{g}0", f"group_z{g}1", f"group_z{g}2")
        g_s[g] = add_up([gb_ref[g, core, z, y]] + [g_z[g, o] for o in range(3)]).astype(low)
        links.start(f"group_x{g}", g_s.at[g], g_x.at[g], across_dev)

    def group_end(g):
        links.arrived(f"group_x{g}")
        square_out[g, core] = add_up([g_s[g], g_x[g]]).astype(low)
        links.start(f"group_gather{g}", square_out.at[g, core], square_out.at[g, core], near_dev)

    def vector_step(i, device):
        if i:
            links.arrived(f"vector{i - 1}")
            vec_parts[i] = vec_parts[i - 1] + vec_got[i - 1]
        if device is not None:
            links.start(f"vector{i}", vec_parts.at[i], vec_got.at[i], device)

    def vector_z():
        vector_step(3, None)
        for o in range(3):
            links.start(f"vector_z{o}", vec_parts.at[3], vec_got.at[3 + o], z_dev[o])

    def vector_end():
        links.arrived("vector_z0", "vector_z1", "vector_z2")
        vector_out[...] = vec_parts[3] + (vec_got[3] + (vec_got[4] + vec_got[5]))

    row = lax.broadcasted_iota(jnp.int32, (PAIR, size), 0)

    def attend_step(step):
        slot = step % 2
        group, r = divmod(step, rows_here)

        def one_pair(n, carry):
            local = pl.ds(pl.multiple_of(n * PAIR, PAIR), PAIR)
            columns = pl.ds(pl.multiple_of(group * per_group + n * PAIR, PAIR), PAIR)
            pair = group * (per_group // PAIR) + n
            grad = grad_ref[slot, :, local]
            q_both = split_heads(q_ref[slot, :, local])
            g_both = split_heads(grad)
            product = grad.astype(jnp.float32) * context_ref[slot, :, local].astype(jnp.float32)
            product = product.T
            delta = jnp.concatenate(
                [
                    jnp.sum(product[:HEAD_DIM], axis=0, keepdims=True),
                    jnp.sum(product[HEAD_DIM:], axis=0, keepdims=True),
                ],
                axis=1,
            )
            lse = jnp.concatenate(
                [lse_ref[r, pl.ds(2 * pair, 1), :], lse_ref[r, pl.ds(2 * pair + 1, 1), :]], axis=1
            )
            dq = jnp.zeros((PAIR, 2 * size), jnp.float32)
            for j in range(4):
                rows = pl.ds(j * size, size)
                keys = k_ref[slot, rows, local]
                bias = bias_ref[r, rows, :]
                bias = jnp.concatenate([bias, bias], axis=1)
                probs = jnp.exp(dot_nt(keys, q_both) + bias - lse)
                grad_s = probs * (dot_nt(v_ref[slot, rows, local], g_both) - delta)
                grad_s = grad_s.astype(low)
                dv_ref[r, rows, columns] = matmul(probs.astype(low), g_both).astype(low)
                dk_ref[r, rows, columns] = matmul(grad_s, q_both).astype(low)
                dq = dq + matmul(keys.T, grad_s)
            dq = jnp.where(row < HEAD_DIM, dq[:, :size], dq[:, size:]) * HEAD_DIM ** (-0.5)
            dq_ref[r, :, columns] = dq.T.astype(low)
            return carry

        lax.fori_loop(0, per_group // PAIR, one_pair, 0)

    def weight_group(g):
        columns = pl.ds(g * per_group, per_group)
        for n, source in enumerate((dq_ref, dk_ref, dv_ref)):
            keys = source.shape[1]
            part = sum(
                matmul(x_t[r, :, :keys], source[r, :, columns]) for r in range(rows_here)
            )
            if not fused:
                square_out[n, :, columns] = part.astype(low)
                continue
            depth = gb_ref.shape[4]
            for h in range(2):
                half = part[:, h * cut : (h + 1) * cut].astype(low)
                gb_ref[g, h, :, :, :, n * cut : (n + 1) * cut] = half.reshape(4, 2, depth, cut)
        for n, source in enumerate((dq_ref, dv_ref)):
            total = sum(
                jnp.sum(source[r, :, columns].astype(jnp.float32), axis=0, keepdims=True)
                for r in range(rows_here)
            )
            vec_parts[0, n : n + 1, columns] = total

    def input_parts(r):
        for j in range(4):
            rows = pl.ds(j * size, size)
            part = dot_nt(dk_ref[r, rows, :], w_key[...]) + dot_nt(dv_ref[r, rows, :], w_value[...])
            if j == 0:
                dx_acc[r] = dx_acc[r] + part + dot_nt(dq_ref[r], w_query[...])
            elif j == 2:
                dx_far[r] = part.astype(low)
            else:
                dx_sent[r, j // 2] = part.astype(low)
        links.start(f"dx_near{r}", dx_sent.at[r], dx_near_got.at[r], near_dev)

    def input_near(r):
        links.arrived(f"dx_near{r}")
        dx_far[r] = add_up([dx_far[r], dx_near_got[r, 1]]).astype(low)
        links.start(f"dx_far{r}", dx_far.at[r], dx_far_got.at[r], across_dev)
        dx_acc[r] = dx_acc[r] + dx_near_got[r, 0].astype(jnp.float32)

    def input_done(r):
        links.arrived(f"dx_far{r}")
        dx_out[r] = add_up([dx_acc[r], dx_far_got[r]]).astype(low)

    def prepare_row(r):
        slot = r % 2
        for j in range(4):
            seg_key = jnp.broadcast_to(
                ids_ref[j, r : r + 1, :].astype(jnp.float32), (PAIR, size)
            ).T[:, :1]
            seg_query = ids_ref[0, r : r + 1, :].astype(jnp.float32)
            rows = slice(j * size, (j + 1) * size)
            bias_ref[r, rows, :] = jnp.where(seg_key == seg_query, 0.0, MASKED)
            block = x_ref[r] if j == 0 else x_got[slot, j - 1]
            x_t[r, :, rows] = block.T

    plan = {
        "step0": [pool_one],
        "step1": [out_z],
        "step2": [pool_two],
        "group0": [lambda: group_core(0)],
        "step3": [lambda: down_z(0)],
        "step4": [up_y],
        "step5": [lambda: group_y(0)],
        "group1": [lambda: group_core(1), lambda: down_z(1)],
        "step6": [lambda: group_y(1), out_far],
        "input0": [],
        "step7": [lambda: input_near(0), up_z, lambda: down_far(0)],
        "input1": [lambda: group_z(0)],
        "step8": [lambda: input_near(1), lambda: down_far(1), out_end],
        "group2": [lambda: group_core(2), lambda: vector_step(0, near_dev)],
        "input2": [lambda: group_z(1), lambda: group_y(2)],
    }

    def after(name):
        if fused:
            for action in plan[name]:
                action()

    steps = groups * rows_here
    for step in range(steps):
        group, r = divmod(step, rows_here)
        for item in load_step(step):
            item.wait()
        if step + 1 < steps:
            for item in load_step(step + 1):
                item.start()
        if group == 0:
            prepare_row(r)
        attend_step(step)
        after(f"step{step}")
        if group == groups - 1:
            if r == 0:
                load_mixed.wait()
            if r + 1 == rows_here:
                weight_group(group)
                after(f"group{group}")
            input_parts(r)
            after(f"input{r}")
        elif r + 1 == rows_here:
            weight_group(group)
            after(f"group{group}")

    if not fused:
        vector_out[...] = vec_parts[0]
        pool_one()
        for r in range(rows_here):
            input_near(r)
        pool_two()
        for r in range(rows_here):
            input_done(r)
        links.finish()
        return

    vector_step(1, across_dev)
    input_near(2)
    up_far()
    input_done(0)
    vector_step(2, y_dev)
    down_end()
    group_far(0)
    group_z(2)
    vector_z()
    input_done(1)
    up_end()
    group_end(0)
    group_far(1)
    vector_end()
    group_end(1)
    input_done(2)
    group_far(2)
    group_end(2)
    links.arrived("down_gather", "out_gather", "up_near0", "up_near1")
    links.arrived("group_gather0", "group_gather1", "group_gather2")
    links.finish()


def attend_back(
    fused, x, ids, lse, w_query, w_key, w_value, pool, counts, vectors,
    x_got, q, k, v, context, grad, mixed, up, down, out,
):
    rows_here, size, width = x.shape
    keys = size * 4
    half = width // 2
    low = jnp.bfloat16
    f32 = jnp.float32
    whole = pl.BlockSpec(memory_space=pltpu.VMEM)
    outside = pl.BlockSpec(memory_space=pl.ANY)
    shape = jax.ShapeDtypeStruct
    per_group = 2 * PAIR
    groups = width // per_group
    up_rows, down_rows = (up.shape[3], down.shape[2]) if fused else (16, 16)
    w = width if fused else 128
    h = half if fused else 128
    c = 3 * per_group // 2 if fused else 128
    square_shape = (groups, 2, up_rows, c) if fused else (3, width, width)
    vec = vectors.shape
    scratch = [
        pltpu.VMEM((2, 3, size, width), low),
        pltpu.VMEM((rows_here, width, keys), low),
        pltpu.VMEM((2, size, per_group), low),
        pltpu.VMEM((2, keys, per_group), low),
        pltpu.VMEM((2, keys, per_group), low),
        pltpu.VMEM((2, size, per_group), low),
        pltpu.VMEM((2, size, per_group), low),
        pltpu.VMEM((rows_here, keys, size), f32),
        pltpu.VMEM((rows_here, size, width), low),
        pltpu.VMEM((rows_here, keys, width), low),
        pltpu.VMEM((rows_here, keys, width), low),
        pltpu.VMEM((rows_here, size, width), f32),
        pltpu.VMEM((rows_here, 2, size, width), low),
        pltpu.VMEM((rows_here, size, width), low),
        pltpu.VMEM((rows_here, 2, size, width), low),
        pltpu.VMEM((rows_here, size, width), low),
        pltpu.VMEM(pool.shape, low),
        pltpu.VMEM((2,) + pool.shape, low),
        pltpu.VMEM((4,) + vec, f32),
        pltpu.VMEM((6,) + vec, f32),
        pltpu.VMEM((groups, 2, 4, 2, up_rows, c), low),
        pltpu.VMEM((groups, 4, 2, up_rows, c), low),
        pltpu.VMEM((groups, 4, up_rows, c), low),
        pltpu.VMEM((groups, 3, up_rows, c), low),
        pltpu.VMEM((groups, up_rows, c), low),
        pltpu.VMEM((groups, up_rows, c), low),
        pltpu.VMEM((4, 2, up_rows, w), low),
        pltpu.VMEM((4, 2, up_rows, w), low),
        pltpu.VMEM((4, up_rows, w), low),
        pltpu.VMEM((3, up_rows, w), low),
        pltpu.VMEM((4, down_rows, w), low),
        pltpu.VMEM((4, down_rows, w), low),
        pltpu.VMEM((3, down_rows, w), low),
        pltpu.VMEM((down_rows, w), low),
        pltpu.VMEM((down_rows, w), low),
        pltpu.VMEM((4, up_rows, h), low),
        pltpu.VMEM((4, up_rows, h), low),
        pltpu.VMEM((3, up_rows, h), low),
        pltpu.VMEM((up_rows, h), low),
        pltpu.VMEM((up_rows, h), low),
        pltpu.SemaphoreType.DMA((64,)),
        pltpu.SemaphoreType.DMA((64,)),
        pltpu.SemaphoreType.DMA((2, 6)),
        pltpu.SemaphoreType.DMA((4,)),
    ]
    return pl.pallas_call(
        functools.partial(attend_back_kernel, fused),
        out_shape=(
            shape((rows_here, size, width), low),
            shape(pool.shape, f32),
            shape(vec, f32),
            shape(square_shape, low),
            shape((4, up_rows, w), low),
            shape((2, down_rows, w), low),
            shape((2, up_rows, h), low),
        ),
        in_specs=[whole] * 9 + [outside] * 10,
        out_specs=(whole,) * 7,
        scratch_shapes=scratch,
        compiler_params=pltpu.CompilerParams(
            vmem_limit_bytes=63 * 2**20, collective_id=1, has_side_effects=True
        ),
        cost_estimate=pl.CostEstimate(
            flops=rows_here
            * (4 * (size + 2 * keys) * width * width + 40 * size * keys * width),
            bytes_accessed=2 * (16 * width * width + 9 * keys * width),
            transcendentals=rows_here * HEADS * size * keys,
        ),
    )(
        x, ids, lse, w_query, w_key, w_value, pool, counts, vectors,
        x_got, q, k, v, context, grad, mixed, up, down, out,
    )


def radices_of(count):
    if count == 8:
        return ((1, 2), (2, 4))
    digits = []
    stride = 1
    while stride < count:
        digits.append((stride, 2))
        stride *= 2
    return tuple(digits)


def exchange(piece, axis_name, stride, offset):
    count = lax.axis_size(axis_name)
    pairs = [(i, i ^ (offset * stride)) for i in range(count)]
    return lax.ppermute(piece, axis_name, pairs)


def digit_of(axis_name, stride, radix):
    return (lax.axis_index(axis_name) // stride) % radix


def scatter_digit(pieces, place, axis_name, stride, radix):
    here = digit_of(axis_name, stride, radix)
    received = [
        exchange(
            lax.dynamic_index_in_dim(pieces, here ^ offset, place, keepdims=False).astype(
                jnp.bfloat16
            ),
            axis_name, stride, offset,
        )
        for offset in range(1, radix)
    ]
    total = lax.dynamic_index_in_dim(pieces, here, place, keepdims=False).astype(jnp.float32)
    for item in received:
        total = total + item.astype(jnp.float32)
    return total.astype(jnp.bfloat16)


def halve(piece, place, axis_name, stride):
    half = piece.shape[place] // 2
    here = digit_of(axis_name, stride, 2)
    sent = lax.dynamic_slice_in_dim(piece, (1 - here) * half, half, place).astype(jnp.bfloat16)
    kept = lax.dynamic_slice_in_dim(piece, here * half, half, place).astype(jnp.float32)
    return (kept + exchange(sent, axis_name, stride, 1).astype(jnp.float32)).astype(jnp.bfloat16)


def join(piece, place, axis_name, stride):
    here = digit_of(axis_name, stride, 2)
    other = exchange(piece, axis_name, stride, 1)
    first = jnp.where(here == 0, piece, other)
    second = jnp.where(here == 0, other, piece)
    return jnp.concatenate([first, second], axis=place)


def scatter_rows(group, dp_size):
    digits = radices_of(dp_size)
    shape = tuple(r for _, r in reversed(digits))
    group = group.reshape(shape + (group.shape[0] // dp_size, group.shape[1]))
    for place, (stride, radix) in zip(range(len(digits) - 1, -1, -1), digits):
        group = scatter_digit(group, place, "dp", stride, radix)
    return group


def finish_weight(flat, dp_size, side):
    flat = scatter_rows(flat, dp_size)
    flat = flat.astype(jnp.float32) + exchange(flat, "ctx", 2, 1).astype(jnp.float32)
    return join(flat.astype(jnp.bfloat16), side, "ctx", 1).astype(jnp.float32)


def reduce_weight(gradient, dp_size, side):
    return finish_weight(halve(gradient, side, "ctx", 1), dp_size, side)


def per_device(
    hidden_in,
    seg_ids,
    valid,
    w_query,
    b_query,
    w_key,
    w_value,
    b_value,
    w_out,
    b_out,
    gain_attn,
    shift_attn,
    w_up,
    b_up,
    w_down,
    b_down,
    gain_ffn,
    shift_ffn,
    pooled_text_gradient,
):
    row_count, group_size, model_width = hidden_in.shape
    dp_size, ctx_size = lax.axis_size("dp"), lax.axis_size("ctx")
    vectors = jnp.concatenate(
        [b_query, b_value, b_out, gain_attn, shift_attn, b_down, gain_ffn, shift_ffn, b_up]
    )
    vectors = jnp.pad(vectors, (0, -vectors.shape[0] % (8 * model_width)))
    vectors = vectors.astype(jnp.float32).reshape(-1, model_width)
    ids = jnp.concatenate([seg_ids, valid], axis=0)
    ids = jnp.pad(ids, ((0, 8 - ids.shape[0]), (0, 0)))
    q_all, context, lse_all, ids_got, x_got, k_all, v_all = attend(
        hidden_in, ids, vectors, w_query, w_key, w_value
    )
    pool, counts, vector_parts, grad_context, grad_mixed, out, final_out, up, down = middle(
        hidden_in, context, ids_got, vectors, pooled_text_gradient, w_out, w_up, w_down, dp_size
    )
    ff_width = w_up.shape[1]
    rows_here, ff_here = model_width // dp_size, ff_width // dp_size
    fused = dp_size == 8 and rows_here % 16 == 0 and model_width % 768 == 0
    if fused:
        up_part = up.reshape(2, 4, 2, rows_here, -1)
        down_part = down.reshape(4, 2, ff_here // 2, -1)
        out_part = out.reshape(4, 2, rows_here, -1)
    else:
        up_part = down_part = out_part = jnp.zeros((16, 128), jnp.bfloat16)
    grad_input, pooled, vector_sum, squares, up_sum, down_sum, out_sum = attend_back(
        fused, hidden_in, ids_got, lse_all, w_query, w_key, w_value,
        pool, counts, vector_parts, x_got, q_all, k_all, v_all, context, grad_context, grad_mixed,
        up_part, down_part, out_part,
    )
    pooled = pooled.reshape(row_count, NSEG, model_width)
    wide_out = lambda piece: piece.astype(jnp.float32)
    if fused:
        cut = squares.shape[-1] // 3
        square_sums = [
            wide_out(squares[..., n * cut : (n + 1) * cut])
            .transpose(2, 0, 1, 3)
            .reshape(rows_here, model_width)
            for n in range(3)
        ]
        square_sums.append(wide_out(out_sum).transpose(1, 0, 2).reshape(rows_here, model_width))
        up_sum = (
            wide_out(up_sum).reshape(2, 2, rows_here, -1).transpose(2, 1, 0, 3)
            .reshape(rows_here, ff_width)
        )
        down_sum = wide_out(down_sum).reshape(ff_here, model_width)
    else:
        square_sums = [reduce_weight(squares[n], dp_size, 1) for n in range(3)]
        square_sums.append(finish_weight(out, dp_size, 1))
        up_sum = finish_weight(up.transpose(1, 0, 2).reshape(model_width, -1), dp_size, 1)
        down_sum = finish_weight(down.reshape(-1, model_width), dp_size, 0)
        vector_sum = lax.psum(vector_sum, ("dp", "ctx"))
    place = lax.axis_index("dp")
    sums = lax.dynamic_slice_in_dim(vector_sum[:8], place * rows_here, rows_here, 1)
    sum_bu = lax.dynamic_slice_in_dim(
        vector_sum[8 : 8 + ff_width // model_width].reshape(-1), place * ff_here, ff_here
    )
    results = (
        square_sums[0], sums[0], square_sums[1], square_sums[2], sums[1], square_sums[3],
        sums[2], sums[3], sums[4], up_sum, sum_bu, down_sum, sums[5], sums[6], sums[7],
    )
    return (
        final_out,
        pooled,
        grad_input,
    ) + tuple(results)


def solution(mesh):
    placed = (
        P("dp", "ctx", None),
        P("dp", "ctx"),
        P("dp", "ctx"),
        P(),
        P(),
        P(),
        P(),
        P(),
        P(),
        P(),
        P(),
        P(),
        P(),
        P(),
        P(),
        P(),
        P(),
        P(),
        P("dp", None, None),
    )
    return jax.shard_map(
        per_device,
        mesh=mesh,
        in_specs=placed,
        out_specs=(
            P("dp", "ctx", None),
            P("dp", None, None),
            P("dp", "ctx", None),
            P("dp", None),
            P("dp"),
            P("dp", None),
            P("dp", None),
            P("dp"),
            P("dp", None),
            P("dp"),
            P("dp"),
            P("dp"),
            P("dp", None),
            P("dp"),
            P("dp", None),
            P("dp"),
            P("dp"),
            P("dp"),
        ),
        check_vma=False,
    )
```

```python
import functools

import jax
import jax.numpy as jnp
from jax import lax
from jax.experimental import pallas as pl
from jax.experimental.pallas import tpu as pltpu
from jax.sharding import PartitionSpec as P

HEADS = 12
HEAD_DIM = 64
NSEG = 16


eps = 1e-12


def matmul(left_side, right_side):
    return jnp.dot(left_side, right_side, preferred_element_type=jnp.float32)


PAIR = 2 * HEAD_DIM
MESH = pl.DeviceIdType.MESH
MASKED = -1e30


def dot_nt(left_side, right_side):
    return lax.dot_general(
        left_side, right_side, (((1,), (1,)), ((), ())), preferred_element_type=jnp.float32
    )


def dot_tn(left_side, right_side):
    return lax.dot_general(
        left_side, right_side, (((0,), (0,)), ((), ())), preferred_element_type=jnp.float32
    )


def split_heads(pair):
    lane = lax.broadcasted_iota(jnp.int32, pair.shape, 1)
    zero = jnp.zeros_like(pair)
    return jnp.concatenate(
        [jnp.where(lane < HEAD_DIM, pair, zero), jnp.where(lane < HEAD_DIM, zero, pair)], axis=0
    )


def text_rows(ids_row, size):
    return jnp.broadcast_to(ids_row.astype(jnp.float32), (PAIR, size)).T


def lanes_of(size):
    return lax.broadcasted_iota(jnp.int32, (size, PAIR), 1)


def key_extra(texts):
    lane = lanes_of(texts.shape[0])
    hot = jnp.where(lane.astype(jnp.float32) == texts, 1.0, 0.0)
    return jnp.where((lane >= NSEG) & (lane < NSEG + 3), 1.0, hot).astype(jnp.bfloat16)


def query_extra(texts):
    lane = lanes_of(texts.shape[0])
    other = (lane < NSEG) & (lane.astype(jnp.float32) != texts)
    return jnp.where(other, MASKED, 0.0)


def with_constant(extra, column):
    lane = lanes_of(extra.shape[0])
    high = column.astype(jnp.bfloat16).astype(jnp.float32)
    middle = (column - high).astype(jnp.bfloat16).astype(jnp.float32)
    rest = column - high - middle
    extra = jnp.where(lane == NSEG, high, extra)
    extra = jnp.where(lane == NSEG + 1, middle, extra)
    return jnp.where(lane == NSEG + 2, rest, extra).astype(jnp.bfloat16)


def attend_kernel(
    x_ref, seg_ref, valid_ref, b_query, b_value, w_query, w_key, w_value,
    q_out, context_out, lse_out, ids_out, x_hbm, k_hbm, v_hbm,
    x_got, k_ref, v_ref, extra_ref, ids_ref, send_sem, recv_sem, local_sem,
):
    rows_here, size, width = x_ref.shape
    me = lax.axis_index("ctx")
    one = me + 1 - 2 * (me % 2)
    two = (me + 2) % 4
    three = (one + 2) % 4
    low = jnp.bfloat16

    ids_ref[...] = jnp.zeros_like(ids_ref)
    ids_ref[0:rows_here, :] = seg_ref[...]
    ids_ref[rows_here : 2 * rows_here, :] = valid_ref[...]
    query_bias = b_query[...].astype(jnp.float32)[None]
    value_bias = b_value[...].astype(jnp.float32)[None]
    barrier = pltpu.get_barrier_semaphore()
    for peer in (one, two, three):
        pl.semaphore_signal(barrier, inc=1, device_id={"ctx": peer}, device_id_type=MESH)
    pl.semaphore_wait(barrier, 3)

    def send(source, target, slot, peer):
        return pltpu.make_async_remote_copy(
            src_ref=source, dst_ref=target, send_sem=send_sem.at[slot],
            recv_sem=recv_sem.at[slot], device_id={"ctx": peer}, device_id_type=MESH,
        )

    ids_out[0] = ids_ref[...]
    ids_sends = [send(ids_ref, ids_out.at[j + 1], j, peer) for j, peer in enumerate((one, two, three))]
    near = send(x_ref, x_got.at[0], 3, one)

    def far(r):
        return send(x_ref.at[r], x_got.at[1, r], 4 + r, two)

    def passed(r):
        return send(x_got.at[1, r], x_got.at[2, r], 4 + rows_here + r, one)

    far(0).start()
    near.start()
    for item in ids_sends:
        item.start()
    for r in range(1, rows_here):
        far(r).start()

    def project(r, x, j):
        rows = pl.ds(j * size, size)
        k_ref[r, rows, :] = matmul(x, w_key[...]).astype(low)
        v_ref[r, rows, :] = (matmul(x, w_value[...]) + value_bias).astype(low)

    def own_row(r, carry):
        x = x_ref[r]
        q = (matmul(x, w_query[...]) + query_bias).astype(low)
        q_out[r] = (q * HEAD_DIM ** (-0.5)).astype(low)
        project(r, x, 0)
        return carry

    lax.fori_loop(0, rows_here, own_row, 0)
    near.wait_recv()

    def near_row(r, carry):
        project(r, x_got[0, r], 1)
        return carry

    lax.fori_loop(0, rows_here, near_row, 0)
    for item in ids_sends:
        item.wait_recv()
    lane = lax.broadcasted_iota(jnp.int32, (size, PAIR), 1)
    far(0).wait_recv()
    passed(0).start()

    def keep(r):
        return (
            pltpu.make_async_copy(k_ref.at[r], k_hbm.at[r], local_sem.at[0, r]),
            pltpu.make_async_copy(v_ref.at[r], v_hbm.at[r], local_sem.at[1, r]),
        )

    for r in range(rows_here):
        project(r, x_got[1, r], 2)
        passed(r).wait_recv()
        project(r, x_got[2, r], 3)
        for item in keep(r):
            item.start()
        for j in range(4):
            texts = text_rows(ids_out[j, r : r + 1, :], size)
            extra_ref[j * size : (j + 1) * size, :] = key_extra(texts)
            if j == 0:
                own_extra = query_extra(texts).astype(low)

        def one_pair(pair, carry, r=r, own_extra=own_extra):
            columns = pl.ds(pl.multiple_of(pair * PAIR, PAIR), PAIR)
            both = split_heads(q_out[r, :, columns])
            both = jnp.concatenate([both, jnp.concatenate([own_extra, own_extra], axis=0)], axis=1)
            keys = jnp.concatenate([k_ref[r, :, columns], extra_ref[...]], axis=1)
            scores = dot_nt(both, keys)
            top = jnp.max(scores, axis=-1, keepdims=True)
            weight = jnp.exp(scores - top)
            total = jnp.sum(weight, axis=-1, keepdims=True)
            mixed = matmul(weight.astype(low), v_ref[r, :, columns]) / total
            context_out[r, :, columns] = jnp.where(
                lane < HEAD_DIM, mixed[:size], mixed[size:]
            ).astype(low)
            lse = top + jnp.log(total)
            stat = lse_out[r]
            stat = jnp.where(lane == 2 * pair, lse[:size], stat)
            lse_out[r] = jnp.where(lane == 2 * pair + 1, lse[size:], stat)
            return carry

        lse_out[r] = jnp.zeros((size, PAIR), jnp.float32)
        lax.fori_loop(0, HEADS // 2, one_pair, 0)
        if r + 1 < rows_here:
            far(r + 1).wait_recv()
            passed(r + 1).start()
    keep_x = pltpu.make_async_copy(x_got, x_hbm, local_sem.at[2, 0])
    keep_x.start()
    for r in range(rows_here):
        for item in keep(r):
            item.wait()
        far(r).wait_send()
        passed(r).wait_send()
    near.wait_send()
    for item in ids_sends:
        item.wait_send()
    keep_x.wait()


def attend(x, seg_ids, valid, b_query, b_value, w_query, w_key, w_value):
    rows_here, size, width = x.shape
    keys = size * 4
    low = jnp.bfloat16
    whole = pl.BlockSpec(memory_space=pltpu.VMEM)
    outside = pl.BlockSpec(memory_space=pl.ANY)
    slots = 4 + 2 * rows_here
    return pl.pallas_call(
        attend_kernel,
        out_shape=(
            jax.ShapeDtypeStruct((rows_here, size, width), low),
            jax.ShapeDtypeStruct((rows_here, size, width), low),
            jax.ShapeDtypeStruct((rows_here, size, PAIR), jnp.float32),
            jax.ShapeDtypeStruct((4, 8, size), jnp.int32),
            jax.ShapeDtypeStruct((3,) + x.shape, low),
            jax.ShapeDtypeStruct((rows_here, keys, width), low),
            jax.ShapeDtypeStruct((rows_here, keys, width), low),
        ),
        in_specs=[whole] * 8,
        out_specs=(whole, whole, whole, whole, outside, outside, outside),
        scratch_shapes=[
            pltpu.VMEM((3,) + x.shape, low),
            pltpu.VMEM((rows_here, keys, width), low),
            pltpu.VMEM((rows_here, keys, width), low),
            pltpu.VMEM((keys, PAIR), low),
            pltpu.VMEM((8, size), jnp.int32),
            pltpu.SemaphoreType.DMA((slots,)),
            pltpu.SemaphoreType.DMA((slots,)),
            pltpu.SemaphoreType.DMA((3, rows_here)),
        ],
        compiler_params=pltpu.CompilerParams(
            vmem_limit_bytes=56 * 2**20, collective_id=0, has_side_effects=True
        ),
        cost_estimate=pl.CostEstimate(
            flops=rows_here * (2 * (size + 2 * keys) * width * width + 16 * size * keys * width),
            bytes_accessed=2 * (3 * width * width + 9 * keys * width),
            transcendentals=rows_here * HEADS * size * keys,
        ),
    )(x, seg_ids, valid, b_query, b_value, w_query, w_key, w_value)


def gelu_both(u):
    size = jnp.abs(u)
    t = 1.0 / (1.0 + (0.3275911 * 0.5**0.5) * size)
    bell = jnp.exp(-0.5 * u * u)
    poly = t * (
        0.127414796 + t * (-0.142248368 + t * (0.7107068705 + t * (-0.7265760135 + t * 0.5307027145)))
    )
    tail = poly * bell
    cdf = jnp.where(u >= 0.0, 1.0 - tail, tail)
    return u * cdf, cdf + u * bell * 0.3989422804014327


def normalize(values_in):
    centre = jnp.mean(values_in, axis=-1, keepdims=True)
    centred = values_in - centre
    spread = jnp.mean(centred * centred, axis=-1, keepdims=True)
    scale = lax.rsqrt(spread + eps)
    return centred * scale, scale


def normalize_back(grad, unit, scale):
    mean_one = jnp.mean(grad, axis=-1, keepdims=True)
    mean_two = jnp.mean(grad * unit, axis=-1, keepdims=True)
    return (grad - mean_one - unit * mean_two) * scale


def column_sum(values_in):
    return jnp.sum(values_in, axis=0, keepdims=True)


B_QUERY, B_VALUE, B_OUT, GAIN_ONE, SHIFT_ONE, B_DOWN, GAIN_TWO, SHIFT_TWO, B_UP = range(9)


def middle_kernel(
    fused,
    x_ref, context_ref, ids_ref, b_out, gain_one, shift_one, b_up, b_down, gain_two, shift_two,
    text_ref, w_out, up_hbm, down_hbm,
    pool_out, count_out, vector_out, grad_out, mixed_out, wo_out, final_hbm, up_out, down_out, far_out,
    vec_ref, w_up, w_down, unit_ref, scale_ref, normed_ref, normed_t, act_ref, slope_ref, acc_ref,
    g_ref, final_ref, upg_ref, up_got, downg_ref, down_got, wo_sent, wo_got, down_y, down_x,
    send_sem, recv_sem, load_sem, store_sem,
):
    rows_here, size, width = x_ref.shape
    tokens = rows_here * size
    parts = w_up.shape[0]
    half = width // 2
    low = jnp.bfloat16
    f32 = jnp.float32
    me = lax.axis_index("ctx")
    core = me % 2
    near = {"ctx": me + 1 - 2 * core}
    side = me // 2
    place = lax.axis_index("dp")
    y = place % 2
    y_dev = {"dp": place + 1 - 2 * y}
    across_dev = {"ctx": (me + 2) % 4}
    peers = [near, across_dev, y_dev] if fused else [near]
    barrier = pltpu.get_barrier_semaphore()
    for peer in peers:
        pl.semaphore_signal(barrier, inc=1, device_id=peer, device_id_type=MESH)
    for row, source in (
        (B_OUT, b_out), (GAIN_ONE, gain_one), (SHIFT_ONE, shift_one), (B_DOWN, b_down),
        (GAIN_TWO, gain_two), (SHIFT_TWO, shift_two),
    ):
        vec_ref[row : row + 1, :] = source[...].astype(f32)[None]
    for i in range(parts):
        vec_ref[B_UP + i : B_UP + i + 1, :] = (
            b_up[i * width : (i + 1) * width].astype(f32)[None]
        )

    def vec(row):
        return vec_ref[row : row + 1, :]

    loads = []
    for i in range(parts):
        loads.append(
            (
                pltpu.make_async_copy(
                    up_hbm.at[:, pl.ds(i * width, width)], w_up.at[i], load_sem.at[0, i]
                ),
                pltpu.make_async_copy(
                    down_hbm.at[pl.ds(i * width, width)], w_down.at[i], load_sem.at[1, i]
                ),
            )
        )
    for pair in loads:
        for item in pair:
            item.start()

    def rows_of(r):
        return pl.ds(pl.multiple_of(r * size, size), size)

    text = lax.broadcasted_iota(jnp.int32, (NSEG, size), 0)

    def members(j, r):
        seg = ids_ref[j, r : r + 1, :]
        real = ids_ref[j, rows_here + r : rows_here + r + 1, :]
        return jnp.where((text == seg) & (real == 1), 1.0, 0.0)

    for r in range(rows_here):
        number = sum(jnp.sum(members(j, r), axis=1, keepdims=True) for j in range(4))
        count_out[r * NSEG : (r + 1) * NSEG, :] = jnp.maximum(number, 1.0)

    def first_norm(r, carry):
        rows = rows_of(r)
        mixed = x_ref[r].astype(f32) + (matmul(context_ref[r], w_out[...]) + vec(B_OUT))
        unit, scale = normalize(mixed)
        unit_ref[rows, :] = unit
        scale_ref[rows, :] = scale
        normed_ref[rows, :] = (unit * vec(GAIN_ONE) + vec(SHIFT_ONE)).astype(low)
        return carry

    lax.fori_loop(0, rows_here, first_norm, 0)
    for pair in loads:
        for item in pair:
            item.wait()

    def forward_part(i, carry):
        pre = matmul(normed_ref[...], w_up[i]) + vec_ref[pl.ds(B_UP + i, 1), :]
        act, slope = gelu_both(pre)
        act = act.astype(low)
        act_ref[i] = act
        slope_ref[i] = slope.astype(low)
        part = matmul(act, w_down[i])

        @pl.when(i == 0)
        def _():
            acc_ref[...] = part

        @pl.when(i > 0)
        def _():
            acc_ref[...] += part

        return carry

    lax.fori_loop(0, parts, forward_part, 0)
    normed_t[...] = normed_ref[...].T

    store_final = []
    vector_out[...] = jnp.zeros_like(vector_out)
    for r in range(rows_here):
        rows = pl.ds(r * size, size)
        normed = unit_ref[rows, :] * vec(GAIN_ONE) + vec(SHIFT_ONE)
        summed = normed + (acc_ref[rows, :] + vec(B_DOWN))
        unit, scale = normalize(summed)
        final = unit * vec(GAIN_TWO) + vec(SHIFT_TWO)
        high = final.astype(low)
        final_ref[r] = high
        item = pltpu.make_async_copy(final_ref.at[r], final_hbm.at[r], store_sem.at[r])
        item.start()
        store_final.append(item)
        own = members(0, r)
        own_low = own.astype(low)
        rest = (final - high.astype(f32)).astype(low)
        pool = matmul(own_low, high) + matmul(own_low, rest)
        pool_out[r * NSEG : (r + 1) * NSEG, :] = pool.astype(low)
        share = text_ref[r] / count_out[r * NSEG : (r + 1) * NSEG, :]
        first = share.astype(low)
        second = (share - first.astype(f32)).astype(low)
        third = (share - first.astype(f32) - second.astype(f32)).astype(low)
        grad = dot_tn(
            jnp.concatenate([own_low] * 3, axis=0), jnp.concatenate([first, second, third], axis=0)
        )
        back = normalize_back(grad * vec(GAIN_TWO), unit, scale)
        back_low = back.astype(low)
        acc_ref[rows, :] = back
        g_ref[rows, :] = back_low
        vector_out[GAIN_TWO : GAIN_TWO + 1, :] += column_sum(grad * unit)
        vector_out[SHIFT_TWO : SHIFT_TWO + 1, :] += column_sum(grad)
        vector_out[B_DOWN : B_DOWN + 1, :] += column_sum(back_low.astype(f32))

    pl.semaphore_wait(barrier, len(peers))

    def remote(source, target, slot, device=near):
        return pltpu.make_async_remote_copy(
            src_ref=source, dst_ref=target, send_sem=send_sem.at[slot],
            recv_sem=recv_sem.at[slot], device_id=device, device_id_type=MESH,
        )

    per_part = downg_ref.shape[0] // parts
    mine = parts // 2

    def up_send(i):
        return remote(upg_ref.at[i], up_got.at[i], i)

    def down_send(i):
        chunk = pl.ds(i * per_part, per_part)
        return remote(downg_ref.at[chunk, 1 - core], down_got.at[chunk], parts + i)

    def down_part(i, carry):
        part = dot_tn(act_ref[i], g_ref[...]).astype(low)
        downg_ref[pl.ds(i * per_part, per_part)] = part.reshape((per_part,) + downg_ref.shape[1:])
        down_send(i).start()
        return carry

    lax.fori_loop(0, parts, down_part, 0)

    def backward_part(step, carry):
        i = (step + mine * (1 - core)) % parts
        back = dot_nt(g_ref[...], w_down[i])
        back = (back * slope_ref[i].astype(f32)).astype(low)
        vector_out[pl.ds(B_UP + i, 1), :] = column_sum(back.astype(f32))
        acc_ref[...] += dot_nt(back, w_up[i])
        upg_ref[step] = matmul(normed_t[...], back).astype(low)

        @pl.when(step < mine)
        def _():
            up_send(step).start()

        return carry

    def down_sum(i, carry):
        downg_ref[i, core] = (
            downg_ref[i, core].astype(f32) + down_got[i].astype(f32)
        ).astype(low)
        return carry

    piece = downg_ref.shape[2] // 2
    quarter = piece // 2
    rest = pl.ds(pl.multiple_of(piece + quarter * (1 - side), 16), quarter)
    kept = pl.ds(pl.multiple_of(piece + quarter * side, 16), quarter)
    down_moves = []
    if fused:
        for n in range(4):
            down_moves.append(
                remote(
                    downg_ref.at[2 * n + 1 - y, core, pl.ds(0, piece)], down_y.at[n],
                    2 * parts + 1 + n, y_dev,
                )
            )
        for n in range(8):
            down_moves.append(
                remote(
                    downg_ref.at[n, core, rest], down_x.at[n], 2 * parts + 5 + n, across_dev
                )
            )
    lax.fori_loop(0, 1, backward_part, 0)
    for i in range(parts):
        down_send(i).wait_recv()
    lax.fori_loop(0, downg_ref.shape[0], down_sum, 0)
    for item in down_moves:
        item.start()
    lax.fori_loop(1, parts, backward_part, 0)

    def first_back(r, carry):
        rows = rows_of(r)
        unit = unit_ref[rows, :]
        grad = acc_ref[rows, :]
        back = normalize_back(grad * vec(GAIN_ONE), unit, scale_ref[rows, :])
        back_low = back.astype(low)
        mixed_out[r] = back
        g_ref[rows, :] = back_low
        vector_out[GAIN_ONE : GAIN_ONE + 1, :] += column_sum(grad * unit)
        vector_out[SHIFT_ONE : SHIFT_ONE + 1, :] += column_sum(grad)
        vector_out[B_OUT : B_OUT + 1, :] += column_sum(back_low.astype(f32))
        return carry

    lax.fori_loop(0, rows_here, first_back, 0)

    def out_part(h):
        columns = pl.ds(pl.multiple_of(h * half, 128), half)
        total = jnp.zeros((width, half), f32)
        for r in range(rows_here):
            total = total + dot_tn(context_ref[r], g_ref[pl.ds(r * size, size), columns])
        return total

    wo_sent[...] = out_part(1 - core).astype(low)
    wo_send = remote(wo_sent, wo_got, 2 * parts)
    wo_send.start()

    def grad_context(r, carry):
        grad_out[r] = dot_nt(g_ref[rows_of(r), :], w_out[...]).astype(low)
        return carry

    lax.fori_loop(0, rows_here, grad_context, 0)
    own_part = out_part(core)
    for i in range(mine):
        up_send(i).wait_recv()

    def up_sum(n, carry):
        rows = pl.ds(pl.multiple_of(n * 128, 128), 128)
        for i in range(mine):
            upg_ref[mine + i, rows, :] = (
                upg_ref[mine + i, rows, :].astype(f32) + up_got[i, rows, :].astype(f32)
            ).astype(low)
        return carry

    lax.fori_loop(0, width // 128, up_sum, 0)
    store_up = pltpu.make_async_copy(
        upg_ref.at[pl.ds(mine, mine)], up_out, store_sem.at[rows_here + 1]
    )
    store_up.start()
    wo_send.wait_recv()
    wo_out[...] = (own_part + wo_got[...].astype(f32)).astype(low)
    if fused:
        for item in down_moves:
            item.wait_recv()

        def near_sum(n, carry):
            down_y[n] = (
                downg_ref[2 * n + y, core, 0:piece, :].astype(f32) + down_y[n].astype(f32)
            ).astype(low)
            return carry

        def far_sum(n, carry):
            down_x[n] = (
                downg_ref[n, core, kept, :].astype(f32) + down_x[n].astype(f32)
            ).astype(low)
            return carry

        lax.fori_loop(0, 4, near_sum, 0)
        lax.fori_loop(0, 8, far_sum, 0)
        stores = [
            pltpu.make_async_copy(down_y, down_out, store_sem.at[rows_here]),
            pltpu.make_async_copy(down_x, far_out, store_sem.at[rows_here + 2]),
        ]
    else:
        stores = [
            pltpu.make_async_copy(downg_ref.at[:, core], down_out, store_sem.at[rows_here])
        ]
    for item in stores:
        item.start()
    for i in range(parts):
        down_send(i).wait_send()
    for i in range(mine):
        up_send(i).wait_send()
    wo_send.wait_send()
    for item in down_moves:
        item.wait_send()
    for item in store_final + stores + [store_up]:
        item.wait()


def middle(fused, x, context, ids, vectors, text_gradient, w_out, w_up, w_down, dp_size):
    rows_here, size, width = x.shape
    ff = w_up.shape[1]
    parts = ff // width
    tokens = rows_here * size
    low = jnp.bfloat16
    f32 = jnp.float32
    shape = jax.ShapeDtypeStruct
    whole = pl.BlockSpec(memory_space=pltpu.VMEM)
    outside = pl.BlockSpec(memory_space=pl.ANY)
    chunks = max(dp_size, parts)
    chunk = ff // chunks // 2
    vec = (8 + parts + (-parts) % 8, width)
    if fused:
        down_shape, far_shape = (4, chunk // 2, width), (8, chunk // 4, width)
    else:
        down_shape, far_shape = (chunks, chunk, width), (8, 16, 128)
    return pl.pallas_call(
        functools.partial(middle_kernel, fused),
        out_shape=(
            shape((rows_here * NSEG, width), low),
            shape((rows_here * NSEG, 1), f32),
            shape(vec, f32),
            shape((rows_here, size, width), low),
            shape((rows_here, size, width), f32),
            shape((width, width // 2), low),
            shape((rows_here, size, width), low),
            shape((parts // 2, width, width), low),
            shape(down_shape, low),
            shape(far_shape, low),
        ),
        in_specs=[whole] * 12 + [outside] * 2,
        out_specs=(whole,) * 6 + (outside,) * 4,
        scratch_shapes=[
            pltpu.VMEM(vec, f32),
            pltpu.VMEM((parts, width, width), low),
            pltpu.VMEM((parts, width, width), low),
            pltpu.VMEM((tokens, width), f32),
            pltpu.VMEM((tokens, 1), f32),
            pltpu.VMEM((tokens, width), low),
            pltpu.VMEM((width, tokens), low),
            pltpu.VMEM((parts, tokens, width), low),
            pltpu.VMEM((parts, tokens, width), low),
            pltpu.VMEM((tokens, width), f32),
            pltpu.VMEM((tokens, width), low),
            pltpu.VMEM((rows_here, size, width), low),
            pltpu.VMEM((parts, width, width), low),
            pltpu.VMEM((parts // 2, width, width), low),
            pltpu.VMEM((chunks, 2, chunk, width), low),
            pltpu.VMEM((chunks, chunk, width), low),
            pltpu.VMEM((width, width // 2), low),
            pltpu.VMEM((width, width // 2), low),
            pltpu.VMEM(down_shape if fused else (16, 128), low),
            pltpu.VMEM(far_shape, low),
            pltpu.SemaphoreType.DMA((2 * parts + 13,)),
            pltpu.SemaphoreType.DMA((2 * parts + 13,)),
            pltpu.SemaphoreType.DMA((2, parts)),
            pltpu.SemaphoreType.DMA((rows_here + 3,)),
        ],
        compiler_params=pltpu.CompilerParams(
            vmem_limit_bytes=63 * 2**20, collective_id=2, has_side_effects=True
        ),
        cost_estimate=pl.CostEstimate(
            flops=2 * tokens * width * (6 * ff + 3 * width),
            bytes_accessed=2 * (5 * ff * width + 8 * tokens * width),
            transcendentals=2 * tokens * ff,
        ),
    )(x, context, ids, *vectors, text_gradient, w_out, w_up, w_down)


class Links:
    def __init__(self, send_sem, recv_sem):
        self.send_sem, self.recv_sem = send_sem, recv_sem
        self.slots, self.copies = {}, {}

    def start(self, name, source, target, device):
        slot = self.slots.setdefault(name, len(self.slots))
        copy = pltpu.make_async_remote_copy(
            src_ref=source, dst_ref=target, send_sem=self.send_sem.at[slot],
            recv_sem=self.recv_sem.at[slot], device_id=device, device_id_type=MESH,
        )
        copy.start()
        self.copies[name] = copy

    def arrived(self, *names):
        for name in names:
            self.copies[name].wait_recv()

    def finish(self):
        for copy in self.copies.values():
            copy.wait_send()


def add_into(target, others, count):
    def one(i, carry):
        total = target[i].astype(jnp.float32)
        for other in others:
            total = total + other[i].astype(jnp.float32)
        target[i] = total.astype(target.dtype)
        return carry

    lax.fori_loop(0, count, one, 0)


def add_up(parts):
    total = parts[0].astype(jnp.float32)
    for part in parts[1:]:
        total = total + part.astype(jnp.float32)
    return total


GROUPS = ((0, 4 * PAIR), (4 * PAIR, PAIR), (5 * PAIR, PAIR))


def attend_back_kernel(
    fused, names,
    x_ref, ids_ref, lse_ref, w_query, w_key, w_value, pool_ref, count_ref, vector_ref,
    x_hbm, q_hbm, k_hbm, v_hbm, context_hbm, grad_hbm, mixed_hbm, up_hbm, down_hbm, far_hbm, out_hbm,
    dx_out, pool_out, vector_out, *rest,
):
    ref = dict(zip(names, rest))
    square_out, up_out, down_out, wo_out = (ref[n] for n in ("square", "up", "down", "wo"))
    q_ref, k_ref, v_ref, context_ref, grad_ref = (ref[n] for n in ("q", "k", "v", "context", "grad"))
    dq_ref, dk_ref, dv_ref, x_t, x_got = (ref[n] for n in ("dq", "dk", "dv", "x_t", "x_got"))
    extra_ref, penal_ref = ref["extra"], ref["penal"]
    dx_acc, dx_sent, dx_far, dx_got, dx_far_got = (
        ref[n] for n in ("dx_acc", "dx_sent", "dx_far", "dx_got", "dx_far_got")
    )
    pool_parts, pool_got, vec_parts, vec_got = (
        ref[n] for n in ("pool_parts", "pool_got", "vec_parts", "vec_got")
    )
    row_sem, local_sem = ref["row_sem"], ref["local_sem"]
    rows_here, size, width = x_ref.shape
    low = jnp.bfloat16
    me, place = lax.axis_index("ctx"), lax.axis_index("dp")
    core, side = me % 2, me // 2
    near, across = me + 1 - 2 * core, (me + 2) % 4
    near_dev, across_dev = {"ctx": near}, {"ctx": across}
    y, z = place % 2, place // 2
    y_dev = {"dp": place + 1 - 2 * y}
    z_at = (z + 1 - 2 * (z % 2), (z + 2) % 4, 3 - z)
    z_dev = [{"dp": other * 2 + y} for other in z_at]
    peers = [near_dev, across_dev] + ([y_dev] + z_dev if fused else [])

    barrier = pltpu.get_barrier_semaphore()
    for peer in peers:
        pl.semaphore_signal(barrier, inc=1, device_id=peer, device_id_type=MESH)
    pl.semaphore_wait(barrier, len(peers))
    links = Links(ref["send_sem"], ref["recv_sem"])

    first_cut = GROUPS[1][0]
    blocks = [(0, first_cut, r) for r in range(rows_here)]
    blocks += [(first_cut, width - first_cut, r) for r in range(rows_here)]

    def load_block(step):
        slot = step % 2
        start, count, r = blocks[step]
        columns, local = pl.ds(start, count), pl.ds(0, count)
        pairs = (
            (k_hbm, k_ref), (v_hbm, v_ref), (q_hbm, q_ref), (context_hbm, context_ref),
            (grad_hbm, grad_ref),
        )
        copies = [
            pltpu.make_async_copy(
                source.at[r, :, columns], target.at[slot, :, local], row_sem.at[slot, i]
            )
            for i, (source, target) in enumerate(pairs)
        ]
        if step < rows_here:
            copies.append(pltpu.make_async_copy(x_hbm.at[:, r], x_got.at[slot], row_sem.at[slot, 5]))
        return copies

    for item in load_block(0):
        item.start()
    load_mixed = pltpu.make_async_copy(mixed_hbm, dx_acc, local_sem.at[0])
    links.start("pool0", pool_ref, pool_got.at[0], near_dev)
    if fused:
        u_ref, u_x, u_y, u_z = (ref[n] for n in ("u", "u_x", "u_y", "u_z"))
        a_ref, a_z, a_s, a_x = (ref[n] for n in ("a", "a_z", "a_s", "a_x"))
        b_ref, b_y, b_z = (ref[n] for n in ("b", "b_y", "b_z"))
        o_ref, o_y, o_z, o_s, o_x = (ref[n] for n in ("o", "o_y", "o_z", "o_s", "o_x"))
        half_rows = u_ref.shape[2] // 2
        links.start("up_x0", up_hbm.at[1 - side, :, :, pl.ds(0, half_rows)], u_x.at[0], across_dev)
        links.start("b_y", far_hbm.at[:, 1 - y], b_y, y_dev)
        for o in range(3):
            links.start(f"a_z{o}", down_hbm.at[z_at[o]], a_z.at[o], z_dev[o])
        load_parts = [
            pltpu.make_async_copy(far_hbm.at[:, y], b_ref, local_sem.at[1]),
            pltpu.make_async_copy(down_hbm.at[z], a_ref, local_sem.at[2]),
            pltpu.make_async_copy(up_hbm.at[side], u_ref, local_sem.at[3]),
            pltpu.make_async_copy(out_hbm.at[:, y], o_ref, local_sem.at[4]),
        ]
        for item in load_parts:
            item.start()
    load_mixed.start()
    vec_parts[0] = vector_ref[...]

    def pool_one():
        links.arrived("pool0")
        pool_parts[...] = add_up([pool_ref[...], pool_got[0]]).astype(low)
        links.start("pool1", pool_parts, pool_got.at[1], across_dev)

    def pool_two():
        links.arrived("pool1")
        pool_out[...] = add_up([pool_parts[...], pool_got[1]]) / count_ref[...]

    def send_z(name, source, target):
        for o in range(3):
            links.start(f"{name}{o}", source(z_at[o]), target(o), z_dev[o])

    def arrived_z(name):
        links.arrived(f"{name}0", f"{name}1", f"{name}2")

    def out_y():
        links.start("out_y", out_hbm.at[:, 1 - y], o_y, y_dev)

    def out_z():
        load_parts[3].wait()
        links.arrived("out_y")
        add_into(o_ref, [o_y], 4)
        send_z("out_z", lambda i: o_ref.at[i], lambda o: o_z.at[o])

    def out_far():
        arrived_z("out_z")
        o_s[...] = add_up([o_ref[z]] + [o_z[o] for o in range(3)]).astype(low)
        links.start("out_x", o_s, o_x, across_dev)

    def out_end():
        links.arrived("out_x")
        wo_out[core] = add_up([o_s[...], o_x[...]]).astype(low)
        links.start("out_gather", wo_out.at[core], wo_out.at[core], near_dev)

    def down_z():
        load_parts[0].wait()
        links.arrived("b_y")
        add_into(b_ref, [b_y], 4)
        send_z("b_z", lambda i: b_ref.at[i], lambda o: b_z.at[o])

    def down_near_far():
        load_parts[1].wait()
        arrived_z("a_z")
        a_s[...] = add_up([a_ref[...]] + [a_z[o] for o in range(3)]).astype(low)
        links.start("a_x", a_s, a_x, across_dev)

    def down_far():
        arrived_z("b_z")
        count = b_ref.shape[1]
        own = pl.ds(pl.multiple_of(2 * count + side * count, 16), count)
        down_out[core, own] = add_up([b_ref[z]] + [b_z[o] for o in range(3)]).astype(low)
        links.start("b_x", down_out.at[core, own], down_out.at[core, own], across_dev)

    def down_end():
        links.arrived("a_x", "b_x")
        down_out[core, 0 : a_s.shape[0]] = add_up([a_s[...], a_x[...]]).astype(low)
        links.start("down_gather", down_out.at[core], down_out.at[core], near_dev)

    def up_x():
        rows = pl.ds(half_rows, half_rows)
        links.start("up_x1", up_hbm.at[1 - side, :, :, rows], u_x.at[1], across_dev)

    def up_y(h):
        if h == 0:
            load_parts[2].wait()
        rows = pl.ds(h * half_rows, half_rows)
        links.arrived(f"up_x{h}")
        for i in range(4):
            add_into(u_ref.at[i, :, rows], [u_x.at[h, i]], 2)
        links.start(f"up_y{h}", u_ref.at[:, 1 - y, rows], u_y.at[h], y_dev)

    def up_z(h):
        rows = pl.ds(h * half_rows, half_rows)
        links.arrived(f"up_y{h}")
        for i in range(4):
            u_ref[i, y, rows] = add_up([u_ref[i, y, rows], u_y[h, i]]).astype(low)
        send_z(f"up_z{h}", lambda i: u_ref.at[i, y, rows], lambda o: u_z.at[o, rows])

    def up_far():
        arrived_z("up_z0")
        arrived_z("up_z1")
        up_out[me] = add_up([u_ref[z, y]] + [u_z[o] for o in range(3)]).astype(low)
        links.start("up_gather", up_out.at[me], up_out.at[me], across_dev)

    def up_end():
        links.arrived("up_gather")
        links.start("up_near0", up_out.at[me], up_out.at[me], near_dev)
        links.start("up_near1", up_out.at[across], up_out.at[across], near_dev)

    def part(name, g):
        return ref[f"{name}{g}"]

    def group_core(g):
        links.start(f"group_core{g}", part("g", g).at[1 - core], part("g_got", g), near_dev)

    def group_y(g):
        links.arrived(f"group_core{g}")
        for i in range(4):
            add_into(part("g", g).at[core, i], [part("g_got", g).at[i]], 2)
        links.start(f"group_y{g}", part("g", g).at[core, :, 1 - y], part("g_y", g), y_dev)

    def group_z(g):
        links.arrived(f"group_y{g}")
        own = part("g", g)
        for i in range(4):
            own[core, i, y] = add_up([own[core, i, y], part("g_y", g)[i]]).astype(low)
        send_z(f"group_z{g}", lambda i: own.at[core, i, y], lambda o: part("g_z", g).at[o])

    def group_far(g):
        arrived_z(f"group_z{g}")
        pieces = [part("g", g)[core, z, y]] + [part("g_z", g)[o] for o in range(3)]
        part("g_s", g)[...] = add_up(pieces).astype(low)
        links.start(f"group_x{g}", part("g_s", g), part("g_x", g), across_dev)

    def group_end(g):
        links.arrived(f"group_x{g}")
        out = part("square", g)
        out[core] = add_up([part("g_s", g)[...], part("g_x", g)[...]]).astype(low)
        links.start(f"group_gather{g}", out.at[core], out.at[core], near_dev)

    def vector_step(i, device):
        if i:
            links.arrived(f"vector{i - 1}")
            vec_parts[i] = vec_parts[i - 1] + vec_got[i - 1]
        if device is not None:
            links.start(f"vector{i}", vec_parts.at[i], vec_got.at[i], device)

    def vector_z():
        vector_step(3, None)
        for o in range(3):
            links.start(f"vector_z{o}", vec_parts.at[3], vec_got.at[3 + o], z_dev[o])

    def vector_end():
        arrived_z("vector_z")
        vector_out[...] = vec_parts[3] + (vec_got[3] + (vec_got[4] + vec_got[5]))

    row = lax.broadcasted_iota(jnp.int32, (PAIR, size), 0)
    lane = lanes_of(size)

    def attend_pairs(step, first, last):
        slot = step % 2
        start, _, r = blocks[step]

        def one_pair(n, carry):
            local = pl.ds(pl.multiple_of(n * PAIR, PAIR), PAIR)
            columns = pl.ds(pl.multiple_of(start + n * PAIR, PAIR), PAIR)
            head = 2 * (start // PAIR + n)
            grad = grad_ref[slot, :, local]
            q_both = split_heads(q_ref[slot, :, local])
            g_both = split_heads(grad)
            product = grad.astype(jnp.float32) * context_ref[slot, :, local].astype(jnp.float32)
            stat = lse_ref[r]
            penal = penal_ref[r]
            q_extra, g_extra = [], []
            for h in range(2):
                lse = jnp.sum(jnp.where(lane == head + h, stat, 0.0), axis=1, keepdims=True)
                ours = (lane < HEAD_DIM) if h == 0 else (lane >= HEAD_DIM)
                delta = jnp.sum(jnp.where(ours, product, 0.0), axis=1, keepdims=True)
                q_extra.append(with_constant(penal, -lse))
                g_extra.append(with_constant(jnp.zeros_like(penal), -delta))
            q_wide = jnp.concatenate([q_both, jnp.concatenate(q_extra, axis=0)], axis=1)
            g_wide = jnp.concatenate([g_both, jnp.concatenate(g_extra, axis=0)], axis=1)
            dq = jnp.zeros((PAIR, 2 * size), jnp.float32)
            for j in range(4):
                rows = pl.ds(j * size, size)
                keys = k_ref[slot, rows, local]
                extra = extra_ref[r, rows, :]
                probs = jnp.exp(dot_nt(jnp.concatenate([keys, extra], axis=1), q_wide))
                values = jnp.concatenate([v_ref[slot, rows, local], extra], axis=1)
                grad_s = (probs * dot_nt(values, g_wide)).astype(low)
                dv_ref[r, rows, columns] = matmul(probs.astype(low), g_both).astype(low)
                dk_ref[r, rows, columns] = matmul(grad_s, q_both).astype(low)
                dq = dq + matmul(keys.T, grad_s)
            dq = jnp.where(row < HEAD_DIM, dq[:, :size], dq[:, size:]) * HEAD_DIM ** (-0.5)
            dq_ref[r, :, columns] = dq.T.astype(low)
            return carry

        lax.fori_loop(first, last, one_pair, 0)

    def weight_group(g):
        start, count = GROUPS[g]
        if fused:
            depth = part("g", g).shape[3]

        def one_part(i, carry):
            columns = pl.ds(pl.multiple_of(start + i * PAIR, PAIR), PAIR)
            for n, source in enumerate((dq_ref, dk_ref, dv_ref)):
                keys = source.shape[1]
                total = sum(
                    matmul(x_t[r, :, :keys], source[r, :, columns]) for r in range(rows_here)
                ).astype(low)
                if not fused:
                    square_out[n, :, columns] = total
                    continue
                total = total.reshape(4, 2, 2, depth, PAIR)
                target = pl.ds(pl.multiple_of(n * count + i * PAIR, PAIR), PAIR)
                for h in range(2):
                    part("g", g)[h, :, :, :, target] = total[:, :, h]
            return carry

        lax.fori_loop(0, count // PAIR, one_part, 0)
        columns = pl.ds(start, count)
        for n, source in enumerate((dq_ref, dv_ref)):
            vec_parts[0, n : n + 1, columns] = sum(
                jnp.sum(source[r, :, columns].astype(jnp.float32), axis=0, keepdims=True)
                for r in range(rows_here)
            )

    def input_parts(r):
        for j in (3, 2, 1, 0):
            rows = pl.ds(j * size, size)
            total = dot_nt(dk_ref[r, rows, :], w_key[...]) + dot_nt(dv_ref[r, rows, :], w_value[...])
            if j == 0:
                dx_acc[r] = dx_acc[r] + total + dot_nt(dq_ref[r], w_query[...])
            elif j == 2:
                dx_far[r] = total.astype(low)
            else:
                n = j // 2
                dx_sent[r, n] = total.astype(low)
                links.start(f"dx_near{r}{n}", dx_sent.at[r, n], dx_got.at[r, n], near_dev)

    def input_far(r):
        links.arrived(f"dx_near{r}1")
        dx_far[r] = add_up([dx_far[r], dx_got[r, 1]]).astype(low)
        links.start(f"dx_far{r}", dx_far.at[r], dx_far_got.at[r], across_dev)

    def input_done(r):
        links.arrived(f"dx_near{r}0", f"dx_far{r}")
        dx_out[r] = add_up([dx_acc[r], dx_got[r, 0], dx_far_got[r]]).astype(low)

    def prepare_row(r):
        slot = r % 2
        for j in range(4):
            rows = slice(j * size, (j + 1) * size)
            texts = text_rows(ids_ref[j, r : r + 1, :], size)
            extra_ref[r, rows, :] = key_extra(texts)
            if j == 0:
                penal_ref[r] = query_extra(texts)
            block = x_ref[r] if j == 0 else x_got[slot, j - 1]
            x_t[r, :, rows] = block.T

    def begin(step):
        for item in load_block(step):
            item.wait()
        if step + 1 < len(blocks):
            for item in load_block(step + 1):
                item.start()

    def do(*actions):
        if fused:
            for action, *given in actions:
                action(*given)

    most = first_cut // PAIR
    begin(0)
    prepare_row(0)
    attend_pairs(0, 0, most // 2)
    do((pool_one,))
    attend_pairs(0, most // 2, most)
    do((down_z,), (out_y,))
    begin(1)
    prepare_row(1)
    attend_pairs(1, 0, most // 2)
    do((up_x,), (pool_two,))
    attend_pairs(1, most // 2, most)
    do((up_y, 0), (down_near_far,))
    begin(2)
    prepare_row(2)
    attend_pairs(2, 0, most // 2)
    do((out_z,))
    attend_pairs(2, most // 2, most)
    do((up_z, 0), (down_far,))
    weight_group(0)
    do((group_core, 0), (up_y, 1))
    begin(3)
    attend_pairs(3, 0, 2)
    do((group_y, 0), (down_end,), (out_far,))
    load_mixed.wait()
    input_parts(0)
    do((up_z, 1))
    begin(4)
    attend_pairs(4, 0, 2)
    do((input_far, 0), (out_end,))
    input_parts(1)
    do((group_z, 0))
    begin(5)
    attend_pairs(5, 0, 1)
    do((input_far, 1))
    weight_group(1)
    do((group_core, 1))
    attend_pairs(5, 1, 2)
    do((group_y, 1), (up_far,))
    weight_group(2)
    do((group_core, 2), (vector_step, 0, near_dev))
    input_parts(2)
    if not fused:
        vector_out[...] = vec_parts[0]
        pool_one()
        for r in range(3):
            input_far(r)
        pool_two()
        for r in range(3):
            input_done(r)
        links.finish()
        return
    do((group_y, 2), (group_z, 1), (vector_step, 1, across_dev))
    do((input_far, 2), (group_far, 0), (group_z, 2), (input_done, 0))
    do((vector_step, 2, y_dev), (up_end,), (input_done, 1), (group_far, 1), (vector_z,))
    do((group_end, 0), (group_far, 2), (group_end, 1), (vector_end,))
    do((group_end, 2), (input_done, 2))
    links.arrived("down_gather", "out_gather", "up_near0", "up_near1")
    links.arrived("group_gather0", "group_gather1", "group_gather2")
    links.finish()


def attend_back(
    fused, x, ids, lse, w_query, w_key, w_value, pool, counts, vectors,
    x_got, q, k, v, context, grad, mixed, up, down, far, out,
):
    rows_here, size, width = x.shape
    keys = size * 4
    low = jnp.bfloat16
    f32 = jnp.float32
    whole = pl.BlockSpec(memory_space=pltpu.VMEM)
    outside = pl.BlockSpec(memory_space=pl.ANY)
    shape = jax.ShapeDtypeStruct
    most = GROUPS[0][1]
    vec = vectors.shape
    outs = {}
    if fused:
        depth = up.shape[3]
        for g, (_, count) in enumerate(GROUPS):
            outs[f"square{g}"] = shape((2, depth // 2, 3 * count), low)
        outs["up"] = shape((4, depth, width), low)
        outs["down"] = shape((2, 2 * down.shape[1], width), low)
        outs["wo"] = shape((2, depth, width // 2), low)
        outs["square"] = shape((8, 128), low)
    else:
        outs["square"] = shape((3, width, width), low)
        for name in ("up", "down", "wo"):
            outs[name] = shape((8, 128), low)
    scratch = {
        "x_got": pltpu.VMEM((2, 3, size, width), low),
        "x_t": pltpu.VMEM((rows_here, width, keys), low),
        "q": pltpu.VMEM((2, size, most), low),
        "k": pltpu.VMEM((2, keys, most), low),
        "v": pltpu.VMEM((2, keys, most), low),
        "context": pltpu.VMEM((2, size, most), low),
        "grad": pltpu.VMEM((2, size, most), low),
        "extra": pltpu.VMEM((rows_here, keys, PAIR), low),
        "penal": pltpu.VMEM((rows_here, size, PAIR), f32),
        "dq": pltpu.VMEM((rows_here, size, width), low),
        "dk": pltpu.VMEM((rows_here, keys, width), low),
        "dv": pltpu.VMEM((rows_here, keys, width), low),
        "dx_acc": pltpu.VMEM((rows_here, size, width), f32),
        "dx_sent": pltpu.VMEM((rows_here, 2, size, width), low),
        "dx_far": pltpu.VMEM((rows_here, size, width), low),
        "dx_got": pltpu.VMEM((rows_here, 2, size, width), low),
        "dx_far_got": pltpu.VMEM((rows_here, size, width), low),
        "pool_parts": pltpu.VMEM(pool.shape, low),
        "pool_got": pltpu.VMEM((2,) + pool.shape, low),
        "vec_parts": pltpu.VMEM((4,) + vec, f32),
        "vec_got": pltpu.VMEM((6,) + vec, f32),
        "send_sem": pltpu.SemaphoreType.DMA((72,)),
        "recv_sem": pltpu.SemaphoreType.DMA((72,)),
        "row_sem": pltpu.SemaphoreType.DMA((2, 6)),
        "local_sem": pltpu.SemaphoreType.DMA((5,)),
    }
    if fused:
        for g, (_, count) in enumerate(GROUPS):
            tail = (depth // 2, 3 * count)
            scratch[f"g{g}"] = pltpu.VMEM((2, 4, 2) + tail, low)
            scratch[f"g_got{g}"] = pltpu.VMEM((4, 2) + tail, low)
            scratch[f"g_y{g}"] = pltpu.VMEM((4,) + tail, low)
            scratch[f"g_z{g}"] = pltpu.VMEM((3,) + tail, low)
            scratch[f"g_s{g}"] = pltpu.VMEM(tail, low)
            scratch[f"g_x{g}"] = pltpu.VMEM(tail, low)
        b_rows = far.shape[2]
        scratch["u"] = pltpu.VMEM((4, 2, depth, width), low)
        scratch["u_x"] = pltpu.VMEM((2, 4, 2, depth // 2, width), low)
        scratch["u_y"] = pltpu.VMEM((2, 4, depth // 2, width), low)
        scratch["u_z"] = pltpu.VMEM((3, depth, width), low)
        scratch["a"] = pltpu.VMEM(down.shape[1:], low)
        scratch["a_z"] = pltpu.VMEM((3,) + down.shape[1:], low)
        scratch["a_s"] = pltpu.VMEM(down.shape[1:], low)
        scratch["a_x"] = pltpu.VMEM(down.shape[1:], low)
        scratch["b"] = pltpu.VMEM((4, b_rows, width), low)
        scratch["b_y"] = pltpu.VMEM((4, b_rows, width), low)
        scratch["b_z"] = pltpu.VMEM((3, b_rows, width), low)
        for name, lead in (("o", (4,)), ("o_y", (4,)), ("o_z", (3,)), ("o_s", ()), ("o_x", ())):
            scratch[name] = pltpu.VMEM(lead + (depth, width // 2), low)
    names = tuple(outs) + tuple(scratch)
    got = pl.pallas_call(
        functools.partial(attend_back_kernel, fused, names),
        out_shape=(
            shape((rows_here, size, width), low),
            shape(pool.shape, f32),
            shape(vec, f32),
        )
        + tuple(outs.values()),
        in_specs=[whole] * 9 + [outside] * 11,
        out_specs=(whole,) * (3 + len(outs)),
        scratch_shapes=list(scratch.values()),
        compiler_params=pltpu.CompilerParams(
            vmem_limit_bytes=63 * 2**20, collective_id=1, has_side_effects=True
        ),
        cost_estimate=pl.CostEstimate(
            flops=rows_here
            * (4 * (size + 2 * keys) * width * width + 40 * size * keys * width),
            bytes_accessed=2 * (16 * width * width + 9 * keys * width),
            transcendentals=rows_here * HEADS * size * keys,
        ),
    )(
        x, ids, lse, w_query, w_key, w_value, pool, counts, vectors,
        x_got, q, k, v, context, grad, mixed, up, down, far, out,
    )
    return got[:3] + (dict(zip(outs, got[3:])),)


def outputs_kernel(
    square0, square1, square2, wo, up, down, pool, final_hbm, dx_hbm,
    wq_out, wk_out, wv_out, wo_out, up_out, down_out, pool_out, final_out, dx_out, sem,
):
    copies = [
        pltpu.make_async_copy(final_hbm, final_out, sem.at[0]),
        pltpu.make_async_copy(dx_hbm, dx_out, sem.at[1]),
    ]
    for item in copies:
        item.start()
    f32 = jnp.float32
    pool_out[...] = pool[...].reshape(pool_out.shape)
    for (start, count), square in zip(GROUPS, (square0, square1, square2)):
        rows = square.shape[1]
        for n, out in enumerate((wq_out, wk_out, wv_out)):
            for h in range(2):
                out[h * rows : (h + 1) * rows, start : start + count] = square[
                    h, :, n * count : (n + 1) * count
                ].astype(f32)
    for h in range(2):
        half = wo.shape[2]
        wo_out[:, h * half : (h + 1) * half] = wo[h].astype(f32)
        rows = down.shape[1]
        down_out[h * rows : (h + 1) * rows, :] = down[h].astype(f32)
    for i in range(4):
        place, width = (i % 2) * 2 + i // 2, up.shape[2]
        up_out[:, place * width : (place + 1) * width] = up[i].astype(f32)
    for item in copies:
        item.wait()


def outputs(squares, wo, up, down, pool, final, dx):
    f32 = jnp.float32
    whole = pl.BlockSpec(memory_space=pltpu.VMEM)
    outside = pl.BlockSpec(memory_space=pl.ANY)
    shape = jax.ShapeDtypeStruct
    rows, width = up.shape[1:]
    row_count = final.shape[0]
    return pl.pallas_call(
        outputs_kernel,
        out_shape=(
            shape((rows, width), f32), shape((rows, width), f32), shape((rows, width), f32),
            shape((rows, width), f32), shape((rows, 4 * width), f32),
            shape((2 * down.shape[1], width), f32),
            shape((row_count, pool.shape[0] // row_count, width), f32),
            shape(final.shape, final.dtype), shape(dx.shape, dx.dtype),
        ),
        in_specs=[whole] * 7 + [outside] * 2,
        out_specs=(whole,) * 7 + (outside,) * 2,
        scratch_shapes=[pltpu.SemaphoreType.DMA((2,))],
        compiler_params=pltpu.CompilerParams(vmem_limit_bytes=32 * 2**20),
    )(*squares, wo, up, down, pool, final, dx)


def radices_of(count):
    if count == 8:
        return ((1, 2), (2, 4))
    digits = []
    stride = 1
    while stride < count:
        digits.append((stride, 2))
        stride *= 2
    return tuple(digits)


def exchange(piece, axis_name, stride, offset):
    count = lax.axis_size(axis_name)
    pairs = [(i, i ^ (offset * stride)) for i in range(count)]
    return lax.ppermute(piece, axis_name, pairs)


def digit_of(axis_name, stride, radix):
    return (lax.axis_index(axis_name) // stride) % radix


def scatter_digit(pieces, place, axis_name, stride, radix):
    here = digit_of(axis_name, stride, radix)
    received = [
        exchange(
            lax.dynamic_index_in_dim(pieces, here ^ offset, place, keepdims=False).astype(
                jnp.bfloat16
            ),
            axis_name, stride, offset,
        )
        for offset in range(1, radix)
    ]
    total = lax.dynamic_index_in_dim(pieces, here, place, keepdims=False).astype(jnp.float32)
    for item in received:
        total = total + item.astype(jnp.float32)
    return total.astype(jnp.bfloat16)


def halve(piece, place, axis_name, stride):
    half = piece.shape[place] // 2
    here = digit_of(axis_name, stride, 2)
    sent = lax.dynamic_slice_in_dim(piece, (1 - here) * half, half, place).astype(jnp.bfloat16)
    kept = lax.dynamic_slice_in_dim(piece, here * half, half, place).astype(jnp.float32)
    return (kept + exchange(sent, axis_name, stride, 1).astype(jnp.float32)).astype(jnp.bfloat16)


def join(piece, place, axis_name, stride):
    here = digit_of(axis_name, stride, 2)
    other = exchange(piece, axis_name, stride, 1)
    first = jnp.where(here == 0, piece, other)
    second = jnp.where(here == 0, other, piece)
    return jnp.concatenate([first, second], axis=place)


def scatter_rows(group, dp_size):
    digits = radices_of(dp_size)
    shape = tuple(r for _, r in reversed(digits))
    group = group.reshape(shape + (group.shape[0] // dp_size, group.shape[1]))
    for place, (stride, radix) in zip(range(len(digits) - 1, -1, -1), digits):
        group = scatter_digit(group, place, "dp", stride, radix)
    return group


def finish_weight(flat, dp_size, side):
    flat = scatter_rows(flat, dp_size)
    flat = flat.astype(jnp.float32) + exchange(flat, "ctx", 2, 1).astype(jnp.float32)
    return join(flat.astype(jnp.bfloat16), side, "ctx", 1).astype(jnp.float32)


def reduce_weight(gradient, dp_size, side):
    return finish_weight(halve(gradient, side, "ctx", 1), dp_size, side)


def per_device(
    hidden_in,
    seg_ids,
    valid,
    w_query,
    b_query,
    w_key,
    w_value,
    b_value,
    w_out,
    b_out,
    gain_attn,
    shift_attn,
    w_up,
    b_up,
    w_down,
    b_down,
    gain_ffn,
    shift_ffn,
    pooled_text_gradient,
):
    row_count, group_size, model_width = hidden_in.shape
    dp_size = lax.axis_size("dp")
    ff_width = w_up.shape[1]
    rows_here, ff_here = model_width // dp_size, ff_width // dp_size
    fused = dp_size == 8 and rows_here % 32 == 0 and ff_here % 128 == 0
    q_all, context, lse_all, ids_got, x_got, k_all, v_all = attend(
        hidden_in, seg_ids, valid, b_query, b_value, w_query, w_key, w_value
    )
    vectors = (b_out, gain_attn, shift_attn, b_up, b_down, gain_ffn, shift_ffn)
    pool, counts, vector_parts, grad_context, grad_mixed, out, final_out, up, down, far = middle(
        fused, hidden_in, context, ids_got, vectors, pooled_text_gradient, w_out, w_up, w_down,
        dp_size,
    )
    if fused:
        up_part = up.reshape(2, 4, 2, rows_here, -1)
        far_part = far.reshape((4, 2) + far.shape[1:])
        out_part = out.reshape(4, 2, rows_here, -1)
    else:
        up_part = far_part = out_part = jnp.zeros((16, 128), jnp.bfloat16)
    grad_input, pooled, vector_sum, sums_of = attend_back(
        fused, hidden_in, ids_got, lse_all, w_query, w_key, w_value,
        pool, counts, vector_parts, x_got, q_all, k_all, v_all, context, grad_context, grad_mixed,
        up_part, down, far_part, out_part,
    )
    if fused:
        *square_sums, up_sum, down_sum, pooled, final_out, grad_input = outputs(
            [sums_of[f"square{g}"] for g in range(3)], sums_of["wo"], sums_of["up"],
            sums_of["down"], pooled, final_out, grad_input,
        )
    else:
        squares = sums_of["square"]
        square_sums = [reduce_weight(squares[n], dp_size, 1) for n in range(3)]
        square_sums.append(finish_weight(out, dp_size, 1))
        up_sum = finish_weight(up.transpose(1, 0, 2).reshape(model_width, -1), dp_size, 1)
        down_sum = finish_weight(down.reshape(-1, model_width), dp_size, 0)
        vector_sum = lax.psum(vector_sum, ("dp", "ctx"))
        pooled = pooled.reshape(row_count, NSEG, model_width)
    place = lax.axis_index("dp")
    sums = lax.dynamic_slice_in_dim(vector_sum[:8], place * rows_here, rows_here, 1)
    sum_bu = lax.dynamic_slice_in_dim(
        vector_sum[8 : 8 + ff_width // model_width].reshape(-1), place * ff_here, ff_here
    )
    results = (
        square_sums[0], sums[0], square_sums[1], square_sums[2], sums[1], square_sums[3],
        sums[2], sums[3], sums[4], up_sum, sum_bu, down_sum, sums[5], sums[6], sums[7],
    )
    return (
        final_out,
        pooled,
        grad_input,
    ) + tuple(results)


def solution(mesh):
    placed = (
        P("dp", "ctx", None),
        P("dp", "ctx"),
        P("dp", "ctx"),
        P(),
        P(),
        P(),
        P(),
        P(),
        P(),
        P(),
        P(),
        P(),
        P(),
        P(),
        P(),
        P(),
        P(),
        P(),
        P("dp", None, None),
    )
    return jax.shard_map(
        per_device,
        mesh=mesh,
        in_specs=placed,
        out_specs=(
            P("dp", "ctx", None),
            P("dp", None, None),
            P("dp", "ctx", None),
            P("dp", None),
            P("dp"),
            P("dp", None),
            P("dp", None),
            P("dp"),
            P("dp", None),
            P("dp"),
            P("dp"),
            P("dp"),
            P("dp", None),
            P("dp"),
            P("dp", None),
            P("dp"),
            P("dp"),
            P("dp"),
        ),
        check_vma=False,
    )
```

```python
import functools
import types

import jax
import jax.numpy as jnp
from jax import lax
from jax.experimental import pallas as pl
from jax.experimental.pallas import tpu as pltpu
from jax.sharding import PartitionSpec as P

HEADS = 12
HEAD_DIM = 64
NSEG = 16


eps = 1e-12


def matmul(left_side, right_side):
    return jnp.dot(left_side, right_side, preferred_element_type=jnp.float32)


PAIR = 2 * HEAD_DIM
MESH = pl.DeviceIdType.MESH
MASKED = -1e30


def dot_nt(left_side, right_side):
    return lax.dot_general(
        left_side, right_side, (((1,), (1,)), ((), ())), preferred_element_type=jnp.float32
    )


def dot_tn(left_side, right_side):
    return lax.dot_general(
        left_side, right_side, (((0,), (0,)), ((), ())), preferred_element_type=jnp.float32
    )


def split_heads(pair):
    lane = lax.broadcasted_iota(jnp.int32, pair.shape, 1)
    zero = jnp.zeros_like(pair)
    return jnp.concatenate(
        [jnp.where(lane < HEAD_DIM, pair, zero), jnp.where(lane < HEAD_DIM, zero, pair)], axis=0
    )


def text_rows(ids_row, size):
    return jnp.broadcast_to(ids_row.astype(jnp.float32), (PAIR, size)).T


def lanes_of(size):
    return lax.broadcasted_iota(jnp.int32, (size, PAIR), 1)


def key_extra(texts):
    lane = lanes_of(texts.shape[0])
    hot = jnp.where(lane.astype(jnp.float32) == texts, 1.0, 0.0)
    return jnp.where((lane >= NSEG) & (lane < 4 * NSEG), 1.0, hot).astype(jnp.bfloat16)


def query_extra(texts):
    lane = lanes_of(texts.shape[0])
    other = (lane < NSEG) & (lane.astype(jnp.float32) != texts)
    return jnp.where(other, MASKED, 0.0)


def with_constants(extra, constants):
    lane = lanes_of(extra.shape[0])
    high = constants.astype(jnp.bfloat16).astype(jnp.float32)
    middle = (constants - high).astype(jnp.bfloat16).astype(jnp.float32)
    rest = constants - high - middle
    terms = jnp.where(lane < 2 * NSEG, high, jnp.where(lane < 3 * NSEG, middle, rest))
    kept = (lane >= NSEG) & (lane < 4 * NSEG)
    return jnp.where(kept, terms, extra).astype(jnp.bfloat16)


def of_head(extra, head):
    lane = lanes_of(extra.shape[0])
    kept = (lane < NSEG) | (lane % NSEG == head)
    return jnp.where(kept, extra, jnp.zeros_like(extra))


def attend_kernel(
    x_ref, seg_ref, valid_ref, b_query, b_value, w_query, w_key, w_value,
    q_out, context_out, lse_out, ids_out, x_hbm, k_hbm, v_hbm,
    x_got, k_ref, v_ref, extra_ref, ids_ref, send_sem, recv_sem, local_sem,
):
    rows_here, size, width = x_ref.shape
    me = lax.axis_index("ctx")
    one = me + 1 - 2 * (me % 2)
    two = (me + 2) % 4
    three = (one + 2) % 4
    low = jnp.bfloat16

    ids_ref[...] = jnp.zeros_like(ids_ref)
    ids_ref[0:rows_here, :] = seg_ref[...]
    ids_ref[rows_here : 2 * rows_here, :] = valid_ref[...]
    query_bias = b_query[...].astype(jnp.float32)[None]
    value_bias = b_value[...].astype(jnp.float32)[None]
    barrier = pltpu.get_barrier_semaphore()
    for peer in (one, two, three):
        pl.semaphore_signal(barrier, inc=1, device_id={"ctx": peer}, device_id_type=MESH)
    pl.semaphore_wait(barrier, 3)

    def send(source, target, slot, peer):
        return pltpu.make_async_remote_copy(
            src_ref=source, dst_ref=target, send_sem=send_sem.at[slot],
            recv_sem=recv_sem.at[slot], device_id={"ctx": peer}, device_id_type=MESH,
        )

    ids_out[0] = ids_ref[...]
    ids_sends = [send(ids_ref, ids_out.at[j + 1], j, peer) for j, peer in enumerate((one, two, three))]
    near = send(x_ref, x_got.at[0], 3, one)

    def far(r):
        return send(x_ref.at[r], x_got.at[1, r], 4 + r, two)

    def passed(r):
        return send(x_got.at[1, r], x_got.at[2, r], 4 + rows_here + r, one)

    far(0).start()
    near.start()
    for item in ids_sends:
        item.start()
    for r in range(1, rows_here):
        far(r).start()

    def project(x, r, j):
        count = x.shape[0] // size
        k = matmul(x, w_key[...]).astype(low)
        v = (matmul(x, w_value[...]) + value_bias).astype(low)
        for n in range(count):
            rows = pl.ds((j + n if r is not None else j) * size, size)
            k_ref[n if r is None else r, rows, :] = k[n * size : (n + 1) * size]
            v_ref[n if r is None else r, rows, :] = v[n * size : (n + 1) * size]

    own = x_ref[...].reshape(rows_here * size, width)
    q = (matmul(own, w_query[...]) + query_bias).astype(low)
    q_out[...] = (q * HEAD_DIM ** (-0.5)).astype(low).reshape(q_out.shape)
    project(own, None, 0)
    near.wait_recv()
    project(x_got[0].reshape(rows_here * size, width), None, 1)
    for item in ids_sends:
        item.wait_recv()
    lane = lax.broadcasted_iota(jnp.int32, (size, PAIR), 1)
    far(0).wait_recv()
    passed(0).start()

    def keep(r):
        return (
            pltpu.make_async_copy(k_ref.at[r], k_hbm.at[r], local_sem.at[0, r]),
            pltpu.make_async_copy(v_ref.at[r], v_hbm.at[r], local_sem.at[1, r]),
            pltpu.make_async_copy(x_got.at[:, r], x_hbm.at[:, r], local_sem.at[2, r]),
        )

    for r in range(rows_here):
        passed(r).wait_recv()
        project(jnp.concatenate([x_got[1, r], x_got[2, r]], axis=0), r, 2)
        for item in keep(r):
            item.start()
        for j in range(4):
            texts = text_rows(ids_out[j, r : r + 1, :], size)
            extra_ref[j * size : (j + 1) * size, :] = key_extra(texts)
            if j == 0:
                own_extra = query_extra(texts).astype(low)

        def two_pairs(n, carry, r=r, own_extra=own_extra):
            extras = jnp.concatenate([own_extra, own_extra], axis=0)
            columns, scores = [], []
            for pair in (2 * n, 2 * n + 1):
                columns.append(pl.ds(pl.multiple_of(pair * PAIR, PAIR), PAIR))
                both = split_heads(q_out[r, :, columns[-1]])
                keys = jnp.concatenate([k_ref[r, :, columns[-1]], extra_ref[...]], axis=1)
                scores.append(dot_nt(jnp.concatenate([both, extras], axis=1), keys))
            stat = lse_out[r]
            for i in range(2):
                top = jnp.max(scores[i], axis=-1, keepdims=True)
                weight = jnp.exp(scores[i] - top)
                total = jnp.sum(weight, axis=-1, keepdims=True)
                mixed = matmul(weight.astype(low), v_ref[r, :, columns[i]]) * (1.0 / total)
                context_out[r, :, columns[i]] = jnp.where(
                    lane < HEAD_DIM, mixed[:size], mixed[size:]
                ).astype(low)
                lse = top + jnp.log(total)
                for h in range(2):
                    ours = lane % NSEG == 4 * n + 2 * i + h
                    stat = jnp.where(ours, lse[h * size : (h + 1) * size], stat)
            lse_out[r] = stat
            return carry

        lse_out[r] = jnp.zeros((size, PAIR), jnp.float32)
        lax.fori_loop(0, HEADS // 4, two_pairs, 0)
        if r + 1 < rows_here:
            far(r + 1).wait_recv()
            passed(r + 1).start()
    for r in range(rows_here):
        for item in keep(r):
            item.wait()
        far(r).wait_send()
        passed(r).wait_send()
    near.wait_send()
    for item in ids_sends:
        item.wait_send()


def attend(x, seg_ids, valid, b_query, b_value, w_query, w_key, w_value):
    rows_here, size, width = x.shape
    keys = size * 4
    low = jnp.bfloat16
    whole = pl.BlockSpec(memory_space=pltpu.VMEM)
    outside = pl.BlockSpec(memory_space=pl.ANY)
    slots = 4 + 2 * rows_here
    return pl.pallas_call(
        attend_kernel,
        out_shape=(
            jax.ShapeDtypeStruct((rows_here, size, width), low),
            jax.ShapeDtypeStruct((rows_here, size, width), low),
            jax.ShapeDtypeStruct((rows_here, size, PAIR), jnp.float32),
            jax.ShapeDtypeStruct((4, 8, size), jnp.int32),
            jax.ShapeDtypeStruct((3,) + x.shape, low),
            jax.ShapeDtypeStruct((rows_here, keys, width), low),
            jax.ShapeDtypeStruct((rows_here, keys, width), low),
        ),
        in_specs=[whole] * 8,
        out_specs=(whole, whole, whole, whole, outside, outside, outside),
        scratch_shapes=[
            pltpu.VMEM((3,) + x.shape, low),
            pltpu.VMEM((rows_here, keys, width), low),
            pltpu.VMEM((rows_here, keys, width), low),
            pltpu.VMEM((keys, PAIR), low),
            pltpu.VMEM((8, size), jnp.int32),
            pltpu.SemaphoreType.DMA((slots,)),
            pltpu.SemaphoreType.DMA((slots,)),
            pltpu.SemaphoreType.DMA((3, rows_here)),
        ],
        compiler_params=pltpu.CompilerParams(
            vmem_limit_bytes=56 * 2**20, collective_id=0, has_side_effects=True
        ),
        cost_estimate=pl.CostEstimate(
            flops=rows_here * (2 * (size + 2 * keys) * width * width + 16 * size * keys * width),
            bytes_accessed=2 * (3 * width * width + 9 * keys * width),
            transcendentals=rows_here * HEADS * size * keys,
        ),
    )(x, seg_ids, valid, b_query, b_value, w_query, w_key, w_value)


def gelu_both(u):
    size = jnp.abs(u)
    t = 1.0 / (1.0 + (0.3275911 * 0.5**0.5) * size)
    bell = jnp.exp(-0.5 * u * u)
    poly = t * (
        0.127414796 + t * (-0.142248368 + t * (0.7107068705 + t * (-0.7265760135 + t * 0.5307027145)))
    )
    tail = poly * bell
    cdf = jnp.where(u >= 0.0, 1.0 - tail, tail)
    return u * cdf, cdf + u * bell * 0.3989422804014327


def normalize(values_in):
    centre = jnp.mean(values_in, axis=-1, keepdims=True)
    centred = values_in - centre
    spread = jnp.mean(centred * centred, axis=-1, keepdims=True)
    scale = lax.rsqrt(spread + eps)
    return centred * scale, scale


def normalize_back(grad, unit, scale):
    mean_one = jnp.mean(grad, axis=-1, keepdims=True)
    mean_two = jnp.mean(grad * unit, axis=-1, keepdims=True)
    return (grad - mean_one - unit * mean_two) * scale


def column_sum(values_in):
    return jnp.sum(values_in, axis=0, keepdims=True)


B_QUERY, B_VALUE, B_OUT, GAIN_ONE, SHIFT_ONE, B_DOWN, GAIN_TWO, SHIFT_TWO, B_UP = range(9)


def middle_kernel(
    fused,
    x_ref, context_ref, ids_ref, b_out, gain_one, shift_one, b_up, b_down, gain_two, shift_two,
    text_ref, w_out, up_hbm, down_hbm,
    pool_out, count_out, vector_out, grad_out, mixed_out, wo_out, final_hbm, up_out, down_out, far_out,
    vec_ref, w_up, w_down, unit_ref, scale_ref, normed_ref, normed_t, act_ref, slope_ref, acc_ref, pre_one, pre_two,
    g_ref, final_ref, upg_ref, up_got, downg_ref, down_got, wo_sent, wo_got, down_y, down_x,
    send_sem, recv_sem, load_sem, store_sem,
):
    rows_here, size, width = x_ref.shape
    tokens = rows_here * size
    parts = w_up.shape[0]
    half = width // 2
    low = jnp.bfloat16
    f32 = jnp.float32
    me = lax.axis_index("ctx")
    core = me % 2
    near = {"ctx": me + 1 - 2 * core}
    side = me // 2
    place = lax.axis_index("dp")
    y = place % 2
    y_dev = {"dp": place + 1 - 2 * y}
    across_dev = {"ctx": (me + 2) % 4}
    peers = [near, across_dev, y_dev] if fused else [near]
    barrier = pltpu.get_barrier_semaphore()
    for peer in peers:
        pl.semaphore_signal(barrier, inc=1, device_id=peer, device_id_type=MESH)
    for row, source in (
        (B_OUT, b_out), (GAIN_ONE, gain_one), (SHIFT_ONE, shift_one), (B_DOWN, b_down),
        (GAIN_TWO, gain_two), (SHIFT_TWO, shift_two),
    ):
        vec_ref[row : row + 1, :] = source[...].astype(f32)[None]
    for i in range(parts):
        vec_ref[B_UP + i : B_UP + i + 1, :] = (
            b_up[i * width : (i + 1) * width].astype(f32)[None]
        )

    def vec(row):
        return vec_ref[row : row + 1, :]

    loads = []
    for i in range(parts):
        loads.append(
            (
                pltpu.make_async_copy(
                    up_hbm.at[:, pl.ds(i * width, width)], w_up.at[i], load_sem.at[0, i]
                ),
                pltpu.make_async_copy(
                    down_hbm.at[pl.ds(i * width, width)], w_down.at[i], load_sem.at[1, i]
                ),
            )
        )
    for pair in loads:
        for item in pair:
            item.start()

    def rows_of(r):
        return pl.ds(pl.multiple_of(r * size, size), size)

    text = lax.broadcasted_iota(jnp.int32, (NSEG, size), 0)

    def members(j, r):
        seg = ids_ref[j, r : r + 1, :]
        real = ids_ref[j, rows_here + r : rows_here + r + 1, :]
        return jnp.where((text == seg) & (real == 1), 1.0, 0.0)

    for r in range(rows_here):
        number = sum(jnp.sum(members(j, r), axis=1, keepdims=True) for j in range(4))
        count_out[r * NSEG : (r + 1) * NSEG, :] = jnp.maximum(number, 1.0)

    def first_norm(r, carry):
        rows = rows_of(r)
        mixed = x_ref[r].astype(f32) + (matmul(context_ref[r], w_out[...]) + vec(B_OUT))
        unit, scale = normalize(mixed)
        unit_ref[rows, :] = unit
        scale_ref[rows, :] = scale
        normed_ref[rows, :] = (unit * vec(GAIN_ONE) + vec(SHIFT_ONE)).astype(low)
        return carry

    lax.fori_loop(0, rows_here, first_norm, 0)
    for pair in loads:
        for item in pair:
            item.wait()

    def forward_part(i, following, now, then):
        for r in range(rows_here):
            rows = pl.ds(r * size, size)
            then[rows, :] = matmul(normed_ref[rows, :], w_up[following])
            act, slope = gelu_both(now[rows, :] + vec_ref[pl.ds(B_UP + i, 1), :])
            act = act.astype(low)
            act_ref[i, rows, :] = act
            slope_ref[i, rows, :] = slope.astype(low)
            acc_ref[rows, :] += matmul(act, w_down[i])

    def forward_parts(n, carry):
        forward_part(2 * n, 2 * n + 1, pre_one, pre_two)
        forward_part(2 * n + 1, jnp.minimum(2 * n + 2, parts - 1), pre_two, pre_one)
        return carry

    acc_ref[...] = jnp.zeros_like(acc_ref)
    pre_one[...] = matmul(normed_ref[...], w_up[0])
    lax.fori_loop(0, parts // 2, forward_parts, 0)
    normed_t[...] = normed_ref[...].T

    store_final = []
    vector_out[...] = jnp.zeros_like(vector_out)
    for r in range(rows_here):
        rows = pl.ds(r * size, size)
        normed = unit_ref[rows, :] * vec(GAIN_ONE) + vec(SHIFT_ONE)
        summed = normed + (acc_ref[rows, :] + vec(B_DOWN))
        unit, scale = normalize(summed)
        final = unit * vec(GAIN_TWO) + vec(SHIFT_TWO)
        high = final.astype(low)
        final_ref[r] = high
        item = pltpu.make_async_copy(final_ref.at[r], final_hbm.at[r], store_sem.at[r])
        item.start()
        store_final.append(item)
        own = members(0, r)
        own_low = own.astype(low)
        rest = (final - high.astype(f32)).astype(low)
        pool = matmul(own_low, high) + matmul(own_low, rest)
        pool_out[r * NSEG : (r + 1) * NSEG, :] = pool.astype(low)
        share = text_ref[r] / count_out[r * NSEG : (r + 1) * NSEG, :]
        first = share.astype(low)
        second = (share - first.astype(f32)).astype(low)
        third = (share - first.astype(f32) - second.astype(f32)).astype(low)
        grad = dot_tn(
            jnp.concatenate([own_low] * 3, axis=0), jnp.concatenate([first, second, third], axis=0)
        )
        back = normalize_back(grad * vec(GAIN_TWO), unit, scale)
        back_low = back.astype(low)
        acc_ref[rows, :] = back
        g_ref[rows, :] = back_low
        vector_out[GAIN_TWO : GAIN_TWO + 1, :] += column_sum(grad * unit)
        vector_out[SHIFT_TWO : SHIFT_TWO + 1, :] += column_sum(grad)
        vector_out[B_DOWN : B_DOWN + 1, :] += column_sum(back_low.astype(f32))

    pl.semaphore_wait(barrier, len(peers))

    def remote(source, target, slot, device=near):
        return pltpu.make_async_remote_copy(
            src_ref=source, dst_ref=target, send_sem=send_sem.at[slot],
            recv_sem=recv_sem.at[slot], device_id=device, device_id_type=MESH,
        )

    per_part = downg_ref.shape[0] // parts
    mine = parts // 2

    def up_send(i):
        return remote(upg_ref.at[i], up_got.at[i], i)

    def down_send(i):
        chunk = pl.ds(i * per_part, per_part)
        return remote(downg_ref.at[chunk, 1 - core], down_got.at[chunk], parts + i)

    def down_part(i, carry):
        part = dot_tn(act_ref[i], g_ref[...]).astype(low)
        downg_ref[pl.ds(i * per_part, per_part)] = part.reshape((per_part,) + downg_ref.shape[1:])
        down_send(i).start()
        return carry

    lax.fori_loop(0, parts, down_part, 0)

    def backward_part(step, carry):
        i = (step + mine * (1 - core)) % parts
        back = dot_nt(g_ref[...], w_down[i])
        back = (back * slope_ref[i].astype(f32)).astype(low)
        vector_out[pl.ds(B_UP + i, 1), :] = column_sum(back.astype(f32))
        acc_ref[...] += dot_nt(back, w_up[i])
        upg_ref[step] = matmul(normed_t[...], back).astype(low)

        @pl.when(step < mine)
        def _():
            up_send(step).start()

        return carry

    def down_sum(i, carry):
        downg_ref[i, core] = (
            downg_ref[i, core].astype(f32) + down_got[i].astype(f32)
        ).astype(low)
        return carry

    piece = downg_ref.shape[2] // 2
    quarter = piece // 2
    rest = pl.ds(pl.multiple_of(piece + quarter * (1 - side), 16), quarter)
    kept = pl.ds(pl.multiple_of(piece + quarter * side, 16), quarter)
    down_moves = []
    if fused:
        for n in range(4):
            down_moves.append(
                remote(
                    downg_ref.at[2 * n + 1 - y, core, pl.ds(0, piece)], down_y.at[n],
                    2 * parts + 1 + n, y_dev,
                )
            )
        for n in range(8):
            down_moves.append(
                remote(
                    downg_ref.at[n, core, rest], down_x.at[n], 2 * parts + 5 + n, across_dev
                )
            )
    lax.fori_loop(0, 1, backward_part, 0)
    for i in range(parts):
        down_send(i).wait_recv()
    lax.fori_loop(0, downg_ref.shape[0], down_sum, 0)
    for item in down_moves:
        item.start()
    lax.fori_loop(1, parts, backward_part, 0)

    def first_back(r, carry):
        rows = rows_of(r)
        unit = unit_ref[rows, :]
        grad = acc_ref[rows, :]
        back = normalize_back(grad * vec(GAIN_ONE), unit, scale_ref[rows, :])
        back_low = back.astype(low)
        mixed_out[r] = back
        g_ref[rows, :] = back_low
        vector_out[GAIN_ONE : GAIN_ONE + 1, :] += column_sum(grad * unit)
        vector_out[SHIFT_ONE : SHIFT_ONE + 1, :] += column_sum(grad)
        vector_out[B_OUT : B_OUT + 1, :] += column_sum(back_low.astype(f32))
        return carry

    lax.fori_loop(0, rows_here, first_back, 0)

    def out_part(h):
        columns = pl.ds(pl.multiple_of(h * half, 128), half)
        total = jnp.zeros((width, half), f32)
        for r in range(rows_here):
            total = total + dot_tn(context_ref[r], g_ref[pl.ds(r * size, size), columns])
        return total

    wo_sent[...] = out_part(1 - core).astype(low)
    wo_send = remote(wo_sent, wo_got, 2 * parts)
    wo_send.start()

    def grad_context(r, carry):
        grad_out[r] = dot_nt(g_ref[rows_of(r), :], w_out[...]).astype(low)
        return carry

    lax.fori_loop(0, rows_here, grad_context, 0)
    own_part = out_part(core)
    for i in range(mine):
        up_send(i).wait_recv()

    def up_sum(n, carry):
        rows = pl.ds(pl.multiple_of(n * 128, 128), 128)
        for i in range(mine):
            upg_ref[mine + i, rows, :] = (
                upg_ref[mine + i, rows, :].astype(f32) + up_got[i, rows, :].astype(f32)
            ).astype(low)
        return carry

    lax.fori_loop(0, width // 128, up_sum, 0)
    store_up = pltpu.make_async_copy(
        upg_ref.at[pl.ds(mine, mine)], up_out, store_sem.at[rows_here + 1]
    )
    store_up.start()
    wo_send.wait_recv()
    wo_out[...] = (own_part + wo_got[...].astype(f32)).astype(low)
    if fused:
        for item in down_moves:
            item.wait_recv()

        def near_sum(n, carry):
            down_y[n] = (
                downg_ref[2 * n + y, core, 0:piece, :].astype(f32) + down_y[n].astype(f32)
            ).astype(low)
            return carry

        def far_sum(n, carry):
            down_x[n] = (
                downg_ref[n, core, kept, :].astype(f32) + down_x[n].astype(f32)
            ).astype(low)
            return carry

        lax.fori_loop(0, 4, near_sum, 0)
        lax.fori_loop(0, 8, far_sum, 0)
        stores = [
            pltpu.make_async_copy(down_y, down_out, store_sem.at[rows_here]),
            pltpu.make_async_copy(down_x, far_out, store_sem.at[rows_here + 2]),
        ]
    else:
        stores = [
            pltpu.make_async_copy(downg_ref.at[:, core], down_out, store_sem.at[rows_here])
        ]
    for item in stores:
        item.start()
    for i in range(parts):
        down_send(i).wait_send()
    for i in range(mine):
        up_send(i).wait_send()
    wo_send.wait_send()
    for item in down_moves:
        item.wait_send()
    for item in store_final + stores + [store_up]:
        item.wait()


def middle(fused, x, context, ids, vectors, text_gradient, w_out, w_up, w_down, dp_size):
    rows_here, size, width = x.shape
    ff = w_up.shape[1]
    parts = ff // width
    tokens = rows_here * size
    low = jnp.bfloat16
    f32 = jnp.float32
    shape = jax.ShapeDtypeStruct
    whole = pl.BlockSpec(memory_space=pltpu.VMEM)
    outside = pl.BlockSpec(memory_space=pl.ANY)
    chunks = max(dp_size, parts)
    chunk = ff // chunks // 2
    vec = (8 + parts + (-parts) % 8, width)
    if fused:
        down_shape, far_shape = (4, chunk // 2, width), (8, chunk // 4, width)
    else:
        down_shape, far_shape = (chunks, chunk, width), (8, 16, 128)
    return pl.pallas_call(
        functools.partial(middle_kernel, fused),
        out_shape=(
            shape((rows_here * NSEG, width), low),
            shape((rows_here * NSEG, 1), f32),
            shape(vec, f32),
            shape((rows_here, size, width), low),
            shape((rows_here, size, width), f32),
            shape((width, width // 2), low),
            shape((rows_here, size, width), low),
            shape((parts // 2, width, width), low),
            shape(down_shape, low),
            shape(far_shape, low),
        ),
        in_specs=[whole] * 12 + [outside] * 2,
        out_specs=(whole,) * 6 + (outside,) * 4,
        scratch_shapes=[
            pltpu.VMEM(vec, f32),
            pltpu.VMEM((parts, width, width), low),
            pltpu.VMEM((parts, width, width), low),
            pltpu.VMEM((tokens, width), f32),
            pltpu.VMEM((tokens, 1), f32),
            pltpu.VMEM((tokens, width), low),
            pltpu.VMEM((width, tokens), low),
            pltpu.VMEM((parts, tokens, width), low),
            pltpu.VMEM((parts, tokens, width), low),
            pltpu.VMEM((tokens, width), f32),
            pltpu.VMEM((tokens, width), f32),
            pltpu.VMEM((tokens, width), f32),
            pltpu.VMEM((tokens, width), low),
            pltpu.VMEM((rows_here, size, width), low),
            pltpu.VMEM((parts, width, width), low),
            pltpu.VMEM((parts // 2, width, width), low),
            pltpu.VMEM((chunks, 2, chunk, width), low),
            pltpu.VMEM((chunks, chunk, width), low),
            pltpu.VMEM((width, width // 2), low),
            pltpu.VMEM((width, width // 2), low),
            pltpu.VMEM(down_shape if fused else (16, 128), low),
            pltpu.VMEM(far_shape, low),
            pltpu.SemaphoreType.DMA((2 * parts + 13,)),
            pltpu.SemaphoreType.DMA((2 * parts + 13,)),
            pltpu.SemaphoreType.DMA((2, parts)),
            pltpu.SemaphoreType.DMA((rows_here + 3,)),
        ],
        compiler_params=pltpu.CompilerParams(
            vmem_limit_bytes=63 * 2**20, collective_id=2, has_side_effects=True
        ),
        cost_estimate=pl.CostEstimate(
            flops=2 * tokens * width * (6 * ff + 3 * width),
            bytes_accessed=2 * (5 * ff * width + 8 * tokens * width),
            transcendentals=2 * tokens * ff,
        ),
    )(x, context, ids, *vectors, text_gradient, w_out, w_up, w_down)


class Links:
    def __init__(self, send_sem, recv_sem):
        self.send_sem, self.recv_sem = send_sem, recv_sem
        self.slots, self.copies = {}, {}

    def start(self, name, source, target, device):
        slot = self.slots.setdefault(name, len(self.slots))
        copy = pltpu.make_async_remote_copy(
            src_ref=source, dst_ref=target, send_sem=self.send_sem.at[slot],
            recv_sem=self.recv_sem.at[slot], device_id=device, device_id_type=MESH,
        )
        copy.start()
        self.copies[name] = copy

    def arrived(self, *names):
        for name in names:
            self.copies[name].wait_recv()

    def finish(self):
        for copy in self.copies.values():
            copy.wait_send()


def add_into(target, others, count):
    def one(i, carry):
        total = target[i].astype(jnp.float32)
        for other in others:
            total = total + other[i].astype(jnp.float32)
        target[i] = total.astype(target.dtype)
        return carry

    lax.fori_loop(0, count, one, 0)


def add_up(parts):
    total = parts[0].astype(jnp.float32)
    for part in parts[1:]:
        total = total + part.astype(jnp.float32)
    return total


POOL, UP, DOWN_A, DOWN_B, DOWN, OUT, GROUP, DX, VECTOR = range(9)
STEP, NEAR, FAR, SIDE, LINE, GATHER = range(6)

GROUPS = ((0, 4 * PAIR), (4 * PAIR, PAIR), (5 * PAIR, PAIR))


def attend_back_kernel(
    fused, count_out, out_tree, tree,
    x_ref, ids_ref, lse_ref, w_query, w_key, w_value, pool_ref, count_ref, vector_ref,
    x_hbm, q_hbm, k_hbm, v_hbm, context_hbm, grad_hbm, mixed_hbm, up_hbm, down_hbm, far_hbm, out_hbm,
    dx_out, pool_out, vector_out, *rest,
):
    outs = types.SimpleNamespace(**jax.tree.unflatten(out_tree, rest[:count_out]))
    ref = types.SimpleNamespace(**jax.tree.unflatten(tree, rest[count_out:]))
    square_out, up_out, down_out, wo_out = outs.square, outs.up, outs.down, outs.wo
    q_ref, k_ref, v_ref, context_ref, grad_ref = ref.q, ref.k, ref.v, ref.context, ref.grad
    dq_ref, dk_ref, dv_ref, x_t, x_got = ref.dq, ref.dk, ref.dv, ref.x_t, ref.x_got
    extra_ref, penal_ref, delta_ref = ref.extra, ref.penal, ref.delta
    dx_acc, dx_sent, dx_far, dx_got, dx_far_got = (
        ref.dx_acc, ref.dx_sent, ref.dx_far, ref.dx_got, ref.dx_far_got
    )
    pool_parts, pool_got, vec_parts, vec_got = (
        ref.pool_parts, ref.pool_got, ref.vec_parts, ref.vec_got
    )
    row_sem, local_sem = ref.row_sem, ref.local_sem
    rows_here, size, width = x_ref.shape
    low = jnp.bfloat16
    me, place = lax.axis_index("ctx"), lax.axis_index("dp")
    core, side = me % 2, me // 2
    near, across = me + 1 - 2 * core, (me + 2) % 4
    near_dev, across_dev = {"ctx": near}, {"ctx": across}
    y, z = place % 2, place // 2
    y_dev = {"dp": place + 1 - 2 * y}
    z_at = (z + 1 - 2 * (z % 2), (z + 2) % 4, 3 - z)
    z_dev = [{"dp": other * 2 + y} for other in z_at]
    peers = [near_dev, across_dev] + ([y_dev] + z_dev if fused else [])

    barrier = pltpu.get_barrier_semaphore()
    for peer in peers:
        pl.semaphore_signal(barrier, inc=1, device_id=peer, device_id_type=MESH)
    pl.semaphore_wait(barrier, len(peers))
    links = Links(ref.send_sem, ref.recv_sem)

    first_cut = GROUPS[1][0]
    blocks = [(0, first_cut, r) for r in range(rows_here)]
    blocks += [(first_cut, width - first_cut, r) for r in range(rows_here)]

    def load_block(step):
        slot = step % 2
        start, count, r = blocks[step]
        columns, local = pl.ds(start, count), pl.ds(0, count)
        pairs = (
            (k_hbm, k_ref), (v_hbm, v_ref), (q_hbm, q_ref), (context_hbm, context_ref),
            (grad_hbm, grad_ref),
        )
        copies = [
            pltpu.make_async_copy(
                source.at[r, :, columns], target.at[slot, :, local], row_sem.at[slot, i]
            )
            for i, (source, target) in enumerate(pairs)
        ]
        if step < rows_here:
            copies.append(pltpu.make_async_copy(x_hbm.at[:, r], x_got.at[slot], row_sem.at[slot, 5]))
        return copies

    for item in load_block(0):
        item.start()
    load_mixed = pltpu.make_async_copy(mixed_hbm, dx_acc, local_sem.at[0])
    links.start((POOL, STEP, 0), pool_ref, pool_got.at[0], near_dev)
    if fused:
        u_ref, u_x, u_y, u_z = ref.u, ref.u_x, ref.u_y, ref.u_z
        a_ref, a_z, a_s, a_x = ref.a, ref.a_z, ref.a_s, ref.a_x
        b_ref, b_y, b_z = ref.b, ref.b_y, ref.b_z
        o_ref, o_y, o_z, o_s, o_x = ref.o, ref.o_y, ref.o_z, ref.o_s, ref.o_x
        half_rows = u_ref.shape[2] // 2
        links.start((UP, FAR, 0), up_hbm.at[1 - side, :, :, pl.ds(0, half_rows)], u_x.at[0], across_dev)
        links.start((DOWN_B, SIDE), far_hbm.at[:, 1 - y], b_y, y_dev)
        for o in range(3):
            links.start((DOWN_A, LINE, o), down_hbm.at[z_at[o]], a_z.at[o], z_dev[o])
        load_parts = [
            pltpu.make_async_copy(far_hbm.at[:, y], b_ref, local_sem.at[1]),
            pltpu.make_async_copy(down_hbm.at[z], a_ref, local_sem.at[2]),
            pltpu.make_async_copy(up_hbm.at[side], u_ref, local_sem.at[3]),
            pltpu.make_async_copy(out_hbm.at[:, y], o_ref, local_sem.at[4]),
        ]
        for item in load_parts:
            item.start()
    load_mixed.start()
    vec_parts[0] = vector_ref[...]

    def pool_one():
        links.arrived((POOL, STEP, 0))
        pool_parts[...] = add_up([pool_ref[...], pool_got[0]]).astype(low)
        links.start((POOL, STEP, 1), pool_parts, pool_got.at[1], across_dev)

    def pool_two():
        links.arrived((POOL, STEP, 1))
        pool_out[...] = add_up([pool_parts[...], pool_got[1]]) / count_ref[...]

    def send_z(name, source, target):
        for o in range(3):
            links.start(name + (o,), source(z_at[o]), target(o), z_dev[o])

    def arrived_z(name):
        links.arrived(*(name + (o,) for o in range(3)))

    def out_y():
        links.start((OUT, SIDE), out_hbm.at[:, 1 - y], o_y, y_dev)

    def out_z():
        load_parts[3].wait()
        links.arrived((OUT, SIDE))
        add_into(o_ref, [o_y], 4)
        send_z((OUT, LINE), lambda i: o_ref.at[i], lambda o: o_z.at[o])

    def out_far():
        arrived_z((OUT, LINE))
        o_s[...] = add_up([o_ref[z]] + [o_z[o] for o in range(3)]).astype(low)
        links.start((OUT, FAR), o_s, o_x, across_dev)

    def out_end():
        links.arrived((OUT, FAR))
        wo_out[core] = add_up([o_s[...], o_x[...]]).astype(low)
        links.start((OUT, GATHER), wo_out.at[core], wo_out.at[core], near_dev)

    def down_z():
        load_parts[0].wait()
        links.arrived((DOWN_B, SIDE))
        add_into(b_ref, [b_y], 4)
        send_z((DOWN_B, LINE), lambda i: b_ref.at[i], lambda o: b_z.at[o])

    def down_near_far():
        load_parts[1].wait()
        arrived_z((DOWN_A, LINE))
        a_s[...] = add_up([a_ref[...]] + [a_z[o] for o in range(3)]).astype(low)
        links.start((DOWN_A, FAR), a_s, a_x, across_dev)

    def down_far():
        arrived_z((DOWN_B, LINE))
        count = b_ref.shape[1]
        own = pl.ds(pl.multiple_of(2 * count + side * count, 16), count)
        down_out[core, own] = add_up([b_ref[z]] + [b_z[o] for o in range(3)]).astype(low)
        links.start((DOWN_B, FAR), down_out.at[core, own], down_out.at[core, own], across_dev)

    def down_end():
        links.arrived((DOWN_A, FAR), (DOWN_B, FAR))
        down_out[core, 0 : a_s.shape[0]] = add_up([a_s[...], a_x[...]]).astype(low)
        links.start((DOWN, GATHER), down_out.at[core], down_out.at[core], near_dev)

    def up_x():
        rows = pl.ds(half_rows, half_rows)
        links.start((UP, FAR, 1), up_hbm.at[1 - side, :, :, rows], u_x.at[1], across_dev)

    def up_y(h):
        if h == 0:
            load_parts[2].wait()
        rows = pl.ds(h * half_rows, half_rows)
        links.arrived((UP, FAR, h))
        for i in range(4):
            add_into(u_ref.at[i, :, rows], [u_x.at[h, i]], 2)
        links.start((UP, SIDE, h), u_ref.at[:, 1 - y, rows], u_y.at[h], y_dev)

    def up_z(h):
        rows = pl.ds(h * half_rows, half_rows)
        links.arrived((UP, SIDE, h))
        for i in range(4):
            u_ref[i, y, rows] = add_up([u_ref[i, y, rows], u_y[h, i]]).astype(low)
        send_z((UP, LINE, h), lambda i: u_ref.at[i, y, rows], lambda o: u_z.at[o, rows])

    def up_far():
        arrived_z((UP, LINE, 0))
        arrived_z((UP, LINE, 1))
        up_out[me] = add_up([u_ref[z, y]] + [u_z[o] for o in range(3)]).astype(low)
        links.start((UP, GATHER), up_out.at[me], up_out.at[me], across_dev)

    def up_end():
        links.arrived((UP, GATHER))
        links.start((UP, NEAR, 0), up_out.at[me], up_out.at[me], near_dev)
        links.start((UP, NEAR, 1), up_out.at[across], up_out.at[across], near_dev)

    def group_core(g):
        links.start((GROUP, NEAR, g), ref.g[g].at[1 - core], ref.g_got[g], near_dev)

    def group_y(g):
        links.arrived((GROUP, NEAR, g))
        for i in range(4):
            add_into(ref.g[g].at[core, i], [ref.g_got[g].at[i]], 2)
        links.start((GROUP, SIDE, g), ref.g[g].at[core, :, 1 - y], ref.g_y[g], y_dev)

    def group_z(g):
        links.arrived((GROUP, SIDE, g))
        own = ref.g[g]
        for i in range(4):
            own[core, i, y] = add_up([own[core, i, y], ref.g_y[g][i]]).astype(low)
        send_z((GROUP, LINE, g), lambda i: own.at[core, i, y], lambda o: ref.g_z[g].at[o])

    def group_far(g):
        arrived_z((GROUP, LINE, g))
        pieces = [ref.g[g][core, z, y]] + [ref.g_z[g][o] for o in range(3)]
        ref.g_s[g][...] = add_up(pieces).astype(low)
        links.start((GROUP, FAR, g), ref.g_s[g], ref.g_x[g], across_dev)

    def group_end(g):
        links.arrived((GROUP, FAR, g))
        out = outs.squares[g]
        out[core] = add_up([ref.g_s[g][...], ref.g_x[g][...]]).astype(low)
        links.start((GROUP, GATHER, g), out.at[core], out.at[core], near_dev)

    def vector_step(i, device):
        if i:
            links.arrived((VECTOR, STEP, i - 1))
            vec_parts[i] = vec_parts[i - 1] + vec_got[i - 1]
        if device is not None:
            links.start((VECTOR, STEP, i), vec_parts.at[i], vec_got.at[i], device)

    def vector_z():
        vector_step(3, None)
        for o in range(3):
            links.start((VECTOR, LINE, o), vec_parts.at[3], vec_got.at[3 + o], z_dev[o])

    def vector_end():
        arrived_z((VECTOR, LINE))
        vector_out[...] = vec_parts[3] + (vec_got[3] + (vec_got[4] + vec_got[5]))

    row = lax.broadcasted_iota(jnp.int32, (PAIR, size), 0)

    def find_delta(step):
        slot = step % 2
        start, count, _ = blocks[step]
        lane = lax.broadcasted_iota(jnp.int32, (count, PAIR), 1)
        head = (start + lax.broadcasted_iota(jnp.int32, (count, PAIR), 0)) // HEAD_DIM
        member = jnp.where((lane % NSEG == head) & (lane >= NSEG) & (lane < 4 * NSEG), 1.0, 0.0)
        member = member.astype(low)
        local = pl.ds(0, count)
        product = grad_ref[slot, :, local].astype(jnp.float32) * context_ref[
            slot, :, local
        ].astype(jnp.float32)
        total = jnp.zeros((size, PAIR), jnp.float32)
        for _ in range(3):
            term = product.astype(low)
            total = total + matmul(term, member)
            product = product - term.astype(jnp.float32)
        delta_ref[...] = with_constants(jnp.zeros_like(total), -total)

    def attend_pairs(step, first, last):
        slot = step % 2
        start, _, r = blocks[step]

        def one_pair(n, carry):
            local = pl.ds(pl.multiple_of(n * PAIR, PAIR), PAIR)
            columns = pl.ds(pl.multiple_of(start + n * PAIR, PAIR), PAIR)
            head = 2 * (start // PAIR + n)
            q_both = split_heads(q_ref[slot, :, local])
            g_both = split_heads(grad_ref[slot, :, local])
            q_extra = [of_head(penal_ref[r], head + h) for h in range(2)]
            g_extra = [of_head(delta_ref[...], head + h) for h in range(2)]
            q_wide = jnp.concatenate([q_both, jnp.concatenate(q_extra, axis=0)], axis=1)
            g_wide = jnp.concatenate([g_both, jnp.concatenate(g_extra, axis=0)], axis=1)
            dq = jnp.zeros((PAIR, 2 * size), jnp.float32)
            for j in range(4):
                rows = pl.ds(j * size, size)
                keys = k_ref[slot, rows, local]
                extra = extra_ref[r, rows, :]
                probs = jnp.exp(dot_nt(jnp.concatenate([keys, extra], axis=1), q_wide))
                values = jnp.concatenate([v_ref[slot, rows, local], extra], axis=1)
                grad_s = (probs * dot_nt(values, g_wide)).astype(low)
                dv_ref[r, rows, columns] = matmul(probs.astype(low), g_both).astype(low)
                dk_ref[r, rows, columns] = matmul(grad_s, q_both).astype(low)
                dq = dq + matmul(keys.T, grad_s)
            dq = jnp.where(row < HEAD_DIM, dq[:, :size], dq[:, size:]) * HEAD_DIM ** (-0.5)
            dq_ref[r, :, columns] = dq.T.astype(low)
            return carry

        lax.fori_loop(first, last, one_pair, 0)

    def weight_group(g):
        start, count = GROUPS[g]
        if fused:
            depth = ref.g[g].shape[3]

        def keep(n, i, total):
            total = total.astype(low)
            wide = total.shape[1]
            if not fused:
                square_out[n, :, pl.ds(pl.multiple_of(start + i * PAIR, PAIR), wide)] = total
                return
            total = total.reshape(4, 2, 2, depth, wide)
            target = pl.ds(pl.multiple_of(n * count + i * PAIR, PAIR), wide)
            for h in range(2):
                ref.g[g][h, :, :, :, target] = total[:, :, h]

        def of_source(source, columns):
            keys = source.shape[1]
            return sum(
                matmul(x_t[r, :, :keys], source[r, :, columns]) for r in range(rows_here)
            )

        def one_part(i, carry):
            columns = pl.ds(pl.multiple_of(start + 2 * i * PAIR, PAIR), 2 * PAIR)
            for n, source in enumerate((dq_ref, dk_ref, dv_ref)):
                keep(n, 2 * i, of_source(source, columns))
            return carry

        if count % (2 * PAIR):
            columns = pl.ds(start, count)
            keep(0, 0, of_source(dq_ref, columns))
            both = sum(
                matmul(
                    x_t[r],
                    jnp.concatenate([dk_ref[r, :, columns], dv_ref[r, :, columns]], axis=1),
                )
                for r in range(rows_here)
            )
            keep(1, 0, both[:, :count])
            keep(2, 0, both[:, count:])
        else:
            lax.fori_loop(0, count // (2 * PAIR), one_part, 0)
        columns = pl.ds(start, count)
        for n, source in enumerate((dq_ref, dv_ref)):
            vec_parts[0, n : n + 1, columns] = sum(
                jnp.sum(source[r, :, columns].astype(jnp.float32), axis=0, keepdims=True)
                for r in range(rows_here)
            )

    def input_parts(r):
        for j in (3, 2, 1, 0):
            rows = pl.ds(j * size, size)
            total = dot_nt(dk_ref[r, rows, :], w_key[...]) + dot_nt(dv_ref[r, rows, :], w_value[...])
            if j == 0:
                dx_acc[r] = dx_acc[r] + total + dot_nt(dq_ref[r], w_query[...])
            elif j == 2:
                dx_far[r] = total.astype(low)
            else:
                n = j // 2
                dx_sent[r, n] = total.astype(low)
                links.start((DX, NEAR, r, n), dx_sent.at[r, n], dx_got.at[r, n], near_dev)

    def input_far(r):
        links.arrived((DX, NEAR, r, 1))
        dx_far[r] = add_up([dx_far[r], dx_got[r, 1]]).astype(low)
        links.start((DX, FAR, r), dx_far.at[r], dx_far_got.at[r], across_dev)

    def input_done(r):
        links.arrived((DX, NEAR, r, 0), (DX, FAR, r))
        dx_out[r] = add_up([dx_acc[r], dx_got[r, 0], dx_far_got[r]]).astype(low)

    def prepare_row(r):
        slot = r % 2
        for j in range(4):
            rows = slice(j * size, (j + 1) * size)
            texts = text_rows(ids_ref[j, r : r + 1, :], size)
            extra_ref[r, rows, :] = key_extra(texts)
            if j == 0:
                penal_ref[r] = with_constants(query_extra(texts), -lse_ref[r])
            block = x_ref[r] if j == 0 else x_got[slot, j - 1]
            x_t[r, :, rows] = block.T

    def begin(step):
        for item in load_block(step):
            item.wait()
        if step + 1 < len(blocks):
            for item in load_block(step + 1):
                item.start()
        find_delta(step)

    def do(*actions):
        if fused:
            for action, *given in actions:
                action(*given)

    most = first_cut // PAIR
    begin(0)
    prepare_row(0)
    attend_pairs(0, 0, most // 2)
    do((pool_one,))
    attend_pairs(0, most // 2, most)
    do((down_z,), (out_y,))
    begin(1)
    prepare_row(1)
    attend_pairs(1, 0, most // 2)
    do((up_x,), (pool_two,))
    attend_pairs(1, most // 2, most)
    do((up_y, 0), (down_near_far,))
    begin(2)
    prepare_row(2)
    attend_pairs(2, 0, most // 2)
    do((out_z,))
    attend_pairs(2, most // 2, most)
    do((up_z, 0), (down_far,))
    weight_group(0)
    do((group_core, 0), (up_y, 1))
    begin(3)
    attend_pairs(3, 0, 2)
    do((group_y, 0), (down_end,), (out_far,))
    load_mixed.wait()
    input_parts(0)
    do((up_z, 1))
    begin(4)
    attend_pairs(4, 0, 2)
    do((input_far, 0), (out_end,))
    input_parts(1)
    do((group_z, 0))
    begin(5)
    attend_pairs(5, 0, 1)
    do((input_far, 1))
    weight_group(1)
    do((group_core, 1))
    attend_pairs(5, 1, 2)
    do((group_y, 1), (up_far,))
    weight_group(2)
    do((group_core, 2), (vector_step, 0, near_dev))
    input_parts(2)
    if not fused:
        vector_out[...] = vec_parts[0]
        pool_one()
        for r in range(3):
            input_far(r)
        pool_two()
        for r in range(3):
            input_done(r)
        links.finish()
        return
    do((group_y, 2), (group_z, 1), (vector_step, 1, across_dev))
    do((input_far, 2), (group_far, 0), (group_z, 2), (input_done, 0))
    do((vector_step, 2, y_dev), (up_end,), (input_done, 1), (group_far, 1), (vector_z,))
    do((group_end, 0), (group_far, 2), (group_end, 1), (vector_end,))
    do((group_end, 2), (input_done, 2))
    links.arrived((DOWN, GATHER), (OUT, GATHER), (UP, NEAR, 0), (UP, NEAR, 1))
    links.arrived((GROUP, GATHER, 0), (GROUP, GATHER, 1), (GROUP, GATHER, 2))
    links.finish()


def attend_back(
    fused, x, ids, lse, w_query, w_key, w_value, pool, counts, vectors,
    x_got, q, k, v, context, grad, mixed, up, down, far, out,
):
    rows_here, size, width = x.shape
    keys = size * 4
    low = jnp.bfloat16
    f32 = jnp.float32
    whole = pl.BlockSpec(memory_space=pltpu.VMEM)
    outside = pl.BlockSpec(memory_space=pl.ANY)
    shape = jax.ShapeDtypeStruct
    most = GROUPS[0][1]
    vec = vectors.shape
    small = shape((8, 128), low)
    if fused:
        depth = up.shape[3]
        outs = dict(
            squares=[shape((2, depth // 2, 3 * count), low) for _, count in GROUPS],
            up=shape((4, depth, width), low),
            down=shape((2, 2 * down.shape[1], width), low),
            wo=shape((2, depth, width // 2), low),
            square=small,
        )
    else:
        outs = dict(
            squares=[], up=small, down=small, wo=small, square=shape((3, width, width), low)
        )
    scratch = dict(
        x_got=pltpu.VMEM((2, 3, size, width), low),
        x_t=pltpu.VMEM((rows_here, width, keys), low),
        q=pltpu.VMEM((2, size, most), low),
        k=pltpu.VMEM((2, keys, most), low),
        v=pltpu.VMEM((2, keys, most), low),
        context=pltpu.VMEM((2, size, most), low),
        grad=pltpu.VMEM((2, size, most), low),
        extra=pltpu.VMEM((rows_here, keys, PAIR), low),
        penal=pltpu.VMEM((rows_here, size, PAIR), low),
        delta=pltpu.VMEM((size, PAIR), low),
        dq=pltpu.VMEM((rows_here, size, width), low),
        dk=pltpu.VMEM((rows_here, keys, width), low),
        dv=pltpu.VMEM((rows_here, keys, width), low),
        dx_acc=pltpu.VMEM((rows_here, size, width), f32),
        dx_sent=pltpu.VMEM((rows_here, 2, size, width), low),
        dx_far=pltpu.VMEM((rows_here, size, width), low),
        dx_got=pltpu.VMEM((rows_here, 2, size, width), low),
        dx_far_got=pltpu.VMEM((rows_here, size, width), low),
        pool_parts=pltpu.VMEM(pool.shape, low),
        pool_got=pltpu.VMEM((2,) + pool.shape, low),
        vec_parts=pltpu.VMEM((4,) + vec, f32),
        vec_got=pltpu.VMEM((6,) + vec, f32),
        send_sem=pltpu.SemaphoreType.DMA((72,)),
        recv_sem=pltpu.SemaphoreType.DMA((72,)),
        row_sem=pltpu.SemaphoreType.DMA((2, 6)),
        local_sem=pltpu.SemaphoreType.DMA((5,)),
    )
    if fused:
        tails = [(depth // 2, 3 * count) for _, count in GROUPS]
        spread = lambda *lead: [pltpu.VMEM(lead + tail, low) for tail in tails]
        b_rows = far.shape[2]
        narrow = (depth, width // 2)
        scratch.update(
            g=spread(2, 4, 2), g_got=spread(4, 2), g_y=spread(4), g_z=spread(3),
            g_s=spread(), g_x=spread(),
            u=pltpu.VMEM((4, 2, depth, width), low),
            u_x=pltpu.VMEM((2, 4, 2, depth // 2, width), low),
            u_y=pltpu.VMEM((2, 4, depth // 2, width), low),
            u_z=pltpu.VMEM((3, depth, width), low),
            a=pltpu.VMEM(down.shape[1:], low),
            a_z=pltpu.VMEM((3,) + down.shape[1:], low),
            a_s=pltpu.VMEM(down.shape[1:], low),
            a_x=pltpu.VMEM(down.shape[1:], low),
            b=pltpu.VMEM((4, b_rows, width), low),
            b_y=pltpu.VMEM((4, b_rows, width), low),
            b_z=pltpu.VMEM((3, b_rows, width), low),
            o=pltpu.VMEM((4,) + narrow, low),
            o_y=pltpu.VMEM((4,) + narrow, low),
            o_z=pltpu.VMEM((3,) + narrow, low),
            o_s=pltpu.VMEM(narrow, low),
            o_x=pltpu.VMEM(narrow, low),
        )
    out_leaves, out_tree = jax.tree.flatten(outs)
    leaves, tree = jax.tree.flatten(scratch)
    count_out = len(out_leaves)
    got = pl.pallas_call(
        functools.partial(attend_back_kernel, fused, count_out, out_tree, tree),
        out_shape=(
            shape((rows_here, size, width), low),
            shape(pool.shape, f32),
            shape(vec, f32),
        )
        + tuple(out_leaves),
        in_specs=[whole] * 9 + [outside] * 11,
        out_specs=(whole,) * (3 + count_out),
        scratch_shapes=leaves,
        compiler_params=pltpu.CompilerParams(
            vmem_limit_bytes=63 * 2**20, collective_id=1, has_side_effects=True
        ),
        cost_estimate=pl.CostEstimate(
            flops=rows_here
            * (4 * (size + 2 * keys) * width * width + 40 * size * keys * width),
            bytes_accessed=2 * (16 * width * width + 9 * keys * width),
            transcendentals=rows_here * HEADS * size * keys,
        ),
    )(
        x, ids, lse, w_query, w_key, w_value, pool, counts, vectors,
        x_got, q, k, v, context, grad, mixed, up, down, far, out,
    )
    return got[:3] + (types.SimpleNamespace(**jax.tree.unflatten(out_tree, got[3:])),)


def outputs_kernel(
    square0, square1, square2, wo, up, down, pool, final_hbm, dx_hbm,
    wq_out, wk_out, wv_out, wo_out, up_out, down_out, pool_out, final_out, dx_out, sem,
):
    copies = [
        pltpu.make_async_copy(final_hbm, final_out, sem.at[0]),
        pltpu.make_async_copy(dx_hbm, dx_out, sem.at[1]),
    ]
    for item in copies:
        item.start()
    f32 = jnp.float32
    pool_out[...] = pool[...].reshape(pool_out.shape)
    for (start, count), square in zip(GROUPS, (square0, square1, square2)):
        rows = square.shape[1]
        for n, out in enumerate((wq_out, wk_out, wv_out)):
            for h in range(2):
                out[h * rows : (h + 1) * rows, start : start + count] = square[
                    h, :, n * count : (n + 1) * count
                ].astype(f32)
    for h in range(2):
        half = wo.shape[2]
        wo_out[:, h * half : (h + 1) * half] = wo[h].astype(f32)
        rows = down.shape[1]
        down_out[h * rows : (h + 1) * rows, :] = down[h].astype(f32)
    for i in range(4):
        place, width = (i % 2) * 2 + i // 2, up.shape[2]
        up_out[:, place * width : (place + 1) * width] = up[i].astype(f32)
    for item in copies:
        item.wait()


def outputs(squares, wo, up, down, pool, final, dx):
    f32 = jnp.float32
    whole = pl.BlockSpec(memory_space=pltpu.VMEM)
    outside = pl.BlockSpec(memory_space=pl.ANY)
    shape = jax.ShapeDtypeStruct
    rows, width = up.shape[1:]
    row_count = final.shape[0]
    return pl.pallas_call(
        outputs_kernel,
        out_shape=(
            shape((rows, width), f32), shape((rows, width), f32), shape((rows, width), f32),
            shape((rows, width), f32), shape((rows, 4 * width), f32),
            shape((2 * down.shape[1], width), f32),
            shape((row_count, pool.shape[0] // row_count, width), f32),
            shape(final.shape, final.dtype), shape(dx.shape, dx.dtype),
        ),
        in_specs=[whole] * 7 + [outside] * 2,
        out_specs=(whole,) * 7 + (outside,) * 2,
        scratch_shapes=[pltpu.SemaphoreType.DMA((2,))],
        compiler_params=pltpu.CompilerParams(vmem_limit_bytes=63 * 2**20),
    )(*squares, wo, up, down, pool, final, dx)


def radices_of(count):
    if count == 8:
        return ((1, 2), (2, 4))
    digits = []
    stride = 1
    while stride < count:
        digits.append((stride, 2))
        stride *= 2
    return tuple(digits)


def exchange(piece, axis_name, stride, offset):
    count = lax.axis_size(axis_name)
    pairs = [(i, i ^ (offset * stride)) for i in range(count)]
    return lax.ppermute(piece, axis_name, pairs)


def digit_of(axis_name, stride, radix):
    return (lax.axis_index(axis_name) // stride) % radix


def scatter_digit(pieces, place, axis_name, stride, radix):
    here = digit_of(axis_name, stride, radix)
    received = [
        exchange(
            lax.dynamic_index_in_dim(pieces, here ^ offset, place, keepdims=False).astype(
                jnp.bfloat16
            ),
            axis_name, stride, offset,
        )
        for offset in range(1, radix)
    ]
    total = lax.dynamic_index_in_dim(pieces, here, place, keepdims=False).astype(jnp.float32)
    for item in received:
        total = total + item.astype(jnp.float32)
    return total.astype(jnp.bfloat16)


def halve(piece, place, axis_name, stride):
    half = piece.shape[place] // 2
    here = digit_of(axis_name, stride, 2)
    sent = lax.dynamic_slice_in_dim(piece, (1 - here) * half, half, place).astype(jnp.bfloat16)
    kept = lax.dynamic_slice_in_dim(piece, here * half, half, place).astype(jnp.float32)
    return (kept + exchange(sent, axis_name, stride, 1).astype(jnp.float32)).astype(jnp.bfloat16)


def join(piece, place, axis_name, stride):
    here = digit_of(axis_name, stride, 2)
    other = exchange(piece, axis_name, stride, 1)
    first = jnp.where(here == 0, piece, other)
    second = jnp.where(here == 0, other, piece)
    return jnp.concatenate([first, second], axis=place)


def scatter_rows(group, dp_size):
    digits = radices_of(dp_size)
    shape = tuple(r for _, r in reversed(digits))
    group = group.reshape(shape + (group.shape[0] // dp_size, group.shape[1]))
    for place, (stride, radix) in zip(range(len(digits) - 1, -1, -1), digits):
        group = scatter_digit(group, place, "dp", stride, radix)
    return group


def finish_weight(flat, dp_size, side):
    flat = scatter_rows(flat, dp_size)
    flat = flat.astype(jnp.float32) + exchange(flat, "ctx", 2, 1).astype(jnp.float32)
    return join(flat.astype(jnp.bfloat16), side, "ctx", 1).astype(jnp.float32)


def reduce_weight(gradient, dp_size, side):
    return finish_weight(halve(gradient, side, "ctx", 1), dp_size, side)


def per_device(
    hidden_in,
    seg_ids,
    valid,
    w_query,
    b_query,
    w_key,
    w_value,
    b_value,
    w_out,
    b_out,
    gain_attn,
    shift_attn,
    w_up,
    b_up,
    w_down,
    b_down,
    gain_ffn,
    shift_ffn,
    pooled_text_gradient,
):
    row_count, group_size, model_width = hidden_in.shape
    dp_size = lax.axis_size("dp")
    ff_width = w_up.shape[1]
    rows_here, ff_here = model_width // dp_size, ff_width // dp_size
    fused = dp_size == 8 and rows_here % 32 == 0 and ff_here % 128 == 0
    q_all, context, lse_all, ids_got, x_got, k_all, v_all = attend(
        hidden_in, seg_ids, valid, b_query, b_value, w_query, w_key, w_value
    )
    vectors = (b_out, gain_attn, shift_attn, b_up, b_down, gain_ffn, shift_ffn)
    pool, counts, vector_parts, grad_context, grad_mixed, out, final_out, up, down, far = middle(
        fused, hidden_in, context, ids_got, vectors, pooled_text_gradient, w_out, w_up, w_down,
        dp_size,
    )
    if fused:
        up_part = up.reshape(2, 4, 2, rows_here, -1)
        far_part = far.reshape((4, 2) + far.shape[1:])
        out_part = out.reshape(4, 2, rows_here, -1)
    else:
        up_part = far_part = out_part = jnp.zeros((16, 128), jnp.bfloat16)
    grad_input, pooled, vector_sum, sums_of = attend_back(
        fused, hidden_in, ids_got, lse_all, w_query, w_key, w_value,
        pool, counts, vector_parts, x_got, q_all, k_all, v_all, context, grad_context, grad_mixed,
        up_part, down, far_part, out_part,
    )
    if fused:
        *square_sums, up_sum, down_sum, pooled, final_out, grad_input = outputs(
            sums_of.squares, sums_of.wo, sums_of.up, sums_of.down, pooled, final_out, grad_input
        )
    else:
        squares = sums_of.square
        square_sums = [reduce_weight(squares[n], dp_size, 1) for n in range(3)]
        square_sums.append(finish_weight(out, dp_size, 1))
        up_sum = finish_weight(up.transpose(1, 0, 2).reshape(model_width, -1), dp_size, 1)
        down_sum = finish_weight(down.reshape(-1, model_width), dp_size, 0)
        vector_sum = lax.psum(vector_sum, ("dp", "ctx"))
        pooled = pooled.reshape(row_count, NSEG, model_width)
    place = lax.axis_index("dp")
    sums = lax.dynamic_slice_in_dim(vector_sum[:8], place * rows_here, rows_here, 1)
    sum_bu = lax.dynamic_slice_in_dim(
        vector_sum[8 : 8 + ff_width // model_width].reshape(-1), place * ff_here, ff_here
    )
    results = (
        square_sums[0], sums[0], square_sums[1], square_sums[2], sums[1], square_sums[3],
        sums[2], sums[3], sums[4], up_sum, sum_bu, down_sum, sums[5], sums[6], sums[7],
    )
    return (
        final_out,
        pooled,
        grad_input,
    ) + tuple(results)


def solution(mesh):
    placed = (
        P("dp", "ctx", None),
        P("dp", "ctx"),
        P("dp", "ctx"),
        P(),
        P(),
        P(),
        P(),
        P(),
        P(),
        P(),
        P(),
        P(),
        P(),
        P(),
        P(),
        P(),
        P(),
        P(),
        P("dp", None, None),
    )
    return jax.shard_map(
        per_device,
        mesh=mesh,
        in_specs=placed,
        out_specs=(
            P("dp", "ctx", None),
            P("dp", None, None),
            P("dp", "ctx", None),
            P("dp", None),
            P("dp"),
            P("dp", None),
            P("dp", None),
            P("dp"),
            P("dp", None),
            P("dp"),
            P("dp"),
            P("dp"),
            P("dp", None),
            P("dp"),
            P("dp", None),
            P("dp"),
            P("dp"),
            P("dp"),
        ),
        check_vma=False,
    )
```

```python
import functools
import types

import jax
import jax.numpy as jnp
from jax import lax
from jax.experimental import pallas as pl
from jax.experimental.pallas import tpu as pltpu
from jax.sharding import PartitionSpec as P

HEADS = 12
HEAD_DIM = 64
NSEG = 16


eps = 1e-12


def matmul(left_side, right_side):
    return jnp.dot(left_side, right_side, preferred_element_type=jnp.float32)


PAIR = 2 * HEAD_DIM
MESH = pl.DeviceIdType.MESH
MASKED = -1e30


def dot_nt(left_side, right_side):
    return lax.dot_general(
        left_side, right_side, (((1,), (1,)), ((), ())), preferred_element_type=jnp.float32
    )


def dot_tn(left_side, right_side):
    return lax.dot_general(
        left_side, right_side, (((0,), (0,)), ((), ())), preferred_element_type=jnp.float32
    )


def split_heads(pair):
    lane = lax.broadcasted_iota(jnp.int32, pair.shape, 1)
    zero = jnp.zeros_like(pair)
    return jnp.concatenate(
        [jnp.where(lane < HEAD_DIM, pair, zero), jnp.where(lane < HEAD_DIM, zero, pair)], axis=0
    )


def text_rows(ids_row, size):
    return jnp.broadcast_to(ids_row.astype(jnp.float32), (PAIR, size)).T


def lanes_of(size):
    return lax.broadcasted_iota(jnp.int32, (size, PAIR), 1)


def key_extra(texts):
    lane = lanes_of(texts.shape[0])
    hot = jnp.where(lane.astype(jnp.float32) == texts, 1.0, 0.0)
    return jnp.where((lane >= NSEG) & (lane < 4 * NSEG), 1.0, hot).astype(jnp.bfloat16)


def query_extra(texts):
    lane = lanes_of(texts.shape[0])
    other = (lane < NSEG) & (lane.astype(jnp.float32) != texts)
    return jnp.where(other, MASKED, 0.0)


def with_constants(extra, constants):
    lane = lanes_of(extra.shape[0])
    high = constants.astype(jnp.bfloat16).astype(jnp.float32)
    middle = (constants - high).astype(jnp.bfloat16).astype(jnp.float32)
    rest = constants - high - middle
    terms = jnp.where(lane < 2 * NSEG, high, jnp.where(lane < 3 * NSEG, middle, rest))
    kept = (lane >= NSEG) & (lane < 4 * NSEG)
    return jnp.where(kept, terms, extra).astype(jnp.bfloat16)


def of_head(extra, head):
    lane = lanes_of(extra.shape[0])
    kept = (lane < NSEG) | (lane % NSEG == head)
    return jnp.where(kept, extra, jnp.zeros_like(extra))


def attend_kernel(
    x_ref, seg_ref, valid_ref, b_query, b_value, w_query, w_key, w_value,
    q_out, context_out, lse_out, ids_out, x_hbm, k_hbm, v_hbm,
    x_got, k_ref, v_ref, extra_ref, ids_ref, score_one, score_two, send_sem, recv_sem, local_sem,
):
    rows_here, size, width = x_ref.shape
    me = lax.axis_index("ctx")
    one = me + 1 - 2 * (me % 2)
    two = (me + 2) % 4
    three = (one + 2) % 4
    low = jnp.bfloat16

    ids_ref[...] = jnp.zeros_like(ids_ref)
    ids_ref[0:rows_here, :] = seg_ref[...]
    ids_ref[rows_here : 2 * rows_here, :] = valid_ref[...]
    query_bias = b_query[...].astype(jnp.float32)[None]
    value_bias = b_value[...].astype(jnp.float32)[None]
    barrier = pltpu.get_barrier_semaphore()
    for peer in (one, two, three):
        pl.semaphore_signal(barrier, inc=1, device_id={"ctx": peer}, device_id_type=MESH)
    pl.semaphore_wait(barrier, 3)

    def send(source, target, slot, peer):
        return pltpu.make_async_remote_copy(
            src_ref=source, dst_ref=target, send_sem=send_sem.at[slot],
            recv_sem=recv_sem.at[slot], device_id={"ctx": peer}, device_id_type=MESH,
        )

    ids_out[0] = ids_ref[...]
    ids_sends = [send(ids_ref, ids_out.at[j + 1], j, peer) for j, peer in enumerate((one, two, three))]
    near = send(x_ref, x_got.at[0], 3, one)

    def far(r):
        return send(x_ref.at[r], x_got.at[1, r], 4 + r, two)

    def passed(r):
        return send(x_got.at[1, r], x_got.at[2, r], 4 + rows_here + r, one)

    far(0).start()
    near.start()
    for item in ids_sends:
        item.start()
    for r in range(1, rows_here):
        far(r).start()

    def project(x, r, j):
        count = x.shape[0] // size
        k = matmul(x, w_key[...]).astype(low)
        v = (matmul(x, w_value[...]) + value_bias).astype(low)
        for n in range(count):
            rows = pl.ds((j + n if r is not None else j) * size, size)
            k_ref[n if r is None else r, rows, :] = k[n * size : (n + 1) * size]
            v_ref[n if r is None else r, rows, :] = v[n * size : (n + 1) * size]

    own = x_ref[...].reshape(rows_here * size, width)
    q = (matmul(own, w_query[...]) + query_bias).astype(low)
    q_out[...] = (q * HEAD_DIM ** (-0.5)).astype(low).reshape(q_out.shape)
    project(own, None, 0)
    near.wait_recv()
    project(x_got[0].reshape(rows_here * size, width), None, 1)
    for item in ids_sends:
        item.wait_recv()
    lane = lax.broadcasted_iota(jnp.int32, (size, PAIR), 1)
    far(0).wait_recv()
    passed(0).start()

    def keep(r):
        return (
            pltpu.make_async_copy(k_ref.at[r], k_hbm.at[r], local_sem.at[0, r]),
            pltpu.make_async_copy(v_ref.at[r], v_hbm.at[r], local_sem.at[1, r]),
            pltpu.make_async_copy(x_got.at[:, r], x_hbm.at[:, r], local_sem.at[2, r]),
        )

    for r in range(rows_here):
        passed(r).wait_recv()
        project(jnp.concatenate([x_got[1, r], x_got[2, r]], axis=0), r, 2)
        for item in keep(r):
            item.start()
        for j in range(4):
            texts = text_rows(ids_out[j, r : r + 1, :], size)
            extra_ref[j * size : (j + 1) * size, :] = key_extra(texts)
            if j == 0:
                own_extra = query_extra(texts).astype(low)

        def score(pair, target, r=r, own_extra=own_extra):
            columns = pl.ds(pl.multiple_of(pair * PAIR, PAIR), PAIR)
            both = split_heads(q_out[r, :, columns])
            extras = jnp.concatenate([own_extra, own_extra], axis=0)
            keys = jnp.concatenate([k_ref[r, :, columns], extra_ref[...]], axis=1)
            target[...] = dot_nt(jnp.concatenate([both, extras], axis=1), keys)

        def one_pair(pair, source, stat, r=r):
            columns = pl.ds(pl.multiple_of(pair * PAIR, PAIR), PAIR)
            scores = source[...]
            top = jnp.max(scores, axis=-1, keepdims=True)
            weight = jnp.exp(scores - top)
            total = jnp.sum(weight, axis=-1, keepdims=True)
            mixed = matmul(weight.astype(low), v_ref[r, :, columns]) * (1.0 / total)
            context_out[r, :, columns] = jnp.where(
                lane < HEAD_DIM, mixed[:size], mixed[size:]
            ).astype(low)
            lse = top + jnp.log(total)
            for h in range(2):
                ours = lane % NSEG == 2 * pair + h
                stat = jnp.where(ours, lse[h * size : (h + 1) * size], stat)
            return stat

        def two_pairs(n, carry, r=r):
            stat = lse_out[r]
            score(2 * n + 1, score_two)
            stat = one_pair(2 * n, score_one, stat)
            score(jnp.minimum(2 * n + 2, HEADS // 2 - 1), score_one)
            lse_out[r] = one_pair(2 * n + 1, score_two, stat)
            return carry

        score(0, score_one)
        lse_out[r] = jnp.zeros((size, PAIR), jnp.float32)
        lax.fori_loop(0, HEADS // 4, two_pairs, 0)
        if r + 1 < rows_here:
            far(r + 1).wait_recv()
            passed(r + 1).start()
    for r in range(rows_here):
        for item in keep(r):
            item.wait()
        far(r).wait_send()
        passed(r).wait_send()
    near.wait_send()
    for item in ids_sends:
        item.wait_send()


def attend(x, seg_ids, valid, b_query, b_value, w_query, w_key, w_value):
    rows_here, size, width = x.shape
    keys = size * 4
    low = jnp.bfloat16
    whole = pl.BlockSpec(memory_space=pltpu.VMEM)
    outside = pl.BlockSpec(memory_space=pl.ANY)
    slots = 4 + 2 * rows_here
    return pl.pallas_call(
        attend_kernel,
        out_shape=(
            jax.ShapeDtypeStruct((rows_here, size, width), low),
            jax.ShapeDtypeStruct((rows_here, size, width), low),
            jax.ShapeDtypeStruct((rows_here, size, PAIR), jnp.float32),
            jax.ShapeDtypeStruct((4, 8, size), jnp.int32),
            jax.ShapeDtypeStruct((3,) + x.shape, low),
            jax.ShapeDtypeStruct((rows_here, keys, width), low),
            jax.ShapeDtypeStruct((rows_here, keys, width), low),
        ),
        in_specs=[whole] * 8,
        out_specs=(whole, whole, whole, whole, outside, outside, outside),
        scratch_shapes=[
            pltpu.VMEM((3,) + x.shape, low),
            pltpu.VMEM((rows_here, keys, width), low),
            pltpu.VMEM((rows_here, keys, width), low),
            pltpu.VMEM((keys, PAIR), low),
            pltpu.VMEM((8, size), jnp.int32),
            pltpu.VMEM((2 * size, keys), jnp.float32),
            pltpu.VMEM((2 * size, keys), jnp.float32),
            pltpu.SemaphoreType.DMA((slots,)),
            pltpu.SemaphoreType.DMA((slots,)),
            pltpu.SemaphoreType.DMA((3, rows_here)),
        ],
        compiler_params=pltpu.CompilerParams(
            vmem_limit_bytes=56 * 2**20, collective_id=0, has_side_effects=True
        ),
        cost_estimate=pl.CostEstimate(
            flops=rows_here * (2 * (size + 2 * keys) * width * width + 16 * size * keys * width),
            bytes_accessed=2 * (3 * width * width + 9 * keys * width),
            transcendentals=rows_here * HEADS * size * keys,
        ),
    )(x, seg_ids, valid, b_query, b_value, w_query, w_key, w_value)


def gelu_both(u):
    size = jnp.abs(u)
    t = 1.0 / (1.0 + (0.3275911 * 0.5**0.5) * size)
    bell = jnp.exp(-0.5 * u * u)
    poly = t * (
        0.127414796 + t * (-0.142248368 + t * (0.7107068705 + t * (-0.7265760135 + t * 0.5307027145)))
    )
    tail = poly * bell
    cdf = jnp.where(u >= 0.0, 1.0 - tail, tail)
    return u * cdf, cdf + u * bell * 0.3989422804014327


def normalize(values_in):
    centre = jnp.mean(values_in, axis=-1, keepdims=True)
    centred = values_in - centre
    spread = jnp.mean(centred * centred, axis=-1, keepdims=True)
    scale = lax.rsqrt(spread + eps)
    return centred * scale, scale


def normalize_back(grad, unit, scale):
    mean_one = jnp.mean(grad, axis=-1, keepdims=True)
    mean_two = jnp.mean(grad * unit, axis=-1, keepdims=True)
    return (grad - mean_one - unit * mean_two) * scale


def column_sum(values_in):
    return jnp.sum(values_in, axis=0, keepdims=True)


B_QUERY, B_VALUE, B_OUT, GAIN_ONE, SHIFT_ONE, B_DOWN, GAIN_TWO, SHIFT_TWO, B_UP = range(9)


def middle_kernel(
    fused,
    x_ref, context_ref, ids_ref, b_out, gain_one, shift_one, b_up, b_down, gain_two, shift_two,
    text_ref, w_out, up_hbm, down_hbm,
    pool_out, count_out, vector_out, grad_out, mixed_out, wo_out, final_hbm, up_out, down_out, far_out,
    vec_ref, w_up, w_down, unit_ref, scale_ref, normed_ref, normed_t, act_ref, slope_ref, acc_ref, pre_one, pre_two,
    g_ref, final_ref, upg_ref, up_got, downg_ref, down_got, wo_sent, wo_got, down_y, down_x,
    send_sem, recv_sem, load_sem, store_sem,
):
    rows_here, size, width = x_ref.shape
    tokens = rows_here * size
    parts = w_up.shape[0]
    half = width // 2
    low = jnp.bfloat16
    f32 = jnp.float32
    me = lax.axis_index("ctx")
    core = me % 2
    near = {"ctx": me + 1 - 2 * core}
    side = me // 2
    place = lax.axis_index("dp")
    y = place % 2
    y_dev = {"dp": place + 1 - 2 * y}
    across_dev = {"ctx": (me + 2) % 4}
    peers = [near, across_dev, y_dev] if fused else [near]
    barrier = pltpu.get_barrier_semaphore()
    for peer in peers:
        pl.semaphore_signal(barrier, inc=1, device_id=peer, device_id_type=MESH)
    for row, source in (
        (B_OUT, b_out), (GAIN_ONE, gain_one), (SHIFT_ONE, shift_one), (B_DOWN, b_down),
        (GAIN_TWO, gain_two), (SHIFT_TWO, shift_two),
    ):
        vec_ref[row : row + 1, :] = source[...].astype(f32)[None]
    for i in range(parts):
        vec_ref[B_UP + i : B_UP + i + 1, :] = (
            b_up[i * width : (i + 1) * width].astype(f32)[None]
        )

    def vec(row):
        return vec_ref[row : row + 1, :]

    loads = []
    for i in range(parts):
        loads.append(
            (
                pltpu.make_async_copy(
                    up_hbm.at[:, pl.ds(i * width, width)], w_up.at[i], load_sem.at[0, i]
                ),
                pltpu.make_async_copy(
                    down_hbm.at[pl.ds(i * width, width)], w_down.at[i], load_sem.at[1, i]
                ),
            )
        )
    for pair in loads:
        for item in pair:
            item.start()

    def rows_of(r):
        return pl.ds(pl.multiple_of(r * size, size), size)

    text = lax.broadcasted_iota(jnp.int32, (NSEG, size), 0)

    def members(j, r):
        seg = ids_ref[j, r : r + 1, :]
        real = ids_ref[j, rows_here + r : rows_here + r + 1, :]
        return jnp.where((text == seg) & (real == 1), 1.0, 0.0)

    for r in range(rows_here):
        number = sum(jnp.sum(members(j, r), axis=1, keepdims=True) for j in range(4))
        count_out[r * NSEG : (r + 1) * NSEG, :] = jnp.maximum(number, 1.0)

    def first_norm(r, carry):
        rows = rows_of(r)
        mixed = x_ref[r].astype(f32) + (matmul(context_ref[r], w_out[...]) + vec(B_OUT))
        unit, scale = normalize(mixed)
        unit_ref[rows, :] = unit
        scale_ref[rows, :] = scale
        normed_ref[rows, :] = (unit * vec(GAIN_ONE) + vec(SHIFT_ONE)).astype(low)
        return carry

    lax.fori_loop(0, rows_here, first_norm, 0)
    for pair in loads:
        for item in pair:
            item.wait()

    def forward_part(i, following, now, then):
        for r in range(rows_here):
            rows = pl.ds(r * size, size)
            then[rows, :] = matmul(normed_ref[rows, :], w_up[following])
            act, slope = gelu_both(now[rows, :] + vec_ref[pl.ds(B_UP + i, 1), :])
            act_ref[i, rows, :] = act.astype(low)
            slope_ref[i, rows, :] = slope.astype(low)

    def forward_parts(n, carry):
        forward_part(2 * n, 2 * n + 1, pre_one, pre_two)
        forward_part(2 * n + 1, jnp.minimum(2 * n + 2, parts - 1), pre_two, pre_one)
        return carry

    pre_one[...] = matmul(normed_ref[...], w_up[0])
    lax.fori_loop(0, parts // 2, forward_parts, 0)

    def side_by_side(ref, *index):
        return jnp.concatenate([ref[(i,) + index] for i in range(parts)], axis=1)

    normed_t[...] = normed_ref[...].T

    store_final = []
    vector_out[...] = jnp.zeros_like(vector_out)
    for r in range(rows_here):
        rows = pl.ds(r * size, size)
        normed = unit_ref[rows, :] * vec(GAIN_ONE) + vec(SHIFT_ONE)
        ffn = matmul(
            side_by_side(act_ref, rows), w_down[...].reshape(parts * width, width)
        )
        summed = normed + (ffn + vec(B_DOWN))
        unit, scale = normalize(summed)
        final = unit * vec(GAIN_TWO) + vec(SHIFT_TWO)
        high = final.astype(low)
        final_ref[r] = high
        item = pltpu.make_async_copy(final_ref.at[r], final_hbm.at[r], store_sem.at[r])
        item.start()
        store_final.append(item)
        own = members(0, r)
        own_low = own.astype(low)
        rest = (final - high.astype(f32)).astype(low)
        pool = matmul(own_low, high) + matmul(own_low, rest)
        pool_out[r * NSEG : (r + 1) * NSEG, :] = pool.astype(low)
        share = text_ref[r] / count_out[r * NSEG : (r + 1) * NSEG, :]
        first = share.astype(low)
        second = (share - first.astype(f32)).astype(low)
        third = (share - first.astype(f32) - second.astype(f32)).astype(low)
        grad = dot_tn(
            jnp.concatenate([own_low] * 3, axis=0), jnp.concatenate([first, second, third], axis=0)
        )
        back = normalize_back(grad * vec(GAIN_TWO), unit, scale)
        back_low = back.astype(low)
        acc_ref[rows, :] = back
        g_ref[rows, :] = back_low
        vector_out[GAIN_TWO : GAIN_TWO + 1, :] += column_sum(grad * unit)
        vector_out[SHIFT_TWO : SHIFT_TWO + 1, :] += column_sum(grad)
        vector_out[B_DOWN : B_DOWN + 1, :] += column_sum(back_low.astype(f32))

    pl.semaphore_wait(barrier, len(peers))

    def remote(source, target, slot, device=near):
        return pltpu.make_async_remote_copy(
            src_ref=source, dst_ref=target, send_sem=send_sem.at[slot],
            recv_sem=recv_sem.at[slot], device_id=device, device_id_type=MESH,
        )

    per_part = downg_ref.shape[0] // parts
    mine = parts // 2

    def up_send(i):
        return remote(upg_ref.at[i], up_got.at[i], i)

    def down_send(i):
        chunk = pl.ds(i * per_part, per_part)
        return remote(downg_ref.at[chunk, 1 - core], down_got.at[chunk], parts + i)

    def down_part(i, carry):
        part = dot_tn(act_ref[i], g_ref[...]).astype(low)
        downg_ref[pl.ds(i * per_part, per_part)] = part.reshape((per_part,) + downg_ref.shape[1:])
        down_send(i).start()
        return carry

    lax.fori_loop(0, parts, down_part, 0)

    def backward_part(step, carry):
        i = (step + mine * (1 - core)) % parts
        back = dot_nt(g_ref[...], w_down[i])
        back = (back * slope_ref[i].astype(f32)).astype(low)
        slope_ref[i] = back
        vector_out[pl.ds(B_UP + i, 1), :] = column_sum(back.astype(f32))
        upg_ref[step] = matmul(normed_t[...], back).astype(low)

        @pl.when(step < mine)
        def _():
            up_send(step).start()

        return carry

    def down_sum(i, carry):
        downg_ref[i, core] = (
            downg_ref[i, core].astype(f32) + down_got[i].astype(f32)
        ).astype(low)
        return carry

    piece = downg_ref.shape[2] // 2
    quarter = piece // 2
    rest = pl.ds(pl.multiple_of(piece + quarter * (1 - side), 16), quarter)
    kept = pl.ds(pl.multiple_of(piece + quarter * side, 16), quarter)
    down_moves = []
    if fused:
        for n in range(4):
            down_moves.append(
                remote(
                    downg_ref.at[2 * n + 1 - y, core, pl.ds(0, piece)], down_y.at[n],
                    2 * parts + 1 + n, y_dev,
                )
            )
        for n in range(8):
            down_moves.append(
                remote(
                    downg_ref.at[n, core, rest], down_x.at[n], 2 * parts + 5 + n, across_dev
                )
            )
    lax.fori_loop(0, 1, backward_part, 0)
    for i in range(parts):
        down_send(i).wait_recv()
    lax.fori_loop(0, downg_ref.shape[0], down_sum, 0)
    for item in down_moves:
        item.start()
    lax.fori_loop(1, parts, backward_part, 0)

    def first_back(r, carry):
        rows = rows_of(r)
        unit = unit_ref[rows, :]
        grad = acc_ref[rows, :] + dot_nt(side_by_side(slope_ref, rows), side_by_side(w_up))
        back = normalize_back(grad * vec(GAIN_ONE), unit, scale_ref[rows, :])
        back_low = back.astype(low)
        mixed_out[r] = back
        g_ref[rows, :] = back_low
        vector_out[GAIN_ONE : GAIN_ONE + 1, :] += column_sum(grad * unit)
        vector_out[SHIFT_ONE : SHIFT_ONE + 1, :] += column_sum(grad)
        vector_out[B_OUT : B_OUT + 1, :] += column_sum(back_low.astype(f32))
        return carry

    lax.fori_loop(0, rows_here, first_back, 0)

    def out_part(h):
        columns = pl.ds(pl.multiple_of(h * half, 128), half)
        total = jnp.zeros((width, half), f32)
        for r in range(rows_here):
            total = total + dot_tn(context_ref[r], g_ref[pl.ds(r * size, size), columns])
        return total

    wo_sent[...] = out_part(1 - core).astype(low)
    wo_send = remote(wo_sent, wo_got, 2 * parts)
    wo_send.start()

    def grad_context(r, carry):
        grad_out[r] = dot_nt(g_ref[rows_of(r), :], w_out[...]).astype(low)
        return carry

    lax.fori_loop(0, rows_here, grad_context, 0)
    own_part = out_part(core)
    for i in range(mine):
        up_send(i).wait_recv()

    def up_sum(n, carry):
        rows = pl.ds(pl.multiple_of(n * 128, 128), 128)
        for i in range(mine):
            upg_ref[mine + i, rows, :] = (
                upg_ref[mine + i, rows, :].astype(f32) + up_got[i, rows, :].astype(f32)
            ).astype(low)
        return carry

    lax.fori_loop(0, width // 128, up_sum, 0)
    store_up = pltpu.make_async_copy(
        upg_ref.at[pl.ds(mine, mine)], up_out, store_sem.at[rows_here + 1]
    )
    store_up.start()
    wo_send.wait_recv()
    wo_out[...] = (own_part + wo_got[...].astype(f32)).astype(low)
    if fused:
        for item in down_moves:
            item.wait_recv()

        def near_sum(n, carry):
            down_y[n] = (
                downg_ref[2 * n + y, core, 0:piece, :].astype(f32) + down_y[n].astype(f32)
            ).astype(low)
            return carry

        def far_sum(n, carry):
            down_x[n] = (
                downg_ref[n, core, kept, :].astype(f32) + down_x[n].astype(f32)
            ).astype(low)
            return carry

        lax.fori_loop(0, 4, near_sum, 0)
        lax.fori_loop(0, 8, far_sum, 0)
        stores = [
            pltpu.make_async_copy(down_y, down_out, store_sem.at[rows_here]),
            pltpu.make_async_copy(down_x, far_out, store_sem.at[rows_here + 2]),
        ]
    else:
        stores = [
            pltpu.make_async_copy(downg_ref.at[:, core], down_out, store_sem.at[rows_here])
        ]
    for item in stores:
        item.start()
    for i in range(parts):
        down_send(i).wait_send()
    for i in range(mine):
        up_send(i).wait_send()
    wo_send.wait_send()
    for item in down_moves:
        item.wait_send()
    for item in store_final + stores + [store_up]:
        item.wait()


def middle(fused, x, context, ids, vectors, text_gradient, w_out, w_up, w_down, dp_size):
    rows_here, size, width = x.shape
    ff = w_up.shape[1]
    parts = ff // width
    tokens = rows_here * size
    low = jnp.bfloat16
    f32 = jnp.float32
    shape = jax.ShapeDtypeStruct
    whole = pl.BlockSpec(memory_space=pltpu.VMEM)
    outside = pl.BlockSpec(memory_space=pl.ANY)
    chunks = max(dp_size, parts)
    chunk = ff // chunks // 2
    vec = (8 + parts + (-parts) % 8, width)
    if fused:
        down_shape, far_shape = (4, chunk // 2, width), (8, chunk // 4, width)
    else:
        down_shape, far_shape = (chunks, chunk, width), (8, 16, 128)
    return pl.pallas_call(
        functools.partial(middle_kernel, fused),
        out_shape=(
            shape((rows_here * NSEG, width), low),
            shape((rows_here * NSEG, 1), f32),
            shape(vec, f32),
            shape((rows_here, size, width), low),
            shape((rows_here, size, width), f32),
            shape((width, width // 2), low),
            shape((rows_here, size, width), low),
            shape((parts // 2, width, width), low),
            shape(down_shape, low),
            shape(far_shape, low),
        ),
        in_specs=[whole] * 12 + [outside] * 2,
        out_specs=(whole,) * 6 + (outside,) * 4,
        scratch_shapes=[
            pltpu.VMEM(vec, f32),
            pltpu.VMEM((parts, width, width), low),
            pltpu.VMEM((parts, width, width), low),
            pltpu.VMEM((tokens, width), f32),
            pltpu.VMEM((tokens, 1), f32),
            pltpu.VMEM((tokens, width), low),
            pltpu.VMEM((width, tokens), low),
            pltpu.VMEM((parts, tokens, width), low),
            pltpu.VMEM((parts, tokens, width), low),
            pltpu.VMEM((tokens, width), f32),
            pltpu.VMEM((tokens, width), f32),
            pltpu.VMEM((tokens, width), f32),
            pltpu.VMEM((tokens, width), low),
            pltpu.VMEM((rows_here, size, width), low),
            pltpu.VMEM((parts, width, width), low),
            pltpu.VMEM((parts // 2, width, width), low),
            pltpu.VMEM((chunks, 2, chunk, width), low),
            pltpu.VMEM((chunks, chunk, width), low),
            pltpu.VMEM((width, width // 2), low),
            pltpu.VMEM((width, width // 2), low),
            pltpu.VMEM(down_shape if fused else (16, 128), low),
            pltpu.VMEM(far_shape, low),
            pltpu.SemaphoreType.DMA((2 * parts + 13,)),
            pltpu.SemaphoreType.DMA((2 * parts + 13,)),
            pltpu.SemaphoreType.DMA((2, parts)),
            pltpu.SemaphoreType.DMA((rows_here + 3,)),
        ],
        compiler_params=pltpu.CompilerParams(
            vmem_limit_bytes=63 * 2**20, collective_id=2, has_side_effects=True
        ),
        cost_estimate=pl.CostEstimate(
            flops=2 * tokens * width * (6 * ff + 3 * width),
            bytes_accessed=2 * (5 * ff * width + 8 * tokens * width),
            transcendentals=2 * tokens * ff,
        ),
    )(x, context, ids, *vectors, text_gradient, w_out, w_up, w_down)


class Links:
    def __init__(self, send_sem, recv_sem):
        self.send_sem, self.recv_sem = send_sem, recv_sem
        self.slots, self.copies = {}, {}

    def start(self, name, source, target, device):
        slot = self.slots.setdefault(name, len(self.slots))
        copy = pltpu.make_async_remote_copy(
            src_ref=source, dst_ref=target, send_sem=self.send_sem.at[slot],
            recv_sem=self.recv_sem.at[slot], device_id=device, device_id_type=MESH,
        )
        copy.start()
        self.copies[name] = copy

    def arrived(self, *names):
        for name in names:
            self.copies[name].wait_recv()

    def finish(self):
        for copy in self.copies.values():
            copy.wait_send()


def add_into(target, others, count):
    def one(i, carry):
        total = target[i].astype(jnp.float32)
        for other in others:
            total = total + other[i].astype(jnp.float32)
        target[i] = total.astype(target.dtype)
        return carry

    lax.fori_loop(0, count, one, 0)


def add_up(parts):
    total = parts[0].astype(jnp.float32)
    for part in parts[1:]:
        total = total + part.astype(jnp.float32)
    return total


POOL, UP, DOWN_A, DOWN_B, DOWN, OUT, GROUP, DX, VECTOR = range(9)
STEP, NEAR, FAR, SIDE, LINE, GATHER = range(6)

GROUPS = ((0, 4 * PAIR), (4 * PAIR, PAIR), (5 * PAIR, PAIR))


def attend_back_kernel(
    fused, count_out, out_tree, tree,
    x_ref, ids_ref, lse_ref, w_query, w_key, w_value, pool_ref, count_ref, vector_ref,
    x_hbm, q_hbm, k_hbm, v_hbm, context_hbm, grad_hbm, mixed_hbm, up_ref, down_ref, far_ref, out_ref,
    dx_out, pool_out, vector_out, *rest,
):
    outs = types.SimpleNamespace(**jax.tree.unflatten(out_tree, rest[:count_out]))
    ref = types.SimpleNamespace(**jax.tree.unflatten(tree, rest[count_out:]))
    square_out, up_out, down_out, wo_out = outs.square, outs.up, outs.down, outs.wo
    q_ref, k_ref, v_ref, context_ref, grad_ref = ref.q, ref.k, ref.v, ref.context, ref.grad
    dq_ref, dk_ref, dv_ref, x_t, x_got = ref.dq, ref.dk, ref.dv, ref.x_t, ref.x_got
    extra_ref, penal_ref, delta_ref = ref.extra, ref.penal, ref.delta
    dx_acc, dx_sent, dx_far, dx_got, dx_far_got = (
        ref.dx_acc, ref.dx_sent, ref.dx_far, ref.dx_got, ref.dx_far_got
    )
    pool_parts, pool_got, vec_parts, vec_got = (
        ref.pool_parts, ref.pool_got, ref.vec_parts, ref.vec_got
    )
    row_sem, local_sem = ref.row_sem, ref.local_sem
    rows_here, size, width = x_ref.shape
    low = jnp.bfloat16
    me, place = lax.axis_index("ctx"), lax.axis_index("dp")
    core, side = me % 2, me // 2
    near, across = me + 1 - 2 * core, (me + 2) % 4
    near_dev, across_dev = {"ctx": near}, {"ctx": across}
    y, z = place % 2, place // 2
    y_dev = {"dp": place + 1 - 2 * y}
    z_at = (z + 1 - 2 * (z % 2), (z + 2) % 4, 3 - z)
    z_dev = [{"dp": other * 2 + y} for other in z_at]
    peers = [near_dev, across_dev] + ([y_dev] + z_dev if fused else [])

    barrier = pltpu.get_barrier_semaphore()
    for peer in peers:
        pl.semaphore_signal(barrier, inc=1, device_id=peer, device_id_type=MESH)
    pl.semaphore_wait(barrier, len(peers))
    links = Links(ref.send_sem, ref.recv_sem)

    first_cut = GROUPS[1][0]
    blocks = [(0, first_cut, r) for r in range(rows_here)]
    blocks += [(first_cut, width - first_cut, r) for r in range(rows_here)]

    def load_block(step):
        slot = step % 2
        start, count, r = blocks[step]
        columns, local = pl.ds(start, count), pl.ds(0, count)
        pairs = (
            (k_hbm, k_ref), (v_hbm, v_ref), (q_hbm, q_ref), (context_hbm, context_ref),
            (grad_hbm, grad_ref),
        )
        copies = [
            pltpu.make_async_copy(
                source.at[r, :, columns], target.at[slot, :, local], row_sem.at[slot, i]
            )
            for i, (source, target) in enumerate(pairs)
        ]
        if step < rows_here:
            copies.append(pltpu.make_async_copy(x_hbm.at[:, r], x_got.at[slot], row_sem.at[slot, 5]))
        return copies

    for item in load_block(0):
        item.start()
    load_mixed = pltpu.make_async_copy(mixed_hbm, dx_acc, local_sem.at[0])
    links.start((POOL, STEP, 0), pool_ref, pool_got.at[0], near_dev)
    if fused:
        u_ref, u_x, u_y, u_z = ref.u, ref.u_x, ref.u_y, ref.u_z
        a_z, a_s, a_x = ref.a_z, ref.a_s, ref.a_x
        b_ref, b_y, b_z = ref.b, ref.b_y, ref.b_z
        o_ref, o_y, o_z, o_s, o_x = ref.o, ref.o_y, ref.o_z, ref.o_s, ref.o_x
        half_rows = u_ref.shape[2] // 2
        links.start((UP, FAR, 0), up_ref.at[1 - side, :, :, pl.ds(0, half_rows)], u_x.at[0], across_dev)
        links.start((DOWN_B, SIDE), far_ref.at[:, 1 - y], b_y, y_dev)
        for o in range(3):
            links.start((DOWN_A, LINE, o), down_ref.at[z_at[o]], a_z.at[o], z_dev[o])
    load_mixed.start()
    vec_parts[0] = vector_ref[...]

    def pool_one():
        links.arrived((POOL, STEP, 0))
        pool_parts[...] = add_up([pool_ref[...], pool_got[0]]).astype(low)
        links.start((POOL, STEP, 1), pool_parts, pool_got.at[1], across_dev)

    def pool_two():
        links.arrived((POOL, STEP, 1))
        pool_out[...] = add_up([pool_parts[...], pool_got[1]]) / count_ref[...]

    def send_z(name, source, target):
        for o in range(3):
            links.start(name + (o,), source(z_at[o]), target(o), z_dev[o])

    def arrived_z(name):
        links.arrived(*(name + (o,) for o in range(3)))

    def out_y():
        links.start((OUT, SIDE), out_ref.at[:, 1 - y], o_y, y_dev)

    def out_z():
        links.arrived((OUT, SIDE))
        for i in range(4):
            o_ref[i] = add_up([out_ref[i, y], o_y[i]]).astype(low)
        send_z((OUT, LINE), lambda i: o_ref.at[i], lambda o: o_z.at[o])

    def out_far():
        arrived_z((OUT, LINE))
        o_s[...] = add_up([o_ref[z]] + [o_z[o] for o in range(3)]).astype(low)
        links.start((OUT, FAR), o_s, o_x, across_dev)

    def out_end():
        links.arrived((OUT, FAR))
        wo_out[core] = add_up([o_s[...], o_x[...]]).astype(low)
        links.start((OUT, GATHER), wo_out.at[core], wo_out.at[core], near_dev)

    def down_z():
        links.arrived((DOWN_B, SIDE))
        for i in range(4):
            b_ref[i] = add_up([far_ref[i, y], b_y[i]]).astype(low)
        send_z((DOWN_B, LINE), lambda i: b_ref.at[i], lambda o: b_z.at[o])

    def down_near_far():
        arrived_z((DOWN_A, LINE))
        a_s[...] = add_up([down_ref[z]] + [a_z[o] for o in range(3)]).astype(low)
        links.start((DOWN_A, FAR), a_s, a_x, across_dev)

    def down_far():
        arrived_z((DOWN_B, LINE))
        count = b_ref.shape[1]
        own = pl.ds(pl.multiple_of(2 * count + side * count, 16), count)
        down_out[core, own] = add_up([b_ref[z]] + [b_z[o] for o in range(3)]).astype(low)
        links.start((DOWN_B, FAR), down_out.at[core, own], down_out.at[core, own], across_dev)

    def down_end():
        links.arrived((DOWN_A, FAR), (DOWN_B, FAR))
        down_out[core, 0 : a_s.shape[0]] = add_up([a_s[...], a_x[...]]).astype(low)
        links.start((DOWN, GATHER), down_out.at[core], down_out.at[core], near_dev)

    def up_x():
        rows = pl.ds(half_rows, half_rows)
        links.start((UP, FAR, 1), up_ref.at[1 - side, :, :, rows], u_x.at[1], across_dev)

    def up_y(h):
        rows = pl.ds(h * half_rows, half_rows)
        links.arrived((UP, FAR, h))
        for i in range(4):
            for j in range(2):
                u_ref[i, j, rows] = add_up([up_ref[side, i, j, rows], u_x[h, i, j]]).astype(low)
        links.start((UP, SIDE, h), u_ref.at[:, 1 - y, rows], u_y.at[h], y_dev)

    def up_z(h):
        rows = pl.ds(h * half_rows, half_rows)
        links.arrived((UP, SIDE, h))
        for i in range(4):
            u_ref[i, y, rows] = add_up([u_ref[i, y, rows], u_y[h, i]]).astype(low)
        send_z((UP, LINE, h), lambda i: u_ref.at[i, y, rows], lambda o: u_z.at[o, rows])

    def up_far():
        arrived_z((UP, LINE, 0))
        arrived_z((UP, LINE, 1))
        up_out[me] = add_up([u_ref[z, y]] + [u_z[o] for o in range(3)]).astype(low)
        links.start((UP, GATHER), up_out.at[me], up_out.at[me], across_dev)

    def up_end():
        links.arrived((UP, GATHER))
        links.start((UP, NEAR, 0), up_out.at[me], up_out.at[me], near_dev)
        links.start((UP, NEAR, 1), up_out.at[across], up_out.at[across], near_dev)

    def group_core(g):
        links.start((GROUP, NEAR, g), ref.g[g].at[1 - core], ref.g_got[g], near_dev)

    def group_y(g):
        links.arrived((GROUP, NEAR, g))
        for i in range(4):
            add_into(ref.g[g].at[core, i], [ref.g_got[g].at[i]], 2)
        links.start((GROUP, SIDE, g), ref.g[g].at[core, :, 1 - y], ref.g_y[g], y_dev)

    def group_z(g):
        links.arrived((GROUP, SIDE, g))
        own = ref.g[g]
        for i in range(4):
            own[core, i, y] = add_up([own[core, i, y], ref.g_y[g][i]]).astype(low)
        send_z((GROUP, LINE, g), lambda i: own.at[core, i, y], lambda o: ref.g_z[g].at[o])

    def group_far(g):
        arrived_z((GROUP, LINE, g))
        pieces = [ref.g[g][core, z, y]] + [ref.g_z[g][o] for o in range(3)]
        ref.g_s[g][...] = add_up(pieces).astype(low)
        links.start((GROUP, FAR, g), ref.g_s[g], ref.g_x[g], across_dev)

    def group_end(g):
        links.arrived((GROUP, FAR, g))
        out = outs.squares[g]
        out[core] = add_up([ref.g_s[g][...], ref.g_x[g][...]]).astype(low)
        links.start((GROUP, GATHER, g), out.at[core], out.at[core], near_dev)

    def vector_step(i, device):
        if i:
            links.arrived((VECTOR, STEP, i - 1))
            vec_parts[i] = vec_parts[i - 1] + vec_got[i - 1]
        if device is not None:
            links.start((VECTOR, STEP, i), vec_parts.at[i], vec_got.at[i], device)

    def vector_z():
        vector_step(3, None)
        for o in range(3):
            links.start((VECTOR, LINE, o), vec_parts.at[3], vec_got.at[3 + o], z_dev[o])

    def vector_end():
        arrived_z((VECTOR, LINE))
        vector_out[...] = vec_parts[3] + (vec_got[3] + (vec_got[4] + vec_got[5]))

    row = lax.broadcasted_iota(jnp.int32, (PAIR, size), 0)

    def find_delta(step):
        slot = step % 2
        start, count, _ = blocks[step]
        lane = lax.broadcasted_iota(jnp.int32, (count, PAIR), 1)
        head = (start + lax.broadcasted_iota(jnp.int32, (count, PAIR), 0)) // HEAD_DIM
        member = jnp.where((lane % NSEG == head) & (lane >= NSEG) & (lane < 4 * NSEG), 1.0, 0.0)
        member = member.astype(low)
        local = pl.ds(0, count)
        product = grad_ref[slot, :, local].astype(jnp.float32) * context_ref[
            slot, :, local
        ].astype(jnp.float32)
        total = jnp.zeros((size, PAIR), jnp.float32)
        for _ in range(3):
            term = product.astype(low)
            total = total + matmul(term, member)
            product = product - term.astype(jnp.float32)
        delta_ref[...] = with_constants(jnp.zeros_like(total), -total)

    def attend_pairs(step, first, last):
        slot = step % 2
        start, _, r = blocks[step]

        def one_pair(n, carry):
            local = pl.ds(pl.multiple_of(n * PAIR, PAIR), PAIR)
            columns = pl.ds(pl.multiple_of(start + n * PAIR, PAIR), PAIR)
            head = 2 * (start // PAIR + n)
            q_both = split_heads(q_ref[slot, :, local])
            g_both = split_heads(grad_ref[slot, :, local])
            q_extra = [of_head(penal_ref[r], head + h) for h in range(2)]
            g_extra = [of_head(delta_ref[...], head + h) for h in range(2)]
            q_wide = jnp.concatenate([q_both, jnp.concatenate(q_extra, axis=0)], axis=1)
            g_wide = jnp.concatenate([g_both, jnp.concatenate(g_extra, axis=0)], axis=1)
            dq = jnp.zeros((PAIR, 2 * size), jnp.float32)

            def products(j):
                rows = pl.ds(j * size, size)
                extra = extra_ref[r, rows, :]
                keys = jnp.concatenate([k_ref[slot, rows, local], extra], axis=1)
                values = jnp.concatenate([v_ref[slot, rows, local], extra], axis=1)
                return dot_nt(keys, q_wide), dot_nt(values, g_wide)

            ahead = products(0)
            for j in range(4):
                rows = pl.ds(j * size, size)
                scores, grad_p = ahead
                if j < 3:
                    ahead = products(j + 1)
                probs = jnp.exp(scores)
                grad_s = (probs * grad_p).astype(low)
                dv_ref[r, rows, columns] = matmul(probs.astype(low), g_both).astype(low)
                dk_ref[r, rows, columns] = matmul(grad_s, q_both).astype(low)
                dq = dq + matmul(k_ref[slot, rows, local].T, grad_s)
            dq = jnp.where(row < HEAD_DIM, dq[:, :size], dq[:, size:]) * HEAD_DIM ** (-0.5)
            dq_ref[r, :, columns] = dq.T.astype(low)
            return carry

        lax.fori_loop(first, last, one_pair, 0)

    def weight_group(g):
        start, count = GROUPS[g]
        if fused:
            depth = ref.g[g].shape[3]

        def keep(n, i, total):
            total = total.astype(low)
            wide = total.shape[1]
            if not fused:
                square_out[n, :, pl.ds(pl.multiple_of(start + i * PAIR, PAIR), wide)] = total
                return
            total = total.reshape(4, 2, 2, depth, wide)
            target = pl.ds(pl.multiple_of(n * count + i * PAIR, PAIR), wide)
            for h in range(2):
                ref.g[g][h, :, :, :, target] = total[:, :, h]

        def of_source(source, columns):
            keys = source.shape[1]
            return sum(
                matmul(x_t[r, :, :keys], source[r, :, columns]) for r in range(rows_here)
            )

        def one_part(i, carry):
            columns = pl.ds(pl.multiple_of(start + 2 * i * PAIR, PAIR), 2 * PAIR)
            for n, source in enumerate((dq_ref, dk_ref, dv_ref)):
                keep(n, 2 * i, of_source(source, columns))
            return carry

        if count % (2 * PAIR):
            columns = pl.ds(start, count)
            keep(0, 0, of_source(dq_ref, columns))
            both = sum(
                matmul(
                    x_t[r],
                    jnp.concatenate([dk_ref[r, :, columns], dv_ref[r, :, columns]], axis=1),
                )
                for r in range(rows_here)
            )
            keep(1, 0, both[:, :count])
            keep(2, 0, both[:, count:])
        else:
            lax.fori_loop(0, count // (2 * PAIR), one_part, 0)
        columns = pl.ds(start, count)
        for n, source in enumerate((dq_ref, dv_ref)):
            vec_parts[0, n : n + 1, columns] = sum(
                jnp.sum(source[r, :, columns].astype(jnp.float32), axis=0, keepdims=True)
                for r in range(rows_here)
            )

    def input_parts(r):
        for j in (3, 2, 1, 0):
            rows = pl.ds(j * size, size)
            total = dot_nt(dk_ref[r, rows, :], w_key[...]) + dot_nt(dv_ref[r, rows, :], w_value[...])
            if j == 0:
                dx_acc[r] = dx_acc[r] + total + dot_nt(dq_ref[r], w_query[...])
            elif j == 2:
                dx_far[r] = total.astype(low)
            else:
                n = j // 2
                dx_sent[r, n] = total.astype(low)
                links.start((DX, NEAR, r, n), dx_sent.at[r, n], dx_got.at[r, n], near_dev)

    def input_far(r):
        links.arrived((DX, NEAR, r, 1))
        dx_far[r] = add_up([dx_far[r], dx_got[r, 1]]).astype(low)
        links.start((DX, FAR, r), dx_far.at[r], dx_far_got.at[r], across_dev)

    def input_done(r):
        links.arrived((DX, NEAR, r, 0), (DX, FAR, r))
        dx_out[r] = add_up([dx_acc[r], dx_got[r, 0], dx_far_got[r]]).astype(low)

    def prepare_row(r):
        slot = r % 2
        for j in range(4):
            rows = slice(j * size, (j + 1) * size)
            texts = text_rows(ids_ref[j, r : r + 1, :], size)
            extra_ref[r, rows, :] = key_extra(texts)
            if j == 0:
                penal_ref[r] = with_constants(query_extra(texts), -lse_ref[r])
            block = x_ref[r] if j == 0 else x_got[slot, j - 1]
            x_t[r, :, rows] = block.T

    def begin(step):
        for item in load_block(step):
            item.wait()
        if step + 1 < len(blocks):
            for item in load_block(step + 1):
                item.start()
        find_delta(step)

    def do(*actions):
        if fused:
            for action, *given in actions:
                action(*given)

    most = first_cut // PAIR
    begin(0)
    prepare_row(0)
    attend_pairs(0, 0, most // 2)
    do((pool_one,))
    attend_pairs(0, most // 2, most)
    do((down_z,), (out_y,))
    begin(1)
    prepare_row(1)
    attend_pairs(1, 0, most // 2)
    do((up_x,), (pool_two,))
    attend_pairs(1, most // 2, most)
    do((up_y, 0), (down_near_far,))
    begin(2)
    prepare_row(2)
    attend_pairs(2, 0, most // 2)
    do((out_z,))
    attend_pairs(2, most // 2, most)
    do((up_z, 0), (down_far,))
    weight_group(0)
    do((group_core, 0), (up_y, 1))
    begin(3)
    attend_pairs(3, 0, 2)
    do((group_y, 0), (down_end,), (out_far,))
    load_mixed.wait()
    input_parts(0)
    do((up_z, 1))
    begin(4)
    attend_pairs(4, 0, 2)
    do((input_far, 0), (out_end,))
    input_parts(1)
    do((group_z, 0))
    begin(5)
    attend_pairs(5, 0, 1)
    do((input_far, 1))
    weight_group(1)
    do((group_core, 1))
    attend_pairs(5, 1, 2)
    do((group_y, 1), (up_far,))
    weight_group(2)
    do((group_core, 2), (vector_step, 0, near_dev))
    input_parts(2)
    if not fused:
        vector_out[...] = vec_parts[0]
        pool_one()
        for r in range(3):
            input_far(r)
        pool_two()
        for r in range(3):
            input_done(r)
        links.finish()
        return
    do((group_y, 2), (group_z, 1), (vector_step, 1, across_dev))
    do((input_far, 2), (group_far, 0), (group_z, 2), (input_done, 0))
    do((vector_step, 2, y_dev), (up_end,), (input_done, 1), (group_far, 1), (vector_z,))
    do((group_end, 0), (group_far, 2), (group_end, 1), (vector_end,))
    do((group_end, 2), (input_done, 2))
    links.arrived((DOWN, GATHER), (OUT, GATHER), (UP, NEAR, 0), (UP, NEAR, 1))
    links.arrived((GROUP, GATHER, 0), (GROUP, GATHER, 1), (GROUP, GATHER, 2))
    links.finish()


def attend_back(
    fused, x, ids, lse, w_query, w_key, w_value, pool, counts, vectors,
    x_got, q, k, v, context, grad, mixed, up, down, far, out,
):
    rows_here, size, width = x.shape
    keys = size * 4
    low = jnp.bfloat16
    f32 = jnp.float32
    whole = pl.BlockSpec(memory_space=pltpu.VMEM)
    outside = pl.BlockSpec(memory_space=pl.ANY)
    shape = jax.ShapeDtypeStruct
    most = GROUPS[0][1]
    vec = vectors.shape
    small = shape((8, 128), low)
    if fused:
        depth = up.shape[3]
        outs = dict(
            squares=[shape((2, depth // 2, 3 * count), low) for _, count in GROUPS],
            up=shape((4, depth, width), low),
            down=shape((2, 2 * down.shape[1], width), low),
            wo=shape((2, depth, width // 2), low),
            square=small,
        )
    else:
        outs = dict(
            squares=[], up=small, down=small, wo=small, square=shape((3, width, width), low)
        )
    scratch = dict(
        x_got=pltpu.VMEM((2, 3, size, width), low),
        x_t=pltpu.VMEM((rows_here, width, keys), low),
        q=pltpu.VMEM((2, size, most), low),
        k=pltpu.VMEM((2, keys, most), low),
        v=pltpu.VMEM((2, keys, most), low),
        context=pltpu.VMEM((2, size, most), low),
        grad=pltpu.VMEM((2, size, most), low),
        extra=pltpu.VMEM((rows_here, keys, PAIR), low),
        penal=pltpu.VMEM((rows_here, size, PAIR), low),
        delta=pltpu.VMEM((size, PAIR), low),
        dq=pltpu.VMEM((rows_here, size, width), low),
        dk=pltpu.VMEM((rows_here, keys, width), low),
        dv=pltpu.VMEM((rows_here, keys, width), low),
        dx_acc=pltpu.VMEM((rows_here, size, width), f32),
        dx_sent=pltpu.VMEM((rows_here, 2, size, width), low),
        dx_far=pltpu.VMEM((rows_here, size, width), low),
        dx_got=pltpu.VMEM((rows_here, 2, size, width), low),
        dx_far_got=pltpu.VMEM((rows_here, size, width), low),
        pool_parts=pltpu.VMEM(pool.shape, low),
        pool_got=pltpu.VMEM((2,) + pool.shape, low),
        vec_parts=pltpu.VMEM((4,) + vec, f32),
        vec_got=pltpu.VMEM((6,) + vec, f32),
        send_sem=pltpu.SemaphoreType.DMA((72,)),
        recv_sem=pltpu.SemaphoreType.DMA((72,)),
        row_sem=pltpu.SemaphoreType.DMA((2, 6)),
        local_sem=pltpu.SemaphoreType.DMA((5,)),
    )
    if fused:
        tails = [(depth // 2, 3 * count) for _, count in GROUPS]
        spread = lambda *lead: [pltpu.VMEM(lead + tail, low) for tail in tails]
        b_rows = far.shape[2]
        narrow = (depth, width // 2)
        scratch.update(
            g=spread(2, 4, 2), g_got=spread(4, 2), g_y=spread(4), g_z=spread(3),
            g_s=spread(), g_x=spread(),
            u=pltpu.VMEM((4, 2, depth, width), low),
            u_x=pltpu.VMEM((2, 4, 2, depth // 2, width), low),
            u_y=pltpu.VMEM((2, 4, depth // 2, width), low),
            u_z=pltpu.VMEM((3, depth, width), low),
            a_z=pltpu.VMEM((3,) + down.shape[1:], low),
            a_s=pltpu.VMEM(down.shape[1:], low),
            a_x=pltpu.VMEM(down.shape[1:], low),
            b=pltpu.VMEM((4, b_rows, width), low),
            b_y=pltpu.VMEM((4, b_rows, width), low),
            b_z=pltpu.VMEM((3, b_rows, width), low),
            o=pltpu.VMEM((4,) + narrow, low),
            o_y=pltpu.VMEM((4,) + narrow, low),
            o_z=pltpu.VMEM((3,) + narrow, low),
            o_s=pltpu.VMEM(narrow, low),
            o_x=pltpu.VMEM(narrow, low),
        )
    out_leaves, out_tree = jax.tree.flatten(outs)
    leaves, tree = jax.tree.flatten(scratch)
    count_out = len(out_leaves)
    got = pl.pallas_call(
        functools.partial(attend_back_kernel, fused, count_out, out_tree, tree),
        out_shape=(
            shape((rows_here, size, width), low),
            shape(pool.shape, f32),
            shape(vec, f32),
        )
        + tuple(out_leaves),
        in_specs=[whole] * 9 + [outside] * 7 + [whole] * 4,
        out_specs=(whole,) * (3 + count_out),
        scratch_shapes=leaves,
        compiler_params=pltpu.CompilerParams(
            vmem_limit_bytes=63 * 2**20, collective_id=1, has_side_effects=True
        ),
        cost_estimate=pl.CostEstimate(
            flops=rows_here
            * (4 * (size + 2 * keys) * width * width + 40 * size * keys * width),
            bytes_accessed=2 * (16 * width * width + 9 * keys * width),
            transcendentals=rows_here * HEADS * size * keys,
        ),
    )(
        x, ids, lse, w_query, w_key, w_value, pool, counts, vectors,
        x_got, q, k, v, context, grad, mixed, up, down, far, out,
    )
    return got[:3] + (types.SimpleNamespace(**jax.tree.unflatten(out_tree, got[3:])),)


def outputs_kernel(
    square0, square1, square2, wo, up, down, pool, final, dx,
    wq_out, wk_out, wv_out, wo_out, up_out, down_out, pool_out, final_out, dx_out,
):
    final_out[...] = final[...]
    dx_out[...] = dx[...]
    f32 = jnp.float32
    pool_out[...] = pool[...].reshape(pool_out.shape)
    for (start, count), square in zip(GROUPS, (square0, square1, square2)):
        rows = square.shape[1]
        for n, out in enumerate((wq_out, wk_out, wv_out)):
            for h in range(2):
                out[h * rows : (h + 1) * rows, start : start + count] = square[
                    h, :, n * count : (n + 1) * count
                ].astype(f32)
    for h in range(2):
        half = wo.shape[2]
        wo_out[:, h * half : (h + 1) * half] = wo[h].astype(f32)
        rows = down.shape[1]
        down_out[h * rows : (h + 1) * rows, :] = down[h].astype(f32)
    for i in range(4):
        place, width = (i % 2) * 2 + i // 2, up.shape[2]
        up_out[:, place * width : (place + 1) * width] = up[i].astype(f32)


def outputs(squares, wo, up, down, pool, final, dx):
    f32 = jnp.float32
    whole = pl.BlockSpec(memory_space=pltpu.VMEM)
    shape = jax.ShapeDtypeStruct
    rows, width = up.shape[1:]
    row_count = final.shape[0]
    return pl.pallas_call(
        outputs_kernel,
        out_shape=(
            shape((rows, width), f32), shape((rows, width), f32), shape((rows, width), f32),
            shape((rows, width), f32), shape((rows, 4 * width), f32),
            shape((2 * down.shape[1], width), f32),
            shape((row_count, pool.shape[0] // row_count, width), f32),
            shape(final.shape, final.dtype), shape(dx.shape, dx.dtype),
        ),
        in_specs=[whole] * 9,
        out_specs=(whole,) * 9,
        compiler_params=pltpu.CompilerParams(vmem_limit_bytes=63 * 2**20),
    )(*squares, wo, up, down, pool, final, dx)


def radices_of(count):
    if count == 8:
        return ((1, 2), (2, 4))
    digits = []
    stride = 1
    while stride < count:
        digits.append((stride, 2))
        stride *= 2
    return tuple(digits)


def exchange(piece, axis_name, stride, offset):
    count = lax.axis_size(axis_name)
    pairs = [(i, i ^ (offset * stride)) for i in range(count)]
    return lax.ppermute(piece, axis_name, pairs)


def digit_of(axis_name, stride, radix):
    return (lax.axis_index(axis_name) // stride) % radix


def scatter_digit(pieces, place, axis_name, stride, radix):
    here = digit_of(axis_name, stride, radix)
    received = [
        exchange(
            lax.dynamic_index_in_dim(pieces, here ^ offset, place, keepdims=False).astype(
                jnp.bfloat16
            ),
            axis_name, stride, offset,
        )
        for offset in range(1, radix)
    ]
    total = lax.dynamic_index_in_dim(pieces, here, place, keepdims=False).astype(jnp.float32)
    for item in received:
        total = total + item.astype(jnp.float32)
    return total.astype(jnp.bfloat16)


def halve(piece, place, axis_name, stride):
    half = piece.shape[place] // 2
    here = digit_of(axis_name, stride, 2)
    sent = lax.dynamic_slice_in_dim(piece, (1 - here) * half, half, place).astype(jnp.bfloat16)
    kept = lax.dynamic_slice_in_dim(piece, here * half, half, place).astype(jnp.float32)
    return (kept + exchange(sent, axis_name, stride, 1).astype(jnp.float32)).astype(jnp.bfloat16)


def join(piece, place, axis_name, stride):
    here = digit_of(axis_name, stride, 2)
    other = exchange(piece, axis_name, stride, 1)
    first = jnp.where(here == 0, piece, other)
    second = jnp.where(here == 0, other, piece)
    return jnp.concatenate([first, second], axis=place)


def scatter_rows(group, dp_size):
    digits = radices_of(dp_size)
    shape = tuple(r for _, r in reversed(digits))
    group = group.reshape(shape + (group.shape[0] // dp_size, group.shape[1]))
    for place, (stride, radix) in zip(range(len(digits) - 1, -1, -1), digits):
        group = scatter_digit(group, place, "dp", stride, radix)
    return group


def finish_weight(flat, dp_size, side):
    flat = scatter_rows(flat, dp_size)
    flat = flat.astype(jnp.float32) + exchange(flat, "ctx", 2, 1).astype(jnp.float32)
    return join(flat.astype(jnp.bfloat16), side, "ctx", 1).astype(jnp.float32)


def reduce_weight(gradient, dp_size, side):
    return finish_weight(halve(gradient, side, "ctx", 1), dp_size, side)


def per_device(
    hidden_in,
    seg_ids,
    valid,
    w_query,
    b_query,
    w_key,
    w_value,
    b_value,
    w_out,
    b_out,
    gain_attn,
    shift_attn,
    w_up,
    b_up,
    w_down,
    b_down,
    gain_ffn,
    shift_ffn,
    pooled_text_gradient,
):
    row_count, group_size, model_width = hidden_in.shape
    dp_size = lax.axis_size("dp")
    ff_width = w_up.shape[1]
    rows_here, ff_here = model_width // dp_size, ff_width // dp_size
    fused = dp_size == 8 and rows_here % 32 == 0 and ff_here % 128 == 0
    q_all, context, lse_all, ids_got, x_got, k_all, v_all = attend(
        hidden_in, seg_ids, valid, b_query, b_value, w_query, w_key, w_value
    )
    vectors = (b_out, gain_attn, shift_attn, b_up, b_down, gain_ffn, shift_ffn)
    pool, counts, vector_parts, grad_context, grad_mixed, out, final_out, up, down, far = middle(
        fused, hidden_in, context, ids_got, vectors, pooled_text_gradient, w_out, w_up, w_down,
        dp_size,
    )
    if fused:
        up_part = up.reshape(2, 4, 2, rows_here, -1)
        far_part = far.reshape((4, 2) + far.shape[1:])
        out_part = out.reshape(4, 2, rows_here, -1)
    else:
        up_part = far_part = out_part = jnp.zeros((16, 128), jnp.bfloat16)
    grad_input, pooled, vector_sum, sums_of = attend_back(
        fused, hidden_in, ids_got, lse_all, w_query, w_key, w_value,
        pool, counts, vector_parts, x_got, q_all, k_all, v_all, context, grad_context, grad_mixed,
        up_part, down, far_part, out_part,
    )
    if fused:
        *square_sums, up_sum, down_sum, pooled, final_out, grad_input = outputs(
            sums_of.squares, sums_of.wo, sums_of.up, sums_of.down, pooled, final_out, grad_input
        )
    else:
        squares = sums_of.square
        square_sums = [reduce_weight(squares[n], dp_size, 1) for n in range(3)]
        square_sums.append(finish_weight(out, dp_size, 1))
        up_sum = finish_weight(up.transpose(1, 0, 2).reshape(model_width, -1), dp_size, 1)
        down_sum = finish_weight(down.reshape(-1, model_width), dp_size, 0)
        vector_sum = lax.psum(vector_sum, ("dp", "ctx"))
        pooled = pooled.reshape(row_count, NSEG, model_width)
    place = lax.axis_index("dp")
    sums = lax.dynamic_slice_in_dim(vector_sum[:8], place * rows_here, rows_here, 1)
    sum_bu = lax.dynamic_slice_in_dim(
        vector_sum[8 : 8 + ff_width // model_width].reshape(-1), place * ff_here, ff_here
    )
    results = (
        square_sums[0], sums[0], square_sums[1], square_sums[2], sums[1], square_sums[3],
        sums[2], sums[3], sums[4], up_sum, sum_bu, down_sum, sums[5], sums[6], sums[7],
    )
    return (
        final_out,
        pooled,
        grad_input,
    ) + tuple(results)


def solution(mesh):
    placed = (
        P("dp", "ctx", None),
        P("dp", "ctx"),
        P("dp", "ctx"),
        P(),
        P(),
        P(),
        P(),
        P(),
        P(),
        P(),
        P(),
        P(),
        P(),
        P(),
        P(),
        P(),
        P(),
        P(),
        P("dp", None, None),
    )
    return jax.shard_map(
        per_device,
        mesh=mesh,
        in_specs=placed,
        out_specs=(
            P("dp", "ctx", None),
            P("dp", None, None),
            P("dp", "ctx", None),
            P("dp", None),
            P("dp"),
            P("dp", None),
            P("dp", None),
            P("dp"),
            P("dp", None),
            P("dp"),
            P("dp"),
            P("dp"),
            P("dp", None),
            P("dp"),
            P("dp", None),
            P("dp"),
            P("dp"),
            P("dp"),
        ),
        check_vma=False,
    )
```

```python
import functools
import types

import jax
import jax.numpy as jnp
from jax import lax
from jax.experimental import pallas as pl
from jax.experimental.pallas import tpu as pltpu
from jax.sharding import PartitionSpec as P

HEADS = 12
HEAD_DIM = 64
NSEG = 16


eps = 1e-12


def matmul(left_side, right_side):
    return jnp.dot(left_side, right_side, preferred_element_type=jnp.float32)


PAIR = 2 * HEAD_DIM
MESH = pl.DeviceIdType.MESH
MASKED = -1e30


def dot_nt(left_side, right_side):
    return lax.dot_general(
        left_side, right_side, (((1,), (1,)), ((), ())), preferred_element_type=jnp.float32
    )


def dot_tn(left_side, right_side):
    return lax.dot_general(
        left_side, right_side, (((0,), (0,)), ((), ())), preferred_element_type=jnp.float32
    )


def split_heads(pair):
    lane = lax.broadcasted_iota(jnp.int32, pair.shape, 1)
    zero = jnp.zeros_like(pair)
    return jnp.concatenate(
        [jnp.where(lane < HEAD_DIM, pair, zero), jnp.where(lane < HEAD_DIM, zero, pair)], axis=0
    )


def text_rows(ids_row, size):
    return jnp.broadcast_to(ids_row.astype(jnp.float32), (PAIR, size)).T


def lanes_of(size):
    return lax.broadcasted_iota(jnp.int32, (size, PAIR), 1)


def key_extra(texts):
    lane = lanes_of(texts.shape[0])
    hot = jnp.where(lane.astype(jnp.float32) == texts, 1.0, 0.0)
    return jnp.where((lane >= NSEG) & (lane < 4 * NSEG), 1.0, hot).astype(jnp.bfloat16)


def query_extra(texts):
    lane = lanes_of(texts.shape[0])
    other = (lane < NSEG) & (lane.astype(jnp.float32) != texts)
    return jnp.where(other, MASKED, 0.0)


def with_constants(extra, constants):
    lane = lanes_of(extra.shape[0])
    high = constants.astype(jnp.bfloat16).astype(jnp.float32)
    middle = (constants - high).astype(jnp.bfloat16).astype(jnp.float32)
    rest = constants - high - middle
    terms = jnp.where(lane < 2 * NSEG, high, jnp.where(lane < 3 * NSEG, middle, rest))
    kept = (lane >= NSEG) & (lane < 4 * NSEG)
    return jnp.where(kept, terms, extra).astype(jnp.bfloat16)


def of_head(extra, head):
    lane = lanes_of(extra.shape[0])
    kept = (lane < NSEG) | (lane % NSEG == head)
    return jnp.where(kept, extra, jnp.zeros_like(extra))


def attend_kernel(
    x_ref, seg_ref, valid_ref, b_query, b_value, w_query, w_key, w_value,
    q_out, context_out, lse_out, ids_out, x_hbm, k_hbm, v_hbm,
    x_got, k_ref, v_ref, extra_ref, ids_ref, score_one, score_two, send_sem, recv_sem, local_sem,
):
    rows_here, size, width = x_ref.shape
    me = lax.axis_index("ctx")
    one = me + 1 - 2 * (me % 2)
    two = (me + 2) % 4
    three = (one + 2) % 4
    low = jnp.bfloat16

    ids_ref[...] = jnp.zeros_like(ids_ref)
    ids_ref[0:rows_here, :] = seg_ref[...]
    ids_ref[rows_here : 2 * rows_here, :] = valid_ref[...]
    query_bias = b_query[...].astype(jnp.float32)[None]
    value_bias = b_value[...].astype(jnp.float32)[None]
    barrier = pltpu.get_barrier_semaphore()
    for peer in (one, two, three):
        pl.semaphore_signal(barrier, inc=1, device_id={"ctx": peer}, device_id_type=MESH)
    pl.semaphore_wait(barrier, 3)

    def send(source, target, slot, peer):
        return pltpu.make_async_remote_copy(
            src_ref=source, dst_ref=target, send_sem=send_sem.at[slot],
            recv_sem=recv_sem.at[slot], device_id={"ctx": peer}, device_id_type=MESH,
        )

    ids_out[0] = ids_ref[...]
    ids_sends = [send(ids_ref, ids_out.at[j + 1], j, peer) for j, peer in enumerate((one, two, three))]
    near = send(x_ref, x_got.at[0], 3, one)

    def far(r):
        return send(x_ref.at[r], x_got.at[1, r], 4 + r, two)

    def passed(r):
        return send(x_got.at[1, r], x_got.at[2, r], 4 + rows_here + r, one)

    far(0).start()
    near.start()
    for item in ids_sends:
        item.start()
    for r in range(1, rows_here):
        far(r).start()

    def project(x, r, j):
        count = x.shape[0] // size
        k = matmul(x, w_key[...]).astype(low)
        v = (matmul(x, w_value[...]) + value_bias).astype(low)
        for n in range(count):
            rows = pl.ds((j + n if r is not None else j) * size, size)
            k_ref[n if r is None else r, rows, :] = k[n * size : (n + 1) * size]
            v_ref[n if r is None else r, rows, :] = v[n * size : (n + 1) * size]

    own = x_ref[...].reshape(rows_here * size, width)
    q = (matmul(own, w_query[...]) + query_bias).astype(low)
    q_out[...] = (q * HEAD_DIM ** (-0.5)).astype(low).reshape(q_out.shape)
    project(own, None, 0)
    near.wait_recv()
    project(x_got[0].reshape(rows_here * size, width), None, 1)
    for item in ids_sends:
        item.wait_recv()
    lane = lax.broadcasted_iota(jnp.int32, (size, PAIR), 1)
    far(0).wait_recv()
    passed(0).start()

    def keep(r):
        return (
            pltpu.make_async_copy(k_ref.at[r], k_hbm.at[r], local_sem.at[0, r]),
            pltpu.make_async_copy(v_ref.at[r], v_hbm.at[r], local_sem.at[1, r]),
            pltpu.make_async_copy(x_got.at[:, r], x_hbm.at[:, r], local_sem.at[2, r]),
        )

    for r in range(rows_here):
        passed(r).wait_recv()
        project(jnp.concatenate([x_got[1, r], x_got[2, r]], axis=0), r, 2)
        for item in keep(r):
            item.start()
        for j in range(4):
            texts = text_rows(ids_out[j, r : r + 1, :], size)
            extra_ref[j * size : (j + 1) * size, :] = key_extra(texts)
            if j == 0:
                own_extra = query_extra(texts).astype(low)

        def score(pair, target, r=r, own_extra=own_extra):
            columns = pl.ds(pl.multiple_of(pair * PAIR, PAIR), PAIR)
            both = split_heads(q_out[r, :, columns])
            extras = jnp.concatenate([own_extra, own_extra], axis=0)
            keys = jnp.concatenate([k_ref[r, :, columns], extra_ref[...]], axis=1)
            target[...] = dot_nt(jnp.concatenate([both, extras], axis=1), keys)

        def one_pair(pair, source, stat, r=r):
            columns = pl.ds(pl.multiple_of(pair * PAIR, PAIR), PAIR)
            scores = source[...]
            top = jnp.max(scores, axis=-1, keepdims=True)
            weight = jnp.exp(scores - top)
            total = jnp.sum(weight, axis=-1, keepdims=True)
            mixed = matmul(weight.astype(low), v_ref[r, :, columns]) * (1.0 / total)
            context_out[r, :, columns] = jnp.where(
                lane < HEAD_DIM, mixed[:size], mixed[size:]
            ).astype(low)
            lse = top + jnp.log(total)
            for h in range(2):
                ours = lane % NSEG == 2 * pair + h
                stat = jnp.where(ours, lse[h * size : (h + 1) * size], stat)
            return stat

        def two_pairs(n, carry, r=r):
            stat = lse_out[r]
            score(2 * n + 1, score_two)
            stat = one_pair(2 * n, score_one, stat)
            score(jnp.minimum(2 * n + 2, HEADS // 2 - 1), score_one)
            lse_out[r] = one_pair(2 * n + 1, score_two, stat)
            return carry

        score(0, score_one)
        lse_out[r] = jnp.zeros((size, PAIR), jnp.float32)
        lax.fori_loop(0, HEADS // 4, two_pairs, 0)
        if r + 1 < rows_here:
            far(r + 1).wait_recv()
            passed(r + 1).start()
    for r in range(rows_here):
        for item in keep(r):
            item.wait()
        far(r).wait_send()
        passed(r).wait_send()
    near.wait_send()
    for item in ids_sends:
        item.wait_send()


def attend(x, seg_ids, valid, b_query, b_value, w_query, w_key, w_value):
    rows_here, size, width = x.shape
    keys = size * 4
    low = jnp.bfloat16
    whole = pl.BlockSpec(memory_space=pltpu.VMEM)
    outside = pl.BlockSpec(memory_space=pl.ANY)
    slots = 4 + 2 * rows_here
    return pl.pallas_call(
        attend_kernel,
        out_shape=(
            jax.ShapeDtypeStruct((rows_here, size, width), low),
            jax.ShapeDtypeStruct((rows_here, size, width), low),
            jax.ShapeDtypeStruct((rows_here, size, PAIR), jnp.float32),
            jax.ShapeDtypeStruct((4, 8, size), jnp.int32),
            jax.ShapeDtypeStruct((3,) + x.shape, low),
            jax.ShapeDtypeStruct((rows_here, keys, width), low),
            jax.ShapeDtypeStruct((rows_here, keys, width), low),
        ),
        in_specs=[whole] * 8,
        out_specs=(whole, whole, whole, whole, outside, outside, outside),
        scratch_shapes=[
            pltpu.VMEM((3,) + x.shape, low),
            pltpu.VMEM((rows_here, keys, width), low),
            pltpu.VMEM((rows_here, keys, width), low),
            pltpu.VMEM((keys, PAIR), low),
            pltpu.VMEM((8, size), jnp.int32),
            pltpu.VMEM((2 * size, keys), jnp.float32),
            pltpu.VMEM((2 * size, keys), jnp.float32),
            pltpu.SemaphoreType.DMA((slots,)),
            pltpu.SemaphoreType.DMA((slots,)),
            pltpu.SemaphoreType.DMA((3, rows_here)),
        ],
        compiler_params=pltpu.CompilerParams(
            vmem_limit_bytes=56 * 2**20, collective_id=0, has_side_effects=True
        ),
        cost_estimate=pl.CostEstimate(
            flops=rows_here * (2 * (size + 2 * keys) * width * width + 16 * size * keys * width),
            bytes_accessed=2 * (3 * width * width + 9 * keys * width),
            transcendentals=rows_here * HEADS * size * keys,
        ),
    )(x, seg_ids, valid, b_query, b_value, w_query, w_key, w_value)


def gelu_both(u):
    size = jnp.abs(u)
    t = 1.0 / (1.0 + (0.3275911 * 0.5**0.5) * size)
    bell = jnp.exp(-0.5 * u * u)
    poly = t * (
        0.127414796 + t * (-0.142248368 + t * (0.7107068705 + t * (-0.7265760135 + t * 0.5307027145)))
    )
    tail = poly * bell
    cdf = jnp.where(u >= 0.0, 1.0 - tail, tail)
    return u * cdf, cdf + u * bell * 0.3989422804014327


def normalize(values_in):
    centre = jnp.mean(values_in, axis=-1, keepdims=True)
    centred = values_in - centre
    spread = jnp.mean(centred * centred, axis=-1, keepdims=True)
    scale = lax.rsqrt(spread + eps)
    return centred * scale, scale


def normalize_back(grad, unit, scale):
    mean_one = jnp.mean(grad, axis=-1, keepdims=True)
    mean_two = jnp.mean(grad * unit, axis=-1, keepdims=True)
    return (grad - mean_one - unit * mean_two) * scale


def column_sum(values_in):
    return jnp.sum(values_in, axis=0, keepdims=True)


B_QUERY, B_VALUE, B_OUT, GAIN_ONE, SHIFT_ONE, B_DOWN, GAIN_TWO, SHIFT_TWO, B_UP = range(9)


def middle_kernel(
    fused,
    x_ref, context_ref, ids_ref, b_out, gain_one, shift_one, b_up, b_down, gain_two, shift_two,
    text_ref, w_out, up_hbm, down_hbm,
    pool_out, count_out, vector_out, grad_out, mixed_out, wo_out, final_hbm, up_out, down_out, far_out,
    vec_ref, w_up, w_down, unit_ref, scale_ref, normed_ref, normed_t, act_ref, slope_ref, acc_ref, pre_one,
    g_ref, g_t_ref, upg_ref, up_got, downg_ref, down_got, wo_sent, wo_got, down_y, down_x,
    send_sem, recv_sem, load_sem, store_sem,
):
    rows_here, size, width = x_ref.shape
    tokens = rows_here * size
    parts = w_up.shape[1] // width
    half = width // 2
    low = jnp.bfloat16
    f32 = jnp.float32
    me = lax.axis_index("ctx")
    core = me % 2
    near = {"ctx": me + 1 - 2 * core}
    side = me // 2
    place = lax.axis_index("dp")
    y = place % 2
    y_dev = {"dp": place + 1 - 2 * y}
    across_dev = {"ctx": (me + 2) % 4}
    peers = [near, across_dev, y_dev] if fused else [near]
    barrier = pltpu.get_barrier_semaphore()
    for peer in peers:
        pl.semaphore_signal(barrier, inc=1, device_id=peer, device_id_type=MESH)
    for row, source in (
        (B_OUT, b_out), (GAIN_ONE, gain_one), (SHIFT_ONE, shift_one), (B_DOWN, b_down),
        (GAIN_TWO, gain_two), (SHIFT_TWO, shift_two),
    ):
        vec_ref[row : row + 1, :] = source[...].astype(f32)[None]
    for i in range(parts):
        vec_ref[B_UP + i : B_UP + i + 1, :] = (
            b_up[i * width : (i + 1) * width].astype(f32)[None]
        )

    def vec(row):
        return vec_ref[row : row + 1, :]

    loads = []
    for i in range(parts):
        loads.append(
            (
                pltpu.make_async_copy(
                    up_hbm.at[:, pl.ds(i * width, width)],
                    w_up.at[:, pl.ds(i * width, width)],
                    load_sem.at[0, i],
                ),
                pltpu.make_async_copy(
                    down_hbm.at[pl.ds(i * width, width)],
                    w_down.at[pl.ds(i * width, width)],
                    load_sem.at[1, i],
                ),
            )
        )
    for pair in loads:
        for item in pair:
            item.start()

    def rows_of(r):
        return pl.ds(pl.multiple_of(r * size, size), size)

    text = lax.broadcasted_iota(jnp.int32, (NSEG, size), 0)

    def members(j, r):
        seg = ids_ref[j, r : r + 1, :]
        real = ids_ref[j, rows_here + r : rows_here + r + 1, :]
        return jnp.where((text == seg) & (real == 1), 1.0, 0.0)

    for r in range(rows_here):
        number = sum(jnp.sum(members(j, r), axis=1, keepdims=True) for j in range(4))
        count_out[r * NSEG : (r + 1) * NSEG, :] = jnp.maximum(number, 1.0)

    def first_norm(r, carry):
        rows = rows_of(r)
        mixed = x_ref[r].astype(f32) + (matmul(context_ref[r], w_out[...]) + vec(B_OUT))
        unit, scale = normalize(mixed)
        unit_ref[rows, :] = unit
        scale_ref[rows, :] = scale
        normed_ref[rows, :] = (unit * vec(GAIN_ONE) + vec(SHIFT_ONE)).astype(low)
        return carry

    lax.fori_loop(0, rows_here, first_norm, 0)
    for pair in loads:
        for item in pair:
            item.wait()

    def units(i):
        return pl.ds(pl.multiple_of(i * width, width), width)

    def forward_part(i, following, now, then):
        for r in range(rows_here):
            rows = pl.ds(r * size, size)
            then[rows, :] = matmul(normed_ref[rows, :], w_up[:, units(following)])
            act, slope = gelu_both(now[rows, :] + vec_ref[pl.ds(B_UP + i, 1), :])
            act_ref[rows, units(i)] = act.astype(low)
            slope_ref[rows, units(i)] = slope.astype(low)

    def forward_parts(n, carry):
        forward_part(2 * n, 2 * n + 1, pre_one, acc_ref)
        forward_part(2 * n + 1, jnp.minimum(2 * n + 2, parts - 1), acc_ref, pre_one)
        return carry

    pre_one[...] = matmul(normed_ref[...], w_up[:, units(0)])
    lax.fori_loop(0, parts // 2, forward_parts, 0)

    def forward_sum(r, carry):
        acc_ref[rows_of(r), :] = matmul(act_ref[rows_of(r), :], w_down[...])
        return carry

    lax.fori_loop(0, rows_here, forward_sum, 0)

    normed_t[...] = normed_ref[...].T

    store_final = []
    vector_out[...] = jnp.zeros_like(vector_out)
    for r in range(rows_here):
        rows = pl.ds(r * size, size)
        normed = unit_ref[rows, :] * vec(GAIN_ONE) + vec(SHIFT_ONE)
        summed = normed + (acc_ref[rows, :] + vec(B_DOWN))
        unit, scale = normalize(summed)
        final = unit * vec(GAIN_TWO) + vec(SHIFT_TWO)
        high = final.astype(low)
        upg_ref[parts - 1, rows, :] = high
        item = pltpu.make_async_copy(
            upg_ref.at[parts - 1, rows], final_hbm.at[r], store_sem.at[r]
        )
        item.start()
        store_final.append(item)
        own = members(0, r)
        own_low = own.astype(low)
        rest = (final - high.astype(f32)).astype(low)
        pool = matmul(own_low, high) + matmul(own_low, rest)
        pool_out[r * NSEG : (r + 1) * NSEG, :] = pool.astype(low)
        share = text_ref[r] / count_out[r * NSEG : (r + 1) * NSEG, :]
        first = share.astype(low)
        second = (share - first.astype(f32)).astype(low)
        third = (share - first.astype(f32) - second.astype(f32)).astype(low)
        grad = dot_tn(
            jnp.concatenate([own_low] * 3, axis=0), jnp.concatenate([first, second, third], axis=0)
        )
        back = normalize_back(grad * vec(GAIN_TWO), unit, scale)
        back_low = back.astype(low)
        acc_ref[rows, :] = back
        g_ref[rows, :] = back_low
        vector_out[GAIN_TWO : GAIN_TWO + 1, :] += column_sum(grad * unit)
        vector_out[SHIFT_TWO : SHIFT_TWO + 1, :] += column_sum(grad)
        vector_out[B_DOWN : B_DOWN + 1, :] += column_sum(back_low.astype(f32))

    pl.semaphore_wait(barrier, len(peers))

    def remote(source, target, slot, device=near):
        return pltpu.make_async_remote_copy(
            src_ref=source, dst_ref=target, send_sem=send_sem.at[slot],
            recv_sem=recv_sem.at[slot], device_id=device, device_id_type=MESH,
        )

    per_part = downg_ref.shape[0] // parts
    mine = parts // 2

    def up_send(i):
        return remote(upg_ref.at[i], up_got.at[i], i)

    def down_send(i):
        chunk = pl.ds(i * per_part, per_part)
        return remote(downg_ref.at[chunk, 1 - core], down_got.at[chunk], parts + i)

    cut = downg_ref.shape[3]

    def down_part(i, carry):
        part = matmul(g_t_ref[...], act_ref[:, units(i)]).astype(low)
        part = part.reshape((2, width // 2, width))
        for n in range(per_part):
            downg_ref[per_part * i + n] = part[:, :, n * cut : (n + 1) * cut]
        down_send(i).start()
        return carry

    g_t_ref[...] = g_ref[...].T
    lax.fori_loop(0, parts, down_part, 0)

    def backward_part(step, carry):
        i = (step + mine * (1 - core)) % parts
        back = dot_nt(g_ref[...], w_down[units(i), :])
        back = (back * slope_ref[:, units(i)].astype(f32)).astype(low)
        slope_ref[:, units(i)] = back
        vector_out[pl.ds(B_UP + i, 1), :] = column_sum(back.astype(f32))
        upg_ref[step] = matmul(normed_t[...], back).astype(low)

        @pl.when(step < mine)
        def _():
            up_send(step).start()

        return carry

    def down_sum(i, carry):
        downg_ref[i, core] = (
            downg_ref[i, core].astype(f32) + down_got[i].astype(f32)
        ).astype(low)
        return carry

    piece = downg_ref.shape[2] // 2
    quarter = piece // 2
    rest = pl.ds(pl.multiple_of(piece + quarter * (1 - side), 16), quarter)
    kept = pl.ds(pl.multiple_of(piece + quarter * side, 16), quarter)
    down_moves = []
    if fused:
        for n in range(4):
            down_moves.append(
                remote(
                    downg_ref.at[2 * n + 1 - y, core, pl.ds(0, piece)], down_y.at[n],
                    2 * parts + 1 + n, y_dev,
                )
            )
        for n in range(8):
            down_moves.append(
                remote(
                    downg_ref.at[n, core, rest], down_x.at[n], 2 * parts + 5 + n, across_dev
                )
            )
    lax.fori_loop(0, 1, backward_part, 0)
    for i in range(parts):
        down_send(i).wait_recv()
    lax.fori_loop(0, downg_ref.shape[0], down_sum, 0)
    for item in down_moves:
        item.start()
    for item in store_final:
        item.wait()
    lax.fori_loop(1, parts, backward_part, 0)

    def first_back(r, carry):
        rows = rows_of(r)
        unit = unit_ref[rows, :]
        grad = acc_ref[rows, :] + dot_nt(slope_ref[rows, :], w_up[...])
        back = normalize_back(grad * vec(GAIN_ONE), unit, scale_ref[rows, :])
        back_low = back.astype(low)
        mixed_out[r] = back
        g_ref[rows, :] = back_low
        vector_out[GAIN_ONE : GAIN_ONE + 1, :] += column_sum(grad * unit)
        vector_out[SHIFT_ONE : SHIFT_ONE + 1, :] += column_sum(grad)
        vector_out[B_OUT : B_OUT + 1, :] += column_sum(back_low.astype(f32))
        return carry

    lax.fori_loop(0, rows_here, first_back, 0)

    for r in range(rows_here):
        g_t_ref[:, r * size : (r + 1) * size] = context_ref[r].T

    def out_part(h):
        columns = pl.ds(pl.multiple_of(h * half, 128), half)
        return matmul(g_t_ref[...], g_ref[:, columns])

    wo_sent[...] = out_part(1 - core).astype(low)
    wo_send = remote(wo_sent, wo_got, 2 * parts)
    wo_send.start()

    def grad_context(r, carry):
        grad_out[r] = dot_nt(g_ref[rows_of(r), :], w_out[...]).astype(low)
        return carry

    lax.fori_loop(0, rows_here, grad_context, 0)
    own_part = out_part(core)
    for i in range(mine):
        up_send(i).wait_recv()

    def up_sum(n, carry):
        rows = pl.ds(pl.multiple_of(n * 128, 128), 128)
        for i in range(mine):
            upg_ref[mine + i, rows, :] = (
                upg_ref[mine + i, rows, :].astype(f32) + up_got[i, rows, :].astype(f32)
            ).astype(low)
        return carry

    lax.fori_loop(0, width // 128, up_sum, 0)
    store_up = pltpu.make_async_copy(
        upg_ref.at[pl.ds(mine, mine)], up_out, store_sem.at[rows_here + 1]
    )
    store_up.start()
    wo_send.wait_recv()
    wo_out[...] = (own_part + wo_got[...].astype(f32)).astype(low)
    if fused:
        for item in down_moves:
            item.wait_recv()

        def near_sum(n, carry):
            down_y[n] = (
                downg_ref[2 * n + y, core, 0:piece, :].astype(f32) + down_y[n].astype(f32)
            ).astype(low)
            return carry

        def far_sum(n, carry):
            down_x[n] = (
                downg_ref[n, core, kept, :].astype(f32) + down_x[n].astype(f32)
            ).astype(low)
            return carry

        lax.fori_loop(0, 4, near_sum, 0)
        lax.fori_loop(0, 8, far_sum, 0)
        stores = [
            pltpu.make_async_copy(down_y, down_out, store_sem.at[rows_here]),
            pltpu.make_async_copy(down_x, far_out, store_sem.at[rows_here + 2]),
        ]
    else:
        stores = [
            pltpu.make_async_copy(downg_ref.at[:, core], down_out, store_sem.at[rows_here])
        ]
    for item in stores:
        item.start()
    for i in range(parts):
        down_send(i).wait_send()
    for i in range(mine):
        up_send(i).wait_send()
    wo_send.wait_send()
    for item in down_moves:
        item.wait_send()
    for item in stores + [store_up]:
        item.wait()


def middle(fused, x, context, ids, vectors, text_gradient, w_out, w_up, w_down, dp_size):
    rows_here, size, width = x.shape
    ff = w_up.shape[1]
    parts = ff // width
    tokens = rows_here * size
    low = jnp.bfloat16
    f32 = jnp.float32
    shape = jax.ShapeDtypeStruct
    whole = pl.BlockSpec(memory_space=pltpu.VMEM)
    outside = pl.BlockSpec(memory_space=pl.ANY)
    chunks = dp_size if fused else parts
    chunk = ff // chunks
    vec = (8 + parts + (-parts) % 8, width)
    if fused:
        down_shape, far_shape = (4, width // 4, chunk), (8, width // 8, chunk)
    else:
        down_shape, far_shape = (chunks, width // 2, chunk), (8, 16, 128)
    return pl.pallas_call(
        functools.partial(middle_kernel, fused),
        out_shape=(
            shape((rows_here * NSEG, width), low),
            shape((rows_here * NSEG, 1), f32),
            shape(vec, f32),
            shape((rows_here, size, width), low),
            shape((rows_here, size, width), f32),
            shape((width, width // 2), low),
            shape((rows_here, size, width), low),
            shape((parts // 2, width, width), low),
            shape(down_shape, low),
            shape(far_shape, low),
        ),
        in_specs=[whole] * 12 + [outside] * 2,
        out_specs=(whole,) * 6 + (outside,) * 4,
        scratch_shapes=[
            pltpu.VMEM(vec, f32),
            pltpu.VMEM((width, ff), low),
            pltpu.VMEM((ff, width), low),
            pltpu.VMEM((tokens, width), f32),
            pltpu.VMEM((tokens, 1), f32),
            pltpu.VMEM((tokens, width), low),
            pltpu.VMEM((width, tokens), low),
            pltpu.VMEM((tokens, ff), low),
            pltpu.VMEM((tokens, ff), low),
            pltpu.VMEM((tokens, width), f32),
            pltpu.VMEM((tokens, width), f32),
            pltpu.VMEM((tokens, width), low),
            pltpu.VMEM((width, tokens), low),
            pltpu.VMEM((parts, width, width), low),
            pltpu.VMEM((parts // 2, width, width), low),
            pltpu.VMEM((chunks, 2, width // 2, chunk), low),
            pltpu.VMEM((chunks, width // 2, chunk), low),
            pltpu.VMEM((width, width // 2), low),
            pltpu.VMEM((width, width // 2), low),
            pltpu.VMEM(down_shape if fused else (16, 128), low),
            pltpu.VMEM(far_shape, low),
            pltpu.SemaphoreType.DMA((2 * parts + 13,)),
            pltpu.SemaphoreType.DMA((2 * parts + 13,)),
            pltpu.SemaphoreType.DMA((2, parts)),
            pltpu.SemaphoreType.DMA((rows_here + 3,)),
        ],
        compiler_params=pltpu.CompilerParams(
            vmem_limit_bytes=63 * 2**20, collective_id=2, has_side_effects=True
        ),
        cost_estimate=pl.CostEstimate(
            flops=2 * tokens * width * (6 * ff + 3 * width),
            bytes_accessed=2 * (5 * ff * width + 8 * tokens * width),
            transcendentals=2 * tokens * ff,
        ),
    )(x, context, ids, *vectors, text_gradient, w_out, w_up, w_down)


class Links:
    def __init__(self, send_sem, recv_sem):
        self.send_sem, self.recv_sem = send_sem, recv_sem
        self.slots, self.copies = {}, {}

    def start(self, name, source, target, device):
        slot = self.slots.setdefault(name, len(self.slots))
        copy = pltpu.make_async_remote_copy(
            src_ref=source, dst_ref=target, send_sem=self.send_sem.at[slot],
            recv_sem=self.recv_sem.at[slot], device_id=device, device_id_type=MESH,
        )
        copy.start()
        self.copies[name] = copy

    def arrived(self, *names):
        for name in names:
            self.copies[name].wait_recv()

    def finish(self):
        for copy in self.copies.values():
            copy.wait_send()


def add_into(target, others, count):
    def one(i, carry):
        total = target[i].astype(jnp.float32)
        for other in others:
            total = total + other[i].astype(jnp.float32)
        target[i] = total.astype(target.dtype)
        return carry

    lax.fori_loop(0, count, one, 0)


def add_up(parts):
    total = parts[0].astype(jnp.float32)
    for part in parts[1:]:
        total = total + part.astype(jnp.float32)
    return total


POOL, UP, DOWN_A, DOWN_B, DOWN, OUT, GROUP, DX, VECTOR = range(9)
STEP, NEAR, FAR, SIDE, LINE, GATHER = range(6)

GROUPS = ((0, 4 * PAIR), (4 * PAIR, PAIR), (5 * PAIR, PAIR))


def attend_back_kernel(
    fused, count_out, out_tree, tree,
    x_ref, ids_ref, lse_ref, w_query, w_key, w_value, pool_ref, count_ref, vector_ref,
    x_hbm, q_hbm, k_hbm, v_hbm, context_hbm, grad_hbm, mixed_hbm, up_ref, down_ref, far_ref, out_ref,
    dx_out, pool_out, vector_out, *rest,
):
    outs = types.SimpleNamespace(**jax.tree.unflatten(out_tree, rest[:count_out]))
    ref = types.SimpleNamespace(**jax.tree.unflatten(tree, rest[count_out:]))
    square_out, up_out, down_out, wo_out = outs.square, outs.up, outs.down, outs.wo
    q_ref, k_ref, v_ref, context_ref, grad_ref = ref.q, ref.k, ref.v, ref.context, ref.grad
    dq_ref, dk_ref, dv_ref, x_t, x_got = ref.dq, ref.dk, ref.dv, ref.x_t, ref.x_got
    extra_ref, penal_ref, delta_ref = ref.extra, ref.penal, ref.delta
    dx_acc, dx_sent, dx_far, dx_got, dx_far_got = (
        ref.dx_acc, ref.dx_sent, ref.dx_far, ref.dx_got, ref.dx_far_got
    )
    pool_parts, pool_got, vec_parts, vec_got = (
        ref.pool_parts, ref.pool_got, ref.vec_parts, ref.vec_got
    )
    row_sem, local_sem = ref.row_sem, ref.local_sem
    rows_here, size, width = x_ref.shape
    low = jnp.bfloat16
    me, place = lax.axis_index("ctx"), lax.axis_index("dp")
    core, side = me % 2, me // 2
    near, across = me + 1 - 2 * core, (me + 2) % 4
    near_dev, across_dev = {"ctx": near}, {"ctx": across}
    y, z = place % 2, place // 2
    y_dev = {"dp": place + 1 - 2 * y}
    z_at = (z + 1 - 2 * (z % 2), (z + 2) % 4, 3 - z)
    z_dev = [{"dp": other * 2 + y} for other in z_at]
    peers = [near_dev, across_dev] + ([y_dev] + z_dev if fused else [])

    barrier = pltpu.get_barrier_semaphore()
    for peer in peers:
        pl.semaphore_signal(barrier, inc=1, device_id=peer, device_id_type=MESH)
    pl.semaphore_wait(barrier, len(peers))
    links = Links(ref.send_sem, ref.recv_sem)

    first_cut = GROUPS[1][0]
    blocks = [(0, first_cut, r) for r in range(rows_here)]
    blocks += [(first_cut, width - first_cut, r) for r in range(rows_here)]

    def load_block(step):
        slot = step % 2
        start, count, r = blocks[step]
        columns, local = pl.ds(start, count), pl.ds(0, count)
        pairs = (
            (k_hbm, k_ref), (v_hbm, v_ref), (q_hbm, q_ref), (context_hbm, context_ref),
            (grad_hbm, grad_ref),
        )
        copies = [
            pltpu.make_async_copy(
                source.at[r, :, columns], target.at[slot, :, local], row_sem.at[slot, i]
            )
            for i, (source, target) in enumerate(pairs)
        ]
        if step < rows_here:
            copies.append(pltpu.make_async_copy(x_hbm.at[:, r], x_got.at[slot], row_sem.at[slot, 5]))
        return copies

    for item in load_block(0):
        item.start()
    load_mixed = pltpu.make_async_copy(mixed_hbm, dx_acc, local_sem.at[0])
    links.start((POOL, STEP, 0), pool_ref, pool_got.at[0], near_dev)
    if fused:
        u_ref, u_x, u_y, u_z = ref.u, ref.u_x, ref.u_y, ref.u_z
        a_z, a_s, a_x = ref.a_z, ref.a_s, ref.a_x
        b_ref, b_y, b_z = ref.b, ref.b_y, ref.b_z
        o_ref, o_y, o_z, o_s, o_x = ref.o, ref.o_y, ref.o_z, ref.o_s, ref.o_x
        half_rows = u_ref.shape[2] // 2
        links.start((UP, FAR, 0), up_ref.at[1 - side, :, :, pl.ds(0, half_rows)], u_x.at[0], across_dev)
        links.start((DOWN_B, SIDE), far_ref.at[:, 1 - y], b_y, y_dev)
        for o in range(3):
            links.start((DOWN_A, LINE, o), down_ref.at[z_at[o]], a_z.at[o], z_dev[o])
    load_mixed.start()
    vec_parts[0] = vector_ref[...]

    def pool_one():
        links.arrived((POOL, STEP, 0))
        pool_parts[...] = add_up([pool_ref[...], pool_got[0]]).astype(low)
        links.start((POOL, STEP, 1), pool_parts, pool_got.at[1], across_dev)

    def pool_two():
        links.arrived((POOL, STEP, 1))
        pool_out[...] = add_up([pool_parts[...], pool_got[1]]) / count_ref[...]

    def send_z(name, source, target):
        for o in range(3):
            links.start(name + (o,), source(z_at[o]), target(o), z_dev[o])

    def arrived_z(name):
        links.arrived(*(name + (o,) for o in range(3)))

    def out_y():
        links.start((OUT, SIDE), out_ref.at[:, 1 - y], o_y, y_dev)

    def out_z():
        links.arrived((OUT, SIDE))
        for i in range(4):
            o_ref[i] = add_up([out_ref[i, y], o_y[i]]).astype(low)
        send_z((OUT, LINE), lambda i: o_ref.at[i], lambda o: o_z.at[o])

    def out_far():
        arrived_z((OUT, LINE))
        o_s[...] = add_up([o_ref[z]] + [o_z[o] for o in range(3)]).astype(low)
        links.start((OUT, FAR), o_s, o_x, across_dev)

    def out_end():
        links.arrived((OUT, FAR))
        wo_out[core] = add_up([o_s[...], o_x[...]]).astype(low)
        links.start((OUT, GATHER), wo_out.at[core], wo_out.at[core], near_dev)

    def down_z():
        links.arrived((DOWN_B, SIDE))
        for i in range(4):
            b_ref[i] = add_up([far_ref[i, y], b_y[i]]).astype(low)
        send_z((DOWN_B, LINE), lambda i: b_ref.at[i], lambda o: b_z.at[o])

    def down_near_far():
        arrived_z((DOWN_A, LINE))
        a_s[...] = add_up([down_ref[z]] + [a_z[o] for o in range(3)]).astype(low)
        links.start((DOWN_A, FAR), a_s, a_x, across_dev)

    def down_far():
        arrived_z((DOWN_B, LINE))
        count = b_ref.shape[1]
        own = pl.ds(pl.multiple_of(2 * count + side * count, 16), count)
        down_out[core, own] = add_up([b_ref[z]] + [b_z[o] for o in range(3)]).astype(low)
        links.start((DOWN_B, FAR), down_out.at[core, own], down_out.at[core, own], across_dev)

    def down_end():
        links.arrived((DOWN_A, FAR), (DOWN_B, FAR))
        down_out[core, 0 : a_s.shape[0]] = add_up([a_s[...], a_x[...]]).astype(low)
        links.start((DOWN, GATHER), down_out.at[core], down_out.at[core], near_dev)

    def up_x():
        rows = pl.ds(half_rows, half_rows)
        links.start((UP, FAR, 1), up_ref.at[1 - side, :, :, rows], u_x.at[1], across_dev)

    def up_y(h):
        rows = pl.ds(h * half_rows, half_rows)
        links.arrived((UP, FAR, h))
        for i in range(4):
            for j in range(2):
                u_ref[i, j, rows] = add_up([up_ref[side, i, j, rows], u_x[h, i, j]]).astype(low)
        links.start((UP, SIDE, h), u_ref.at[:, 1 - y, rows], u_y.at[h], y_dev)

    def up_z(h):
        rows = pl.ds(h * half_rows, half_rows)
        links.arrived((UP, SIDE, h))
        for i in range(4):
            u_ref[i, y, rows] = add_up([u_ref[i, y, rows], u_y[h, i]]).astype(low)
        send_z((UP, LINE, h), lambda i: u_ref.at[i, y, rows], lambda o: u_z.at[o, rows])

    def up_far():
        arrived_z((UP, LINE, 0))
        arrived_z((UP, LINE, 1))
        up_out[me] = add_up([u_ref[z, y]] + [u_z[o] for o in range(3)]).astype(low)
        links.start((UP, GATHER), up_out.at[me], up_out.at[me], across_dev)

    def up_end():
        links.arrived((UP, GATHER))
        links.start((UP, NEAR, 0), up_out.at[me], up_out.at[me], near_dev)
        links.start((UP, NEAR, 1), up_out.at[across], up_out.at[across], near_dev)

    def group_core(g):
        links.start((GROUP, NEAR, g), ref.g[g].at[1 - core], ref.g_got[g], near_dev)

    def group_y(g):
        links.arrived((GROUP, NEAR, g))
        for i in range(4):
            add_into(ref.g[g].at[core, i], [ref.g_got[g].at[i]], 2)
        links.start((GROUP, SIDE, g), ref.g[g].at[core, :, 1 - y], ref.g_y[g], y_dev)

    def group_z(g):
        links.arrived((GROUP, SIDE, g))
        own = ref.g[g]
        for i in range(4):
            own[core, i, y] = add_up([own[core, i, y], ref.g_y[g][i]]).astype(low)
        send_z((GROUP, LINE, g), lambda i: own.at[core, i, y], lambda o: ref.g_z[g].at[o])

    def group_far(g):
        arrived_z((GROUP, LINE, g))
        pieces = [ref.g[g][core, z, y]] + [ref.g_z[g][o] for o in range(3)]
        ref.g_s[g][...] = add_up(pieces).astype(low)
        links.start((GROUP, FAR, g), ref.g_s[g], ref.g_x[g], across_dev)

    def group_end(g):
        links.arrived((GROUP, FAR, g))
        out = outs.squares[g]
        out[core] = add_up([ref.g_s[g][...], ref.g_x[g][...]]).astype(low)
        links.start((GROUP, GATHER, g), out.at[core], out.at[core], near_dev)

    def vector_step(i, device):
        if i:
            links.arrived((VECTOR, STEP, i - 1))
            vec_parts[i] = vec_parts[i - 1] + vec_got[i - 1]
        if device is not None:
            links.start((VECTOR, STEP, i), vec_parts.at[i], vec_got.at[i], device)

    def vector_z():
        vector_step(3, None)
        for o in range(3):
            links.start((VECTOR, LINE, o), vec_parts.at[3], vec_got.at[3 + o], z_dev[o])

    def vector_end():
        arrived_z((VECTOR, LINE))
        vector_out[...] = vec_parts[3] + (vec_got[3] + (vec_got[4] + vec_got[5]))

    row = lax.broadcasted_iota(jnp.int32, (PAIR, size), 0)

    def find_delta(step):
        slot = step % 2
        start, count, _ = blocks[step]
        lane = lax.broadcasted_iota(jnp.int32, (count, PAIR), 1)
        head = (start + lax.broadcasted_iota(jnp.int32, (count, PAIR), 0)) // HEAD_DIM
        member = jnp.where((lane % NSEG == head) & (lane >= NSEG) & (lane < 4 * NSEG), 1.0, 0.0)
        member = member.astype(low)
        local = pl.ds(0, count)
        product = grad_ref[slot, :, local].astype(jnp.float32) * context_ref[
            slot, :, local
        ].astype(jnp.float32)
        total = jnp.zeros((size, PAIR), jnp.float32)
        for _ in range(3):
            term = product.astype(low)
            total = total + matmul(term, member)
            product = product - term.astype(jnp.float32)
        delta_ref[...] = with_constants(jnp.zeros_like(total), -total)

    def attend_pairs(step, first, last):
        slot = step % 2
        start, _, r = blocks[step]

        def one_pair(n, carry):
            local = pl.ds(pl.multiple_of(n * PAIR, PAIR), PAIR)
            columns = pl.ds(pl.multiple_of(start + n * PAIR, PAIR), PAIR)
            head = 2 * (start // PAIR + n)
            q_both = split_heads(q_ref[slot, :, local])
            g_both = split_heads(grad_ref[slot, :, local])
            q_extra = [of_head(penal_ref[r], head + h) for h in range(2)]
            g_extra = [of_head(delta_ref[...], head + h) for h in range(2)]
            q_wide = jnp.concatenate([q_both, jnp.concatenate(q_extra, axis=0)], axis=1)
            g_wide = jnp.concatenate([g_both, jnp.concatenate(g_extra, axis=0)], axis=1)
            q_wide, g_wide = q_wide.T, g_wide.T
            dq = jnp.zeros((PAIR, 2 * size), jnp.float32)

            def products(j):
                rows = pl.ds(j * size, size)
                extra = extra_ref[r, rows, :]
                keys = jnp.concatenate([k_ref[slot, rows, local], extra], axis=1)
                values = jnp.concatenate([v_ref[slot, rows, local], extra], axis=1)
                return matmul(keys, q_wide), matmul(values, g_wide)

            ahead = products(0)
            for j in range(4):
                rows = pl.ds(j * size, size)
                scores, grad_p = ahead
                if j < 3:
                    ahead = products(j + 1)
                probs = jnp.exp(scores)
                grad_s = (probs * grad_p).astype(low)
                dv_ref[r, rows, columns] = matmul(probs.astype(low), g_both).astype(low)
                dk_ref[r, rows, columns] = matmul(grad_s, q_both).astype(low)
                dq = dq + matmul(k_ref[slot, rows, local].T, grad_s)
            dq = jnp.where(row < HEAD_DIM, dq[:, :size], dq[:, size:]) * HEAD_DIM ** (-0.5)
            dq_ref[r, :, columns] = dq.T.astype(low)
            return carry

        lax.fori_loop(first, last, one_pair, 0)

    def weight_group(g):
        start, count = GROUPS[g]
        if fused:
            depth = ref.g[g].shape[3]

        def keep(n, i, total):
            total = total.astype(low)
            wide = total.shape[1]
            if not fused:
                square_out[n, :, pl.ds(pl.multiple_of(start + i * PAIR, PAIR), wide)] = total
                return
            total = total.reshape(4, 2, 2, depth, wide)
            target = pl.ds(pl.multiple_of(n * count + i * PAIR, PAIR), wide)
            for h in range(2):
                ref.g[g][h, :, :, :, target] = total[:, :, h]

        def of_source(source, columns):
            keys = source.shape[1]
            return sum(
                matmul(x_t[r, :, :keys], source[r, :, columns]) for r in range(rows_here)
            )

        def one_part(i, carry):
            columns = pl.ds(pl.multiple_of(start + 2 * i * PAIR, PAIR), 2 * PAIR)
            for n, source in enumerate((dq_ref, dk_ref, dv_ref)):
                keep(n, 2 * i, of_source(source, columns))
            return carry

        if count % (2 * PAIR):
            columns = pl.ds(start, count)
            keep(0, 0, of_source(dq_ref, columns))
            both = sum(
                matmul(
                    x_t[r],
                    jnp.concatenate([dk_ref[r, :, columns], dv_ref[r, :, columns]], axis=1),
                )
                for r in range(rows_here)
            )
            keep(1, 0, both[:, :count])
            keep(2, 0, both[:, count:])
        else:
            lax.fori_loop(0, count // (2 * PAIR), one_part, 0)
        columns = pl.ds(start, count)
        for n, source in enumerate((dq_ref, dv_ref)):
            vec_parts[0, n : n + 1, columns] = sum(
                jnp.sum(source[r, :, columns].astype(jnp.float32), axis=0, keepdims=True)
                for r in range(rows_here)
            )

    def input_parts(r):
        for j in (3, 2, 1, 0):
            rows = pl.ds(j * size, size)
            total = dot_nt(dk_ref[r, rows, :], w_key[...]) + dot_nt(dv_ref[r, rows, :], w_value[...])
            if j == 0:
                dx_acc[r] = dx_acc[r] + total + dot_nt(dq_ref[r], w_query[...])
            elif j == 2:
                dx_far[r] = total.astype(low)
            else:
                n = j // 2
                dx_sent[r, n] = total.astype(low)
                links.start((DX, NEAR, r, n), dx_sent.at[r, n], dx_got.at[r, n], near_dev)

    def input_far(r):
        links.arrived((DX, NEAR, r, 1))
        dx_far[r] = add_up([dx_far[r], dx_got[r, 1]]).astype(low)
        links.start((DX, FAR, r), dx_far.at[r], dx_far_got.at[r], across_dev)

    def input_done(r):
        links.arrived((DX, NEAR, r, 0), (DX, FAR, r))
        dx_out[r] = add_up([dx_acc[r], dx_got[r, 0], dx_far_got[r]]).astype(low)

    def prepare_row(r):
        slot = r % 2
        for j in range(4):
            rows = slice(j * size, (j + 1) * size)
            texts = text_rows(ids_ref[j, r : r + 1, :], size)
            extra_ref[r, rows, :] = key_extra(texts)
            if j == 0:
                penal_ref[r] = with_constants(query_extra(texts), -lse_ref[r])
            block = x_ref[r] if j == 0 else x_got[slot, j - 1]
            x_t[r, :, rows] = block.T

    def begin(step):
        for item in load_block(step):
            item.wait()
        if step + 1 < len(blocks):
            for item in load_block(step + 1):
                item.start()
        find_delta(step)

    def do(*actions):
        if fused:
            for action, *given in actions:
                action(*given)

    most = first_cut // PAIR
    begin(0)
    prepare_row(0)
    attend_pairs(0, 0, most // 2)
    attend_pairs(0, most // 2, most)
    do((pool_one,))
    begin(1)
    prepare_row(1)
    attend_pairs(1, 0, most // 2)
    do((out_y,), (down_z,), (up_x,))
    attend_pairs(1, most // 2, most)
    do((pool_two,))
    begin(2)
    prepare_row(2)
    attend_pairs(2, 0, most // 2)
    do((up_y, 0), (out_z,))
    attend_pairs(2, most // 2, most)
    weight_group(0)
    do((group_core, 0), (down_near_far,), (up_y, 1))
    begin(3)
    attend_pairs(3, 0, 2)
    load_mixed.wait()
    input_parts(0)
    do((down_far,), (group_y, 0), (out_far,), (up_z, 1), (up_z, 0), (input_far, 0))
    begin(4)
    attend_pairs(4, 0, 2)
    input_parts(1)
    begin(5)
    attend_pairs(5, 0, 1)
    weight_group(1)
    do((group_core, 1), (input_far, 1))
    attend_pairs(5, 1, 2)
    do((group_z, 0))
    weight_group(2)
    do((group_core, 2), (vector_step, 0, near_dev))
    input_parts(2)
    if not fused:
        vector_out[...] = vec_parts[0]
        pool_one()
        for r in range(3):
            input_far(r)
        pool_two()
        for r in range(3):
            input_done(r)
        links.finish()
        return
    do((group_y, 2), (group_y, 1), (vector_step, 1, across_dev), (up_far,), (input_far, 2))
    do((group_z, 2), (down_end,), (out_end,), (vector_step, 2, y_dev), (up_end,), (group_z, 1))
    do((vector_z,), (group_far, 0), (group_far, 2), (group_far, 1), (input_done, 0))
    do((group_end, 0), (group_end, 2), (vector_end,), (group_end, 1), (input_done, 1))
    do((input_done, 2))
    links.arrived((DOWN, GATHER), (OUT, GATHER), (UP, NEAR, 0), (UP, NEAR, 1))
    links.arrived(*((GROUP, GATHER, g) for g in range(3)))
    links.finish()


def attend_back(
    fused, x, ids, lse, w_query, w_key, w_value, pool, counts, vectors,
    x_got, q, k, v, context, grad, mixed, up, down, far, out,
):
    rows_here, size, width = x.shape
    keys = size * 4
    low = jnp.bfloat16
    f32 = jnp.float32
    whole = pl.BlockSpec(memory_space=pltpu.VMEM)
    outside = pl.BlockSpec(memory_space=pl.ANY)
    shape = jax.ShapeDtypeStruct
    most = GROUPS[0][1]
    vec = vectors.shape
    small = shape((8, 128), low)
    if fused:
        depth = up.shape[3]
        outs = dict(
            squares=[shape((2, depth // 2, 3 * count), low) for _, count in GROUPS],
            up=shape((4, depth, width), low),
            down=shape((2, 2 * down.shape[1], down.shape[2]), low),
            wo=shape((2, depth, width // 2), low),
            square=small,
        )
    else:
        outs = dict(
            squares=[], up=small, down=small, wo=small, square=shape((3, width, width), low)
        )
    scratch = dict(
        x_got=pltpu.VMEM((2, 3, size, width), low),
        x_t=pltpu.VMEM((rows_here, width, keys), low),
        q=pltpu.VMEM((2, size, most), low),
        k=pltpu.VMEM((2, keys, most), low),
        v=pltpu.VMEM((2, keys, most), low),
        context=pltpu.VMEM((2, size, most), low),
        grad=pltpu.VMEM((2, size, most), low),
        extra=pltpu.VMEM((rows_here, keys, PAIR), low),
        penal=pltpu.VMEM((rows_here, size, PAIR), low),
        delta=pltpu.VMEM((size, PAIR), low),
        dq=pltpu.VMEM((rows_here, size, width), low),
        dk=pltpu.VMEM((rows_here, keys, width), low),
        dv=pltpu.VMEM((rows_here, keys, width), low),
        dx_acc=pltpu.VMEM((rows_here, size, width), f32),
        dx_sent=pltpu.VMEM((rows_here, 2, size, width), low),
        dx_far=pltpu.VMEM((rows_here, size, width), low),
        dx_got=pltpu.VMEM((rows_here, 2, size, width), low),
        dx_far_got=pltpu.VMEM((rows_here, size, width), low),
        pool_parts=pltpu.VMEM(pool.shape, low),
        pool_got=pltpu.VMEM((2,) + pool.shape, low),
        vec_parts=pltpu.VMEM((4,) + vec, f32),
        vec_got=pltpu.VMEM((6,) + vec, f32),
        send_sem=pltpu.SemaphoreType.DMA((72,)),
        recv_sem=pltpu.SemaphoreType.DMA((72,)),
        row_sem=pltpu.SemaphoreType.DMA((2, 6)),
        local_sem=pltpu.SemaphoreType.DMA((5,)),
    )
    if fused:
        tails = [(depth // 2, 3 * count) for _, count in GROUPS]
        spread = lambda *lead: [pltpu.VMEM(lead + tail, low) for tail in tails]
        b_shape = far.shape[2:]
        narrow = (depth, width // 2)
        scratch.update(
            g=spread(2, 4, 2), g_got=spread(4, 2), g_y=spread(4), g_z=spread(3),
            g_s=spread(), g_x=spread(),
            u=pltpu.VMEM((4, 2, depth, width), low),
            u_x=pltpu.VMEM((2, 4, 2, depth // 2, width), low),
            u_y=pltpu.VMEM((2, 4, depth // 2, width), low),
            u_z=pltpu.VMEM((3, depth, width), low),
            a_z=pltpu.VMEM((3,) + down.shape[1:], low),
            a_s=pltpu.VMEM(down.shape[1:], low),
            a_x=pltpu.VMEM(down.shape[1:], low),
            b=pltpu.VMEM((4,) + b_shape, low),
            b_y=pltpu.VMEM((4,) + b_shape, low),
            b_z=pltpu.VMEM((3,) + b_shape, low),
            o=pltpu.VMEM((4,) + narrow, low),
            o_y=pltpu.VMEM((4,) + narrow, low),
            o_z=pltpu.VMEM((3,) + narrow, low),
            o_s=pltpu.VMEM(narrow, low),
            o_x=pltpu.VMEM(narrow, low),
        )
    out_leaves, out_tree = jax.tree.flatten(outs)
    leaves, tree = jax.tree.flatten(scratch)
    count_out = len(out_leaves)
    got = pl.pallas_call(
        functools.partial(attend_back_kernel, fused, count_out, out_tree, tree),
        out_shape=(
            shape((rows_here, size, width), low),
            shape(pool.shape, f32),
            shape(vec, f32),
        )
        + tuple(out_leaves),
        in_specs=[whole] * 9 + [outside] * 7 + [whole] * 4,
        out_specs=(whole,) * (3 + count_out),
        scratch_shapes=leaves,
        compiler_params=pltpu.CompilerParams(
            vmem_limit_bytes=63 * 2**20, collective_id=1, has_side_effects=True
        ),
        cost_estimate=pl.CostEstimate(
            flops=rows_here
            * (4 * (size + 2 * keys) * width * width + 40 * size * keys * width),
            bytes_accessed=2 * (16 * width * width + 9 * keys * width),
            transcendentals=rows_here * HEADS * size * keys,
        ),
    )(
        x, ids, lse, w_query, w_key, w_value, pool, counts, vectors,
        x_got, q, k, v, context, grad, mixed, up, down, far, out,
    )
    return got[:3] + (types.SimpleNamespace(**jax.tree.unflatten(out_tree, got[3:])),)


def outputs_kernel(
    square0, square1, square2, wo, up, down, pool, final, dx,
    wq_out, wk_out, wv_out, wo_out, up_out, down_out, pool_out, final_out, dx_out,
):
    final_out[...] = final[...]
    dx_out[...] = dx[...]
    f32 = jnp.float32
    pool_out[...] = pool[...].reshape(pool_out.shape)
    for (start, count), square in zip(GROUPS, (square0, square1, square2)):
        rows = square.shape[1]
        for n, out in enumerate((wq_out, wk_out, wv_out)):
            for h in range(2):
                out[h * rows : (h + 1) * rows, start : start + count] = square[
                    h, :, n * count : (n + 1) * count
                ].astype(f32)
    for h in range(2):
        half = wo.shape[2]
        wo_out[:, h * half : (h + 1) * half] = wo[h].astype(f32)
        rows = down.shape[1]
        down_out[:, h * rows : (h + 1) * rows] = down[h].astype(f32).T
    for i in range(4):
        place, width = (i % 2) * 2 + i // 2, up.shape[2]
        up_out[:, place * width : (place + 1) * width] = up[i].astype(f32)


def outputs(squares, wo, up, down, pool, final, dx):
    f32 = jnp.float32
    whole = pl.BlockSpec(memory_space=pltpu.VMEM)
    shape = jax.ShapeDtypeStruct
    rows, width = up.shape[1:]
    row_count = final.shape[0]
    return pl.pallas_call(
        outputs_kernel,
        out_shape=(
            shape((rows, width), f32), shape((rows, width), f32), shape((rows, width), f32),
            shape((rows, width), f32), shape((rows, 4 * width), f32),
            shape((down.shape[2], 2 * down.shape[1]), f32),
            shape((row_count, pool.shape[0] // row_count, width), f32),
            shape(final.shape, final.dtype), shape(dx.shape, dx.dtype),
        ),
        in_specs=[whole] * 9,
        out_specs=(whole,) * 9,
        compiler_params=pltpu.CompilerParams(vmem_limit_bytes=63 * 2**20),
    )(*squares, wo, up, down, pool, final, dx)


def radices_of(count):
    if count == 8:
        return ((1, 2), (2, 4))
    digits = []
    stride = 1
    while stride < count:
        digits.append((stride, 2))
        stride *= 2
    return tuple(digits)


def exchange(piece, axis_name, stride, offset):
    count = lax.axis_size(axis_name)
    pairs = [(i, i ^ (offset * stride)) for i in range(count)]
    return lax.ppermute(piece, axis_name, pairs)


def digit_of(axis_name, stride, radix):
    return (lax.axis_index(axis_name) // stride) % radix


def scatter_digit(pieces, place, axis_name, stride, radix):
    here = digit_of(axis_name, stride, radix)
    received = [
        exchange(
            lax.dynamic_index_in_dim(pieces, here ^ offset, place, keepdims=False).astype(
                jnp.bfloat16
            ),
            axis_name, stride, offset,
        )
        for offset in range(1, radix)
    ]
    total = lax.dynamic_index_in_dim(pieces, here, place, keepdims=False).astype(jnp.float32)
    for item in received:
        total = total + item.astype(jnp.float32)
    return total.astype(jnp.bfloat16)


def halve(piece, place, axis_name, stride):
    half = piece.shape[place] // 2
    here = digit_of(axis_name, stride, 2)
    sent = lax.dynamic_slice_in_dim(piece, (1 - here) * half, half, place).astype(jnp.bfloat16)
    kept = lax.dynamic_slice_in_dim(piece, here * half, half, place).astype(jnp.float32)
    return (kept + exchange(sent, axis_name, stride, 1).astype(jnp.float32)).astype(jnp.bfloat16)


def join(piece, place, axis_name, stride):
    here = digit_of(axis_name, stride, 2)
    other = exchange(piece, axis_name, stride, 1)
    first = jnp.where(here == 0, piece, other)
    second = jnp.where(here == 0, other, piece)
    return jnp.concatenate([first, second], axis=place)


def scatter_rows(group, dp_size):
    digits = radices_of(dp_size)
    shape = tuple(r for _, r in reversed(digits))
    group = group.reshape(shape + (group.shape[0] // dp_size, group.shape[1]))
    for place, (stride, radix) in zip(range(len(digits) - 1, -1, -1), digits):
        group = scatter_digit(group, place, "dp", stride, radix)
    return group


def finish_weight(flat, dp_size, side):
    flat = scatter_rows(flat, dp_size)
    flat = flat.astype(jnp.float32) + exchange(flat, "ctx", 2, 1).astype(jnp.float32)
    return join(flat.astype(jnp.bfloat16), side, "ctx", 1).astype(jnp.float32)


def reduce_weight(gradient, dp_size, side):
    return finish_weight(halve(gradient, side, "ctx", 1), dp_size, side)


def per_device(
    hidden_in,
    seg_ids,
    valid,
    w_query,
    b_query,
    w_key,
    w_value,
    b_value,
    w_out,
    b_out,
    gain_attn,
    shift_attn,
    w_up,
    b_up,
    w_down,
    b_down,
    gain_ffn,
    shift_ffn,
    pooled_text_gradient,
):
    row_count, group_size, model_width = hidden_in.shape
    dp_size = lax.axis_size("dp")
    ff_width = w_up.shape[1]
    rows_here, ff_here = model_width // dp_size, ff_width // dp_size
    fused = dp_size == 8 and rows_here % 32 == 0 and ff_here % 128 == 0 and model_width % 128 == 0
    q_all, context, lse_all, ids_got, x_got, k_all, v_all = attend(
        hidden_in, seg_ids, valid, b_query, b_value, w_query, w_key, w_value
    )
    vectors = (b_out, gain_attn, shift_attn, b_up, b_down, gain_ffn, shift_ffn)
    pool, counts, vector_parts, grad_context, grad_mixed, out, final_out, up, down, far = middle(
        fused, hidden_in, context, ids_got, vectors, pooled_text_gradient, w_out, w_up, w_down,
        dp_size,
    )
    if fused:
        up_part = up.reshape(2, 4, 2, rows_here, -1)
        far_part = far.reshape((4, 2) + far.shape[1:])
        out_part = out.reshape(4, 2, rows_here, -1)
    else:
        up_part = far_part = out_part = jnp.zeros((16, 128), jnp.bfloat16)
    grad_input, pooled, vector_sum, sums_of = attend_back(
        fused, hidden_in, ids_got, lse_all, w_query, w_key, w_value,
        pool, counts, vector_parts, x_got, q_all, k_all, v_all, context, grad_context, grad_mixed,
        up_part, down, far_part, out_part,
    )
    if fused:
        *square_sums, up_sum, down_sum, pooled, final_out, grad_input = outputs(
            sums_of.squares, sums_of.wo, sums_of.up, sums_of.down, pooled, final_out, grad_input
        )
    else:
        squares = sums_of.square
        square_sums = [reduce_weight(squares[n], dp_size, 1) for n in range(3)]
        square_sums.append(finish_weight(out, dp_size, 1))
        up_sum = finish_weight(up.transpose(1, 0, 2).reshape(model_width, -1), dp_size, 1)
        down = down.transpose(0, 2, 1).reshape(ff_width, -1)
        down_sum = finish_weight(down, dp_size, 1)
        vector_sum = lax.psum(vector_sum, ("dp", "ctx"))
        pooled = pooled.reshape(row_count, NSEG, model_width)
    place = lax.axis_index("dp")
    sums = lax.dynamic_slice_in_dim(vector_sum[:8], place * rows_here, rows_here, 1)
    sum_bu = lax.dynamic_slice_in_dim(
        vector_sum[8 : 8 + ff_width // model_width].reshape(-1), place * ff_here, ff_here
    )
    results = (
        square_sums[0], sums[0], square_sums[1], square_sums[2], sums[1], square_sums[3],
        sums[2], sums[3], sums[4], up_sum, sum_bu, down_sum, sums[5], sums[6], sums[7],
    )
    return (
        final_out,
        pooled,
        grad_input,
    ) + tuple(results)


def solution(mesh):
    placed = (
        P("dp", "ctx", None),
        P("dp", "ctx"),
        P("dp", "ctx"),
        P(),
        P(),
        P(),
        P(),
        P(),
        P(),
        P(),
        P(),
        P(),
        P(),
        P(),
        P(),
        P(),
        P(),
        P(),
        P("dp", None, None),
    )
    return jax.shard_map(
        per_device,
        mesh=mesh,
        in_specs=placed,
        out_specs=(
            P("dp", "ctx", None),
            P("dp", None, None),
            P("dp", "ctx", None),
            P("dp", None),
            P("dp"),
            P("dp", None),
            P("dp", None),
            P("dp"),
            P("dp", None),
            P("dp"),
            P("dp"),
            P("dp"),
            P("dp", None),
            P("dp"),
            P("dp", None),
            P("dp"),
            P("dp"),
            P("dp"),
        ),
        check_vma=False,
    )
```

```python
import functools
import types

import jax
import jax.numpy as jnp
from jax import lax
from jax.experimental import pallas as pl
from jax.experimental.pallas import tpu as pltpu
from jax.sharding import PartitionSpec as P

HEADS = 12
HEAD_DIM = 64
NSEG = 16


eps = 1e-12


def matmul(left_side, right_side):
    return jnp.dot(left_side, right_side, preferred_element_type=jnp.float32)


PAIR = 2 * HEAD_DIM
MESH = pl.DeviceIdType.MESH
MASKED = -1e30


def dot_nt(left_side, right_side):
    return lax.dot_general(
        left_side, right_side, (((1,), (1,)), ((), ())), preferred_element_type=jnp.float32
    )


def dot_tn(left_side, right_side):
    return lax.dot_general(
        left_side, right_side, (((0,), (0,)), ((), ())), preferred_element_type=jnp.float32
    )


def split_heads(pair):
    lane = lax.broadcasted_iota(jnp.int32, pair.shape, 1)
    zero = jnp.zeros_like(pair)
    return jnp.concatenate(
        [jnp.where(lane < HEAD_DIM, pair, zero), jnp.where(lane < HEAD_DIM, zero, pair)], axis=0
    )


def text_rows(ids_row, size):
    return jnp.broadcast_to(ids_row.astype(jnp.float32), (PAIR, size)).T


def lanes_of(size):
    return lax.broadcasted_iota(jnp.int32, (size, PAIR), 1)


def key_extra(texts):
    lane = lanes_of(texts.shape[0])
    hot = jnp.where(lane.astype(jnp.float32) == texts, 1.0, 0.0)
    return jnp.where((lane >= NSEG) & (lane < 4 * NSEG), 1.0, hot).astype(jnp.bfloat16)


def query_extra(texts):
    lane = lanes_of(texts.shape[0])
    other = (lane < NSEG) & (lane.astype(jnp.float32) != texts)
    return jnp.where(other, MASKED, 0.0)


def with_constants(extra, constants):
    lane = lanes_of(extra.shape[0])
    high = constants.astype(jnp.bfloat16).astype(jnp.float32)
    middle = (constants - high).astype(jnp.bfloat16).astype(jnp.float32)
    rest = constants - high - middle
    terms = jnp.where(lane < 2 * NSEG, high, jnp.where(lane < 3 * NSEG, middle, rest))
    kept = (lane >= NSEG) & (lane < 4 * NSEG)
    return jnp.where(kept, terms, extra).astype(jnp.bfloat16)


def of_head(extra, head):
    lane = lanes_of(extra.shape[0])
    kept = (lane < NSEG) | (lane % NSEG == head)
    return jnp.where(kept, extra, jnp.zeros_like(extra))


def attend_kernel(
    x_ref, seg_ref, valid_ref, b_query, b_value, w_query, w_key, w_value,
    q_out, context_out, lse_out, ids_out, x_hbm, k_hbm, v_hbm,
    x_got, k_ref, v_ref, extra_ref, ids_ref, score_one, score_two, send_sem, recv_sem, local_sem,
):
    rows_here, size, width = x_ref.shape
    me = lax.axis_index("ctx")
    one = me + 1 - 2 * (me % 2)
    two = (me + 2) % 4
    three = (one + 2) % 4
    low = jnp.bfloat16

    ids_ref[...] = jnp.zeros_like(ids_ref)
    ids_ref[0:rows_here, :] = seg_ref[...]
    ids_ref[rows_here : 2 * rows_here, :] = valid_ref[...]
    query_bias = b_query[...].astype(jnp.float32)[None]
    value_bias = b_value[...].astype(jnp.float32)[None]
    barrier = pltpu.get_barrier_semaphore()
    for peer in (one, two, three):
        pl.semaphore_signal(barrier, inc=1, device_id={"ctx": peer}, device_id_type=MESH)
    pl.semaphore_wait(barrier, 3)

    def send(source, target, slot, peer):
        return pltpu.make_async_remote_copy(
            src_ref=source, dst_ref=target, send_sem=send_sem.at[slot],
            recv_sem=recv_sem.at[slot], device_id={"ctx": peer}, device_id_type=MESH,
        )

    ids_out[0] = ids_ref[...]
    ids_sends = [send(ids_ref, ids_out.at[j + 1], j, peer) for j, peer in enumerate((one, two, three))]
    near = send(x_ref, x_got.at[0], 3, one)

    def far(r):
        return send(x_ref.at[r], x_got.at[1, r], 4 + r, two)

    def passed(r):
        return send(x_got.at[1, r], x_got.at[2, r], 4 + rows_here + r, one)

    far(0).start()
    near.start()
    for item in ids_sends:
        item.start()
    for r in range(1, rows_here):
        far(r).start()

    def project(x, r, j):
        count = x.shape[0] // size
        k = matmul(x, w_key[...]).astype(low)
        v = (matmul(x, w_value[...]) + value_bias).astype(low)
        for n in range(count):
            rows = pl.ds((j + n if r is not None else j) * size, size)
            k_ref[n if r is None else r, rows, :] = k[n * size : (n + 1) * size]
            v_ref[n if r is None else r, rows, :] = v[n * size : (n + 1) * size]

    own = x_ref[...].reshape(rows_here * size, width)
    q = (matmul(own, w_query[...]) + query_bias).astype(low)
    q_out[...] = (q * HEAD_DIM ** (-0.5)).astype(low).reshape(q_out.shape)
    project(own, None, 0)
    near.wait_recv()
    project(x_got[0].reshape(rows_here * size, width), None, 1)
    for item in ids_sends:
        item.wait_recv()
    lane = lax.broadcasted_iota(jnp.int32, (size, PAIR), 1)
    far(0).wait_recv()
    passed(0).start()

    def keep(r):
        return (
            pltpu.make_async_copy(k_ref.at[r], k_hbm.at[r], local_sem.at[0, r]),
            pltpu.make_async_copy(v_ref.at[r], v_hbm.at[r], local_sem.at[1, r]),
            pltpu.make_async_copy(x_got.at[:, r], x_hbm.at[:, r], local_sem.at[2, r]),
        )

    for r in range(rows_here):
        passed(r).wait_recv()
        project(jnp.concatenate([x_got[1, r], x_got[2, r]], axis=0), r, 2)
        for item in keep(r):
            item.start()
        for j in range(4):
            texts = text_rows(ids_out[j, r : r + 1, :], size)
            extra_ref[j * size : (j + 1) * size, :] = key_extra(texts)
            if j == 0:
                own_extra = query_extra(texts).astype(low)

        def score(pair, target, r=r, own_extra=own_extra):
            columns = pl.ds(pl.multiple_of(pair * PAIR, PAIR), PAIR)
            both = split_heads(q_out[r, :, columns])
            extras = jnp.concatenate([own_extra, own_extra], axis=0)
            keys = jnp.concatenate([k_ref[r, :, columns], extra_ref[...]], axis=1)
            target[...] = dot_nt(jnp.concatenate([both, extras], axis=1), keys)

        def one_pair(pair, source, stat, r=r):
            columns = pl.ds(pl.multiple_of(pair * PAIR, PAIR), PAIR)
            scores = source[...]
            top = jnp.max(scores, axis=-1, keepdims=True)
            weight = jnp.exp(scores - top)
            total = jnp.sum(weight, axis=-1, keepdims=True)
            mixed = matmul(weight.astype(low), v_ref[r, :, columns]) * (1.0 / total)
            context_out[r, :, columns] = jnp.where(
                lane < HEAD_DIM, mixed[:size], mixed[size:]
            ).astype(low)
            lse = top + jnp.log(total)
            for h in range(2):
                ours = lane % NSEG == 2 * pair + h
                stat = jnp.where(ours, lse[h * size : (h + 1) * size], stat)
            return stat

        def two_pairs(n, carry, r=r):
            stat = lse_out[r]
            score(2 * n + 1, score_two)
            stat = one_pair(2 * n, score_one, stat)
            score(jnp.minimum(2 * n + 2, HEADS // 2 - 1), score_one)
            lse_out[r] = one_pair(2 * n + 1, score_two, stat)
            return carry

        score(0, score_one)
        lse_out[r] = jnp.zeros((size, PAIR), jnp.float32)
        lax.fori_loop(0, HEADS // 4, two_pairs, 0)
        if r + 1 < rows_here:
            far(r + 1).wait_recv()
            passed(r + 1).start()
    for r in range(rows_here):
        for item in keep(r):
            item.wait()
        far(r).wait_send()
        passed(r).wait_send()
    near.wait_send()
    for item in ids_sends:
        item.wait_send()


def attend(x, seg_ids, valid, b_query, b_value, w_query, w_key, w_value):
    rows_here, size, width = x.shape
    keys = size * 4
    low = jnp.bfloat16
    whole = pl.BlockSpec(memory_space=pltpu.VMEM)
    outside = pl.BlockSpec(memory_space=pl.ANY)
    slots = 4 + 2 * rows_here
    return pl.pallas_call(
        attend_kernel,
        out_shape=(
            jax.ShapeDtypeStruct((rows_here, size, width), low),
            jax.ShapeDtypeStruct((rows_here, size, width), low),
            jax.ShapeDtypeStruct((rows_here, size, PAIR), jnp.float32),
            jax.ShapeDtypeStruct((4, 8, size), jnp.int32),
            jax.ShapeDtypeStruct((3,) + x.shape, low),
            jax.ShapeDtypeStruct((rows_here, keys, width), low),
            jax.ShapeDtypeStruct((rows_here, keys, width), low),
        ),
        in_specs=[whole] * 8,
        out_specs=(whole, whole, whole, whole, outside, outside, outside),
        scratch_shapes=[
            pltpu.VMEM((3,) + x.shape, low),
            pltpu.VMEM((rows_here, keys, width), low),
            pltpu.VMEM((rows_here, keys, width), low),
            pltpu.VMEM((keys, PAIR), low),
            pltpu.VMEM((8, size), jnp.int32),
            pltpu.VMEM((2 * size, keys), jnp.float32),
            pltpu.VMEM((2 * size, keys), jnp.float32),
            pltpu.SemaphoreType.DMA((slots,)),
            pltpu.SemaphoreType.DMA((slots,)),
            pltpu.SemaphoreType.DMA((3, rows_here)),
        ],
        compiler_params=pltpu.CompilerParams(
            vmem_limit_bytes=56 * 2**20, collective_id=0, has_side_effects=True
        ),
        cost_estimate=pl.CostEstimate(
            flops=rows_here * (2 * (size + 2 * keys) * width * width + 16 * size * keys * width),
            bytes_accessed=2 * (3 * width * width + 9 * keys * width),
            transcendentals=rows_here * HEADS * size * keys,
        ),
    )(x, seg_ids, valid, b_query, b_value, w_query, w_key, w_value)


def gelu_both(u):
    size = jnp.abs(u)
    t = 1.0 / (1.0 + (0.3275911 * 0.5**0.5) * size)
    bell = jnp.exp(-0.5 * u * u)
    poly = t * (
        0.127414796 + t * (-0.142248368 + t * (0.7107068705 + t * (-0.7265760135 + t * 0.5307027145)))
    )
    tail = poly * bell
    cdf = jnp.where(u >= 0.0, 1.0 - tail, tail)
    return u * cdf, cdf + u * bell * 0.3989422804014327


def normalize(values_in):
    centre = jnp.mean(values_in, axis=-1, keepdims=True)
    centred = values_in - centre
    spread = jnp.mean(centred * centred, axis=-1, keepdims=True)
    scale = lax.rsqrt(spread + eps)
    return centred * scale, scale


def normalize_back(grad, unit, scale):
    mean_one = jnp.mean(grad, axis=-1, keepdims=True)
    mean_two = jnp.mean(grad * unit, axis=-1, keepdims=True)
    return (grad - mean_one - unit * mean_two) * scale


def column_sum(values_in):
    return jnp.sum(values_in, axis=0, keepdims=True)


B_QUERY, B_VALUE, B_OUT, GAIN_ONE, SHIFT_ONE, B_DOWN, GAIN_TWO, SHIFT_TWO, B_UP = range(9)


def middle_kernel(
    fused,
    x_ref, context_ref, ids_ref, b_out, gain_one, shift_one, b_up, b_down, gain_two, shift_two,
    text_ref, w_out, up_hbm, down_hbm,
    pool_out, count_out, vector_out, grad_out, mixed_out, wo_out, final_hbm, up_out, down_out, far_out,
    vec_ref, w_up, w_down, unit_ref, scale_ref, normed_ref, normed_t, act_ref, slope_ref, acc_ref, pre_one,
    g_ref, g_t_ref, upg_ref, up_got, downg_ref, down_got, wo_sent, wo_got, down_y, down_x,
    send_sem, recv_sem, load_sem, store_sem,
):
    rows_here, size, width = x_ref.shape
    tokens = rows_here * size
    parts = w_up.shape[1] // width
    half = width // 2
    low = jnp.bfloat16
    f32 = jnp.float32
    me = lax.axis_index("ctx")
    core = me % 2
    near = {"ctx": me + 1 - 2 * core}
    side = me // 2
    place = lax.axis_index("dp")
    y = place % 2
    y_dev = {"dp": place + 1 - 2 * y}
    across_dev = {"ctx": (me + 2) % 4}
    peers = [near, across_dev, y_dev] if fused else [near]
    barrier = pltpu.get_barrier_semaphore()
    for peer in peers:
        pl.semaphore_signal(barrier, inc=1, device_id=peer, device_id_type=MESH)
    for row, source in (
        (B_OUT, b_out), (GAIN_ONE, gain_one), (SHIFT_ONE, shift_one), (B_DOWN, b_down),
        (GAIN_TWO, gain_two), (SHIFT_TWO, shift_two),
    ):
        vec_ref[row : row + 1, :] = source[...].astype(f32)[None]
    for i in range(parts):
        vec_ref[B_UP + i : B_UP + i + 1, :] = (
            b_up[i * width : (i + 1) * width].astype(f32)[None]
        )

    def vec(row):
        return vec_ref[row : row + 1, :]

    loads = []
    for i in range(parts):
        loads.append(
            (
                pltpu.make_async_copy(
                    up_hbm.at[:, pl.ds(i * width, width)],
                    w_up.at[:, pl.ds(i * width, width)],
                    load_sem.at[0, i],
                ),
                pltpu.make_async_copy(
                    down_hbm.at[pl.ds(i * width, width)],
                    w_down.at[pl.ds(i * width, width)],
                    load_sem.at[1, i],
                ),
            )
        )
    for pair in loads:
        for item in pair:
            item.start()

    def rows_of(r):
        return pl.ds(pl.multiple_of(r * size, size), size)

    text = lax.broadcasted_iota(jnp.int32, (NSEG, size), 0)

    def members(j, r):
        seg = ids_ref[j, r : r + 1, :]
        real = ids_ref[j, rows_here + r : rows_here + r + 1, :]
        return jnp.where((text == seg) & (real == 1), 1.0, 0.0)

    for r in range(rows_here):
        number = sum(jnp.sum(members(j, r), axis=1, keepdims=True) for j in range(4))
        count_out[r * NSEG : (r + 1) * NSEG, :] = jnp.maximum(number, 1.0)

    def first_norm(r, carry):
        rows = rows_of(r)
        mixed = x_ref[r].astype(f32) + (matmul(context_ref[r], w_out[...]) + vec(B_OUT))
        unit, scale = normalize(mixed)
        unit_ref[rows, :] = unit
        scale_ref[rows, :] = scale
        normed_ref[rows, :] = (unit * vec(GAIN_ONE) + vec(SHIFT_ONE)).astype(low)
        return carry

    lax.fori_loop(0, rows_here, first_norm, 0)
    for pair in loads:
        for item in pair:
            item.wait()

    def units(i):
        return pl.ds(pl.multiple_of(i * width, width), width)

    def forward_part(i, following, now, then):
        for r in range(rows_here):
            rows = pl.ds(r * size, size)
            then[rows, :] = matmul(normed_ref[rows, :], w_up[:, units(following)])
            act, slope = gelu_both(now[rows, :] + vec_ref[pl.ds(B_UP + i, 1), :])
            act_ref[rows, units(i)] = act.astype(low)
            slope_ref[rows, units(i)] = slope.astype(low)

    def forward_parts(n, carry):
        forward_part(2 * n, 2 * n + 1, pre_one, acc_ref)
        forward_part(2 * n + 1, jnp.minimum(2 * n + 2, parts - 1), acc_ref, pre_one)
        return carry

    pre_one[...] = matmul(normed_ref[...], w_up[:, units(0)])
    lax.fori_loop(0, parts // 2, forward_parts, 0)

    def forward_sum(r, carry):
        acc_ref[rows_of(r), :] = matmul(act_ref[rows_of(r), :], w_down[...])
        return carry

    lax.fori_loop(0, rows_here, forward_sum, 0)

    normed_t[...] = normed_ref[...].T

    store_final = []
    vector_out[...] = jnp.zeros_like(vector_out)
    for r in range(rows_here):
        rows = pl.ds(r * size, size)
        normed = unit_ref[rows, :] * vec(GAIN_ONE) + vec(SHIFT_ONE)
        summed = normed + (acc_ref[rows, :] + vec(B_DOWN))
        unit, scale = normalize(summed)
        final = unit * vec(GAIN_TWO) + vec(SHIFT_TWO)
        high = final.astype(low)
        upg_ref[parts - 1, rows, :] = high
        item = pltpu.make_async_copy(
            upg_ref.at[parts - 1, rows], final_hbm.at[r], store_sem.at[r]
        )
        item.start()
        store_final.append(item)
        own = members(0, r)
        own_low = own.astype(low)
        rest = (final - high.astype(f32)).astype(low)
        pool = matmul(own_low, high) + matmul(own_low, rest)
        pool_out[r * NSEG : (r + 1) * NSEG, :] = pool.astype(low)
        share = text_ref[r] / count_out[r * NSEG : (r + 1) * NSEG, :]
        first = share.astype(low)
        second = (share - first.astype(f32)).astype(low)
        third = (share - first.astype(f32) - second.astype(f32)).astype(low)
        grad = dot_tn(
            jnp.concatenate([own_low] * 3, axis=0), jnp.concatenate([first, second, third], axis=0)
        )
        back = normalize_back(grad * vec(GAIN_TWO), unit, scale)
        back_low = back.astype(low)
        acc_ref[rows, :] = back
        g_ref[rows, :] = back_low
        vector_out[GAIN_TWO : GAIN_TWO + 1, :] += column_sum(grad * unit)
        vector_out[SHIFT_TWO : SHIFT_TWO + 1, :] += column_sum(grad)
        vector_out[B_DOWN : B_DOWN + 1, :] += column_sum(back_low.astype(f32))

    pl.semaphore_wait(barrier, len(peers))

    def remote(source, target, slot, device=near):
        return pltpu.make_async_remote_copy(
            src_ref=source, dst_ref=target, send_sem=send_sem.at[slot],
            recv_sem=recv_sem.at[slot], device_id=device, device_id_type=MESH,
        )

    per_part = downg_ref.shape[0] // parts
    mine = parts // 2

    def up_send(i):
        return remote(upg_ref.at[i], up_got.at[i], i)

    def down_send(i):
        chunk = pl.ds(i * per_part, per_part)
        return remote(downg_ref.at[chunk, 1 - core], down_got.at[chunk], parts + i)

    cut = downg_ref.shape[3]

    def down_part(i):
        part = matmul(g_t_ref[...], act_ref[:, units(i)]).astype(low)
        part = part.reshape((2, width // 2, width))
        for n in range(per_part):
            downg_ref[per_part * i + n] = part[:, :, n * cut : (n + 1) * cut]
        down_send(i).start()

    def backward_part(step, carry):
        i = (step + mine * (1 - core)) % parts
        back = dot_nt(g_ref[...], w_down[units(i), :])
        back = (back * slope_ref[:, units(i)].astype(f32)).astype(low)
        slope_ref[:, units(i)] = back
        vector_out[pl.ds(B_UP + i, 1), :] = column_sum(back.astype(f32))
        upg_ref[step] = matmul(normed_t[...], back).astype(low)

        @pl.when(step < mine)
        def _():
            up_send(step).start()

        return carry

    piece = downg_ref.shape[2] // 2
    quarter = piece // 2
    rest = pl.ds(pl.multiple_of(piece + quarter * (1 - side), 16), quarter)
    kept = pl.ds(pl.multiple_of(piece + quarter * side, 16), quarter)
    down_moves = []

    def send_on(i):
        down_send(i).wait_recv()
        for n in range(per_part * i, per_part * (i + 1)):
            downg_ref[n, core] = (
                downg_ref[n, core].astype(f32) + down_got[n].astype(f32)
            ).astype(low)
        if not fused:
            return
        moves = [
            remote(
                downg_ref.at[2 * i + 1 - y, core, pl.ds(0, piece)], down_y.at[i],
                2 * parts + 1 + i, y_dev,
            )
        ]
        for n in (2 * i, 2 * i + 1):
            moves.append(
                remote(downg_ref.at[n, core, rest], down_x.at[n], 2 * parts + 5 + n, across_dev)
            )
        for item in moves:
            item.start()
        down_moves.extend(moves)

    g_t_ref[...] = g_ref[...].T
    for i in range(parts):
        down_part(i)
        if i:
            send_on(i - 1)
    lax.fori_loop(0, 1, backward_part, 0)
    send_on(parts - 1)
    for item in store_final:
        item.wait()
    lax.fori_loop(1, parts, backward_part, 0)

    def first_back(r, carry):
        rows = rows_of(r)
        unit = unit_ref[rows, :]
        grad = acc_ref[rows, :] + dot_nt(slope_ref[rows, :], w_up[...])
        back = normalize_back(grad * vec(GAIN_ONE), unit, scale_ref[rows, :])
        back_low = back.astype(low)
        mixed_out[r] = back
        g_ref[rows, :] = back_low
        vector_out[GAIN_ONE : GAIN_ONE + 1, :] += column_sum(grad * unit)
        vector_out[SHIFT_ONE : SHIFT_ONE + 1, :] += column_sum(grad)
        vector_out[B_OUT : B_OUT + 1, :] += column_sum(back_low.astype(f32))
        return carry

    lax.fori_loop(0, rows_here, first_back, 0)

    for r in range(rows_here):
        g_t_ref[:, r * size : (r + 1) * size] = context_ref[r].T

    def out_part(h):
        columns = pl.ds(pl.multiple_of(h * half, 128), half)
        return matmul(g_t_ref[...], g_ref[:, columns])

    wo_sent[...] = out_part(1 - core).astype(low)
    wo_send = remote(wo_sent, wo_got, 2 * parts)
    wo_send.start()

    def grad_context(r, carry):
        grad_out[r] = dot_nt(g_ref[rows_of(r), :], w_out[...]).astype(low)
        return carry

    lax.fori_loop(0, rows_here, grad_context, 0)
    own_part = out_part(core)
    for i in range(mine):
        up_send(i).wait_recv()

    def up_sum(n, carry):
        rows = pl.ds(pl.multiple_of(n * 128, 128), 128)
        for i in range(mine):
            upg_ref[mine + i, rows, :] = (
                upg_ref[mine + i, rows, :].astype(f32) + up_got[i, rows, :].astype(f32)
            ).astype(low)
        return carry

    lax.fori_loop(0, width // 128, up_sum, 0)
    store_up = pltpu.make_async_copy(
        upg_ref.at[pl.ds(mine, mine)], up_out, store_sem.at[rows_here + 1]
    )
    store_up.start()
    wo_send.wait_recv()
    wo_out[...] = (own_part + wo_got[...].astype(f32)).astype(low)
    if fused:
        for item in down_moves:
            item.wait_recv()

        def near_sum(n, carry):
            down_y[n] = (
                downg_ref[2 * n + y, core, 0:piece, :].astype(f32) + down_y[n].astype(f32)
            ).astype(low)
            return carry

        def far_sum(n, carry):
            down_x[n] = (
                downg_ref[n, core, kept, :].astype(f32) + down_x[n].astype(f32)
            ).astype(low)
            return carry

        lax.fori_loop(0, 4, near_sum, 0)
        lax.fori_loop(0, 8, far_sum, 0)
        stores = [
            pltpu.make_async_copy(down_y, down_out, store_sem.at[rows_here]),
            pltpu.make_async_copy(down_x, far_out, store_sem.at[rows_here + 2]),
        ]
    else:
        stores = [
            pltpu.make_async_copy(downg_ref.at[:, core], down_out, store_sem.at[rows_here])
        ]
    for item in stores:
        item.start()
    for i in range(parts):
        down_send(i).wait_send()
    for i in range(mine):
        up_send(i).wait_send()
    wo_send.wait_send()
    for item in down_moves:
        item.wait_send()
    for item in stores + [store_up]:
        item.wait()


def middle(fused, x, context, ids, vectors, text_gradient, w_out, w_up, w_down, dp_size):
    rows_here, size, width = x.shape
    ff = w_up.shape[1]
    parts = ff // width
    tokens = rows_here * size
    low = jnp.bfloat16
    f32 = jnp.float32
    shape = jax.ShapeDtypeStruct
    whole = pl.BlockSpec(memory_space=pltpu.VMEM)
    outside = pl.BlockSpec(memory_space=pl.ANY)
    chunks = dp_size if fused else parts
    chunk = ff // chunks
    vec = (8 + parts + (-parts) % 8, width)
    if fused:
        down_shape, far_shape = (4, width // 4, chunk), (8, width // 8, chunk)
    else:
        down_shape, far_shape = (chunks, width // 2, chunk), (8, 16, 128)
    return pl.pallas_call(
        functools.partial(middle_kernel, fused),
        out_shape=(
            shape((rows_here * NSEG, width), low),
            shape((rows_here * NSEG, 1), f32),
            shape(vec, f32),
            shape((rows_here, size, width), low),
            shape((rows_here, size, width), f32),
            shape((width, width // 2), low),
            shape((rows_here, size, width), low),
            shape((parts // 2, width, width), low),
            shape(down_shape, low),
            shape(far_shape, low),
        ),
        in_specs=[whole] * 12 + [outside] * 2,
        out_specs=(whole,) * 6 + (outside,) * 4,
        scratch_shapes=[
            pltpu.VMEM(vec, f32),
            pltpu.VMEM((width, ff), low),
            pltpu.VMEM((ff, width), low),
            pltpu.VMEM((tokens, width), f32),
            pltpu.VMEM((tokens, 1), f32),
            pltpu.VMEM((tokens, width), low),
            pltpu.VMEM((width, tokens), low),
            pltpu.VMEM((tokens, ff), low),
            pltpu.VMEM((tokens, ff), low),
            pltpu.VMEM((tokens, width), f32),
            pltpu.VMEM((tokens, width), f32),
            pltpu.VMEM((tokens, width), low),
            pltpu.VMEM((width, tokens), low),
            pltpu.VMEM((parts, width, width), low),
            pltpu.VMEM((parts // 2, width, width), low),
            pltpu.VMEM((chunks, 2, width // 2, chunk), low),
            pltpu.VMEM((chunks, width // 2, chunk), low),
            pltpu.VMEM((width, width // 2), low),
            pltpu.VMEM((width, width // 2), low),
            pltpu.VMEM(down_shape if fused else (16, 128), low),
            pltpu.VMEM(far_shape, low),
            pltpu.SemaphoreType.DMA((2 * parts + 13,)),
            pltpu.SemaphoreType.DMA((2 * parts + 13,)),
            pltpu.SemaphoreType.DMA((2, parts)),
            pltpu.SemaphoreType.DMA((rows_here + 3,)),
        ],
        compiler_params=pltpu.CompilerParams(
            vmem_limit_bytes=63 * 2**20, collective_id=2, has_side_effects=True
        ),
        cost_estimate=pl.CostEstimate(
            flops=2 * tokens * width * (6 * ff + 3 * width),
            bytes_accessed=2 * (5 * ff * width + 8 * tokens * width),
            transcendentals=2 * tokens * ff,
        ),
    )(x, context, ids, *vectors, text_gradient, w_out, w_up, w_down)


class Links:
    def __init__(self, send_sem, recv_sem):
        self.send_sem, self.recv_sem = send_sem, recv_sem
        self.slots, self.copies = {}, {}

    def start(self, name, source, target, device):
        slot = self.slots.setdefault(name, len(self.slots))
        copy = pltpu.make_async_remote_copy(
            src_ref=source, dst_ref=target, send_sem=self.send_sem.at[slot],
            recv_sem=self.recv_sem.at[slot], device_id=device, device_id_type=MESH,
        )
        copy.start()
        self.copies[name] = copy

    def arrived(self, *names):
        for name in names:
            self.copies[name].wait_recv()

    def finish(self):
        for copy in self.copies.values():
            copy.wait_send()


def add_into(target, others, count):
    def one(i, carry):
        total = target[i].astype(jnp.float32)
        for other in others:
            total = total + other[i].astype(jnp.float32)
        target[i] = total.astype(target.dtype)
        return carry

    lax.fori_loop(0, count, one, 0)


def add_up(parts):
    total = parts[0].astype(jnp.float32)
    for part in parts[1:]:
        total = total + part.astype(jnp.float32)
    return total


POOL, UP, DOWN_A, DOWN_B, DOWN, OUT, GROUP, DX, VECTOR = range(9)
STEP, NEAR, FAR, SIDE, LINE, GATHER = range(6)

GROUPS = ((0, 4 * PAIR), (4 * PAIR, PAIR), (5 * PAIR, PAIR))


def attend_back_kernel(
    fused, count_out, out_tree, tree,
    x_ref, ids_ref, lse_ref, w_query, w_key, w_value, pool_ref, count_ref, vector_ref,
    x_hbm, q_hbm, k_hbm, v_hbm, context_hbm, grad_hbm, mixed_hbm, up_ref, down_ref, far_ref, out_ref,
    dx_out, pool_out, vector_out, *rest,
):
    outs = types.SimpleNamespace(**jax.tree.unflatten(out_tree, rest[:count_out]))
    ref = types.SimpleNamespace(**jax.tree.unflatten(tree, rest[count_out:]))
    square_out, up_out, down_out, wo_out = outs.square, outs.up, outs.down, outs.wo
    q_ref, k_ref, v_ref, context_ref, grad_ref = ref.q, ref.k, ref.v, ref.context, ref.grad
    dq_ref, dk_ref, dv_ref, x_t, x_got = ref.dq, ref.dk, ref.dv, ref.x_t, ref.x_got
    extra_ref, penal_ref, delta_ref = ref.extra, ref.penal, ref.delta
    dx_acc, dx_sent, dx_far, dx_got, dx_far_got = (
        ref.dx_acc, ref.dx_sent, ref.dx_far, ref.dx_got, ref.dx_far_got
    )
    pool_parts, pool_got, vec_parts, vec_got = (
        ref.pool_parts, ref.pool_got, ref.vec_parts, ref.vec_got
    )
    row_sem, local_sem = ref.row_sem, ref.local_sem
    rows_here, size, width = x_ref.shape
    low = jnp.bfloat16
    me, place = lax.axis_index("ctx"), lax.axis_index("dp")
    core, side = me % 2, me // 2
    near, across = me + 1 - 2 * core, (me + 2) % 4
    near_dev, across_dev = {"ctx": near}, {"ctx": across}
    y, z = place % 2, place // 2
    y_dev = {"dp": place + 1 - 2 * y}
    z_at = (z + 1 - 2 * (z % 2), (z + 2) % 4, 3 - z)
    z_dev = [{"dp": other * 2 + y} for other in z_at]
    peers = [near_dev, across_dev] + ([y_dev] + z_dev if fused else [])

    barrier = pltpu.get_barrier_semaphore()
    for peer in peers:
        pl.semaphore_signal(barrier, inc=1, device_id=peer, device_id_type=MESH)
    pl.semaphore_wait(barrier, len(peers))
    links = Links(ref.send_sem, ref.recv_sem)

    first_cut = GROUPS[1][0]
    blocks = [(0, first_cut, r) for r in range(rows_here)]
    blocks += [(first_cut, width - first_cut, r) for r in range(rows_here)]

    def load_block(step):
        slot = step % 2
        start, count, r = blocks[step]
        columns, local = pl.ds(start, count), pl.ds(0, count)
        pairs = (
            (k_hbm, k_ref), (v_hbm, v_ref), (q_hbm, q_ref), (context_hbm, context_ref),
            (grad_hbm, grad_ref),
        )
        copies = [
            pltpu.make_async_copy(
                source.at[r, :, columns], target.at[slot, :, local], row_sem.at[slot, i]
            )
            for i, (source, target) in enumerate(pairs)
        ]
        if step < rows_here:
            copies.append(pltpu.make_async_copy(x_hbm.at[:, r], x_got.at[slot], row_sem.at[slot, 5]))
        return copies

    for item in load_block(0):
        item.start()
    load_mixed = pltpu.make_async_copy(mixed_hbm, dx_acc, local_sem.at[0])
    links.start((POOL, STEP, 0), pool_ref, pool_got.at[0], near_dev)
    if fused:
        u_ref, u_x, u_y, u_z = ref.u, ref.u_x, ref.u_y, ref.u_z
        a_z, a_s, a_x = ref.a_z, ref.a_s, ref.a_x
        b_ref, b_y, b_z = ref.b, ref.b_y, ref.b_z
        o_ref, o_y, o_z, o_s, o_x = ref.o, ref.o_y, ref.o_z, ref.o_s, ref.o_x
        half_rows = u_ref.shape[2] // 2
        links.start((UP, FAR, 0), up_ref.at[1 - side, :, :, pl.ds(0, half_rows)], u_x.at[0], across_dev)
        links.start((DOWN_B, SIDE), far_ref.at[:, 1 - y], b_y, y_dev)
        for o in range(3):
            links.start((DOWN_A, LINE, o), down_ref.at[z_at[o]], a_z.at[o], z_dev[o])
    load_mixed.start()
    vec_parts[0] = vector_ref[...]

    def pool_one():
        links.arrived((POOL, STEP, 0))
        pool_parts[...] = add_up([pool_ref[...], pool_got[0]]).astype(low)
        links.start((POOL, STEP, 1), pool_parts, pool_got.at[1], across_dev)

    def pool_two():
        links.arrived((POOL, STEP, 1))
        pool_out[...] = add_up([pool_parts[...], pool_got[1]]) / count_ref[...]

    def send_z(name, source, target):
        for o in range(3):
            links.start(name + (o,), source(z_at[o]), target(o), z_dev[o])

    def arrived_z(name):
        links.arrived(*(name + (o,) for o in range(3)))

    def out_y():
        links.start((OUT, SIDE), out_ref.at[:, 1 - y], o_y, y_dev)

    def out_z():
        links.arrived((OUT, SIDE))
        for i in range(4):
            o_ref[i] = add_up([out_ref[i, y], o_y[i]]).astype(low)
        send_z((OUT, LINE), lambda i: o_ref.at[i], lambda o: o_z.at[o])

    def out_far():
        arrived_z((OUT, LINE))
        o_s[...] = add_up([o_ref[z]] + [o_z[o] for o in range(3)]).astype(low)
        links.start((OUT, FAR), o_s, o_x, across_dev)

    def out_end():
        links.arrived((OUT, FAR))
        wo_out[core] = add_up([o_s[...], o_x[...]]).astype(low)
        links.start((OUT, GATHER), wo_out.at[core], wo_out.at[core], near_dev)

    def down_z():
        links.arrived((DOWN_B, SIDE))
        for i in range(4):
            b_ref[i] = add_up([far_ref[i, y], b_y[i]]).astype(low)
        send_z((DOWN_B, LINE), lambda i: b_ref.at[i], lambda o: b_z.at[o])

    def down_near_far():
        arrived_z((DOWN_A, LINE))
        a_s[...] = add_up([down_ref[z]] + [a_z[o] for o in range(3)]).astype(low)
        links.start((DOWN_A, FAR), a_s, a_x, across_dev)

    def down_far():
        arrived_z((DOWN_B, LINE))
        count = b_ref.shape[1]
        own = pl.ds(pl.multiple_of(2 * count + side * count, 16), count)
        down_out[core, own] = add_up([b_ref[z]] + [b_z[o] for o in range(3)]).astype(low)
        links.start((DOWN_B, FAR), down_out.at[core, own], down_out.at[core, own], across_dev)

    def down_end():
        links.arrived((DOWN_A, FAR), (DOWN_B, FAR))
        down_out[core, 0 : a_s.shape[0]] = add_up([a_s[...], a_x[...]]).astype(low)
        links.start((DOWN, GATHER), down_out.at[core], down_out.at[core], near_dev)

    def up_x():
        rows = pl.ds(half_rows, half_rows)
        links.start((UP, FAR, 1), up_ref.at[1 - side, :, :, rows], u_x.at[1], across_dev)

    def up_y(h):
        rows = pl.ds(h * half_rows, half_rows)
        links.arrived((UP, FAR, h))
        for i in range(4):
            for j in range(2):
                u_ref[i, j, rows] = add_up([up_ref[side, i, j, rows], u_x[h, i, j]]).astype(low)
        links.start((UP, SIDE, h), u_ref.at[:, 1 - y, rows], u_y.at[h], y_dev)

    def up_z(h):
        rows = pl.ds(h * half_rows, half_rows)
        links.arrived((UP, SIDE, h))
        for i in range(4):
            u_ref[i, y, rows] = add_up([u_ref[i, y, rows], u_y[h, i]]).astype(low)
        send_z((UP, LINE, h), lambda i: u_ref.at[i, y, rows], lambda o: u_z.at[o, rows])

    def up_far():
        arrived_z((UP, LINE, 0))
        arrived_z((UP, LINE, 1))
        up_out[me] = add_up([u_ref[z, y]] + [u_z[o] for o in range(3)]).astype(low)
        links.start((UP, GATHER), up_out.at[me], up_out.at[me], across_dev)

    def up_end():
        links.arrived((UP, GATHER))
        links.start((UP, NEAR, 0), up_out.at[me], up_out.at[me], near_dev)
        links.start((UP, NEAR, 1), up_out.at[across], up_out.at[across], near_dev)

    def group_core(g):
        links.start((GROUP, NEAR, g), ref.g[g].at[1 - core], ref.g_got[g], near_dev)

    def group_y(g):
        links.arrived((GROUP, NEAR, g))
        for i in range(4):
            add_into(ref.g[g].at[core, i], [ref.g_got[g].at[i]], 2)
        links.start((GROUP, SIDE, g), ref.g[g].at[core, :, 1 - y], ref.g_y[g], y_dev)

    def group_z(g):
        links.arrived((GROUP, SIDE, g))
        own = ref.g[g]
        for i in range(4):
            own[core, i, y] = add_up([own[core, i, y], ref.g_y[g][i]]).astype(low)
        send_z((GROUP, LINE, g), lambda i: own.at[core, i, y], lambda o: ref.g_z[g].at[o])

    def group_far(g):
        arrived_z((GROUP, LINE, g))
        pieces = [ref.g[g][core, z, y]] + [ref.g_z[g][o] for o in range(3)]
        ref.g_s[g][...] = add_up(pieces).astype(low)
        links.start((GROUP, FAR, g), ref.g_s[g], ref.g_x[g], across_dev)

    def group_end(g):
        links.arrived((GROUP, FAR, g))
        out = outs.squares[g]
        out[core] = add_up([ref.g_s[g][...], ref.g_x[g][...]]).astype(low)
        links.start((GROUP, GATHER, g), out.at[core], out.at[core], near_dev)

    def vector_step(i, device):
        if i:
            links.arrived((VECTOR, STEP, i - 1))
            vec_parts[i] = vec_parts[i - 1] + vec_got[i - 1]
        if device is not None:
            links.start((VECTOR, STEP, i), vec_parts.at[i], vec_got.at[i], device)

    def vector_z():
        vector_step(3, None)
        for o in range(3):
            links.start((VECTOR, LINE, o), vec_parts.at[3], vec_got.at[3 + o], z_dev[o])

    def vector_end():
        arrived_z((VECTOR, LINE))
        vector_out[...] = vec_parts[3] + (vec_got[3] + (vec_got[4] + vec_got[5]))

    row = lax.broadcasted_iota(jnp.int32, (PAIR, size), 0)

    def find_delta(step):
        slot = step % 2
        start, count, _ = blocks[step]
        lane = lax.broadcasted_iota(jnp.int32, (count, PAIR), 1)
        head = (start + lax.broadcasted_iota(jnp.int32, (count, PAIR), 0)) // HEAD_DIM
        member = jnp.where((lane % NSEG == head) & (lane >= NSEG) & (lane < 4 * NSEG), 1.0, 0.0)
        member = member.astype(low)
        local = pl.ds(0, count)
        product = grad_ref[slot, :, local].astype(jnp.float32) * context_ref[
            slot, :, local
        ].astype(jnp.float32)
        total = jnp.zeros((size, PAIR), jnp.float32)
        for _ in range(3):
            term = product.astype(low)
            total = total + matmul(term, member)
            product = product - term.astype(jnp.float32)
        delta_ref[...] = with_constants(jnp.zeros_like(total), -total)

    def attend_pairs(step, first, last):
        slot = step % 2
        start, _, r = blocks[step]

        def one_pair(n, carry):
            local = pl.ds(pl.multiple_of(n * PAIR, PAIR), PAIR)
            columns = pl.ds(pl.multiple_of(start + n * PAIR, PAIR), PAIR)
            head = 2 * (start // PAIR + n)
            q_both = split_heads(q_ref[slot, :, local])
            g_both = split_heads(grad_ref[slot, :, local])
            q_extra = [of_head(penal_ref[r], head + h) for h in range(2)]
            g_extra = [of_head(delta_ref[...], head + h) for h in range(2)]
            q_wide = jnp.concatenate([q_both, jnp.concatenate(q_extra, axis=0)], axis=1)
            g_wide = jnp.concatenate([g_both, jnp.concatenate(g_extra, axis=0)], axis=1)
            q_wide, g_wide = q_wide.T, g_wide.T
            dq = jnp.zeros((PAIR, 2 * size), jnp.float32)

            def products(j):
                rows = pl.ds(j * size, size)
                extra = extra_ref[r, rows, :]
                keys = jnp.concatenate([k_ref[slot, rows, local], extra], axis=1)
                values = jnp.concatenate([v_ref[slot, rows, local], extra], axis=1)
                return matmul(keys, q_wide), matmul(values, g_wide)

            ahead = products(0)
            for j in range(4):
                rows = pl.ds(j * size, size)
                scores, grad_p = ahead
                if j < 3:
                    ahead = products(j + 1)
                probs = jnp.exp(scores)
                grad_s = (probs * grad_p).astype(low)
                dv_ref[r, rows, columns] = matmul(probs.astype(low), g_both).astype(low)
                dk_ref[r, rows, columns] = matmul(grad_s, q_both).astype(low)
                dq = dq + matmul(k_ref[slot, rows, local].T, grad_s)
            dq = jnp.where(row < HEAD_DIM, dq[:, :size], dq[:, size:]) * HEAD_DIM ** (-0.5)
            dq_ref[r, :, columns] = dq.T.astype(low)
            return carry

        lax.fori_loop(first, last, one_pair, 0)

    def weight_group(g):
        start, count = GROUPS[g]
        if fused:
            depth = ref.g[g].shape[3]

        def keep(n, i, total):
            total = total.astype(low)
            wide = total.shape[1]
            if not fused:
                square_out[n, :, pl.ds(pl.multiple_of(start + i * PAIR, PAIR), wide)] = total
                return
            total = total.reshape(4, 2, 2, depth, wide)
            target = pl.ds(pl.multiple_of(n * count + i * PAIR, PAIR), wide)
            for h in range(2):
                ref.g[g][h, :, :, :, target] = total[:, :, h]

        def of_source(source, columns):
            keys = source.shape[1]
            return sum(
                matmul(x_t[r, :, :keys], source[r, :, columns]) for r in range(rows_here)
            )

        def one_part(i, carry):
            columns = pl.ds(pl.multiple_of(start + 2 * i * PAIR, PAIR), 2 * PAIR)
            for n, source in enumerate((dq_ref, dk_ref, dv_ref)):
                keep(n, 2 * i, of_source(source, columns))
            return carry

        if count % (2 * PAIR):
            columns = pl.ds(start, count)
            keep(0, 0, of_source(dq_ref, columns))
            both = sum(
                matmul(
                    x_t[r],
                    jnp.concatenate([dk_ref[r, :, columns], dv_ref[r, :, columns]], axis=1),
                )
                for r in range(rows_here)
            )
            keep(1, 0, both[:, :count])
            keep(2, 0, both[:, count:])
        else:
            lax.fori_loop(0, count // (2 * PAIR), one_part, 0)
        columns = pl.ds(start, count)
        for n, source in enumerate((dq_ref, dv_ref)):
            vec_parts[0, n : n + 1, columns] = sum(
                jnp.sum(source[r, :, columns].astype(jnp.float32), axis=0, keepdims=True)
                for r in range(rows_here)
            )

    def input_parts(r, places):
        for j in places:
            rows = pl.ds(j * size, size)
            total = dot_nt(dk_ref[r, rows, :], w_key[...]) + dot_nt(dv_ref[r, rows, :], w_value[...])
            if j == 0:
                dx_acc[r] = dx_acc[r] + total + dot_nt(dq_ref[r], w_query[...])
            elif j == 2:
                dx_far[r] = total.astype(low)
            else:
                n = j // 2
                dx_sent[r, n] = total.astype(low)
                links.start((DX, NEAR, r, n), dx_sent.at[r, n], dx_got.at[r, n], near_dev)

    def input_far(r):
        links.arrived((DX, NEAR, r, 1))
        dx_far[r] = add_up([dx_far[r], dx_got[r, 1]]).astype(low)
        links.start((DX, FAR, r), dx_far.at[r], dx_far_got.at[r], across_dev)

    def input_done(r):
        links.arrived((DX, NEAR, r, 0), (DX, FAR, r))
        dx_out[r] = add_up([dx_acc[r], dx_got[r, 0], dx_far_got[r]]).astype(low)

    def prepare_row(r):
        slot = r % 2
        for j in range(4):
            rows = slice(j * size, (j + 1) * size)
            texts = text_rows(ids_ref[j, r : r + 1, :], size)
            extra_ref[r, rows, :] = key_extra(texts)
            if j == 0:
                penal_ref[r] = with_constants(query_extra(texts), -lse_ref[r])
            block = x_ref[r] if j == 0 else x_got[slot, j - 1]
            x_t[r, :, rows] = block.T

    def begin(step):
        for item in load_block(step):
            item.wait()
        if step + 1 < len(blocks):
            for item in load_block(step + 1):
                item.start()
        find_delta(step)

    def do(*actions):
        if fused:
            for action, *given in actions:
                action(*given)

    most = first_cut // PAIR
    far_places, near_places = (3, 2), (1, 0)
    begin(0)
    prepare_row(0)
    attend_pairs(0, 0, most // 2)
    attend_pairs(0, most // 2, most)
    do((pool_one,))
    begin(1)
    prepare_row(1)
    attend_pairs(1, 0, most // 2)
    do((out_y,), (down_z,), (up_x,))
    attend_pairs(1, most // 2, most)
    do((pool_two,))
    begin(2)
    prepare_row(2)
    attend_pairs(2, 0, most // 2)
    do((up_y, 0), (out_z,))
    attend_pairs(2, most // 2, most)
    weight_group(0)
    do((group_core, 0), (down_near_far,), (up_y, 1))
    begin(3)
    attend_pairs(3, 0, 2)
    load_mixed.wait()
    input_parts(0, far_places)
    do((down_far,), (group_y, 0), (out_far,), (up_z, 1))
    input_parts(0, near_places)
    do((up_z, 0), (input_far, 0))
    begin(4)
    attend_pairs(4, 0, 2)
    input_parts(1, far_places)
    input_parts(1, near_places)
    begin(5)
    attend_pairs(5, 0, 1)
    weight_group(1)
    do((group_core, 1), (input_far, 1))
    attend_pairs(5, 1, 2)
    do((group_z, 0))
    input_parts(2, far_places)
    weight_group(2)
    do((group_core, 2), (vector_step, 0, near_dev), (group_y, 1), (input_far, 2))
    input_parts(2, near_places)
    if not fused:
        vector_out[...] = vec_parts[0]
        pool_one()
        for r in range(3):
            input_far(r)
        pool_two()
        for r in range(3):
            input_done(r)
        links.finish()
        return
    do((group_y, 2), (vector_step, 1, across_dev), (up_far,), (group_z, 1), (group_z, 2))
    do((down_end,), (out_end,), (vector_step, 2, y_dev), (up_end,))
    do((vector_z,), (group_far, 0), (group_far, 1), (group_far, 2), (input_done, 0))
    do((group_end, 0), (input_done, 1), (group_end, 1), (vector_end,), (group_end, 2))
    do((input_done, 2))
    links.arrived((DOWN, GATHER), (OUT, GATHER), (UP, NEAR, 0), (UP, NEAR, 1))
    links.arrived(*((GROUP, GATHER, g) for g in range(3)))
    links.finish()


def attend_back(
    fused, x, ids, lse, w_query, w_key, w_value, pool, counts, vectors,
    x_got, q, k, v, context, grad, mixed, up, down, far, out,
):
    rows_here, size, width = x.shape
    keys = size * 4
    low = jnp.bfloat16
    f32 = jnp.float32
    whole = pl.BlockSpec(memory_space=pltpu.VMEM)
    outside = pl.BlockSpec(memory_space=pl.ANY)
    shape = jax.ShapeDtypeStruct
    most = GROUPS[0][1]
    vec = vectors.shape
    small = shape((8, 128), low)
    if fused:
        depth = up.shape[3]
        outs = dict(
            squares=[shape((2, depth // 2, 3 * count), low) for _, count in GROUPS],
            up=shape((4, depth, width), low),
            down=shape((2, 2 * down.shape[1], down.shape[2]), low),
            wo=shape((2, depth, width // 2), low),
            square=small,
        )
    else:
        outs = dict(
            squares=[], up=small, down=small, wo=small, square=shape((3, width, width), low)
        )
    scratch = dict(
        x_got=pltpu.VMEM((2, 3, size, width), low),
        x_t=pltpu.VMEM((rows_here, width, keys), low),
        q=pltpu.VMEM((2, size, most), low),
        k=pltpu.VMEM((2, keys, most), low),
        v=pltpu.VMEM((2, keys, most), low),
        context=pltpu.VMEM((2, size, most), low),
        grad=pltpu.VMEM((2, size, most), low),
        extra=pltpu.VMEM((rows_here, keys, PAIR), low),
        penal=pltpu.VMEM((rows_here, size, PAIR), low),
        delta=pltpu.VMEM((size, PAIR), low),
        dq=pltpu.VMEM((rows_here, size, width), low),
        dk=pltpu.VMEM((rows_here, keys, width), low),
        dv=pltpu.VMEM((rows_here, keys, width), low),
        dx_acc=pltpu.VMEM((rows_here, size, width), f32),
        dx_sent=pltpu.VMEM((rows_here, 2, size, width), low),
        dx_far=pltpu.VMEM((rows_here, size, width), low),
        dx_got=pltpu.VMEM((rows_here, 2, size, width), low),
        dx_far_got=pltpu.VMEM((rows_here, size, width), low),
        pool_parts=pltpu.VMEM(pool.shape, low),
        pool_got=pltpu.VMEM((2,) + pool.shape, low),
        vec_parts=pltpu.VMEM((4,) + vec, f32),
        vec_got=pltpu.VMEM((6,) + vec, f32),
        send_sem=pltpu.SemaphoreType.DMA((72,)),
        recv_sem=pltpu.SemaphoreType.DMA((72,)),
        row_sem=pltpu.SemaphoreType.DMA((2, 6)),
        local_sem=pltpu.SemaphoreType.DMA((5,)),
    )
    if fused:
        tails = [(depth // 2, 3 * count) for _, count in GROUPS]
        spread = lambda *lead: [pltpu.VMEM(lead + tail, low) for tail in tails]
        b_shape = far.shape[2:]
        narrow = (depth, width // 2)
        scratch.update(
            g=spread(2, 4, 2), g_got=spread(4, 2), g_y=spread(4), g_z=spread(3),
            g_s=spread(), g_x=spread(),
            u=pltpu.VMEM((4, 2, depth, width), low),
            u_x=pltpu.VMEM((2, 4, 2, depth // 2, width), low),
            u_y=pltpu.VMEM((2, 4, depth // 2, width), low),
            u_z=pltpu.VMEM((3, depth, width), low),
            a_z=pltpu.VMEM((3,) + down.shape[1:], low),
            a_s=pltpu.VMEM(down.shape[1:], low),
            a_x=pltpu.VMEM(down.shape[1:], low),
            b=pltpu.VMEM((4,) + b_shape, low),
            b_y=pltpu.VMEM((4,) + b_shape, low),
            b_z=pltpu.VMEM((3,) + b_shape, low),
            o=pltpu.VMEM((4,) + narrow, low),
            o_y=pltpu.VMEM((4,) + narrow, low),
            o_z=pltpu.VMEM((3,) + narrow, low),
            o_s=pltpu.VMEM(narrow, low),
            o_x=pltpu.VMEM(narrow, low),
        )
    out_leaves, out_tree = jax.tree.flatten(outs)
    leaves, tree = jax.tree.flatten(scratch)
    count_out = len(out_leaves)
    got = pl.pallas_call(
        functools.partial(attend_back_kernel, fused, count_out, out_tree, tree),
        out_shape=(
            shape((rows_here, size, width), low),
            shape(pool.shape, f32),
            shape(vec, f32),
        )
        + tuple(out_leaves),
        in_specs=[whole] * 9 + [outside] * 7 + [whole] * 4,
        out_specs=(whole,) * (3 + count_out),
        scratch_shapes=leaves,
        compiler_params=pltpu.CompilerParams(
            vmem_limit_bytes=63 * 2**20, collective_id=1, has_side_effects=True
        ),
        cost_estimate=pl.CostEstimate(
            flops=rows_here
            * (4 * (size + 2 * keys) * width * width + 40 * size * keys * width),
            bytes_accessed=2 * (16 * width * width + 9 * keys * width),
            transcendentals=rows_here * HEADS * size * keys,
        ),
    )(
        x, ids, lse, w_query, w_key, w_value, pool, counts, vectors,
        x_got, q, k, v, context, grad, mixed, up, down, far, out,
    )
    return got[:3] + (types.SimpleNamespace(**jax.tree.unflatten(out_tree, got[3:])),)


def outputs_kernel(
    square0, square1, square2, wo, up, down, pool, final_hbm, dx_hbm,
    wq_out, wk_out, wv_out, wo_out, up_out, down_out, pool_out, final_out, dx_out, passed, sem,
):
    loads = [
        pltpu.make_async_copy(source, passed.at[i], sem.at[0, i])
        for i, source in enumerate((final_hbm, dx_hbm))
    ]
    stores = [
        pltpu.make_async_copy(passed.at[i], target, sem.at[1, i])
        for i, target in enumerate((final_out, dx_out))
    ]
    for item in loads:
        item.start()
    f32 = jnp.float32
    pool_out[...] = pool[...].reshape(pool_out.shape)
    for (start, count), square in zip(GROUPS, (square0, square1, square2)):
        rows = square.shape[1]
        for n, out in enumerate((wq_out, wk_out, wv_out)):
            for h in range(2):
                out[h * rows : (h + 1) * rows, start : start + count] = square[
                    h, :, n * count : (n + 1) * count
                ].astype(f32)
    for h in range(2):
        half = wo.shape[2]
        wo_out[:, h * half : (h + 1) * half] = wo[h].astype(f32)
        loads[h].wait()
        stores[h].start()
        rows = down.shape[1]
        down_out[:, h * rows : (h + 1) * rows] = down[h].astype(f32).T
    for i in range(4):
        place, width = (i % 2) * 2 + i // 2, up.shape[2]
        up_out[:, place * width : (place + 1) * width] = up[i].astype(f32)
    for item in stores:
        item.wait()


def outputs(squares, wo, up, down, pool, final, dx):
    f32 = jnp.float32
    whole = pl.BlockSpec(memory_space=pltpu.VMEM)
    outside = pl.BlockSpec(memory_space=pl.ANY)
    shape = jax.ShapeDtypeStruct
    rows, width = up.shape[1:]
    row_count = final.shape[0]
    return pl.pallas_call(
        outputs_kernel,
        out_shape=(
            shape((rows, width), f32), shape((rows, width), f32), shape((rows, width), f32),
            shape((rows, width), f32), shape((rows, 4 * width), f32),
            shape((down.shape[2], 2 * down.shape[1]), f32),
            shape((row_count, pool.shape[0] // row_count, width), f32),
            shape(final.shape, final.dtype), shape(dx.shape, dx.dtype),
        ),
        in_specs=[whole] * 7 + [outside] * 2,
        out_specs=(whole,) * 7 + (outside,) * 2,
        scratch_shapes=[
            pltpu.VMEM((2,) + final.shape, final.dtype),
            pltpu.SemaphoreType.DMA((2, 2)),
        ],
        compiler_params=pltpu.CompilerParams(vmem_limit_bytes=63 * 2**20),
    )(*squares, wo, up, down, pool, final, dx)


def radices_of(count):
    if count == 8:
        return ((1, 2), (2, 4))
    digits = []
    stride = 1
    while stride < count:
        digits.append((stride, 2))
        stride *= 2
    return tuple(digits)


def exchange(piece, axis_name, stride, offset):
    count = lax.axis_size(axis_name)
    pairs = [(i, i ^ (offset * stride)) for i in range(count)]
    return lax.ppermute(piece, axis_name, pairs)


def digit_of(axis_name, stride, radix):
    return (lax.axis_index(axis_name) // stride) % radix


def scatter_digit(pieces, place, axis_name, stride, radix):
    here = digit_of(axis_name, stride, radix)
    received = [
        exchange(
            lax.dynamic_index_in_dim(pieces, here ^ offset, place, keepdims=False).astype(
                jnp.bfloat16
            ),
            axis_name, stride, offset,
        )
        for offset in range(1, radix)
    ]
    total = lax.dynamic_index_in_dim(pieces, here, place, keepdims=False).astype(jnp.float32)
    for item in received:
        total = total + item.astype(jnp.float32)
    return total.astype(jnp.bfloat16)


def halve(piece, place, axis_name, stride):
    half = piece.shape[place] // 2
    here = digit_of(axis_name, stride, 2)
    sent = lax.dynamic_slice_in_dim(piece, (1 - here) * half, half, place).astype(jnp.bfloat16)
    kept = lax.dynamic_slice_in_dim(piece, here * half, half, place).astype(jnp.float32)
    return (kept + exchange(sent, axis_name, stride, 1).astype(jnp.float32)).astype(jnp.bfloat16)


def join(piece, place, axis_name, stride):
    here = digit_of(axis_name, stride, 2)
    other = exchange(piece, axis_name, stride, 1)
    first = jnp.where(here == 0, piece, other)
    second = jnp.where(here == 0, other, piece)
    return jnp.concatenate([first, second], axis=place)


def scatter_rows(group, dp_size):
    digits = radices_of(dp_size)
    shape = tuple(r for _, r in reversed(digits))
    group = group.reshape(shape + (group.shape[0] // dp_size, group.shape[1]))
    for place, (stride, radix) in zip(range(len(digits) - 1, -1, -1), digits):
        group = scatter_digit(group, place, "dp", stride, radix)
    return group


def finish_weight(flat, dp_size, side):
    flat = scatter_rows(flat, dp_size)
    flat = flat.astype(jnp.float32) + exchange(flat, "ctx", 2, 1).astype(jnp.float32)
    return join(flat.astype(jnp.bfloat16), side, "ctx", 1).astype(jnp.float32)


def reduce_weight(gradient, dp_size, side):
    return finish_weight(halve(gradient, side, "ctx", 1), dp_size, side)


def per_device(
    hidden_in,
    seg_ids,
    valid,
    w_query,
    b_query,
    w_key,
    w_value,
    b_value,
    w_out,
    b_out,
    gain_attn,
    shift_attn,
    w_up,
    b_up,
    w_down,
    b_down,
    gain_ffn,
    shift_ffn,
    pooled_text_gradient,
):
    row_count, group_size, model_width = hidden_in.shape
    dp_size = lax.axis_size("dp")
    ff_width = w_up.shape[1]
    rows_here, ff_here = model_width // dp_size, ff_width // dp_size
    fused = dp_size == 8 and rows_here % 32 == 0 and ff_here % 128 == 0
    fused = fused and model_width % 128 == 0 and ff_width == 4 * model_width
    q_all, context, lse_all, ids_got, x_got, k_all, v_all = attend(
        hidden_in, seg_ids, valid, b_query, b_value, w_query, w_key, w_value
    )
    vectors = (b_out, gain_attn, shift_attn, b_up, b_down, gain_ffn, shift_ffn)
    pool, counts, vector_parts, grad_context, grad_mixed, out, final_out, up, down, far = middle(
        fused, hidden_in, context, ids_got, vectors, pooled_text_gradient, w_out, w_up, w_down,
        dp_size,
    )
    if fused:
        up_part = up.reshape(2, 4, 2, rows_here, -1)
        far_part = far.reshape((4, 2) + far.shape[1:])
        out_part = out.reshape(4, 2, rows_here, -1)
    else:
        up_part = far_part = out_part = jnp.zeros((16, 128), jnp.bfloat16)
    grad_input, pooled, vector_sum, sums_of = attend_back(
        fused, hidden_in, ids_got, lse_all, w_query, w_key, w_value,
        pool, counts, vector_parts, x_got, q_all, k_all, v_all, context, grad_context, grad_mixed,
        up_part, down, far_part, out_part,
    )
    if fused:
        *square_sums, up_sum, down_sum, pooled, final_out, grad_input = outputs(
            sums_of.squares, sums_of.wo, sums_of.up, sums_of.down, pooled, final_out, grad_input
        )
    else:
        squares = sums_of.square
        square_sums = [reduce_weight(squares[n], dp_size, 1) for n in range(3)]
        square_sums.append(finish_weight(out, dp_size, 1))
        up_sum = finish_weight(up.transpose(1, 0, 2).reshape(model_width, -1), dp_size, 1)
        down = down.transpose(0, 2, 1).reshape(ff_width, -1)
        down_sum = finish_weight(down, dp_size, 1)
        vector_sum = lax.psum(vector_sum, ("dp", "ctx"))
        pooled = pooled.reshape(row_count, NSEG, model_width)
    place = lax.axis_index("dp")
    sums = lax.dynamic_slice_in_dim(vector_sum[:8], place * rows_here, rows_here, 1)
    sum_bu = lax.dynamic_slice_in_dim(
        vector_sum[8 : 8 + ff_width // model_width].reshape(-1), place * ff_here, ff_here
    )
    results = (
        square_sums[0], sums[0], square_sums[1], square_sums[2], sums[1], square_sums[3],
        sums[2], sums[3], sums[4], up_sum, sum_bu, down_sum, sums[5], sums[6], sums[7],
    )
    return (
        final_out,
        pooled,
        grad_input,
    ) + tuple(results)


def solution(mesh):
    placed = (
        P("dp", "ctx", None),
        P("dp", "ctx"),
        P("dp", "ctx"),
        P(),
        P(),
        P(),
        P(),
        P(),
        P(),
        P(),
        P(),
        P(),
        P(),
        P(),
        P(),
        P(),
        P(),
        P(),
        P("dp", None, None),
    )
    return jax.shard_map(
        per_device,
        mesh=mesh,
        in_specs=placed,
        out_specs=(
            P("dp", "ctx", None),
            P("dp", None, None),
            P("dp", "ctx", None),
            P("dp", None),
            P("dp"),
            P("dp", None),
            P("dp", None),
            P("dp"),
            P("dp", None),
            P("dp"),
            P("dp"),
            P("dp"),
            P("dp", None),
            P("dp"),
            P("dp", None),
            P("dp"),
            P("dp"),
            P("dp"),
        ),
        check_vma=False,
    )
```

```python
import functools
import types

import jax
import jax.numpy as jnp
from jax import lax
from jax.experimental import pallas as pl
from jax.experimental.pallas import tpu as pltpu
from jax.sharding import PartitionSpec as P

HEADS = 12
HEAD_DIM = 64
NSEG = 16


eps = 1e-12


def matmul(left_side, right_side):
    return jnp.dot(left_side, right_side, preferred_element_type=jnp.float32)


PAIR = 2 * HEAD_DIM
MESH = pl.DeviceIdType.MESH
MASKED = -1e30


def dot_nt(left_side, right_side):
    return lax.dot_general(
        left_side, right_side, (((1,), (1,)), ((), ())), preferred_element_type=jnp.float32
    )


def dot_tn(left_side, right_side):
    return lax.dot_general(
        left_side, right_side, (((0,), (0,)), ((), ())), preferred_element_type=jnp.float32
    )


def split_heads(pair):
    lane = lax.broadcasted_iota(jnp.int32, pair.shape, 1)
    zero = jnp.zeros_like(pair)
    return jnp.concatenate(
        [jnp.where(lane < HEAD_DIM, pair, zero), jnp.where(lane < HEAD_DIM, zero, pair)], axis=0
    )


def text_rows(ids_row, size):
    return jnp.broadcast_to(ids_row.astype(jnp.float32), (PAIR, size)).T


def lanes_of(size):
    return lax.broadcasted_iota(jnp.int32, (size, PAIR), 1)


def key_extra(texts):
    lane = lanes_of(texts.shape[0])
    hot = jnp.where(lane.astype(jnp.float32) == texts, 1.0, 0.0)
    return jnp.where((lane >= NSEG) & (lane < 4 * NSEG), 1.0, hot).astype(jnp.bfloat16)


def query_extra(texts):
    lane = lanes_of(texts.shape[0])
    other = (lane < NSEG) & (lane.astype(jnp.float32) != texts)
    return jnp.where(other, MASKED, 0.0)


def with_constants(extra, constants):
    lane = lanes_of(extra.shape[0])
    high = constants.astype(jnp.bfloat16).astype(jnp.float32)
    middle = (constants - high).astype(jnp.bfloat16).astype(jnp.float32)
    rest = constants - high - middle
    terms = jnp.where(lane < 2 * NSEG, high, jnp.where(lane < 3 * NSEG, middle, rest))
    kept = (lane >= NSEG) & (lane < 4 * NSEG)
    return jnp.where(kept, terms, extra).astype(jnp.bfloat16)


def of_head(extra, head):
    lane = lanes_of(extra.shape[0])
    kept = (lane < NSEG) | (lane % NSEG == head)
    return jnp.where(kept, extra, jnp.zeros_like(extra))


def attend_kernel(
    x_ref, seg_ref, valid_ref, b_query, b_value, w_query, w_key, w_value,
    q_out, context_out, lse_out, ids_out, x_hbm, k_hbm, v_hbm,
    x_got, k_ref, v_ref, extra_ref, part_ref, stat_ref, ids_ref, score_one, score_two, send_sem, recv_sem, local_sem,
):
    rows_here, size, width = x_ref.shape
    me = lax.axis_index("ctx")
    one = me + 1 - 2 * (me % 2)
    two = (me + 2) % 4
    three = (one + 2) % 4
    low = jnp.bfloat16

    ids_ref[...] = jnp.zeros_like(ids_ref)
    ids_ref[0:rows_here, :] = seg_ref[...]
    ids_ref[rows_here : 2 * rows_here, :] = valid_ref[...]
    query_bias = b_query[...].astype(jnp.float32)[None]
    value_bias = b_value[...].astype(jnp.float32)[None]
    barrier = pltpu.get_barrier_semaphore()
    for peer in (one, two, three):
        pl.semaphore_signal(barrier, inc=1, device_id={"ctx": peer}, device_id_type=MESH)
    pl.semaphore_wait(barrier, 3)

    def send(source, target, slot, peer):
        return pltpu.make_async_remote_copy(
            src_ref=source, dst_ref=target, send_sem=send_sem.at[slot],
            recv_sem=recv_sem.at[slot], device_id={"ctx": peer}, device_id_type=MESH,
        )

    ids_out[0] = ids_ref[...]
    ids_sends = [send(ids_ref, ids_out.at[j + 1], j, peer) for j, peer in enumerate((one, two, three))]
    near = send(x_ref, x_got.at[0], 3, one)

    def far(r):
        return send(x_ref.at[r], x_got.at[1, r], 4 + r, two)

    def passed(r):
        return send(x_got.at[1, r], x_got.at[2, r], 4 + rows_here + r, one)

    far(0).start()
    near.start()
    for item in ids_sends:
        item.start()
    for r in range(1, rows_here):
        far(r).start()

    def project(x, r, j):
        count = x.shape[0] // size
        k = matmul(x, w_key[...]).astype(low)
        v = (matmul(x, w_value[...]) + value_bias).astype(low)
        for n in range(count):
            rows = pl.ds((j + n if r is not None else j) * size, size)
            k_ref[n if r is None else r, rows, :] = k[n * size : (n + 1) * size]
            v_ref[n if r is None else r, rows, :] = v[n * size : (n + 1) * size]

    own = x_ref[...].reshape(rows_here * size, width)
    q = (matmul(own, w_query[...]) + query_bias).astype(low)
    q_out[...] = (q * HEAD_DIM ** (-0.5)).astype(low).reshape(q_out.shape)
    project(own, None, 0)
    near.wait_recv()
    project(x_got[0].reshape(rows_here * size, width), None, 1)
    for item in ids_sends:
        item.wait_recv()
    lane = lax.broadcasted_iota(jnp.int32, (size, PAIR), 1)
    last = rows_here - 1
    here, there = pl.ds(0, 2 * size), pl.ds(2 * size, 2 * size)

    def make_extras(r, slot):
        for j in range(4):
            texts = text_rows(ids_out[j, r : r + 1, :], size)
            extra_ref[slot, j * size : (j + 1) * size, :] = key_extra(texts)
        return query_extra(text_rows(ids_out[0, r : r + 1, :], size)).astype(low)

    def wide_scores(r, slot, columns, own_extra, keys):
        both = split_heads(q_out[r, :, columns])
        extras = jnp.concatenate([own_extra, own_extra], axis=0)
        wide = jnp.concatenate([k_ref[r, keys, columns], extra_ref[slot, keys, :]], axis=1)
        return dot_nt(jnp.concatenate([both, extras], axis=1), wide)

    def by_head(pair):
        return pl.ds(pl.multiple_of(pair * PAIR, PAIR), PAIR)

    def join_heads(both):
        return jnp.where(lane < HEAD_DIM, both[:size], both[size:])

    last_extra = make_extras(last, 1)

    def first_step(pair, carry):
        columns = by_head(pair)
        scores = wide_scores(last, 1, columns, last_extra, here)
        top = jnp.max(scores, axis=-1, keepdims=True)
        weight = jnp.exp(scores - top)
        total = jnp.sum(weight, axis=-1, keepdims=True)
        part_ref[:, columns] = join_heads(matmul(weight.astype(low), v_ref[last, here, columns]))
        tops, totals = stat_ref[0], stat_ref[1]
        for h in range(2):
            ours, rows = lane == 2 * pair + h, slice(h * size, (h + 1) * size)
            tops = jnp.where(ours, top[rows], tops)
            totals = jnp.where(ours, total[rows], totals)
        stat_ref[0], stat_ref[1] = tops, totals
        return carry

    def second_step(pair, stat):
        columns = by_head(pair)
        scores = wide_scores(last, 1, columns, last_extra, there)

        def column(i):
            return jnp.concatenate(
                [
                    jnp.sum(
                        jnp.where(lane == 2 * pair + h, stat_ref[i], 0.0), axis=1, keepdims=True
                    )
                    for h in range(2)
                ],
                axis=0,
            )

        first_top = column(0)
        top = jnp.maximum(first_top, jnp.max(scores, axis=-1, keepdims=True))
        weight = jnp.exp(scores - top)
        shrink = jnp.exp(first_top - top)
        total = column(1) * shrink + jnp.sum(weight, axis=-1, keepdims=True)
        mixed = join_heads(matmul(weight.astype(low), v_ref[last, there, columns]))
        mixed = mixed + part_ref[:, columns] * join_heads(jnp.broadcast_to(shrink, (2 * size, PAIR)))
        inverse = join_heads(jnp.broadcast_to(1.0 / total, (2 * size, PAIR)))
        context_out[last, :, columns] = (mixed * inverse).astype(low)
        lse = top + jnp.log(total)
        for h in range(2):
            ours = lane % NSEG == 2 * pair + h
            stat = jnp.where(ours, lse[h * size : (h + 1) * size], stat)
        return stat

    stat_ref[...] = jnp.zeros_like(stat_ref)
    lax.fori_loop(0, HEADS // 2, first_step, 0)
    far(0).wait_recv()
    passed(0).start()

    def keep(r):
        return (
            pltpu.make_async_copy(k_ref.at[r], k_hbm.at[r], local_sem.at[0, r]),
            pltpu.make_async_copy(v_ref.at[r], v_hbm.at[r], local_sem.at[1, r]),
            pltpu.make_async_copy(x_got.at[:, r], x_hbm.at[:, r], local_sem.at[2, r]),
        )

    for r in range(rows_here):
        passed(r).wait_recv()
        project(jnp.concatenate([x_got[1, r], x_got[2, r]], axis=0), r, 2)
        for item in keep(r):
            item.start()
        if r == last:
            lse_out[r] = lax.fori_loop(
                0, HEADS // 2, second_step, jnp.zeros((size, PAIR), jnp.float32)
            )
            continue
        own_extra = make_extras(r, 0)

        def score(pair, target, r=r, own_extra=own_extra):
            target[...] = wide_scores(r, 0, by_head(pair), own_extra, pl.ds(0, 4 * size))

        def one_pair(pair, source, stat, r=r):
            columns = pl.ds(pl.multiple_of(pair * PAIR, PAIR), PAIR)
            scores = source[...]
            top = jnp.max(scores, axis=-1, keepdims=True)
            weight = jnp.exp(scores - top)
            total = jnp.sum(weight, axis=-1, keepdims=True)
            mixed = matmul(weight.astype(low), v_ref[r, :, columns]) * (1.0 / total)
            context_out[r, :, columns] = jnp.where(
                lane < HEAD_DIM, mixed[:size], mixed[size:]
            ).astype(low)
            lse = top + jnp.log(total)
            for h in range(2):
                ours = lane % NSEG == 2 * pair + h
                stat = jnp.where(ours, lse[h * size : (h + 1) * size], stat)
            return stat

        def two_pairs(n, carry, r=r):
            stat = lse_out[r]
            score(2 * n + 1, score_two)
            stat = one_pair(2 * n, score_one, stat)
            score(jnp.minimum(2 * n + 2, HEADS // 2 - 1), score_one)
            lse_out[r] = one_pair(2 * n + 1, score_two, stat)
            return carry

        score(0, score_one)
        lse_out[r] = jnp.zeros((size, PAIR), jnp.float32)
        lax.fori_loop(0, HEADS // 4 - 1, two_pairs, 0)
        far(r + 1).wait_recv()
        passed(r + 1).start()
        lax.fori_loop(HEADS // 4 - 1, HEADS // 4, two_pairs, 0)
    for r in range(rows_here):
        for item in keep(r):
            item.wait()
        far(r).wait_send()
        passed(r).wait_send()
    near.wait_send()
    for item in ids_sends:
        item.wait_send()


def attend(x, seg_ids, valid, b_query, b_value, w_query, w_key, w_value):
    rows_here, size, width = x.shape
    keys = size * 4
    low = jnp.bfloat16
    whole = pl.BlockSpec(memory_space=pltpu.VMEM)
    outside = pl.BlockSpec(memory_space=pl.ANY)
    slots = 4 + 2 * rows_here
    return pl.pallas_call(
        attend_kernel,
        out_shape=(
            jax.ShapeDtypeStruct((rows_here, size, width), low),
            jax.ShapeDtypeStruct((rows_here, size, width), low),
            jax.ShapeDtypeStruct((rows_here, size, PAIR), jnp.float32),
            jax.ShapeDtypeStruct((4, 8, size), jnp.int32),
            jax.ShapeDtypeStruct((3,) + x.shape, low),
            jax.ShapeDtypeStruct((rows_here, keys, width), low),
            jax.ShapeDtypeStruct((rows_here, keys, width), low),
        ),
        in_specs=[whole] * 8,
        out_specs=(whole, whole, whole, whole, outside, outside, outside),
        scratch_shapes=[
            pltpu.VMEM((3,) + x.shape, low),
            pltpu.VMEM((rows_here, keys, width), low),
            pltpu.VMEM((rows_here, keys, width), low),
            pltpu.VMEM((2, keys, PAIR), low),
            pltpu.VMEM((size, width), jnp.float32),
            pltpu.VMEM((2, size, PAIR), jnp.float32),
            pltpu.VMEM((8, size), jnp.int32),
            pltpu.VMEM((2 * size, keys), jnp.float32),
            pltpu.VMEM((2 * size, keys), jnp.float32),
            pltpu.SemaphoreType.DMA((slots,)),
            pltpu.SemaphoreType.DMA((slots,)),
            pltpu.SemaphoreType.DMA((3, rows_here)),
        ],
        compiler_params=pltpu.CompilerParams(
            vmem_limit_bytes=56 * 2**20, collective_id=0, has_side_effects=True
        ),
        cost_estimate=pl.CostEstimate(
            flops=rows_here * (2 * (size + 2 * keys) * width * width + 16 * size * keys * width),
            bytes_accessed=2 * (3 * width * width + 9 * keys * width),
            transcendentals=rows_here * HEADS * size * keys,
        ),
    )(x, seg_ids, valid, b_query, b_value, w_query, w_key, w_value)


def gelu_both(u):
    size = jnp.abs(u)
    t = 1.0 / (1.0 + (0.3275911 * 0.5**0.5) * size)
    bell = jnp.exp(-0.5 * u * u)
    poly = t * (
        0.127414796 + t * (-0.142248368 + t * (0.7107068705 + t * (-0.7265760135 + t * 0.5307027145)))
    )
    tail = poly * bell
    cdf = jnp.where(u >= 0.0, 1.0 - tail, tail)
    return u * cdf, cdf + u * bell * 0.3989422804014327


def normalize(values_in):
    centre = jnp.mean(values_in, axis=-1, keepdims=True)
    centred = values_in - centre
    spread = jnp.mean(centred * centred, axis=-1, keepdims=True)
    scale = lax.rsqrt(spread + eps)
    return centred * scale, scale


def normalize_back(grad, unit, scale):
    mean_one = jnp.mean(grad, axis=-1, keepdims=True)
    mean_two = jnp.mean(grad * unit, axis=-1, keepdims=True)
    return (grad - mean_one - unit * mean_two) * scale


def column_sum(values_in):
    return jnp.sum(values_in, axis=0, keepdims=True)


B_QUERY, B_VALUE, B_OUT, GAIN_ONE, SHIFT_ONE, B_DOWN, GAIN_TWO, SHIFT_TWO, B_UP = range(9)


def middle_kernel(
    fused,
    x_ref, context_ref, ids_ref, b_out, gain_one, shift_one, b_up, b_down, gain_two, shift_two,
    text_ref, w_out, up_hbm, down_hbm,
    pool_out, count_out, vector_out, grad_out, mixed_out, wo_out, final_hbm, up_out, down_out, far_out,
    vec_ref, w_up, w_down, unit_ref, scale_ref, normed_ref, normed_t, act_ref, slope_ref, acc_ref, pre_one, pre_two,
    g_ref, g_t_ref, upg_ref, up_got, downg_ref, down_got, wo_sent, wo_got, down_y, down_x,
    send_sem, recv_sem, load_sem, store_sem,
):
    rows_here, size, width = x_ref.shape
    tokens = rows_here * size
    parts = w_up.shape[1] // width
    half = width // 2
    low = jnp.bfloat16
    f32 = jnp.float32
    me = lax.axis_index("ctx")
    core = me % 2
    near = {"ctx": me + 1 - 2 * core}
    side = me // 2
    place = lax.axis_index("dp")
    y = place % 2
    y_dev = {"dp": place + 1 - 2 * y}
    across_dev = {"ctx": (me + 2) % 4}
    peers = [near, across_dev, y_dev] if fused else [near]
    barrier = pltpu.get_barrier_semaphore()
    for peer in peers:
        pl.semaphore_signal(barrier, inc=1, device_id=peer, device_id_type=MESH)
    for row, source in (
        (B_OUT, b_out), (GAIN_ONE, gain_one), (SHIFT_ONE, shift_one), (B_DOWN, b_down),
        (GAIN_TWO, gain_two), (SHIFT_TWO, shift_two),
    ):
        vec_ref[row : row + 1, :] = source[...].astype(f32)[None]
    for i in range(parts):
        vec_ref[B_UP + i : B_UP + i + 1, :] = (
            b_up[i * width : (i + 1) * width].astype(f32)[None]
        )

    def vec(row):
        return vec_ref[row : row + 1, :]

    loads = []
    for i in range(parts):
        loads.append(
            (
                pltpu.make_async_copy(
                    up_hbm.at[:, pl.ds(i * width, width)],
                    w_up.at[:, pl.ds(i * width, width)],
                    load_sem.at[0, i],
                ),
                pltpu.make_async_copy(
                    down_hbm.at[pl.ds(i * width, width)],
                    w_down.at[pl.ds(i * width, width)],
                    load_sem.at[1, i],
                ),
            )
        )
    for pair in loads:
        for item in pair:
            item.start()

    def rows_of(r):
        return pl.ds(pl.multiple_of(r * size, size), size)

    text = lax.broadcasted_iota(jnp.int32, (NSEG, size), 0)

    def members(j, r):
        seg = ids_ref[j, r : r + 1, :]
        real = ids_ref[j, rows_here + r : rows_here + r + 1, :]
        return jnp.where((text == seg) & (real == 1), 1.0, 0.0)

    for r in range(rows_here):
        number = sum(jnp.sum(members(j, r), axis=1, keepdims=True) for j in range(4))
        count_out[r * NSEG : (r + 1) * NSEG, :] = jnp.maximum(number, 1.0)

    def first_norm(r, carry):
        rows = rows_of(r)
        mixed = x_ref[r].astype(f32) + (matmul(context_ref[r], w_out[...]) + vec(B_OUT))
        unit, scale = normalize(mixed)
        unit_ref[rows, :] = unit
        scale_ref[rows, :] = scale
        normed_ref[rows, :] = (unit * vec(GAIN_ONE) + vec(SHIFT_ONE)).astype(low)
        return carry

    lax.fori_loop(0, rows_here, first_norm, 0)
    for pair in loads:
        for item in pair:
            item.wait()

    def units(i):
        return pl.ds(pl.multiple_of(i * width, width), width)

    def forward_part(i, following, now, then):
        for r in range(rows_here):
            rows = pl.ds(r * size, size)
            then[rows, :] = matmul(normed_ref[rows, :], w_up[:, units(following)])
            act, slope = gelu_both(now[rows, :] + vec_ref[pl.ds(B_UP + i, 1), :])
            act = act.astype(low)
            act_ref[rows, units(i)] = act
            slope_ref[rows, units(i)] = slope.astype(low)
            acc_ref[rows, :] += matmul(act, w_down[units(i), :])

    def forward_parts(n, carry):
        forward_part(2 * n, 2 * n + 1, pre_one, pre_two)
        forward_part(2 * n + 1, jnp.minimum(2 * n + 2, parts - 1), pre_two, pre_one)
        return carry

    acc_ref[...] = jnp.zeros_like(acc_ref)
    pre_one[...] = matmul(normed_ref[...], w_up[:, units(0)])
    lax.fori_loop(0, parts // 2, forward_parts, 0)
    normed_t[...] = normed_ref[...].T

    store_final = []
    vector_out[...] = jnp.zeros_like(vector_out)
    for r in range(rows_here):
        rows = pl.ds(r * size, size)
        normed = unit_ref[rows, :] * vec(GAIN_ONE) + vec(SHIFT_ONE)
        summed = normed + (acc_ref[rows, :] + vec(B_DOWN))
        unit, scale = normalize(summed)
        final = unit * vec(GAIN_TWO) + vec(SHIFT_TWO)
        high = final.astype(low)
        upg_ref[parts - 1, rows, :] = high
        item = pltpu.make_async_copy(
            upg_ref.at[parts - 1, rows], final_hbm.at[r], store_sem.at[r]
        )
        item.start()
        store_final.append(item)
        own = members(0, r)
        own_low = own.astype(low)
        rest = (final - high.astype(f32)).astype(low)
        pool = matmul(own_low, high) + matmul(own_low, rest)
        pool_out[r * NSEG : (r + 1) * NSEG, :] = pool.astype(low)
        share = text_ref[r] / count_out[r * NSEG : (r + 1) * NSEG, :]
        first = share.astype(low)
        second = (share - first.astype(f32)).astype(low)
        third = (share - first.astype(f32) - second.astype(f32)).astype(low)
        grad = dot_tn(
            jnp.concatenate([own_low] * 3, axis=0), jnp.concatenate([first, second, third], axis=0)
        )
        back = normalize_back(grad * vec(GAIN_TWO), unit, scale)
        back_low = back.astype(low)
        acc_ref[rows, :] = back
        g_ref[rows, :] = back_low
        vector_out[GAIN_TWO : GAIN_TWO + 1, :] += column_sum(grad * unit)
        vector_out[SHIFT_TWO : SHIFT_TWO + 1, :] += column_sum(grad)
        vector_out[B_DOWN : B_DOWN + 1, :] += column_sum(back_low.astype(f32))

    pl.semaphore_wait(barrier, len(peers))

    def remote(source, target, slot, device=near):
        return pltpu.make_async_remote_copy(
            src_ref=source, dst_ref=target, send_sem=send_sem.at[slot],
            recv_sem=recv_sem.at[slot], device_id=device, device_id_type=MESH,
        )

    per_part = downg_ref.shape[0] // parts
    mine = parts // 2

    def up_send(i):
        return remote(upg_ref.at[i], up_got.at[i], i)

    def down_send(i):
        chunk = pl.ds(i * per_part, per_part)
        return remote(downg_ref.at[chunk, 1 - core], down_got.at[chunk], parts + i)

    cut = downg_ref.shape[3]

    def down_part(i, carry):
        part = matmul(g_t_ref[...], act_ref[:, units(i)]).astype(low)
        part = part.reshape((2, width // 2, width))
        for n in range(per_part):
            downg_ref[per_part * i + n] = part[:, :, n * cut : (n + 1) * cut]
        down_send(i).start()
        return carry

    g_t_ref[...] = g_ref[...].T
    lax.fori_loop(0, parts, down_part, 0)

    def backward_part(step, carry):
        i = (step + mine * (1 - core)) % parts
        back = dot_nt(g_ref[...], w_down[units(i), :])
        back = (back * slope_ref[:, units(i)].astype(f32)).astype(low)
        acc_ref[...] += dot_nt(back, w_up[:, units(i)])
        vector_out[pl.ds(B_UP + i, 1), :] = column_sum(back.astype(f32))
        upg_ref[step] = matmul(normed_t[...], back).astype(low)

        @pl.when(step < mine)
        def _():
            up_send(step).start()

        return carry

    def down_sum(i, carry):
        downg_ref[i, core] = (
            downg_ref[i, core].astype(f32) + down_got[i].astype(f32)
        ).astype(low)
        return carry

    piece = downg_ref.shape[2] // 2
    quarter = piece // 2
    rest = pl.ds(pl.multiple_of(piece + quarter * (1 - side), 16), quarter)
    kept = pl.ds(pl.multiple_of(piece + quarter * side, 16), quarter)
    down_moves = []
    if fused:
        for n in range(4):
            down_moves.append(
                remote(
                    downg_ref.at[2 * n + 1 - y, core, pl.ds(0, piece)], down_y.at[n],
                    2 * parts + 1 + n, y_dev,
                )
            )
        for n in range(8):
            down_moves.append(
                remote(
                    downg_ref.at[n, core, rest], down_x.at[n], 2 * parts + 5 + n, across_dev
                )
            )
    lax.fori_loop(0, 1, backward_part, 0)
    for i in range(parts):
        down_send(i).wait_recv()
    lax.fori_loop(0, downg_ref.shape[0], down_sum, 0)
    for item in down_moves:
        item.start()
    for item in store_final:
        item.wait()
    lax.fori_loop(1, parts, backward_part, 0)

    def first_back(r, carry):
        rows = rows_of(r)
        unit = unit_ref[rows, :]
        grad = acc_ref[rows, :]
        back = normalize_back(grad * vec(GAIN_ONE), unit, scale_ref[rows, :])
        back_low = back.astype(low)
        mixed_out[r] = back
        g_ref[rows, :] = back_low
        vector_out[GAIN_ONE : GAIN_ONE + 1, :] += column_sum(grad * unit)
        vector_out[SHIFT_ONE : SHIFT_ONE + 1, :] += column_sum(grad)
        vector_out[B_OUT : B_OUT + 1, :] += column_sum(back_low.astype(f32))
        return carry

    lax.fori_loop(0, rows_here, first_back, 0)

    for r in range(rows_here):
        g_t_ref[:, r * size : (r + 1) * size] = context_ref[r].T

    def out_part(h):
        columns = pl.ds(pl.multiple_of(h * half, 128), half)
        return matmul(g_t_ref[...], g_ref[:, columns])

    wo_sent[...] = out_part(1 - core).astype(low)
    wo_send = remote(wo_sent, wo_got, 2 * parts)
    wo_send.start()

    def grad_context(r, carry):
        grad_out[r] = dot_nt(g_ref[rows_of(r), :], w_out[...]).astype(low)
        return carry

    lax.fori_loop(0, rows_here, grad_context, 0)
    own_part = out_part(core)
    for i in range(mine):
        up_send(i).wait_recv()

    def up_sum(n, carry):
        rows = pl.ds(pl.multiple_of(n * 128, 128), 128)
        for i in range(mine):
            upg_ref[mine + i, rows, :] = (
                upg_ref[mine + i, rows, :].astype(f32) + up_got[i, rows, :].astype(f32)
            ).astype(low)
        return carry

    lax.fori_loop(0, width // 128, up_sum, 0)
    store_up = pltpu.make_async_copy(
        upg_ref.at[pl.ds(mine, mine)], up_out, store_sem.at[rows_here + 1]
    )
    store_up.start()
    wo_send.wait_recv()
    wo_out[...] = (own_part + wo_got[...].astype(f32)).astype(low)
    if fused:
        for item in down_moves:
            item.wait_recv()

        def near_sum(n, carry):
            down_y[n] = (
                downg_ref[2 * n + y, core, 0:piece, :].astype(f32) + down_y[n].astype(f32)
            ).astype(low)
            return carry

        def far_sum(n, carry):
            down_x[n] = (
                downg_ref[n, core, kept, :].astype(f32) + down_x[n].astype(f32)
            ).astype(low)
            return carry

        lax.fori_loop(0, 4, near_sum, 0)
        lax.fori_loop(0, 8, far_sum, 0)
        stores = [
            pltpu.make_async_copy(down_y, down_out, store_sem.at[rows_here]),
            pltpu.make_async_copy(down_x, far_out, store_sem.at[rows_here + 2]),
        ]
    else:
        stores = [
            pltpu.make_async_copy(downg_ref.at[:, core], down_out, store_sem.at[rows_here])
        ]
    for item in stores:
        item.start()
    for i in range(parts):
        down_send(i).wait_send()
    for i in range(mine):
        up_send(i).wait_send()
    wo_send.wait_send()
    for item in down_moves:
        item.wait_send()
    for item in stores + [store_up]:
        item.wait()


def middle(fused, x, context, ids, vectors, text_gradient, w_out, w_up, w_down, dp_size):
    rows_here, size, width = x.shape
    ff = w_up.shape[1]
    parts = ff // width
    tokens = rows_here * size
    low = jnp.bfloat16
    f32 = jnp.float32
    shape = jax.ShapeDtypeStruct
    whole = pl.BlockSpec(memory_space=pltpu.VMEM)
    outside = pl.BlockSpec(memory_space=pl.ANY)
    chunks = dp_size if fused else parts
    chunk = ff // chunks
    vec = (8 + parts + (-parts) % 8, width)
    if fused:
        down_shape, far_shape = (4, width // 4, chunk), (8, width // 8, chunk)
    else:
        down_shape, far_shape = (chunks, width // 2, chunk), (8, 16, 128)
    return pl.pallas_call(
        functools.partial(middle_kernel, fused),
        out_shape=(
            shape((rows_here * NSEG, width), low),
            shape((rows_here * NSEG, 1), f32),
            shape(vec, f32),
            shape((rows_here, size, width), low),
            shape((rows_here, size, width), f32),
            shape((width, width // 2), low),
            shape((rows_here, size, width), low),
            shape((parts // 2, width, width), low),
            shape(down_shape, low),
            shape(far_shape, low),
        ),
        in_specs=[whole] * 12 + [outside] * 2,
        out_specs=(whole,) * 6 + (outside,) * 4,
        scratch_shapes=[
            pltpu.VMEM(vec, f32),
            pltpu.VMEM((width, ff), low),
            pltpu.VMEM((ff, width), low),
            pltpu.VMEM((tokens, width), f32),
            pltpu.VMEM((tokens, 1), f32),
            pltpu.VMEM((tokens, width), low),
            pltpu.VMEM((width, tokens), low),
            pltpu.VMEM((tokens, ff), low),
            pltpu.VMEM((tokens, ff), low),
            pltpu.VMEM((tokens, width), f32),
            pltpu.VMEM((tokens, width), f32),
            pltpu.VMEM((tokens, width), f32),
            pltpu.VMEM((tokens, width), low),
            pltpu.VMEM((width, tokens), low),
            pltpu.VMEM((parts, width, width), low),
            pltpu.VMEM((parts // 2, width, width), low),
            pltpu.VMEM((chunks, 2, width // 2, chunk), low),
            pltpu.VMEM((chunks, width // 2, chunk), low),
            pltpu.VMEM((width, width // 2), low),
            pltpu.VMEM((width, width // 2), low),
            pltpu.VMEM(down_shape if fused else (16, 128), low),
            pltpu.VMEM(far_shape, low),
            pltpu.SemaphoreType.DMA((2 * parts + 13,)),
            pltpu.SemaphoreType.DMA((2 * parts + 13,)),
            pltpu.SemaphoreType.DMA((2, parts)),
            pltpu.SemaphoreType.DMA((rows_here + 3,)),
        ],
        compiler_params=pltpu.CompilerParams(
            vmem_limit_bytes=63 * 2**20, collective_id=2, has_side_effects=True
        ),
        cost_estimate=pl.CostEstimate(
            flops=2 * tokens * width * (6 * ff + 3 * width),
            bytes_accessed=2 * (5 * ff * width + 8 * tokens * width),
            transcendentals=2 * tokens * ff,
        ),
    )(x, context, ids, *vectors, text_gradient, w_out, w_up, w_down)


class Links:
    def __init__(self, send_sem, recv_sem):
        self.send_sem, self.recv_sem = send_sem, recv_sem
        self.slots, self.copies = {}, {}

    def start(self, name, source, target, device):
        slot = self.slots.setdefault(name, len(self.slots))
        copy = pltpu.make_async_remote_copy(
            src_ref=source, dst_ref=target, send_sem=self.send_sem.at[slot],
            recv_sem=self.recv_sem.at[slot], device_id=device, device_id_type=MESH,
        )
        copy.start()
        self.copies[name] = copy

    def arrived(self, *names):
        for name in names:
            self.copies[name].wait_recv()

    def finish(self):
        for copy in self.copies.values():
            copy.wait_send()


def add_into(target, others, count):
    def one(i, carry):
        total = target[i].astype(jnp.float32)
        for other in others:
            total = total + other[i].astype(jnp.float32)
        target[i] = total.astype(target.dtype)
        return carry

    lax.fori_loop(0, count, one, 0)


def add_up(parts):
    total = parts[0].astype(jnp.float32)
    for part in parts[1:]:
        total = total + part.astype(jnp.float32)
    return total


POOL, UP, DOWN_A, DOWN_B, DOWN, OUT, GROUP, DX, VECTOR = range(9)
STEP, NEAR, FAR, SIDE, LINE, GATHER = range(6)

GROUPS = ((0, 4 * PAIR), (4 * PAIR, PAIR), (5 * PAIR, PAIR))


def attend_back_kernel(
    fused, count_out, out_tree, tree,
    x_ref, ids_ref, lse_ref, w_query, w_key, w_value, pool_ref, count_ref, vector_ref,
    x_hbm, q_hbm, k_hbm, v_hbm, context_hbm, grad_hbm, mixed_hbm, up_ref, down_ref, far_ref, out_ref,
    dx_out, pool_out, vector_out, *rest,
):
    outs = types.SimpleNamespace(**jax.tree.unflatten(out_tree, rest[:count_out]))
    ref = types.SimpleNamespace(**jax.tree.unflatten(tree, rest[count_out:]))
    square_out, up_out, down_out, wo_out = outs.square, outs.up, outs.down, outs.wo
    q_ref, k_ref, v_ref, context_ref, grad_ref = ref.q, ref.k, ref.v, ref.context, ref.grad
    dq_ref, dk_ref, dv_ref, x_t, x_got = ref.dq, ref.dk, ref.dv, ref.x_t, ref.x_got
    extra_ref, penal_ref, delta_ref = ref.extra, ref.penal, ref.delta
    dx_acc, dx_sent, dx_far, dx_got, dx_far_got = (
        ref.dx_acc, ref.dx_sent, ref.dx_far, ref.dx_got, ref.dx_far_got
    )
    pool_parts, pool_got, vec_parts, vec_got = (
        ref.pool_parts, ref.pool_got, ref.vec_parts, ref.vec_got
    )
    row_sem, local_sem = ref.row_sem, ref.local_sem
    rows_here, size, width = x_ref.shape
    low = jnp.bfloat16
    me, place = lax.axis_index("ctx"), lax.axis_index("dp")
    core, side = me % 2, me // 2
    near, across = me + 1 - 2 * core, (me + 2) % 4
    near_dev, across_dev = {"ctx": near}, {"ctx": across}
    y, z = place % 2, place // 2
    y_dev = {"dp": place + 1 - 2 * y}
    z_at = (z + 1 - 2 * (z % 2), (z + 2) % 4, 3 - z)
    z_dev = [{"dp": other * 2 + y} for other in z_at]
    peers = [near_dev, across_dev] + ([y_dev] + z_dev if fused else [])

    barrier = pltpu.get_barrier_semaphore()
    for peer in peers:
        pl.semaphore_signal(barrier, inc=1, device_id=peer, device_id_type=MESH)
    pl.semaphore_wait(barrier, len(peers))
    links = Links(ref.send_sem, ref.recv_sem)

    first_cut = GROUPS[1][0]
    blocks = [(0, first_cut, r) for r in range(rows_here)]
    blocks += [(first_cut, width - first_cut, r) for r in range(rows_here)]

    def load_block(step):
        slot = step % 2
        start, count, r = blocks[step]
        columns, local = pl.ds(start, count), pl.ds(0, count)
        pairs = (
            (k_hbm, k_ref), (v_hbm, v_ref), (q_hbm, q_ref), (context_hbm, context_ref),
            (grad_hbm, grad_ref),
        )
        copies = [
            pltpu.make_async_copy(
                source.at[r, :, columns], target.at[slot, :, local], row_sem.at[slot, i]
            )
            for i, (source, target) in enumerate(pairs)
        ]
        if step < rows_here:
            copies.append(pltpu.make_async_copy(x_hbm.at[:, r], x_got.at[slot], row_sem.at[slot, 5]))
        return copies

    for item in load_block(0):
        item.start()
    load_mixed = pltpu.make_async_copy(mixed_hbm, dx_acc, local_sem.at[0])
    links.start((POOL, STEP, 0), pool_ref, pool_got.at[0], near_dev)
    if fused:
        u_ref, u_x, u_y, u_z = ref.u, ref.u_x, ref.u_y, ref.u_z
        a_z, a_s, a_x = ref.a_z, ref.a_s, ref.a_x
        b_ref, b_y, b_z = ref.b, ref.b_y, ref.b_z
        o_ref, o_y, o_z, o_s, o_x = ref.o, ref.o_y, ref.o_z, ref.o_s, ref.o_x
        half_rows = u_ref.shape[2] // 2
        links.start((UP, FAR, 0), up_ref.at[1 - side, :, :, pl.ds(0, half_rows)], u_x.at[0], across_dev)
        links.start((DOWN_B, SIDE), far_ref.at[:, 1 - y], b_y, y_dev)
        for o in range(3):
            links.start((DOWN_A, LINE, o), down_ref.at[z_at[o]], a_z.at[o], z_dev[o])
    load_mixed.start()
    vec_parts[0] = vector_ref[...]

    def pool_one():
        links.arrived((POOL, STEP, 0))
        pool_parts[...] = add_up([pool_ref[...], pool_got[0]]).astype(low)
        links.start((POOL, STEP, 1), pool_parts, pool_got.at[1], across_dev)

    def pool_two():
        links.arrived((POOL, STEP, 1))
        pool_out[...] = add_up([pool_parts[...], pool_got[1]]) / count_ref[...]

    def send_z(name, source, target):
        for o in range(3):
            links.start(name + (o,), source(z_at[o]), target(o), z_dev[o])

    def arrived_z(name):
        links.arrived(*(name + (o,) for o in range(3)))

    def out_y():
        links.start((OUT, SIDE), out_ref.at[:, 1 - y], o_y, y_dev)

    def out_z():
        links.arrived((OUT, SIDE))
        for i in range(4):
            o_ref[i] = add_up([out_ref[i, y], o_y[i]]).astype(low)
        send_z((OUT, LINE), lambda i: o_ref.at[i], lambda o: o_z.at[o])

    def out_far():
        arrived_z((OUT, LINE))
        o_s[...] = add_up([o_ref[z]] + [o_z[o] for o in range(3)]).astype(low)
        links.start((OUT, FAR), o_s, o_x, across_dev)

    def out_end():
        links.arrived((OUT, FAR))
        wo_out[core] = add_up([o_s[...], o_x[...]]).astype(low)
        links.start((OUT, GATHER), wo_out.at[core], wo_out.at[core], near_dev)

    def down_z():
        links.arrived((DOWN_B, SIDE))
        for i in range(4):
            b_ref[i] = add_up([far_ref[i, y], b_y[i]]).astype(low)
        send_z((DOWN_B, LINE), lambda i: b_ref.at[i], lambda o: b_z.at[o])

    def down_near_far():
        arrived_z((DOWN_A, LINE))
        a_s[...] = add_up([down_ref[z]] + [a_z[o] for o in range(3)]).astype(low)
        links.start((DOWN_A, FAR), a_s, a_x, across_dev)

    def down_far():
        arrived_z((DOWN_B, LINE))
        count = b_ref.shape[1]
        own = pl.ds(pl.multiple_of(2 * count + side * count, 16), count)
        down_out[core, own] = add_up([b_ref[z]] + [b_z[o] for o in range(3)]).astype(low)
        links.start((DOWN_B, FAR), down_out.at[core, own], down_out.at[core, own], across_dev)

    def down_end():
        links.arrived((DOWN_A, FAR), (DOWN_B, FAR))
        down_out[core, 0 : a_s.shape[0]] = add_up([a_s[...], a_x[...]]).astype(low)
        links.start((DOWN, GATHER), down_out.at[core], down_out.at[core], near_dev)

    def up_x():
        rows = pl.ds(half_rows, half_rows)
        links.start((UP, FAR, 1), up_ref.at[1 - side, :, :, rows], u_x.at[1], across_dev)

    def up_y(h):
        rows = pl.ds(h * half_rows, half_rows)
        links.arrived((UP, FAR, h))
        for i in range(4):
            for j in range(2):
                u_ref[i, j, rows] = add_up([up_ref[side, i, j, rows], u_x[h, i, j]]).astype(low)
        links.start((UP, SIDE, h), u_ref.at[:, 1 - y, rows], u_y.at[h], y_dev)

    def up_z(h):
        rows = pl.ds(h * half_rows, half_rows)
        links.arrived((UP, SIDE, h))
        for i in range(4):
            u_ref[i, y, rows] = add_up([u_ref[i, y, rows], u_y[h, i]]).astype(low)
        send_z((UP, LINE, h), lambda i: u_ref.at[i, y, rows], lambda o: u_z.at[o, rows])

    def up_far():
        arrived_z((UP, LINE, 0))
        arrived_z((UP, LINE, 1))
        up_out[me] = add_up([u_ref[z, y]] + [u_z[o] for o in range(3)]).astype(low)
        links.start((UP, GATHER), up_out.at[me], up_out.at[me], across_dev)

    def up_end():
        links.arrived((UP, GATHER))
        links.start((UP, NEAR, 0), up_out.at[me], up_out.at[me], near_dev)
        links.start((UP, NEAR, 1), up_out.at[across], up_out.at[across], near_dev)

    def group_core(g):
        links.start((GROUP, NEAR, g), ref.g[g].at[1 - core], ref.g_got[g], near_dev)

    def group_y(g):
        links.arrived((GROUP, NEAR, g))
        for i in range(4):
            add_into(ref.g[g].at[core, i], [ref.g_got[g].at[i]], 2)
        links.start((GROUP, SIDE, g), ref.g[g].at[core, :, 1 - y], ref.g_y[g], y_dev)

    def group_z(g):
        links.arrived((GROUP, SIDE, g))
        own = ref.g[g]
        for i in range(4):
            own[core, i, y] = add_up([own[core, i, y], ref.g_y[g][i]]).astype(low)
        send_z((GROUP, LINE, g), lambda i: own.at[core, i, y], lambda o: ref.g_z[g].at[o])

    def group_far(g):
        arrived_z((GROUP, LINE, g))
        pieces = [ref.g[g][core, z, y]] + [ref.g_z[g][o] for o in range(3)]
        ref.g_s[g][...] = add_up(pieces).astype(low)
        links.start((GROUP, FAR, g), ref.g_s[g], ref.g_x[g], across_dev)

    def group_end(g):
        links.arrived((GROUP, FAR, g))
        out = outs.squares[g]
        out[core] = add_up([ref.g_s[g][...], ref.g_x[g][...]]).astype(low)
        links.start((GROUP, GATHER, g), out.at[core], out.at[core], near_dev)

    def vector_step(i, device):
        if i:
            links.arrived((VECTOR, STEP, i - 1))
            vec_parts[i] = vec_parts[i - 1] + vec_got[i - 1]
        if device is not None:
            links.start((VECTOR, STEP, i), vec_parts.at[i], vec_got.at[i], device)

    def vector_z():
        vector_step(3, None)
        for o in range(3):
            links.start((VECTOR, LINE, o), vec_parts.at[3], vec_got.at[3 + o], z_dev[o])

    def vector_end():
        arrived_z((VECTOR, LINE))
        vector_out[...] = vec_parts[3] + (vec_got[3] + (vec_got[4] + vec_got[5]))

    row = lax.broadcasted_iota(jnp.int32, (PAIR, size), 0)

    def find_delta(step):
        slot = step % 2
        start, count, _ = blocks[step]
        lane = lax.broadcasted_iota(jnp.int32, (count, PAIR), 1)
        head = (start + lax.broadcasted_iota(jnp.int32, (count, PAIR), 0)) // HEAD_DIM
        member = jnp.where((lane % NSEG == head) & (lane >= NSEG) & (lane < 4 * NSEG), 1.0, 0.0)
        member = member.astype(low)
        local = pl.ds(0, count)
        product = grad_ref[slot, :, local].astype(jnp.float32) * context_ref[
            slot, :, local
        ].astype(jnp.float32)
        total = jnp.zeros((size, PAIR), jnp.float32)
        for _ in range(3):
            term = product.astype(low)
            total = total + matmul(term, member)
            product = product - term.astype(jnp.float32)
        delta_ref[...] = with_constants(jnp.zeros_like(total), -total)

    def attend_pairs(step, first, last):
        slot = step % 2
        start, _, r = blocks[step]

        def one_pair(n, carry):
            local = pl.ds(pl.multiple_of(n * PAIR, PAIR), PAIR)
            columns = pl.ds(pl.multiple_of(start + n * PAIR, PAIR), PAIR)
            head = 2 * (start // PAIR + n)
            q_both = split_heads(q_ref[slot, :, local])
            g_both = split_heads(grad_ref[slot, :, local])
            q_extra = [of_head(penal_ref[r], head + h) for h in range(2)]
            g_extra = [of_head(delta_ref[...], head + h) for h in range(2)]
            q_wide = jnp.concatenate([q_both, jnp.concatenate(q_extra, axis=0)], axis=1)
            g_wide = jnp.concatenate([g_both, jnp.concatenate(g_extra, axis=0)], axis=1)
            q_wide, g_wide = q_wide.T, g_wide.T
            dq = jnp.zeros((PAIR, 2 * size), jnp.float32)

            def products(j):
                rows = pl.ds(j * size, size)
                extra = extra_ref[r, rows, :]
                keys = jnp.concatenate([k_ref[slot, rows, local], extra], axis=1)
                values = jnp.concatenate([v_ref[slot, rows, local], extra], axis=1)
                return matmul(keys, q_wide), matmul(values, g_wide)

            ahead = products(0)
            for j in range(4):
                rows = pl.ds(j * size, size)
                scores, grad_p = ahead
                if j < 3:
                    ahead = products(j + 1)
                probs = jnp.exp(scores)
                grad_s = (probs * grad_p).astype(low)
                dv_ref[r, rows, columns] = matmul(probs.astype(low), g_both).astype(low)
                dk_ref[r, rows, columns] = matmul(grad_s, q_both).astype(low)
                dq = dq + matmul(k_ref[slot, rows, local].T, grad_s)
            dq = jnp.where(row < HEAD_DIM, dq[:, :size], dq[:, size:]) * HEAD_DIM ** (-0.5)
            dq_ref[r, :, columns] = dq.T.astype(low)
            return carry

        lax.fori_loop(first, last, one_pair, 0)

    def weight_group(g):
        start, count = GROUPS[g]
        if fused:
            depth = ref.g[g].shape[3]

        def keep(n, i, total):
            total = total.astype(low)
            wide = total.shape[1]
            if not fused:
                square_out[n, :, pl.ds(pl.multiple_of(start + i * PAIR, PAIR), wide)] = total
                return
            total = total.reshape(4, 2, 2, depth, wide)
            target = pl.ds(pl.multiple_of(n * count + i * PAIR, PAIR), wide)
            for h in range(2):
                ref.g[g][h, :, :, :, target] = total[:, :, h]

        def of_source(source, columns):
            keys = source.shape[1]
            return sum(
                matmul(x_t[r, :, :keys], source[r, :, columns]) for r in range(rows_here)
            )

        def one_part(i, carry):
            columns = pl.ds(pl.multiple_of(start + 2 * i * PAIR, PAIR), 2 * PAIR)
            for n, source in enumerate((dq_ref, dk_ref, dv_ref)):
                keep(n, 2 * i, of_source(source, columns))
            return carry

        if count % (2 * PAIR):
            columns = pl.ds(start, count)
            keep(0, 0, of_source(dq_ref, columns))
            both = sum(
                matmul(
                    x_t[r],
                    jnp.concatenate([dk_ref[r, :, columns], dv_ref[r, :, columns]], axis=1),
                )
                for r in range(rows_here)
            )
            keep(1, 0, both[:, :count])
            keep(2, 0, both[:, count:])
        else:
            lax.fori_loop(0, count // (2 * PAIR), one_part, 0)
        columns = pl.ds(start, count)
        for n, source in enumerate((dq_ref, dv_ref)):
            vec_parts[0, n : n + 1, columns] = sum(
                jnp.sum(source[r, :, columns].astype(jnp.float32), axis=0, keepdims=True)
                for r in range(rows_here)
            )

    def input_parts(r):
        for j in (3, 2, 1, 0):
            rows = pl.ds(j * size, size)
            total = dot_nt(dk_ref[r, rows, :], w_key[...]) + dot_nt(dv_ref[r, rows, :], w_value[...])
            if j == 0:
                dx_acc[r] = dx_acc[r] + total + dot_nt(dq_ref[r], w_query[...])
            elif j == 2:
                dx_far[r] = total.astype(low)
            else:
                n = j // 2
                dx_sent[r, n] = total.astype(low)
                links.start((DX, NEAR, r, n), dx_sent.at[r, n], dx_got.at[r, n], near_dev)

    def input_far(r):
        links.arrived((DX, NEAR, r, 1))
        dx_far[r] = add_up([dx_far[r], dx_got[r, 1]]).astype(low)
        links.start((DX, FAR, r), dx_far.at[r], dx_far_got.at[r], across_dev)

    def input_done(r):
        links.arrived((DX, NEAR, r, 0), (DX, FAR, r))
        dx_out[r] = add_up([dx_acc[r], dx_got[r, 0], dx_far_got[r]]).astype(low)

    def prepare_row(r):
        slot = r % 2
        for j in range(4):
            rows = slice(j * size, (j + 1) * size)
            texts = text_rows(ids_ref[j, r : r + 1, :], size)
            extra_ref[r, rows, :] = key_extra(texts)
            if j == 0:
                penal_ref[r] = with_constants(query_extra(texts), -lse_ref[r])
            block = x_ref[r] if j == 0 else x_got[slot, j - 1]
            x_t[r, :, rows] = block.T

    def begin(step):
        for item in load_block(step):
            item.wait()
        if step + 1 < len(blocks):
            for item in load_block(step + 1):
                item.start()
        find_delta(step)

    def do(*actions):
        if fused:
            for action, *given in actions:
                action(*given)

    most = first_cut // PAIR
    begin(0)
    prepare_row(0)
    attend_pairs(0, 0, most // 2)
    attend_pairs(0, most // 2, most)
    do((pool_one,))
    begin(1)
    prepare_row(1)
    attend_pairs(1, 0, most // 2)
    do((out_y,), (down_z,), (up_x,))
    attend_pairs(1, most // 2, most)
    do((pool_two,))
    begin(2)
    prepare_row(2)
    attend_pairs(2, 0, most // 2)
    do((up_y, 0), (out_z,))
    attend_pairs(2, most // 2, most)
    weight_group(0)
    do((group_core, 0), (down_near_far,), (up_y, 1))
    begin(3)
    attend_pairs(3, 0, 2)
    load_mixed.wait()
    input_parts(0)
    do((down_far,), (group_y, 0), (out_far,), (up_z, 1), (up_z, 0), (input_far, 0))
    begin(4)
    attend_pairs(4, 0, 2)
    input_parts(1)
    begin(5)
    attend_pairs(5, 0, 1)
    weight_group(1)
    do((group_core, 1), (input_far, 1))
    attend_pairs(5, 1, 2)
    do((group_z, 0))
    weight_group(2)
    do((group_core, 2), (vector_step, 0, near_dev))
    input_parts(2)
    if not fused:
        vector_out[...] = vec_parts[0]
        pool_one()
        for r in range(3):
            input_far(r)
        pool_two()
        for r in range(3):
            input_done(r)
        links.finish()
        return
    do((group_y, 2), (group_y, 1), (vector_step, 1, across_dev), (up_far,), (input_far, 2))
    do((group_z, 2), (down_end,), (out_end,), (vector_step, 2, y_dev), (up_end,), (group_z, 1))
    do((vector_z,), (group_far, 0), (group_far, 2), (group_far, 1), (input_done, 0))
    do((group_end, 0), (group_end, 2), (vector_end,), (group_end, 1), (input_done, 1))
    do((input_done, 2))
    links.arrived((DOWN, GATHER), (OUT, GATHER), (UP, NEAR, 0), (UP, NEAR, 1))
    links.arrived(*((GROUP, GATHER, g) for g in range(3)))
    links.finish()


def attend_back(
    fused, x, ids, lse, w_query, w_key, w_value, pool, counts, vectors,
    x_got, q, k, v, context, grad, mixed, up, down, far, out,
):
    rows_here, size, width = x.shape
    keys = size * 4
    low = jnp.bfloat16
    f32 = jnp.float32
    whole = pl.BlockSpec(memory_space=pltpu.VMEM)
    outside = pl.BlockSpec(memory_space=pl.ANY)
    shape = jax.ShapeDtypeStruct
    most = GROUPS[0][1]
    vec = vectors.shape
    small = shape((8, 128), low)
    if fused:
        depth = up.shape[3]
        outs = dict(
            squares=[shape((2, depth // 2, 3 * count), low) for _, count in GROUPS],
            up=shape((4, depth, width), low),
            down=shape((2, 2 * down.shape[1], down.shape[2]), low),
            wo=shape((2, depth, width // 2), low),
            square=small,
        )
    else:
        outs = dict(
            squares=[], up=small, down=small, wo=small, square=shape((3, width, width), low)
        )
    scratch = dict(
        x_got=pltpu.VMEM((2, 3, size, width), low),
        x_t=pltpu.VMEM((rows_here, width, keys), low),
        q=pltpu.VMEM((2, size, most), low),
        k=pltpu.VMEM((2, keys, most), low),
        v=pltpu.VMEM((2, keys, most), low),
        context=pltpu.VMEM((2, size, most), low),
        grad=pltpu.VMEM((2, size, most), low),
        extra=pltpu.VMEM((rows_here, keys, PAIR), low),
        penal=pltpu.VMEM((rows_here, size, PAIR), low),
        delta=pltpu.VMEM((size, PAIR), low),
        dq=pltpu.VMEM((rows_here, size, width), low),
        dk=pltpu.VMEM((rows_here, keys, width), low),
        dv=pltpu.VMEM((rows_here, keys, width), low),
        dx_acc=pltpu.VMEM((rows_here, size, width), f32),
        dx_sent=pltpu.VMEM((rows_here, 2, size, width), low),
        dx_far=pltpu.VMEM((rows_here, size, width), low),
        dx_got=pltpu.VMEM((rows_here, 2, size, width), low),
        dx_far_got=pltpu.VMEM((rows_here, size, width), low),
        pool_parts=pltpu.VMEM(pool.shape, low),
        pool_got=pltpu.VMEM((2,) + pool.shape, low),
        vec_parts=pltpu.VMEM((4,) + vec, f32),
        vec_got=pltpu.VMEM((6,) + vec, f32),
        send_sem=pltpu.SemaphoreType.DMA((72,)),
        recv_sem=pltpu.SemaphoreType.DMA((72,)),
        row_sem=pltpu.SemaphoreType.DMA((2, 6)),
        local_sem=pltpu.SemaphoreType.DMA((5,)),
    )
    if fused:
        tails = [(depth // 2, 3 * count) for _, count in GROUPS]
        spread = lambda *lead: [pltpu.VMEM(lead + tail, low) for tail in tails]
        b_shape = far.shape[2:]
        narrow = (depth, width // 2)
        scratch.update(
            g=spread(2, 4, 2), g_got=spread(4, 2), g_y=spread(4), g_z=spread(3),
            g_s=spread(), g_x=spread(),
            u=pltpu.VMEM((4, 2, depth, width), low),
            u_x=pltpu.VMEM((2, 4, 2, depth // 2, width), low),
            u_y=pltpu.VMEM((2, 4, depth // 2, width), low),
            u_z=pltpu.VMEM((3, depth, width), low),
            a_z=pltpu.VMEM((3,) + down.shape[1:], low),
            a_s=pltpu.VMEM(down.shape[1:], low),
            a_x=pltpu.VMEM(down.shape[1:], low),
            b=pltpu.VMEM((4,) + b_shape, low),
            b_y=pltpu.VMEM((4,) + b_shape, low),
            b_z=pltpu.VMEM((3,) + b_shape, low),
            o=pltpu.VMEM((4,) + narrow, low),
            o_y=pltpu.VMEM((4,) + narrow, low),
            o_z=pltpu.VMEM((3,) + narrow, low),
            o_s=pltpu.VMEM(narrow, low),
            o_x=pltpu.VMEM(narrow, low),
        )
    out_leaves, out_tree = jax.tree.flatten(outs)
    leaves, tree = jax.tree.flatten(scratch)
    count_out = len(out_leaves)
    got = pl.pallas_call(
        functools.partial(attend_back_kernel, fused, count_out, out_tree, tree),
        out_shape=(
            shape((rows_here, size, width), low),
            shape(pool.shape, f32),
            shape(vec, f32),
        )
        + tuple(out_leaves),
        in_specs=[whole] * 9 + [outside] * 7 + [whole] * 4,
        out_specs=(whole,) * (3 + count_out),
        scratch_shapes=leaves,
        compiler_params=pltpu.CompilerParams(
            vmem_limit_bytes=63 * 2**20, collective_id=1, has_side_effects=True
        ),
        cost_estimate=pl.CostEstimate(
            flops=rows_here
            * (4 * (size + 2 * keys) * width * width + 40 * size * keys * width),
            bytes_accessed=2 * (16 * width * width + 9 * keys * width),
            transcendentals=rows_here * HEADS * size * keys,
        ),
    )(
        x, ids, lse, w_query, w_key, w_value, pool, counts, vectors,
        x_got, q, k, v, context, grad, mixed, up, down, far, out,
    )
    return got[:3] + (types.SimpleNamespace(**jax.tree.unflatten(out_tree, got[3:])),)


def outputs_kernel(
    square0, square1, square2, wo, up, down, pool, final, dx,
    wq_out, wk_out, wv_out, wo_out, up_out, down_out, pool_out, final_out, dx_out,
):
    final_out[...] = final[...]
    dx_out[...] = dx[...]
    f32 = jnp.float32
    pool_out[...] = pool[...].reshape(pool_out.shape)
    for (start, count), square in zip(GROUPS, (square0, square1, square2)):
        rows = square.shape[1]
        for n, out in enumerate((wq_out, wk_out, wv_out)):
            for h in range(2):
                out[h * rows : (h + 1) * rows, start : start + count] = square[
                    h, :, n * count : (n + 1) * count
                ].astype(f32)
    for h in range(2):
        half = wo.shape[2]
        wo_out[:, h * half : (h + 1) * half] = wo[h].astype(f32)
        rows = down.shape[1]
        down_out[:, h * rows : (h + 1) * rows] = down[h].astype(f32).T
    for i in range(4):
        place, width = (i % 2) * 2 + i // 2, up.shape[2]
        up_out[:, place * width : (place + 1) * width] = up[i].astype(f32)


def outputs(squares, wo, up, down, pool, final, dx):
    f32 = jnp.float32
    whole = pl.BlockSpec(memory_space=pltpu.VMEM)
    shape = jax.ShapeDtypeStruct
    rows, width = up.shape[1:]
    row_count = final.shape[0]
    return pl.pallas_call(
        outputs_kernel,
        out_shape=(
            shape((rows, width), f32), shape((rows, width), f32), shape((rows, width), f32),
            shape((rows, width), f32), shape((rows, 4 * width), f32),
            shape((down.shape[2], 2 * down.shape[1]), f32),
            shape((row_count, pool.shape[0] // row_count, width), f32),
            shape(final.shape, final.dtype), shape(dx.shape, dx.dtype),
        ),
        in_specs=[whole] * 9,
        out_specs=(whole,) * 9,
        compiler_params=pltpu.CompilerParams(vmem_limit_bytes=63 * 2**20),
    )(*squares, wo, up, down, pool, final, dx)


def radices_of(count):
    if count == 8:
        return ((1, 2), (2, 4))
    digits = []
    stride = 1
    while stride < count:
        digits.append((stride, 2))
        stride *= 2
    return tuple(digits)


def exchange(piece, axis_name, stride, offset):
    count = lax.axis_size(axis_name)
    pairs = [(i, i ^ (offset * stride)) for i in range(count)]
    return lax.ppermute(piece, axis_name, pairs)


def digit_of(axis_name, stride, radix):
    return (lax.axis_index(axis_name) // stride) % radix


def scatter_digit(pieces, place, axis_name, stride, radix):
    here = digit_of(axis_name, stride, radix)
    received = [
        exchange(
            lax.dynamic_index_in_dim(pieces, here ^ offset, place, keepdims=False).astype(
                jnp.bfloat16
            ),
            axis_name, stride, offset,
        )
        for offset in range(1, radix)
    ]
    total = lax.dynamic_index_in_dim(pieces, here, place, keepdims=False).astype(jnp.float32)
    for item in received:
        total = total + item.astype(jnp.float32)
    return total.astype(jnp.bfloat16)


def halve(piece, place, axis_name, stride):
    half = piece.shape[place] // 2
    here = digit_of(axis_name, stride, 2)
    sent = lax.dynamic_slice_in_dim(piece, (1 - here) * half, half, place).astype(jnp.bfloat16)
    kept = lax.dynamic_slice_in_dim(piece, here * half, half, place).astype(jnp.float32)
    return (kept + exchange(sent, axis_name, stride, 1).astype(jnp.float32)).astype(jnp.bfloat16)


def join(piece, place, axis_name, stride):
    here = digit_of(axis_name, stride, 2)
    other = exchange(piece, axis_name, stride, 1)
    first = jnp.where(here == 0, piece, other)
    second = jnp.where(here == 0, other, piece)
    return jnp.concatenate([first, second], axis=place)


def scatter_rows(group, dp_size):
    digits = radices_of(dp_size)
    shape = tuple(r for _, r in reversed(digits))
    group = group.reshape(shape + (group.shape[0] // dp_size, group.shape[1]))
    for place, (stride, radix) in zip(range(len(digits) - 1, -1, -1), digits):
        group = scatter_digit(group, place, "dp", stride, radix)
    return group


def finish_weight(flat, dp_size, side):
    flat = scatter_rows(flat, dp_size)
    flat = flat.astype(jnp.float32) + exchange(flat, "ctx", 2, 1).astype(jnp.float32)
    return join(flat.astype(jnp.bfloat16), side, "ctx", 1).astype(jnp.float32)


def reduce_weight(gradient, dp_size, side):
    return finish_weight(halve(gradient, side, "ctx", 1), dp_size, side)


def per_device(
    hidden_in,
    seg_ids,
    valid,
    w_query,
    b_query,
    w_key,
    w_value,
    b_value,
    w_out,
    b_out,
    gain_attn,
    shift_attn,
    w_up,
    b_up,
    w_down,
    b_down,
    gain_ffn,
    shift_ffn,
    pooled_text_gradient,
):
    row_count, group_size, model_width = hidden_in.shape
    dp_size = lax.axis_size("dp")
    ff_width = w_up.shape[1]
    rows_here, ff_here = model_width // dp_size, ff_width // dp_size
    fused = dp_size == 8 and rows_here % 32 == 0 and ff_here % 128 == 0 and model_width % 128 == 0
    q_all, context, lse_all, ids_got, x_got, k_all, v_all = attend(
        hidden_in, seg_ids, valid, b_query, b_value, w_query, w_key, w_value
    )
    vectors = (b_out, gain_attn, shift_attn, b_up, b_down, gain_ffn, shift_ffn)
    pool, counts, vector_parts, grad_context, grad_mixed, out, final_out, up, down, far = middle(
        fused, hidden_in, context, ids_got, vectors, pooled_text_gradient, w_out, w_up, w_down,
        dp_size,
    )
    if fused:
        up_part = up.reshape(2, 4, 2, rows_here, -1)
        far_part = far.reshape((4, 2) + far.shape[1:])
        out_part = out.reshape(4, 2, rows_here, -1)
    else:
        up_part = far_part = out_part = jnp.zeros((16, 128), jnp.bfloat16)
    grad_input, pooled, vector_sum, sums_of = attend_back(
        fused, hidden_in, ids_got, lse_all, w_query, w_key, w_value,
        pool, counts, vector_parts, x_got, q_all, k_all, v_all, context, grad_context, grad_mixed,
        up_part, down, far_part, out_part,
    )
    if fused:
        *square_sums, up_sum, down_sum, pooled, final_out, grad_input = outputs(
            sums_of.squares, sums_of.wo, sums_of.up, sums_of.down, pooled, final_out, grad_input
        )
    else:
        squares = sums_of.square
        square_sums = [reduce_weight(squares[n], dp_size, 1) for n in range(3)]
        square_sums.append(finish_weight(out, dp_size, 1))
        up_sum = finish_weight(up.transpose(1, 0, 2).reshape(model_width, -1), dp_size, 1)
        down = down.transpose(0, 2, 1).reshape(ff_width, -1)
        down_sum = finish_weight(down, dp_size, 1)
        vector_sum = lax.psum(vector_sum, ("dp", "ctx"))
        pooled = pooled.reshape(row_count, NSEG, model_width)
    place = lax.axis_index("dp")
    sums = lax.dynamic_slice_in_dim(vector_sum[:8], place * rows_here, rows_here, 1)
    sum_bu = lax.dynamic_slice_in_dim(
        vector_sum[8 : 8 + ff_width // model_width].reshape(-1), place * ff_here, ff_here
    )
    results = (
        square_sums[0], sums[0], square_sums[1], square_sums[2], sums[1], square_sums[3],
        sums[2], sums[3], sums[4], up_sum, sum_bu, down_sum, sums[5], sums[6], sums[7],
    )
    return (
        final_out,
        pooled,
        grad_input,
    ) + tuple(results)


def solution(mesh):
    placed = (
        P("dp", "ctx", None),
        P("dp", "ctx"),
        P("dp", "ctx"),
        P(),
        P(),
        P(),
        P(),
        P(),
        P(),
        P(),
        P(),
        P(),
        P(),
        P(),
        P(),
        P(),
        P(),
        P(),
        P("dp", None, None),
    )
    return jax.shard_map(
        per_device,
        mesh=mesh,
        in_specs=placed,
        out_specs=(
            P("dp", "ctx", None),
            P("dp", None, None),
            P("dp", "ctx", None),
            P("dp", None),
            P("dp"),
            P("dp", None),
            P("dp", None),
            P("dp"),
            P("dp", None),
            P("dp"),
            P("dp"),
            P("dp"),
            P("dp", None),
            P("dp"),
            P("dp", None),
            P("dp"),
            P("dp"),
            P("dp"),
        ),
        check_vma=False,
    )
```

```python
import functools
import types

import jax
import jax.numpy as jnp
from jax import lax
from jax.experimental import pallas as pl
from jax.experimental.pallas import tpu as pltpu
from jax.sharding import PartitionSpec as P

HEADS = 12
HEAD_DIM = 64
NSEG = 16


eps = 1e-12


def matmul(left_side, right_side):
    return jnp.dot(left_side, right_side, preferred_element_type=jnp.float32)


PAIR = 2 * HEAD_DIM
MESH = pl.DeviceIdType.MESH
MASKED = -1e30


def dot_nt(left_side, right_side):
    return lax.dot_general(
        left_side, right_side, (((1,), (1,)), ((), ())), preferred_element_type=jnp.float32
    )


def dot_tn(left_side, right_side):
    return lax.dot_general(
        left_side, right_side, (((0,), (0,)), ((), ())), preferred_element_type=jnp.float32
    )


def split_heads(pair):
    lane = lax.broadcasted_iota(jnp.int32, pair.shape, 1)
    zero = jnp.zeros_like(pair)
    return jnp.concatenate(
        [jnp.where(lane < HEAD_DIM, pair, zero), jnp.where(lane < HEAD_DIM, zero, pair)], axis=0
    )


def text_rows(ids_row, size):
    return jnp.broadcast_to(ids_row.astype(jnp.float32), (PAIR, size)).T


def lanes_of(size):
    return lax.broadcasted_iota(jnp.int32, (size, PAIR), 1)


def key_extra(texts):
    lane = lanes_of(texts.shape[0])
    hot = jnp.where(lane.astype(jnp.float32) == texts, 1.0, 0.0)
    return jnp.where((lane >= NSEG) & (lane < 4 * NSEG), 1.0, hot).astype(jnp.bfloat16)


def query_extra(texts):
    lane = lanes_of(texts.shape[0])
    other = (lane < NSEG) & (lane.astype(jnp.float32) != texts)
    return jnp.where(other, MASKED, 0.0)


def with_constants(extra, constants):
    lane = lanes_of(extra.shape[0])
    high = constants.astype(jnp.bfloat16).astype(jnp.float32)
    middle = (constants - high).astype(jnp.bfloat16).astype(jnp.float32)
    rest = constants - high - middle
    terms = jnp.where(lane < 2 * NSEG, high, jnp.where(lane < 3 * NSEG, middle, rest))
    kept = (lane >= NSEG) & (lane < 4 * NSEG)
    return jnp.where(kept, terms, extra).astype(jnp.bfloat16)


def of_head(extra, head):
    lane = lanes_of(extra.shape[0])
    kept = (lane < NSEG) | (lane % NSEG == head)
    return jnp.where(kept, extra, jnp.zeros_like(extra))


def attend_kernel(
    x_ref, seg_ref, valid_ref, b_query, b_value, w_query, w_key, w_value,
    q_out, context_out, lse_out, ids_out, x_hbm, k_hbm, v_hbm,
    x_got, k_ref, v_ref, extra_ref, ids_ref, score_one, score_two, score_three, send_sem, recv_sem, local_sem,
):
    rows_here, size, width = x_ref.shape
    me = lax.axis_index("ctx")
    one = me + 1 - 2 * (me % 2)
    two = (me + 2) % 4
    three = (one + 2) % 4
    low = jnp.bfloat16

    ids_ref[...] = jnp.zeros_like(ids_ref)
    ids_ref[0:rows_here, :] = seg_ref[...]
    ids_ref[rows_here : 2 * rows_here, :] = valid_ref[...]
    query_bias = b_query[...].astype(jnp.float32)[None]
    value_bias = b_value[...].astype(jnp.float32)[None]
    barrier = pltpu.get_barrier_semaphore()
    for peer in (one, two, three):
        pl.semaphore_signal(barrier, inc=1, device_id={"ctx": peer}, device_id_type=MESH)
    pl.semaphore_wait(barrier, 3)

    def send(source, target, slot, peer):
        return pltpu.make_async_remote_copy(
            src_ref=source, dst_ref=target, send_sem=send_sem.at[slot],
            recv_sem=recv_sem.at[slot], device_id={"ctx": peer}, device_id_type=MESH,
        )

    ids_out[0] = ids_ref[...]
    ids_sends = [send(ids_ref, ids_out.at[j + 1], j, peer) for j, peer in enumerate((one, two, three))]
    near = send(x_ref, x_got.at[0], 3, one)

    def far(r):
        return send(x_ref.at[r], x_got.at[1, r], 4 + r, two)

    def passed(r):
        return send(x_got.at[1, r], x_got.at[2, r], 4 + rows_here + r, one)

    far(0).start()
    near.start()
    for item in ids_sends:
        item.start()
    for r in range(1, rows_here):
        far(r).start()

    def project(x, r, j):
        count = x.shape[0] // size
        k = matmul(x, w_key[...]).astype(low)
        v = (matmul(x, w_value[...]) + value_bias).astype(low)
        for n in range(count):
            rows = pl.ds((j + n if r is not None else j) * size, size)
            k_ref[n if r is None else r, rows, :] = k[n * size : (n + 1) * size]
            v_ref[n if r is None else r, rows, :] = v[n * size : (n + 1) * size]

    own = x_ref[...].reshape(rows_here * size, width)
    q = (matmul(own, w_query[...]) + query_bias).astype(low)
    q_out[...] = (q * HEAD_DIM ** (-0.5)).astype(low).reshape(q_out.shape)
    project(own, None, 0)
    near.wait_recv()
    project(x_got[0].reshape(rows_here * size, width), None, 1)
    for item in ids_sends:
        item.wait_recv()
    lane = lax.broadcasted_iota(jnp.int32, (size, PAIR), 1)
    far(0).wait_recv()
    passed(0).start()

    def keep(r):
        return (
            pltpu.make_async_copy(k_ref.at[r], k_hbm.at[r], local_sem.at[0, r]),
            pltpu.make_async_copy(v_ref.at[r], v_hbm.at[r], local_sem.at[1, r]),
            pltpu.make_async_copy(x_got.at[:, r], x_hbm.at[:, r], local_sem.at[2, r]),
        )

    for r in range(rows_here):
        passed(r).wait_recv()
        project(jnp.concatenate([x_got[1, r], x_got[2, r]], axis=0), r, 2)
        for item in keep(r):
            item.start()
        for j in range(4):
            texts = text_rows(ids_out[j, r : r + 1, :], size)
            extra_ref[j * size : (j + 1) * size, :] = key_extra(texts)
            if j == 0:
                own_extra = query_extra(texts).astype(low)

        def score(pair, target, r=r, own_extra=own_extra):
            columns = pl.ds(pl.multiple_of(pair * PAIR, PAIR), PAIR)
            both = split_heads(q_out[r, :, columns])
            extras = jnp.concatenate([own_extra, own_extra], axis=0)
            keys = jnp.concatenate([k_ref[r, :, columns], extra_ref[...]], axis=1)
            target[...] = dot_nt(jnp.concatenate([both, extras], axis=1), keys)

        def one_pair(pair, source, stat, r=r):
            columns = pl.ds(pl.multiple_of(pair * PAIR, PAIR), PAIR)
            scores = source[...]
            top = jnp.max(scores, axis=-1, keepdims=True)
            weight = jnp.exp(scores - top)
            total = jnp.sum(weight, axis=-1, keepdims=True)
            mixed = matmul(weight.astype(low), v_ref[r, :, columns]) * (1.0 / total)
            context_out[r, :, columns] = jnp.where(
                lane < HEAD_DIM, mixed[:size], mixed[size:]
            ).astype(low)
            lse = top + jnp.log(total)
            for h in range(2):
                ours = lane % NSEG == 2 * pair + h
                stat = jnp.where(ours, lse[h * size : (h + 1) * size], stat)
            return stat

        def three_pairs(n, carry, r=r):
            stat = lse_out[r]
            for i, target in enumerate((score_one, score_two, score_three)):
                score(3 * n + i, target)
            for i, source in enumerate((score_one, score_two, score_three)):
                stat = one_pair(3 * n + i, source, stat)
            lse_out[r] = stat
            return carry

        lse_out[r] = jnp.zeros((size, PAIR), jnp.float32)
        more = r + 1 < rows_here
        if r and more:
            lax.fori_loop(0, HEADS // 12, three_pairs, 0)
            far(r + 1).wait_recv()
            passed(r + 1).start()
            lax.fori_loop(HEADS // 12, HEADS // 6, three_pairs, 0)
        else:
            lax.fori_loop(0, HEADS // 6, three_pairs, 0)
            if more:
                far(r + 1).wait_recv()
                passed(r + 1).start()
    for r in range(rows_here):
        for item in keep(r):
            item.wait()
        far(r).wait_send()
        passed(r).wait_send()
    near.wait_send()
    for item in ids_sends:
        item.wait_send()


def attend(x, seg_ids, valid, b_query, b_value, w_query, w_key, w_value):
    rows_here, size, width = x.shape
    keys = size * 4
    low = jnp.bfloat16
    whole = pl.BlockSpec(memory_space=pltpu.VMEM)
    outside = pl.BlockSpec(memory_space=pl.ANY)
    slots = 4 + 2 * rows_here
    return pl.pallas_call(
        attend_kernel,
        out_shape=(
            jax.ShapeDtypeStruct((rows_here, size, width), low),
            jax.ShapeDtypeStruct((rows_here, size, width), low),
            jax.ShapeDtypeStruct((rows_here, size, PAIR), jnp.float32),
            jax.ShapeDtypeStruct((4, 8, size), jnp.int32),
            jax.ShapeDtypeStruct((3,) + x.shape, low),
            jax.ShapeDtypeStruct((rows_here, keys, width), low),
            jax.ShapeDtypeStruct((rows_here, keys, width), low),
        ),
        in_specs=[whole] * 8,
        out_specs=(whole, whole, whole, whole, outside, outside, outside),
        scratch_shapes=[
            pltpu.VMEM((3,) + x.shape, low),
            pltpu.VMEM((rows_here, keys, width), low),
            pltpu.VMEM((rows_here, keys, width), low),
            pltpu.VMEM((keys, PAIR), low),
            pltpu.VMEM((8, size), jnp.int32),
            pltpu.VMEM((2 * size, keys), jnp.float32),
            pltpu.VMEM((2 * size, keys), jnp.float32),
            pltpu.VMEM((2 * size, keys), jnp.float32),
            pltpu.SemaphoreType.DMA((slots,)),
            pltpu.SemaphoreType.DMA((slots,)),
            pltpu.SemaphoreType.DMA((3, rows_here)),
        ],
        compiler_params=pltpu.CompilerParams(
            vmem_limit_bytes=56 * 2**20, collective_id=0, has_side_effects=True
        ),
        cost_estimate=pl.CostEstimate(
            flops=rows_here * (2 * (size + 2 * keys) * width * width + 16 * size * keys * width),
            bytes_accessed=2 * (3 * width * width + 9 * keys * width),
            transcendentals=rows_here * HEADS * size * keys,
        ),
    )(x, seg_ids, valid, b_query, b_value, w_query, w_key, w_value)


def gelu_both(u):
    size = jnp.abs(u)
    t = 1.0 / (1.0 + (0.3275911 * 0.5**0.5) * size)
    bell = jnp.exp(-0.5 * u * u)
    poly = t * (
        0.127414796 + t * (-0.142248368 + t * (0.7107068705 + t * (-0.7265760135 + t * 0.5307027145)))
    )
    tail = poly * bell
    cdf = jnp.where(u >= 0.0, 1.0 - tail, tail)
    return u * cdf, cdf + u * bell * 0.3989422804014327


def normalize(values_in):
    centre = jnp.mean(values_in, axis=-1, keepdims=True)
    centred = values_in - centre
    spread = jnp.mean(centred * centred, axis=-1, keepdims=True)
    scale = lax.rsqrt(spread + eps)
    return centred * scale, scale


def normalize_back(grad, unit, scale):
    mean_one = jnp.mean(grad, axis=-1, keepdims=True)
    mean_two = jnp.mean(grad * unit, axis=-1, keepdims=True)
    return (grad - mean_one - unit * mean_two) * scale


def column_sum(values_in):
    return jnp.sum(values_in, axis=0, keepdims=True)


B_QUERY, B_VALUE, B_OUT, GAIN_ONE, SHIFT_ONE, B_DOWN, GAIN_TWO, SHIFT_TWO, B_UP = range(9)


def middle_kernel(
    fused,
    x_ref, context_ref, ids_ref, b_out, gain_one, shift_one, b_up, b_down, gain_two, shift_two,
    text_ref, w_out, up_hbm, down_hbm,
    pool_out, count_out, vector_out, grad_out, mixed_out, wo_out, final_hbm, up_out, down_out, far_out,
    vec_ref, w_up, w_down, unit_ref, scale_ref, normed_ref, normed_t, act_ref, slope_ref, acc_ref, pre_one, pre_two,
    g_ref, g_t_ref, upg_ref, up_got, downg_ref, down_got, wo_sent, wo_got, down_y, down_x,
    send_sem, recv_sem, load_sem, store_sem,
):
    rows_here, size, width = x_ref.shape
    tokens = rows_here * size
    parts = w_up.shape[1] // width
    half = width // 2
    low = jnp.bfloat16
    f32 = jnp.float32
    me = lax.axis_index("ctx")
    core = me % 2
    near = {"ctx": me + 1 - 2 * core}
    side = me // 2
    place = lax.axis_index("dp")
    y = place % 2
    y_dev = {"dp": place + 1 - 2 * y}
    across_dev = {"ctx": (me + 2) % 4}
    peers = [near, across_dev, y_dev] if fused else [near]
    barrier = pltpu.get_barrier_semaphore()
    for peer in peers:
        pl.semaphore_signal(barrier, inc=1, device_id=peer, device_id_type=MESH)
    for row, source in (
        (B_OUT, b_out), (GAIN_ONE, gain_one), (SHIFT_ONE, shift_one), (B_DOWN, b_down),
        (GAIN_TWO, gain_two), (SHIFT_TWO, shift_two),
    ):
        vec_ref[row : row + 1, :] = source[...].astype(f32)[None]
    for i in range(parts):
        vec_ref[B_UP + i : B_UP + i + 1, :] = (
            b_up[i * width : (i + 1) * width].astype(f32)[None]
        )

    def vec(row):
        return vec_ref[row : row + 1, :]

    loads = []
    for i in range(parts):
        loads.append(
            (
                pltpu.make_async_copy(
                    up_hbm.at[:, pl.ds(i * width, width)],
                    w_up.at[:, pl.ds(i * width, width)],
                    load_sem.at[0, i],
                ),
                pltpu.make_async_copy(
                    down_hbm.at[pl.ds(i * width, width)],
                    w_down.at[pl.ds(i * width, width)],
                    load_sem.at[1, i],
                ),
            )
        )
    for pair in loads:
        for item in pair:
            item.start()

    def rows_of(r):
        return pl.ds(pl.multiple_of(r * size, size), size)

    text = lax.broadcasted_iota(jnp.int32, (NSEG, size), 0)

    def members(j, r):
        seg = ids_ref[j, r : r + 1, :]
        real = ids_ref[j, rows_here + r : rows_here + r + 1, :]
        return jnp.where((text == seg) & (real == 1), 1.0, 0.0)

    for r in range(rows_here):
        number = sum(jnp.sum(members(j, r), axis=1, keepdims=True) for j in range(4))
        count_out[r * NSEG : (r + 1) * NSEG, :] = jnp.maximum(number, 1.0)

    def first_norm(r, carry):
        rows = rows_of(r)
        mixed = x_ref[r].astype(f32) + (matmul(context_ref[r], w_out[...]) + vec(B_OUT))
        unit, scale = normalize(mixed)
        unit_ref[rows, :] = unit
        scale_ref[rows, :] = scale
        normed_ref[rows, :] = (unit * vec(GAIN_ONE) + vec(SHIFT_ONE)).astype(low)
        return carry

    lax.fori_loop(0, rows_here, first_norm, 0)
    for pair in loads:
        for item in pair:
            item.wait()

    def units(i):
        return pl.ds(pl.multiple_of(i * width, width), width)

    def forward_part(i, following, now, then):
        for r in range(rows_here):
            rows = pl.ds(r * size, size)
            then[rows, :] = matmul(normed_ref[rows, :], w_up[:, units(following)])
            act, slope = gelu_both(now[rows, :] + vec_ref[pl.ds(B_UP + i, 1), :])
            act = act.astype(low)
            act_ref[rows, units(i)] = act
            slope_ref[rows, units(i)] = slope.astype(low)
            acc_ref[rows, :] += matmul(act, w_down[units(i), :])

    def forward_parts(n, carry):
        forward_part(2 * n, 2 * n + 1, pre_one, pre_two)
        forward_part(2 * n + 1, jnp.minimum(2 * n + 2, parts - 1), pre_two, pre_one)
        return carry

    acc_ref[...] = jnp.zeros_like(acc_ref)
    pre_one[...] = matmul(normed_ref[...], w_up[:, units(0)])
    lax.fori_loop(0, parts // 2, forward_parts, 0)
    normed_t[...] = normed_ref[...].T

    store_final = []
    vector_out[...] = jnp.zeros_like(vector_out)
    for r in range(rows_here):
        rows = pl.ds(r * size, size)
        normed = unit_ref[rows, :] * vec(GAIN_ONE) + vec(SHIFT_ONE)
        summed = normed + (acc_ref[rows, :] + vec(B_DOWN))
        unit, scale = normalize(summed)
        final = unit * vec(GAIN_TWO) + vec(SHIFT_TWO)
        high = final.astype(low)
        upg_ref[parts - 1, rows, :] = high
        item = pltpu.make_async_copy(
            upg_ref.at[parts - 1, rows], final_hbm.at[r], store_sem.at[r]
        )
        item.start()
        store_final.append(item)
        own = members(0, r)
        own_low = own.astype(low)
        rest = (final - high.astype(f32)).astype(low)
        pool = matmul(own_low, high) + matmul(own_low, rest)
        pool_out[r * NSEG : (r + 1) * NSEG, :] = pool.astype(low)
        share = text_ref[r] / count_out[r * NSEG : (r + 1) * NSEG, :]
        first = share.astype(low)
        second = (share - first.astype(f32)).astype(low)
        third = (share - first.astype(f32) - second.astype(f32)).astype(low)
        grad = dot_tn(
            jnp.concatenate([own_low] * 3, axis=0), jnp.concatenate([first, second, third], axis=0)
        )
        back = normalize_back(grad * vec(GAIN_TWO), unit, scale)
        back_low = back.astype(low)
        acc_ref[rows, :] = back
        g_ref[rows, :] = back_low
        vector_out[GAIN_TWO : GAIN_TWO + 1, :] += column_sum(grad * unit)
        vector_out[SHIFT_TWO : SHIFT_TWO + 1, :] += column_sum(grad)
        vector_out[B_DOWN : B_DOWN + 1, :] += column_sum(back_low.astype(f32))

    pl.semaphore_wait(barrier, len(peers))

    def remote(source, target, slot, device=near):
        return pltpu.make_async_remote_copy(
            src_ref=source, dst_ref=target, send_sem=send_sem.at[slot],
            recv_sem=recv_sem.at[slot], device_id=device, device_id_type=MESH,
        )

    per_part = downg_ref.shape[0] // parts
    mine = parts // 2

    def up_send(i):
        return remote(upg_ref.at[i], up_got.at[i], i)

    def down_send(i):
        chunk = pl.ds(i * per_part, per_part)
        return remote(downg_ref.at[chunk, 1 - core], down_got.at[chunk], parts + i)

    cut = downg_ref.shape[3]

    def down_part(i, carry):
        part = matmul(g_t_ref[...], act_ref[:, units(i)]).astype(low)
        part = part.reshape((2, width // 2, width))
        for n in range(per_part):
            downg_ref[per_part * i + n] = part[:, :, n * cut : (n + 1) * cut]
        down_send(i).start()
        return carry

    g_t_ref[...] = g_ref[...].T
    lax.fori_loop(0, parts, down_part, 0)

    def backward_part(step, carry):
        i = (step + mine * (1 - core)) % parts
        back = dot_nt(g_ref[...], w_down[units(i), :])
        back = (back * slope_ref[:, units(i)].astype(f32)).astype(low)
        acc_ref[...] += dot_nt(back, w_up[:, units(i)])
        vector_out[pl.ds(B_UP + i, 1), :] = column_sum(back.astype(f32))
        upg_ref[step] = matmul(normed_t[...], back).astype(low)

        @pl.when(step < mine)
        def _():
            up_send(step).start()

        return carry

    def down_sum(i, carry):
        downg_ref[i, core] = (
            downg_ref[i, core].astype(f32) + down_got[i].astype(f32)
        ).astype(low)
        return carry

    piece = downg_ref.shape[2] // 2
    quarter = piece // 2
    rest = pl.ds(pl.multiple_of(piece + quarter * (1 - side), 16), quarter)
    kept = pl.ds(pl.multiple_of(piece + quarter * side, 16), quarter)
    down_moves = []
    if fused:
        for n in range(4):
            down_moves.append(
                remote(
                    downg_ref.at[2 * n + 1 - y, core, pl.ds(0, piece)], down_y.at[n],
                    2 * parts + 1 + n, y_dev,
                )
            )
        for n in range(8):
            down_moves.append(
                remote(
                    downg_ref.at[n, core, rest], down_x.at[n], 2 * parts + 5 + n, across_dev
                )
            )
    lax.fori_loop(0, 1, backward_part, 0)
    for i in range(parts):
        down_send(i).wait_recv()
    lax.fori_loop(0, downg_ref.shape[0], down_sum, 0)
    for item in down_moves:
        item.start()
    for item in store_final:
        item.wait()
    lax.fori_loop(1, parts, backward_part, 0)

    def first_back(r, carry):
        rows = rows_of(r)
        unit = unit_ref[rows, :]
        grad = acc_ref[rows, :]
        back = normalize_back(grad * vec(GAIN_ONE), unit, scale_ref[rows, :])
        back_low = back.astype(low)
        mixed_out[r] = back
        g_ref[rows, :] = back_low
        vector_out[GAIN_ONE : GAIN_ONE + 1, :] += column_sum(grad * unit)
        vector_out[SHIFT_ONE : SHIFT_ONE + 1, :] += column_sum(grad)
        vector_out[B_OUT : B_OUT + 1, :] += column_sum(back_low.astype(f32))
        return carry

    lax.fori_loop(0, rows_here, first_back, 0)

    for r in range(rows_here):
        g_t_ref[:, r * size : (r + 1) * size] = context_ref[r].T

    def out_part(h):
        columns = pl.ds(pl.multiple_of(h * half, 128), half)
        return matmul(g_t_ref[...], g_ref[:, columns])

    wo_sent[...] = out_part(1 - core).astype(low)
    wo_send = remote(wo_sent, wo_got, 2 * parts)
    wo_send.start()

    def grad_context(r, carry):
        grad_out[r] = dot_nt(g_ref[rows_of(r), :], w_out[...]).astype(low)
        return carry

    lax.fori_loop(0, rows_here, grad_context, 0)
    own_part = out_part(core)
    for i in range(mine):
        up_send(i).wait_recv()

    def up_sum(n, carry):
        rows = pl.ds(pl.multiple_of(n * 128, 128), 128)
        for i in range(mine):
            upg_ref[mine + i, rows, :] = (
                upg_ref[mine + i, rows, :].astype(f32) + up_got[i, rows, :].astype(f32)
            ).astype(low)
        return carry

    lax.fori_loop(0, width // 128, up_sum, 0)
    store_up = pltpu.make_async_copy(
        upg_ref.at[pl.ds(mine, mine)], up_out, store_sem.at[rows_here + 1]
    )
    store_up.start()
    wo_send.wait_recv()
    wo_out[...] = (own_part + wo_got[...].astype(f32)).astype(low)
    if fused:
        for item in down_moves:
            item.wait_recv()

        def near_sum(n, carry):
            down_y[n] = (
                downg_ref[2 * n + y, core, 0:piece, :].astype(f32) + down_y[n].astype(f32)
            ).astype(low)
            return carry

        def far_sum(n, carry):
            down_x[n] = (
                downg_ref[n, core, kept, :].astype(f32) + down_x[n].astype(f32)
            ).astype(low)
            return carry

        lax.fori_loop(0, 4, near_sum, 0)
        lax.fori_loop(0, 8, far_sum, 0)
        stores = [
            pltpu.make_async_copy(down_y, down_out, store_sem.at[rows_here]),
            pltpu.make_async_copy(down_x, far_out, store_sem.at[rows_here + 2]),
        ]
    else:
        stores = [
            pltpu.make_async_copy(downg_ref.at[:, core], down_out, store_sem.at[rows_here])
        ]
    for item in stores:
        item.start()
    for i in range(parts):
        down_send(i).wait_send()
    for i in range(mine):
        up_send(i).wait_send()
    wo_send.wait_send()
    for item in down_moves:
        item.wait_send()
    for item in stores + [store_up]:
        item.wait()


def middle(fused, x, context, ids, vectors, text_gradient, w_out, w_up, w_down, dp_size):
    rows_here, size, width = x.shape
    ff = w_up.shape[1]
    parts = ff // width
    tokens = rows_here * size
    low = jnp.bfloat16
    f32 = jnp.float32
    shape = jax.ShapeDtypeStruct
    whole = pl.BlockSpec(memory_space=pltpu.VMEM)
    outside = pl.BlockSpec(memory_space=pl.ANY)
    chunks = dp_size if fused else parts
    chunk = ff // chunks
    vec = (8 + parts + (-parts) % 8, width)
    if fused:
        down_shape, far_shape = (4, width // 4, chunk), (8, width // 8, chunk)
    else:
        down_shape, far_shape = (chunks, width // 2, chunk), (8, 16, 128)
    return pl.pallas_call(
        functools.partial(middle_kernel, fused),
        out_shape=(
            shape((rows_here * NSEG, width), low),
            shape((rows_here * NSEG, 1), f32),
            shape(vec, f32),
            shape((rows_here, size, width), low),
            shape((rows_here, size, width), f32),
            shape((width, width // 2), low),
            shape((rows_here, size, width), low),
            shape((parts // 2, width, width), low),
            shape(down_shape, low),
            shape(far_shape, low),
        ),
        in_specs=[whole] * 12 + [outside] * 2,
        out_specs=(whole,) * 6 + (outside,) * 4,
        scratch_shapes=[
            pltpu.VMEM(vec, f32),
            pltpu.VMEM((width, ff), low),
            pltpu.VMEM((ff, width), low),
            pltpu.VMEM((tokens, width), f32),
            pltpu.VMEM((tokens, 1), f32),
            pltpu.VMEM((tokens, width), low),
            pltpu.VMEM((width, tokens), low),
            pltpu.VMEM((tokens, ff), low),
            pltpu.VMEM((tokens, ff), low),
            pltpu.VMEM((tokens, width), f32),
            pltpu.VMEM((tokens, width), f32),
            pltpu.VMEM((tokens, width), f32),
            pltpu.VMEM((tokens, width), low),
            pltpu.VMEM((width, tokens), low),
            pltpu.VMEM((parts, width, width), low),
            pltpu.VMEM((parts // 2, width, width), low),
            pltpu.VMEM((chunks, 2, width // 2, chunk), low),
            pltpu.VMEM((chunks, width // 2, chunk), low),
            pltpu.VMEM((width, width // 2), low),
            pltpu.VMEM((width, width // 2), low),
            pltpu.VMEM(down_shape if fused else (16, 128), low),
            pltpu.VMEM(far_shape, low),
            pltpu.SemaphoreType.DMA((2 * parts + 13,)),
            pltpu.SemaphoreType.DMA((2 * parts + 13,)),
            pltpu.SemaphoreType.DMA((2, parts)),
            pltpu.SemaphoreType.DMA((rows_here + 3,)),
        ],
        compiler_params=pltpu.CompilerParams(
            vmem_limit_bytes=63 * 2**20, collective_id=2, has_side_effects=True
        ),
        cost_estimate=pl.CostEstimate(
            flops=2 * tokens * width * (6 * ff + 3 * width),
            bytes_accessed=2 * (5 * ff * width + 8 * tokens * width),
            transcendentals=2 * tokens * ff,
        ),
    )(x, context, ids, *vectors, text_gradient, w_out, w_up, w_down)


class Links:
    def __init__(self, send_sem, recv_sem):
        self.send_sem, self.recv_sem = send_sem, recv_sem
        self.slots, self.copies = {}, {}

    def start(self, name, source, target, device):
        slot = self.slots.setdefault(name, len(self.slots))
        copy = pltpu.make_async_remote_copy(
            src_ref=source, dst_ref=target, send_sem=self.send_sem.at[slot],
            recv_sem=self.recv_sem.at[slot], device_id=device, device_id_type=MESH,
        )
        copy.start()
        self.copies[name] = copy

    def arrived(self, *names):
        for name in names:
            self.copies[name].wait_recv()

    def finish(self):
        for copy in self.copies.values():
            copy.wait_send()


def add_into(target, others, count):
    def one(i, carry):
        total = target[i].astype(jnp.float32)
        for other in others:
            total = total + other[i].astype(jnp.float32)
        target[i] = total.astype(target.dtype)
        return carry

    lax.fori_loop(0, count, one, 0)


def add_up(parts):
    total = parts[0].astype(jnp.float32)
    for part in parts[1:]:
        total = total + part.astype(jnp.float32)
    return total


POOL, UP, DOWN_A, DOWN_B, DOWN, OUT, GROUP, DX, VECTOR = range(9)
STEP, NEAR, FAR, SIDE, LINE, GATHER = range(6)

GROUPS = ((0, 4 * PAIR), (4 * PAIR, PAIR), (5 * PAIR, PAIR))


def attend_back_kernel(
    fused, count_out, out_tree, tree,
    x_ref, ids_ref, lse_ref, w_query, w_key, w_value, pool_ref, count_ref, vector_ref,
    x_hbm, q_hbm, k_hbm, v_hbm, context_hbm, grad_hbm, mixed_hbm, up_ref, down_ref, far_ref, out_ref,
    dx_out, pool_out, vector_out, *rest,
):
    outs = types.SimpleNamespace(**jax.tree.unflatten(out_tree, rest[:count_out]))
    ref = types.SimpleNamespace(**jax.tree.unflatten(tree, rest[count_out:]))
    square_out, up_out, down_out, wo_out = outs.square, outs.up, outs.down, outs.wo
    q_ref, k_ref, v_ref, context_ref, grad_ref = ref.q, ref.k, ref.v, ref.context, ref.grad
    dq_ref, dk_ref, dv_ref, x_t, x_got = ref.dq, ref.dk, ref.dv, ref.x_t, ref.x_got
    extra_ref, penal_ref, delta_ref = ref.extra, ref.penal, ref.delta
    dx_acc, dx_sent, dx_far, dx_got, dx_far_got = (
        ref.dx_acc, ref.dx_sent, ref.dx_far, ref.dx_got, ref.dx_far_got
    )
    pool_parts, pool_got, vec_parts, vec_got = (
        ref.pool_parts, ref.pool_got, ref.vec_parts, ref.vec_got
    )
    row_sem, local_sem = ref.row_sem, ref.local_sem
    rows_here, size, width = x_ref.shape
    low = jnp.bfloat16
    me, place = lax.axis_index("ctx"), lax.axis_index("dp")
    core, side = me % 2, me // 2
    near, across = me + 1 - 2 * core, (me + 2) % 4
    near_dev, across_dev = {"ctx": near}, {"ctx": across}
    y, z = place % 2, place // 2
    y_dev = {"dp": place + 1 - 2 * y}
    z_at = (z + 1 - 2 * (z % 2), (z + 2) % 4, 3 - z)
    z_dev = [{"dp": other * 2 + y} for other in z_at]
    peers = [near_dev, across_dev] + ([y_dev] + z_dev if fused else [])

    barrier = pltpu.get_barrier_semaphore()
    for peer in peers:
        pl.semaphore_signal(barrier, inc=1, device_id=peer, device_id_type=MESH)
    pl.semaphore_wait(barrier, len(peers))
    links = Links(ref.send_sem, ref.recv_sem)

    first_cut = GROUPS[1][0]
    blocks = [(0, first_cut, r) for r in range(rows_here)]
    blocks += [(first_cut, width - first_cut, r) for r in range(rows_here)]

    def load_block(step):
        slot = step % 2
        start, count, r = blocks[step]
        columns, local = pl.ds(start, count), pl.ds(0, count)
        pairs = (
            (k_hbm, k_ref), (v_hbm, v_ref), (q_hbm, q_ref), (context_hbm, context_ref),
            (grad_hbm, grad_ref),
        )
        copies = [
            pltpu.make_async_copy(
                source.at[r, :, columns], target.at[slot, :, local], row_sem.at[slot, i]
            )
            for i, (source, target) in enumerate(pairs)
        ]
        if step < rows_here:
            copies.append(pltpu.make_async_copy(x_hbm.at[:, r], x_got.at[slot], row_sem.at[slot, 5]))
        return copies

    for item in load_block(0):
        item.start()
    load_mixed = pltpu.make_async_copy(mixed_hbm, dx_acc, local_sem.at[0])
    links.start((POOL, STEP, 0), pool_ref, pool_got.at[0], near_dev)
    if fused:
        u_ref, u_x, u_y, u_z = ref.u, ref.u_x, ref.u_y, ref.u_z
        a_z, a_s, a_x = ref.a_z, ref.a_s, ref.a_x
        b_ref, b_y, b_z = ref.b, ref.b_y, ref.b_z
        o_ref, o_y, o_z, o_s, o_x = ref.o, ref.o_y, ref.o_z, ref.o_s, ref.o_x
        half_rows = u_ref.shape[2] // 2
        links.start((UP, FAR, 0), up_ref.at[1 - side, :, :, pl.ds(0, half_rows)], u_x.at[0], across_dev)
        links.start((DOWN_B, SIDE), far_ref.at[:, 1 - y], b_y, y_dev)
        for o in range(3):
            links.start((DOWN_A, LINE, o), down_ref.at[z_at[o]], a_z.at[o], z_dev[o])
    load_mixed.start()
    vec_parts[0] = vector_ref[...]

    def pool_one():
        links.arrived((POOL, STEP, 0))
        pool_parts[...] = add_up([pool_ref[...], pool_got[0]]).astype(low)
        links.start((POOL, STEP, 1), pool_parts, pool_got.at[1], across_dev)

    def pool_two():
        links.arrived((POOL, STEP, 1))
        pool_out[...] = add_up([pool_parts[...], pool_got[1]]) / count_ref[...]

    def send_z(name, source, target):
        for o in range(3):
            links.start(name + (o,), source(z_at[o]), target(o), z_dev[o])

    def arrived_z(name):
        links.arrived(*(name + (o,) for o in range(3)))

    def out_y():
        links.start((OUT, SIDE), out_ref.at[:, 1 - y], o_y, y_dev)

    def out_z():
        links.arrived((OUT, SIDE))
        for i in range(4):
            o_ref[i] = add_up([out_ref[i, y], o_y[i]]).astype(low)
        send_z((OUT, LINE), lambda i: o_ref.at[i], lambda o: o_z.at[o])

    def out_far():
        arrived_z((OUT, LINE))
        o_s[...] = add_up([o_ref[z]] + [o_z[o] for o in range(3)]).astype(low)
        links.start((OUT, FAR), o_s, o_x, across_dev)

    def out_end():
        links.arrived((OUT, FAR))
        wo_out[core] = add_up([o_s[...], o_x[...]]).astype(low)
        links.start((OUT, GATHER), wo_out.at[core], wo_out.at[core], near_dev)

    def down_z():
        links.arrived((DOWN_B, SIDE))
        for i in range(4):
            b_ref[i] = add_up([far_ref[i, y], b_y[i]]).astype(low)
        send_z((DOWN_B, LINE), lambda i: b_ref.at[i], lambda o: b_z.at[o])

    def down_near_far():
        arrived_z((DOWN_A, LINE))
        a_s[...] = add_up([down_ref[z]] + [a_z[o] for o in range(3)]).astype(low)
        links.start((DOWN_A, FAR), a_s, a_x, across_dev)

    def down_far():
        arrived_z((DOWN_B, LINE))
        count = b_ref.shape[1]
        own = pl.ds(pl.multiple_of(2 * count + side * count, 16), count)
        down_out[core, own] = add_up([b_ref[z]] + [b_z[o] for o in range(3)]).astype(low)
        links.start((DOWN_B, FAR), down_out.at[core, own], down_out.at[core, own], across_dev)

    def down_end():
        links.arrived((DOWN_A, FAR), (DOWN_B, FAR))
        down_out[core, 0 : a_s.shape[0]] = add_up([a_s[...], a_x[...]]).astype(low)
        links.start((DOWN, GATHER), down_out.at[core], down_out.at[core], near_dev)

    def up_x():
        rows = pl.ds(half_rows, half_rows)
        links.start((UP, FAR, 1), up_ref.at[1 - side, :, :, rows], u_x.at[1], across_dev)

    def up_y(h):
        rows = pl.ds(h * half_rows, half_rows)
        links.arrived((UP, FAR, h))
        for i in range(4):
            for j in range(2):
                u_ref[i, j, rows] = add_up([up_ref[side, i, j, rows], u_x[h, i, j]]).astype(low)
        links.start((UP, SIDE, h), u_ref.at[:, 1 - y, rows], u_y.at[h], y_dev)

    def up_z(h):
        rows = pl.ds(h * half_rows, half_rows)
        links.arrived((UP, SIDE, h))
        for i in range(4):
            u_ref[i, y, rows] = add_up([u_ref[i, y, rows], u_y[h, i]]).astype(low)
        send_z((UP, LINE, h), lambda i: u_ref.at[i, y, rows], lambda o: u_z.at[o, rows])

    def up_far():
        arrived_z((UP, LINE, 0))
        arrived_z((UP, LINE, 1))
        up_out[me] = add_up([u_ref[z, y]] + [u_z[o] for o in range(3)]).astype(low)
        links.start((UP, GATHER), up_out.at[me], up_out.at[me], across_dev)

    def up_end():
        links.arrived((UP, GATHER))
        links.start((UP, NEAR, 0), up_out.at[me], up_out.at[me], near_dev)
        links.start((UP, NEAR, 1), up_out.at[across], up_out.at[across], near_dev)

    def group_core(g):
        links.start((GROUP, NEAR, g), ref.g[g].at[1 - core], ref.g_got[g], near_dev)

    def group_y(g):
        links.arrived((GROUP, NEAR, g))
        for i in range(4):
            add_into(ref.g[g].at[core, i], [ref.g_got[g].at[i]], 2)
        links.start((GROUP, SIDE, g), ref.g[g].at[core, :, 1 - y], ref.g_y[g], y_dev)

    def group_z(g):
        links.arrived((GROUP, SIDE, g))
        own = ref.g[g]
        for i in range(4):
            own[core, i, y] = add_up([own[core, i, y], ref.g_y[g][i]]).astype(low)
        send_z((GROUP, LINE, g), lambda i: own.at[core, i, y], lambda o: ref.g_z[g].at[o])

    def group_far(g):
        arrived_z((GROUP, LINE, g))
        pieces = [ref.g[g][core, z, y]] + [ref.g_z[g][o] for o in range(3)]
        ref.g_s[g][...] = add_up(pieces).astype(low)
        links.start((GROUP, FAR, g), ref.g_s[g], ref.g_x[g], across_dev)

    def group_end(g):
        links.arrived((GROUP, FAR, g))
        out = outs.squares[g]
        out[core] = add_up([ref.g_s[g][...], ref.g_x[g][...]]).astype(low)
        links.start((GROUP, GATHER, g), out.at[core], out.at[core], near_dev)

    def vector_step(i, device):
        if i:
            links.arrived((VECTOR, STEP, i - 1))
            vec_parts[i] = vec_parts[i - 1] + vec_got[i - 1]
        if device is not None:
            links.start((VECTOR, STEP, i), vec_parts.at[i], vec_got.at[i], device)

    def vector_z():
        vector_step(3, None)
        for o in range(3):
            links.start((VECTOR, LINE, o), vec_parts.at[3], vec_got.at[3 + o], z_dev[o])

    def vector_end():
        arrived_z((VECTOR, LINE))
        vector_out[...] = vec_parts[3] + (vec_got[3] + (vec_got[4] + vec_got[5]))

    row = lax.broadcasted_iota(jnp.int32, (PAIR, size), 0)

    def find_delta(step):
        slot = step % 2
        start, count, _ = blocks[step]
        lane = lax.broadcasted_iota(jnp.int32, (count, PAIR), 1)
        head = (start + lax.broadcasted_iota(jnp.int32, (count, PAIR), 0)) // HEAD_DIM
        member = jnp.where((lane % NSEG == head) & (lane >= NSEG) & (lane < 4 * NSEG), 1.0, 0.0)
        member = member.astype(low)
        local = pl.ds(0, count)
        product = grad_ref[slot, :, local].astype(jnp.float32) * context_ref[
            slot, :, local
        ].astype(jnp.float32)
        total = jnp.zeros((size, PAIR), jnp.float32)
        for _ in range(3):
            term = product.astype(low)
            total = total + matmul(term, member)
            product = product - term.astype(jnp.float32)
        delta_ref[...] = with_constants(jnp.zeros_like(total), -total)

    def attend_pairs(step, first, last):
        slot = step % 2
        start, _, r = blocks[step]

        class Pair:
            def __init__(self, n):
                self.local = pl.ds(n * PAIR, PAIR)
                self.columns = pl.ds(start + n * PAIR, PAIR)
                head = 2 * (start // PAIR + n)
                self.q_both = split_heads(q_ref[slot, :, self.local])
                self.g_both = split_heads(grad_ref[slot, :, self.local])
                q_extra = [of_head(penal_ref[r], head + h) for h in range(2)]
                g_extra = [of_head(delta_ref[...], head + h) for h in range(2)]
                q_wide = jnp.concatenate([self.q_both, jnp.concatenate(q_extra, axis=0)], axis=1)
                g_wide = jnp.concatenate([self.g_both, jnp.concatenate(g_extra, axis=0)], axis=1)
                self.q_wide, self.g_wide = q_wide.T, g_wide.T
                self.dq = jnp.zeros((PAIR, 2 * size), jnp.float32)

            def products(self, j):
                rows = pl.ds(j * size, size)
                extra = extra_ref[r, rows, :]
                keys = jnp.concatenate([k_ref[slot, rows, self.local], extra], axis=1)
                values = jnp.concatenate([v_ref[slot, rows, self.local], extra], axis=1)
                return matmul(keys, self.q_wide), matmul(values, self.g_wide)

            def block(self, j, scores, grad_p):
                rows = pl.ds(j * size, size)
                probs = jnp.exp(scores)
                grad_s = (probs * grad_p).astype(low)
                dv_ref[r, rows, self.columns] = matmul(probs.astype(low), self.g_both).astype(low)
                dk_ref[r, rows, self.columns] = matmul(grad_s, self.q_both).astype(low)
                self.dq = self.dq + matmul(k_ref[slot, rows, self.local].T, grad_s)

            def end(self):
                dq = jnp.where(row < HEAD_DIM, self.dq[:, :size], self.dq[:, size:])
                dq_ref[r, :, self.columns] = (dq * HEAD_DIM ** (-0.5)).T.astype(low)

        pairs = [Pair(n) for n in range(first, last)]
        for j in range(4):
            ready = [pair.products(j) for pair in pairs]
            for pair, (scores, grad_p) in zip(pairs, ready):
                pair.block(j, scores, grad_p)
        for pair in pairs:
            pair.end()

    def weight_group(g):
        start, count = GROUPS[g]
        if fused:
            depth = ref.g[g].shape[3]

        def keep(n, i, total):
            total = total.astype(low)
            wide = total.shape[1]
            if not fused:
                square_out[n, :, pl.ds(pl.multiple_of(start + i * PAIR, PAIR), wide)] = total
                return
            total = total.reshape(4, 2, 2, depth, wide)
            target = pl.ds(pl.multiple_of(n * count + i * PAIR, PAIR), wide)
            for h in range(2):
                ref.g[g][h, :, :, :, target] = total[:, :, h]

        def of_source(source, columns):
            keys = source.shape[1]
            return sum(
                matmul(x_t[r, :, :keys], source[r, :, columns]) for r in range(rows_here)
            )

        def one_part(i, carry):
            columns = pl.ds(pl.multiple_of(start + 2 * i * PAIR, PAIR), 2 * PAIR)
            for n, source in enumerate((dq_ref, dk_ref, dv_ref)):
                keep(n, 2 * i, of_source(source, columns))
            return carry

        if count % (2 * PAIR):
            columns = pl.ds(start, count)
            keep(0, 0, of_source(dq_ref, columns))
            both = sum(
                matmul(
                    x_t[r],
                    jnp.concatenate([dk_ref[r, :, columns], dv_ref[r, :, columns]], axis=1),
                )
                for r in range(rows_here)
            )
            keep(1, 0, both[:, :count])
            keep(2, 0, both[:, count:])
        else:
            lax.fori_loop(0, count // (2 * PAIR), one_part, 0)
        columns = pl.ds(start, count)
        for n, source in enumerate((dq_ref, dv_ref)):
            vec_parts[0, n : n + 1, columns] = sum(
                jnp.sum(source[r, :, columns].astype(jnp.float32), axis=0, keepdims=True)
                for r in range(rows_here)
            )

    def input_parts(r):
        for j in (3, 2, 1, 0):
            rows = pl.ds(j * size, size)
            total = dot_nt(dk_ref[r, rows, :], w_key[...]) + dot_nt(dv_ref[r, rows, :], w_value[...])
            if j == 0:
                dx_acc[r] = dx_acc[r] + total + dot_nt(dq_ref[r], w_query[...])
            elif j == 2:
                dx_far[r] = total.astype(low)
            else:
                n = j // 2
                dx_sent[r, n] = total.astype(low)
                links.start((DX, NEAR, r, n), dx_sent.at[r, n], dx_got.at[r, n], near_dev)

    def input_far(r):
        links.arrived((DX, NEAR, r, 1))
        dx_far[r] = add_up([dx_far[r], dx_got[r, 1]]).astype(low)
        links.start((DX, FAR, r), dx_far.at[r], dx_far_got.at[r], across_dev)

    def input_done(r):
        links.arrived((DX, NEAR, r, 0), (DX, FAR, r))
        dx_out[r] = add_up([dx_acc[r], dx_got[r, 0], dx_far_got[r]]).astype(low)

    def prepare_row(r):
        slot = r % 2
        for j in range(4):
            rows = slice(j * size, (j + 1) * size)
            texts = text_rows(ids_ref[j, r : r + 1, :], size)
            extra_ref[r, rows, :] = key_extra(texts)
            if j == 0:
                penal_ref[r] = with_constants(query_extra(texts), -lse_ref[r])
            block = x_ref[r] if j == 0 else x_got[slot, j - 1]
            x_t[r, :, rows] = block.T

    def begin(step):
        for item in load_block(step):
            item.wait()
        if step + 1 < len(blocks):
            for item in load_block(step + 1):
                item.start()
        find_delta(step)

    def do(*actions):
        if fused:
            for action, *given in actions:
                action(*given)

    most = first_cut // PAIR
    begin(0)
    prepare_row(0)
    attend_pairs(0, 0, most // 2)
    attend_pairs(0, most // 2, most)
    do((pool_one,))
    begin(1)
    prepare_row(1)
    attend_pairs(1, 0, most // 2)
    do((out_y,), (down_z,), (up_x,))
    attend_pairs(1, most // 2, most)
    do((pool_two,))
    begin(2)
    prepare_row(2)
    attend_pairs(2, 0, most // 2)
    do((up_y, 0), (out_z,))
    attend_pairs(2, most // 2, most)
    weight_group(0)
    do((group_core, 0), (down_near_far,), (up_y, 1))
    begin(3)
    attend_pairs(3, 0, 2)
    load_mixed.wait()
    input_parts(0)
    do((down_far,), (group_y, 0), (out_far,), (up_z, 1), (up_z, 0), (input_far, 0))
    begin(4)
    attend_pairs(4, 0, 2)
    input_parts(1)
    begin(5)
    attend_pairs(5, 0, 1)
    weight_group(1)
    do((group_core, 1), (input_far, 1))
    attend_pairs(5, 1, 2)
    do((group_z, 0))
    weight_group(2)
    do((group_core, 2), (vector_step, 0, near_dev))
    input_parts(2)
    if not fused:
        vector_out[...] = vec_parts[0]
        pool_one()
        for r in range(3):
            input_far(r)
        pool_two()
        for r in range(3):
            input_done(r)
        links.finish()
        return
    do((group_y, 2), (group_y, 1), (vector_step, 1, across_dev), (up_far,), (input_far, 2))
    do((group_z, 2), (down_end,), (out_end,), (vector_step, 2, y_dev), (up_end,), (group_z, 1))
    do((vector_z,), (group_far, 0), (group_far, 2), (group_far, 1), (input_done, 0))
    do((group_end, 0), (group_end, 2), (vector_end,), (group_end, 1), (input_done, 1))
    do((input_done, 2))
    links.arrived((DOWN, GATHER), (OUT, GATHER), (UP, NEAR, 0), (UP, NEAR, 1))
    links.arrived(*((GROUP, GATHER, g) for g in range(3)))
    links.finish()


def attend_back(
    fused, x, ids, lse, w_query, w_key, w_value, pool, counts, vectors,
    x_got, q, k, v, context, grad, mixed, up, down, far, out,
):
    rows_here, size, width = x.shape
    keys = size * 4
    low = jnp.bfloat16
    f32 = jnp.float32
    whole = pl.BlockSpec(memory_space=pltpu.VMEM)
    outside = pl.BlockSpec(memory_space=pl.ANY)
    shape = jax.ShapeDtypeStruct
    most = GROUPS[0][1]
    vec = vectors.shape
    small = shape((8, 128), low)
    if fused:
        depth = up.shape[3]
        outs = dict(
            squares=[shape((2, depth // 2, 3 * count), low) for _, count in GROUPS],
            up=shape((4, depth, width), low),
            down=shape((2, 2 * down.shape[1], down.shape[2]), low),
            wo=shape((2, depth, width // 2), low),
            square=small,
        )
    else:
        outs = dict(
            squares=[], up=small, down=small, wo=small, square=shape((3, width, width), low)
        )
    scratch = dict(
        x_got=pltpu.VMEM((2, 3, size, width), low),
        x_t=pltpu.VMEM((rows_here, width, keys), low),
        q=pltpu.VMEM((2, size, most), low),
        k=pltpu.VMEM((2, keys, most), low),
        v=pltpu.VMEM((2, keys, most), low),
        context=pltpu.VMEM((2, size, most), low),
        grad=pltpu.VMEM((2, size, most), low),
        extra=pltpu.VMEM((rows_here, keys, PAIR), low),
        penal=pltpu.VMEM((rows_here, size, PAIR), low),
        delta=pltpu.VMEM((size, PAIR), low),
        dq=pltpu.VMEM((rows_here, size, width), low),
        dk=pltpu.VMEM((rows_here, keys, width), low),
        dv=pltpu.VMEM((rows_here, keys, width), low),
        dx_acc=pltpu.VMEM((rows_here, size, width), f32),
        dx_sent=pltpu.VMEM((rows_here, 2, size, width), low),
        dx_far=pltpu.VMEM((rows_here, size, width), low),
        dx_got=pltpu.VMEM((rows_here, 2, size, width), low),
        dx_far_got=pltpu.VMEM((rows_here, size, width), low),
        pool_parts=pltpu.VMEM(pool.shape, low),
        pool_got=pltpu.VMEM((2,) + pool.shape, low),
        vec_parts=pltpu.VMEM((4,) + vec, f32),
        vec_got=pltpu.VMEM((6,) + vec, f32),
        send_sem=pltpu.SemaphoreType.DMA((72,)),
        recv_sem=pltpu.SemaphoreType.DMA((72,)),
        row_sem=pltpu.SemaphoreType.DMA((2, 6)),
        local_sem=pltpu.SemaphoreType.DMA((5,)),
    )
    if fused:
        tails = [(depth // 2, 3 * count) for _, count in GROUPS]
        spread = lambda *lead: [pltpu.VMEM(lead + tail, low) for tail in tails]
        b_shape = far.shape[2:]
        narrow = (depth, width // 2)
        scratch.update(
            g=spread(2, 4, 2), g_got=spread(4, 2), g_y=spread(4), g_z=spread(3),
            g_s=spread(), g_x=spread(),
            u=pltpu.VMEM((4, 2, depth, width), low),
            u_x=pltpu.VMEM((2, 4, 2, depth // 2, width), low),
            u_y=pltpu.VMEM((2, 4, depth // 2, width), low),
            u_z=pltpu.VMEM((3, depth, width), low),
            a_z=pltpu.VMEM((3,) + down.shape[1:], low),
            a_s=pltpu.VMEM(down.shape[1:], low),
            a_x=pltpu.VMEM(down.shape[1:], low),
            b=pltpu.VMEM((4,) + b_shape, low),
            b_y=pltpu.VMEM((4,) + b_shape, low),
            b_z=pltpu.VMEM((3,) + b_shape, low),
            o=pltpu.VMEM((4,) + narrow, low),
            o_y=pltpu.VMEM((4,) + narrow, low),
            o_z=pltpu.VMEM((3,) + narrow, low),
            o_s=pltpu.VMEM(narrow, low),
            o_x=pltpu.VMEM(narrow, low),
        )
    out_leaves, out_tree = jax.tree.flatten(outs)
    leaves, tree = jax.tree.flatten(scratch)
    count_out = len(out_leaves)
    got = pl.pallas_call(
        functools.partial(attend_back_kernel, fused, count_out, out_tree, tree),
        out_shape=(
            shape((rows_here, size, width), low),
            shape(pool.shape, f32),
            shape(vec, f32),
        )
        + tuple(out_leaves),
        in_specs=[whole] * 9 + [outside] * 7 + [whole] * 4,
        out_specs=(whole,) * (3 + count_out),
        scratch_shapes=leaves,
        compiler_params=pltpu.CompilerParams(
            vmem_limit_bytes=63 * 2**20, collective_id=1, has_side_effects=True
        ),
        cost_estimate=pl.CostEstimate(
            flops=rows_here
            * (4 * (size + 2 * keys) * width * width + 40 * size * keys * width),
            bytes_accessed=2 * (16 * width * width + 9 * keys * width),
            transcendentals=rows_here * HEADS * size * keys,
        ),
    )(
        x, ids, lse, w_query, w_key, w_value, pool, counts, vectors,
        x_got, q, k, v, context, grad, mixed, up, down, far, out,
    )
    return got[:3] + (types.SimpleNamespace(**jax.tree.unflatten(out_tree, got[3:])),)


def outputs_kernel(
    square0, square1, square2, wo, up, down, pool, final, dx,
    wq_out, wk_out, wv_out, wo_out, up_out, down_out, pool_out, final_out, dx_out,
):
    final_out[...] = final[...]
    dx_out[...] = dx[...]
    f32 = jnp.float32
    pool_out[...] = pool[...].reshape(pool_out.shape)
    for (start, count), square in zip(GROUPS, (square0, square1, square2)):
        rows = square.shape[1]
        for n, out in enumerate((wq_out, wk_out, wv_out)):
            for h in range(2):
                out[h * rows : (h + 1) * rows, start : start + count] = square[
                    h, :, n * count : (n + 1) * count
                ].astype(f32)
    for h in range(2):
        half = wo.shape[2]
        wo_out[:, h * half : (h + 1) * half] = wo[h].astype(f32)
        rows = down.shape[1]
        down_out[:, h * rows : (h + 1) * rows] = down[h].astype(f32).T
    for i in range(4):
        place, width = (i % 2) * 2 + i // 2, up.shape[2]
        up_out[:, place * width : (place + 1) * width] = up[i].astype(f32)


def outputs(squares, wo, up, down, pool, final, dx):
    f32 = jnp.float32
    whole = pl.BlockSpec(memory_space=pltpu.VMEM)
    shape = jax.ShapeDtypeStruct
    rows, width = up.shape[1:]
    row_count = final.shape[0]
    return pl.pallas_call(
        outputs_kernel,
        out_shape=(
            shape((rows, width), f32), shape((rows, width), f32), shape((rows, width), f32),
            shape((rows, width), f32), shape((rows, 4 * width), f32),
            shape((down.shape[2], 2 * down.shape[1]), f32),
            shape((row_count, pool.shape[0] // row_count, width), f32),
            shape(final.shape, final.dtype), shape(dx.shape, dx.dtype),
        ),
        in_specs=[whole] * 9,
        out_specs=(whole,) * 9,
        compiler_params=pltpu.CompilerParams(vmem_limit_bytes=63 * 2**20),
    )(*squares, wo, up, down, pool, final, dx)


def radices_of(count):
    if count == 8:
        return ((1, 2), (2, 4))
    digits = []
    stride = 1
    while stride < count:
        digits.append((stride, 2))
        stride *= 2
    return tuple(digits)


def exchange(piece, axis_name, stride, offset):
    count = lax.axis_size(axis_name)
    pairs = [(i, i ^ (offset * stride)) for i in range(count)]
    return lax.ppermute(piece, axis_name, pairs)


def digit_of(axis_name, stride, radix):
    return (lax.axis_index(axis_name) // stride) % radix


def scatter_digit(pieces, place, axis_name, stride, radix):
    here = digit_of(axis_name, stride, radix)
    received = [
        exchange(
            lax.dynamic_index_in_dim(pieces, here ^ offset, place, keepdims=False).astype(
                jnp.bfloat16
            ),
            axis_name, stride, offset,
        )
        for offset in range(1, radix)
    ]
    total = lax.dynamic_index_in_dim(pieces, here, place, keepdims=False).astype(jnp.float32)
    for item in received:
        total = total + item.astype(jnp.float32)
    return total.astype(jnp.bfloat16)


def halve(piece, place, axis_name, stride):
    half = piece.shape[place] // 2
    here = digit_of(axis_name, stride, 2)
    sent = lax.dynamic_slice_in_dim(piece, (1 - here) * half, half, place).astype(jnp.bfloat16)
    kept = lax.dynamic_slice_in_dim(piece, here * half, half, place).astype(jnp.float32)
    return (kept + exchange(sent, axis_name, stride, 1).astype(jnp.float32)).astype(jnp.bfloat16)


def join(piece, place, axis_name, stride):
    here = digit_of(axis_name, stride, 2)
    other = exchange(piece, axis_name, stride, 1)
    first = jnp.where(here == 0, piece, other)
    second = jnp.where(here == 0, other, piece)
    return jnp.concatenate([first, second], axis=place)


def scatter_rows(group, dp_size):
    digits = radices_of(dp_size)
    shape = tuple(r for _, r in reversed(digits))
    group = group.reshape(shape + (group.shape[0] // dp_size, group.shape[1]))
    for place, (stride, radix) in zip(range(len(digits) - 1, -1, -1), digits):
        group = scatter_digit(group, place, "dp", stride, radix)
    return group


def finish_weight(flat, dp_size, side):
    flat = scatter_rows(flat, dp_size)
    flat = flat.astype(jnp.float32) + exchange(flat, "ctx", 2, 1).astype(jnp.float32)
    return join(flat.astype(jnp.bfloat16), side, "ctx", 1).astype(jnp.float32)


def reduce_weight(gradient, dp_size, side):
    return finish_weight(halve(gradient, side, "ctx", 1), dp_size, side)


def per_device(
    hidden_in,
    seg_ids,
    valid,
    w_query,
    b_query,
    w_key,
    w_value,
    b_value,
    w_out,
    b_out,
    gain_attn,
    shift_attn,
    w_up,
    b_up,
    w_down,
    b_down,
    gain_ffn,
    shift_ffn,
    pooled_text_gradient,
):
    row_count, group_size, model_width = hidden_in.shape
    dp_size = lax.axis_size("dp")
    ff_width = w_up.shape[1]
    rows_here, ff_here = model_width // dp_size, ff_width // dp_size
    fused = dp_size == 8 and rows_here % 32 == 0 and ff_here % 128 == 0 and model_width % 128 == 0
    q_all, context, lse_all, ids_got, x_got, k_all, v_all = attend(
        hidden_in, seg_ids, valid, b_query, b_value, w_query, w_key, w_value
    )
    vectors = (b_out, gain_attn, shift_attn, b_up, b_down, gain_ffn, shift_ffn)
    pool, counts, vector_parts, grad_context, grad_mixed, out, final_out, up, down, far = middle(
        fused, hidden_in, context, ids_got, vectors, pooled_text_gradient, w_out, w_up, w_down,
        dp_size,
    )
    if fused:
        up_part = up.reshape(2, 4, 2, rows_here, -1)
        far_part = far.reshape((4, 2) + far.shape[1:])
        out_part = out.reshape(4, 2, rows_here, -1)
    else:
        up_part = far_part = out_part = jnp.zeros((16, 128), jnp.bfloat16)
    grad_input, pooled, vector_sum, sums_of = attend_back(
        fused, hidden_in, ids_got, lse_all, w_query, w_key, w_value,
        pool, counts, vector_parts, x_got, q_all, k_all, v_all, context, grad_context, grad_mixed,
        up_part, down, far_part, out_part,
    )
    if fused:
        *square_sums, up_sum, down_sum, pooled, final_out, grad_input = outputs(
            sums_of.squares, sums_of.wo, sums_of.up, sums_of.down, pooled, final_out, grad_input
        )
    else:
        squares = sums_of.square
        square_sums = [reduce_weight(squares[n], dp_size, 1) for n in range(3)]
        square_sums.append(finish_weight(out, dp_size, 1))
        up_sum = finish_weight(up.transpose(1, 0, 2).reshape(model_width, -1), dp_size, 1)
        down = down.transpose(0, 2, 1).reshape(ff_width, -1)
        down_sum = finish_weight(down, dp_size, 1)
        vector_sum = lax.psum(vector_sum, ("dp", "ctx"))
        pooled = pooled.reshape(row_count, NSEG, model_width)
    place = lax.axis_index("dp")
    sums = lax.dynamic_slice_in_dim(vector_sum[:8], place * rows_here, rows_here, 1)
    sum_bu = lax.dynamic_slice_in_dim(
        vector_sum[8 : 8 + ff_width // model_width].reshape(-1), place * ff_here, ff_here
    )
    results = (
        square_sums[0], sums[0], square_sums[1], square_sums[2], sums[1], square_sums[3],
        sums[2], sums[3], sums[4], up_sum, sum_bu, down_sum, sums[5], sums[6], sums[7],
    )
    return (
        final_out,
        pooled,
        grad_input,
    ) + tuple(results)


def solution(mesh):
    placed = (
        P("dp", "ctx", None),
        P("dp", "ctx"),
        P("dp", "ctx"),
        P(),
        P(),
        P(),
        P(),
        P(),
        P(),
        P(),
        P(),
        P(),
        P(),
        P(),
        P(),
        P(),
        P(),
        P(),
        P("dp", None, None),
    )
    return jax.shard_map(
        per_device,
        mesh=mesh,
        in_specs=placed,
        out_specs=(
            P("dp", "ctx", None),
            P("dp", None, None),
            P("dp", "ctx", None),
            P("dp", None),
            P("dp"),
            P("dp", None),
            P("dp", None),
            P("dp"),
            P("dp", None),
            P("dp"),
            P("dp"),
            P("dp"),
            P("dp", None),
            P("dp"),
            P("dp", None),
            P("dp"),
            P("dp"),
            P("dp"),
        ),
        check_vma=False,
    )
```

```python
import functools
import types

import jax
import jax.numpy as jnp
from jax import lax
from jax.experimental import pallas as pl
from jax.experimental.pallas import tpu as pltpu
from jax.sharding import PartitionSpec as P

HEADS = 12
HEAD_DIM = 64
NSEG = 16


eps = 1e-12


def matmul(left_side, right_side):
    return jnp.dot(left_side, right_side, preferred_element_type=jnp.float32)


PAIR = 2 * HEAD_DIM
MESH = pl.DeviceIdType.MESH
MASKED = -1e30


def dot_nt(left_side, right_side):
    return lax.dot_general(
        left_side, right_side, (((1,), (1,)), ((), ())), preferred_element_type=jnp.float32
    )


def dot_tn(left_side, right_side):
    return lax.dot_general(
        left_side, right_side, (((0,), (0,)), ((), ())), preferred_element_type=jnp.float32
    )


def split_heads(pair):
    lane = lax.broadcasted_iota(jnp.int32, pair.shape, 1)
    zero = jnp.zeros_like(pair)
    return jnp.concatenate(
        [jnp.where(lane < HEAD_DIM, pair, zero), jnp.where(lane < HEAD_DIM, zero, pair)], axis=0
    )


def text_rows(ids_row, size):
    return jnp.broadcast_to(ids_row.astype(jnp.float32), (PAIR, size)).T


def lanes_of(size):
    return lax.broadcasted_iota(jnp.int32, (size, PAIR), 1)


def key_extra(texts):
    lane = lanes_of(texts.shape[0])
    hot = jnp.where(lane.astype(jnp.float32) == texts, 1.0, 0.0)
    return jnp.where((lane >= NSEG) & (lane < 4 * NSEG), 1.0, hot).astype(jnp.bfloat16)


def query_extra(texts):
    lane = lanes_of(texts.shape[0])
    other = (lane < NSEG) & (lane.astype(jnp.float32) != texts)
    return jnp.where(other, MASKED, 0.0)


def with_constants(extra, constants):
    lane = lanes_of(extra.shape[0])
    high = constants.astype(jnp.bfloat16).astype(jnp.float32)
    middle = (constants - high).astype(jnp.bfloat16).astype(jnp.float32)
    rest = constants - high - middle
    terms = jnp.where(lane < 2 * NSEG, high, jnp.where(lane < 3 * NSEG, middle, rest))
    kept = (lane >= NSEG) & (lane < 4 * NSEG)
    return jnp.where(kept, terms, extra).astype(jnp.bfloat16)


def of_head(extra, head):
    lane = lanes_of(extra.shape[0])
    kept = (lane < NSEG) | (lane % NSEG == head)
    return jnp.where(kept, extra, jnp.zeros_like(extra))


def attend_kernel(
    x_ref, seg_ref, valid_ref, b_query, b_value, w_query, w_key, w_value,
    q_out, context_out, lse_out, ids_out, x_hbm, k_hbm, v_hbm,
    x_got, k_ref, v_ref, extra_ref, ids_ref, score_one, score_two, score_three, send_sem, recv_sem, local_sem,
):
    rows_here, size, width = x_ref.shape
    me = lax.axis_index("ctx")
    one = me + 1 - 2 * (me % 2)
    two = (me + 2) % 4
    three = (one + 2) % 4
    low = jnp.bfloat16

    ids_ref[...] = jnp.zeros_like(ids_ref)
    ids_ref[0:rows_here, :] = seg_ref[...]
    ids_ref[rows_here : 2 * rows_here, :] = valid_ref[...]
    query_bias = b_query[...].astype(jnp.float32)[None]
    value_bias = b_value[...].astype(jnp.float32)[None]
    barrier = pltpu.get_barrier_semaphore()
    for peer in (one, two, three):
        pl.semaphore_signal(barrier, inc=1, device_id={"ctx": peer}, device_id_type=MESH)
    pl.semaphore_wait(barrier, 3)

    def send(source, target, slot, peer):
        return pltpu.make_async_remote_copy(
            src_ref=source, dst_ref=target, send_sem=send_sem.at[slot],
            recv_sem=recv_sem.at[slot], device_id={"ctx": peer}, device_id_type=MESH,
        )

    ids_out[0] = ids_ref[...]
    ids_sends = [send(ids_ref, ids_out.at[j + 1], j, peer) for j, peer in enumerate((one, two, three))]
    near = send(x_ref, x_got.at[0], 3, one)

    def far(r):
        return send(x_ref.at[r], x_got.at[1, r], 4 + r, two)

    def passed(r):
        return send(x_got.at[1, r], x_got.at[2, r], 4 + rows_here + r, one)

    far(0).start()
    near.start()
    for item in ids_sends:
        item.start()
    for r in range(1, rows_here):
        far(r).start()

    def project(x, r, j):
        count = x.shape[0] // size
        k = matmul(x, w_key[...]).astype(low)
        v = (matmul(x, w_value[...]) + value_bias).astype(low)
        for n in range(count):
            rows = pl.ds((j + n if r is not None else j) * size, size)
            k_ref[n if r is None else r, rows, :] = k[n * size : (n + 1) * size]
            v_ref[n if r is None else r, rows, :] = v[n * size : (n + 1) * size]

    own = x_ref[...].reshape(rows_here * size, width)
    q = (matmul(own, w_query[...]) + query_bias).astype(low)
    q_out[...] = (q * HEAD_DIM ** (-0.5)).astype(low).reshape(q_out.shape)
    project(own, None, 0)
    near.wait_recv()
    project(x_got[0].reshape(rows_here * size, width), None, 1)
    for item in ids_sends:
        item.wait_recv()
    lane = lax.broadcasted_iota(jnp.int32, (size, PAIR), 1)
    far(0).wait_recv()
    passed(0).start()

    def keep(r):
        return (
            pltpu.make_async_copy(k_ref.at[r], k_hbm.at[r], local_sem.at[0, r]),
            pltpu.make_async_copy(v_ref.at[r], v_hbm.at[r], local_sem.at[1, r]),
            pltpu.make_async_copy(x_got.at[:, r], x_hbm.at[:, r], local_sem.at[2, r]),
        )

    for r in range(rows_here):
        project(x_got[1, r], r, 2)
        passed(r).wait_recv()
        project(x_got[2, r], r, 3)
        for item in keep(r):
            item.start()
        for j in range(4):
            texts = text_rows(ids_out[j, r : r + 1, :], size)
            extra_ref[j * size : (j + 1) * size, :] = key_extra(texts)
            if j == 0:
                own_extra = query_extra(texts).astype(low)

        def score(pair, target, r=r, own_extra=own_extra):
            columns = pl.ds(pl.multiple_of(pair * PAIR, PAIR), PAIR)
            both = split_heads(q_out[r, :, columns])
            extras = jnp.concatenate([own_extra, own_extra], axis=0)
            keys = jnp.concatenate([k_ref[r, :, columns], extra_ref[...]], axis=1)
            target[...] = dot_nt(jnp.concatenate([both, extras], axis=1), keys)

        def one_pair(pair, source, stat, r=r):
            columns = pl.ds(pl.multiple_of(pair * PAIR, PAIR), PAIR)
            scores = source[...]
            top = jnp.max(scores, axis=-1, keepdims=True)
            weight = jnp.exp(scores - top)
            total = jnp.sum(weight, axis=-1, keepdims=True)
            mixed = matmul(weight.astype(low), v_ref[r, :, columns]) * (1.0 / total)
            context_out[r, :, columns] = jnp.where(
                lane < HEAD_DIM, mixed[:size], mixed[size:]
            ).astype(low)
            lse = top + jnp.log(total)
            for h in range(2):
                ours = lane % NSEG == 2 * pair + h
                stat = jnp.where(ours, lse[h * size : (h + 1) * size], stat)
            return stat

        def three_pairs(n, carry, r=r):
            stat = lse_out[r]
            for i, target in enumerate((score_one, score_two, score_three)):
                score(3 * n + i, target)
            for i, source in enumerate((score_one, score_two, score_three)):
                stat = one_pair(3 * n + i, source, stat)
            lse_out[r] = stat
            return carry

        lse_out[r] = jnp.zeros((size, PAIR), jnp.float32)
        more = r + 1 < rows_here
        if r and more:
            lax.fori_loop(0, HEADS // 12, three_pairs, 0)
            far(r + 1).wait_recv()
            passed(r + 1).start()
            lax.fori_loop(HEADS // 12, HEADS // 6, three_pairs, 0)
        else:
            lax.fori_loop(0, HEADS // 6, three_pairs, 0)
            if more:
                far(r + 1).wait_recv()
                passed(r + 1).start()
    for r in range(rows_here):
        for item in keep(r):
            item.wait()
        far(r).wait_send()
        passed(r).wait_send()
    near.wait_send()
    for item in ids_sends:
        item.wait_send()


def attend(x, seg_ids, valid, b_query, b_value, w_query, w_key, w_value):
    rows_here, size, width = x.shape
    keys = size * 4
    low = jnp.bfloat16
    whole = pl.BlockSpec(memory_space=pltpu.VMEM)
    outside = pl.BlockSpec(memory_space=pl.ANY)
    slots = 4 + 2 * rows_here
    return pl.pallas_call(
        attend_kernel,
        out_shape=(
            jax.ShapeDtypeStruct((rows_here, size, width), low),
            jax.ShapeDtypeStruct((rows_here, size, width), low),
            jax.ShapeDtypeStruct((rows_here, size, PAIR), jnp.float32),
            jax.ShapeDtypeStruct((4, 8, size), jnp.int32),
            jax.ShapeDtypeStruct((3,) + x.shape, low),
            jax.ShapeDtypeStruct((rows_here, keys, width), low),
            jax.ShapeDtypeStruct((rows_here, keys, width), low),
        ),
        in_specs=[whole] * 8,
        out_specs=(whole, whole, whole, whole, outside, outside, outside),
        scratch_shapes=[
            pltpu.VMEM((3,) + x.shape, low),
            pltpu.VMEM((rows_here, keys, width), low),
            pltpu.VMEM((rows_here, keys, width), low),
            pltpu.VMEM((keys, PAIR), low),
            pltpu.VMEM((8, size), jnp.int32),
            pltpu.VMEM((2 * size, keys), jnp.float32),
            pltpu.VMEM((2 * size, keys), jnp.float32),
            pltpu.VMEM((2 * size, keys), jnp.float32),
            pltpu.SemaphoreType.DMA((slots,)),
            pltpu.SemaphoreType.DMA((slots,)),
            pltpu.SemaphoreType.DMA((3, rows_here)),
        ],
        compiler_params=pltpu.CompilerParams(
            vmem_limit_bytes=56 * 2**20, collective_id=0, has_side_effects=True
        ),
        cost_estimate=pl.CostEstimate(
            flops=rows_here * (2 * (size + 2 * keys) * width * width + 16 * size * keys * width),
            bytes_accessed=2 * (3 * width * width + 9 * keys * width),
            transcendentals=rows_here * HEADS * size * keys,
        ),
    )(x, seg_ids, valid, b_query, b_value, w_query, w_key, w_value)


def gelu_both(u):
    size = jnp.abs(u)
    t = 1.0 / (1.0 + (0.3275911 * 0.5**0.5) * size)
    bell = jnp.exp(-0.5 * u * u)
    poly = t * (
        0.127414796 + t * (-0.142248368 + t * (0.7107068705 + t * (-0.7265760135 + t * 0.5307027145)))
    )
    tail = poly * bell
    cdf = jnp.where(u >= 0.0, 1.0 - tail, tail)
    return u * cdf, cdf + u * bell * 0.3989422804014327


def normalize(values_in):
    centre = jnp.mean(values_in, axis=-1, keepdims=True)
    centred = values_in - centre
    spread = jnp.mean(centred * centred, axis=-1, keepdims=True)
    scale = lax.rsqrt(spread + eps)
    return centred * scale, scale


def normalize_back(grad, unit, scale):
    mean_one = jnp.mean(grad, axis=-1, keepdims=True)
    mean_two = jnp.mean(grad * unit, axis=-1, keepdims=True)
    return (grad - mean_one - unit * mean_two) * scale


def column_sum(values_in):
    return jnp.sum(values_in, axis=0, keepdims=True)


B_QUERY, B_VALUE, B_OUT, GAIN_ONE, SHIFT_ONE, B_DOWN, GAIN_TWO, SHIFT_TWO, B_UP = range(9)


def middle_kernel(
    fused,
    x_ref, context_ref, ids_ref, b_out, gain_one, shift_one, b_up, b_down, gain_two, shift_two,
    text_ref, w_out, up_hbm, down_hbm,
    pool_out, count_out, vector_out, grad_out, mixed_out, wo_out, final_hbm, up_out, down_out, far_out,
    vec_ref, w_up, w_down, unit_ref, scale_ref, normed_ref, normed_t, act_ref, slope_ref, acc_ref, pre_one, pre_two,
    g_ref, g_t_ref, upg_ref, up_got, downg_ref, down_got, wo_sent, wo_got, down_y, down_x,
    send_sem, recv_sem, load_sem, store_sem,
):
    rows_here, size, width = x_ref.shape
    tokens = rows_here * size
    parts = w_up.shape[1] // width
    half = width // 2
    low = jnp.bfloat16
    f32 = jnp.float32
    me = lax.axis_index("ctx")
    core = me % 2
    near = {"ctx": me + 1 - 2 * core}
    side = me // 2
    place = lax.axis_index("dp")
    y = place % 2
    y_dev = {"dp": place + 1 - 2 * y}
    across_dev = {"ctx": (me + 2) % 4}
    peers = [near, across_dev, y_dev] if fused else [near]
    barrier = pltpu.get_barrier_semaphore()
    for peer in peers:
        pl.semaphore_signal(barrier, inc=1, device_id=peer, device_id_type=MESH)
    for row, source in (
        (B_OUT, b_out), (GAIN_ONE, gain_one), (SHIFT_ONE, shift_one), (B_DOWN, b_down),
        (GAIN_TWO, gain_two), (SHIFT_TWO, shift_two),
    ):
        vec_ref[row : row + 1, :] = source[...].astype(f32)[None]
    for i in range(parts):
        vec_ref[B_UP + i : B_UP + i + 1, :] = (
            b_up[i * width : (i + 1) * width].astype(f32)[None]
        )

    def vec(row):
        return vec_ref[row : row + 1, :]

    loads = []
    for i in range(parts):
        loads.append(
            (
                pltpu.make_async_copy(
                    up_hbm.at[:, pl.ds(i * width, width)],
                    w_up.at[:, pl.ds(i * width, width)],
                    load_sem.at[0, i],
                ),
                pltpu.make_async_copy(
                    down_hbm.at[pl.ds(i * width, width)],
                    w_down.at[pl.ds(i * width, width)],
                    load_sem.at[1, i],
                ),
            )
        )
    for pair in loads:
        for item in pair:
            item.start()

    def rows_of(r):
        return pl.ds(pl.multiple_of(r * size, size), size)

    text = lax.broadcasted_iota(jnp.int32, (NSEG, size), 0)

    def members(j, r):
        seg = ids_ref[j, r : r + 1, :]
        real = ids_ref[j, rows_here + r : rows_here + r + 1, :]
        return jnp.where((text == seg) & (real == 1), 1.0, 0.0)

    for r in range(rows_here):
        number = sum(jnp.sum(members(j, r), axis=1, keepdims=True) for j in range(4))
        count_out[r * NSEG : (r + 1) * NSEG, :] = jnp.maximum(number, 1.0)

    def first_norm(r):
        rows = pl.ds(r * size, size)
        mixed = x_ref[r].astype(f32) + (matmul(context_ref[r], w_out[...]) + vec(B_OUT))
        unit, scale = normalize(mixed)
        unit_ref[rows, :] = unit
        scale_ref[rows, :] = scale
        normed_ref[rows, :] = (unit * vec(GAIN_ONE) + vec(SHIFT_ONE)).astype(low)

    for r in range(rows_here):
        first_norm(r)
    for pair in loads:
        for item in pair:
            item.wait()

    def units(i):
        return pl.ds(pl.multiple_of(i * width, width), width)

    def forward_part(i, following, now, then):
        for r in range(rows_here):
            rows = pl.ds(r * size, size)
            then[rows, :] = matmul(normed_ref[rows, :], w_up[:, units(following)])
            act, slope = gelu_both(now[rows, :] + vec_ref[pl.ds(B_UP + i, 1), :])
            act = act.astype(low)
            act_ref[rows, units(i)] = act
            slope_ref[rows, units(i)] = slope.astype(low)
            acc_ref[rows, :] += matmul(act, w_down[units(i), :])

    def forward_parts(n, carry):
        forward_part(2 * n, 2 * n + 1, pre_one, pre_two)
        forward_part(2 * n + 1, jnp.minimum(2 * n + 2, parts - 1), pre_two, pre_one)
        return carry

    acc_ref[...] = jnp.zeros_like(acc_ref)
    pre_one[...] = matmul(normed_ref[...], w_up[:, units(0)])
    lax.fori_loop(0, parts // 2, forward_parts, 0)
    normed_t[...] = normed_ref[...].T

    store_final = []
    vector_out[...] = jnp.zeros_like(vector_out)
    for r in range(rows_here):
        rows = pl.ds(r * size, size)
        normed = unit_ref[rows, :] * vec(GAIN_ONE) + vec(SHIFT_ONE)
        summed = normed + (acc_ref[rows, :] + vec(B_DOWN))
        unit, scale = normalize(summed)
        final = unit * vec(GAIN_TWO) + vec(SHIFT_TWO)
        high = final.astype(low)
        upg_ref[parts - 1, rows, :] = high
        item = pltpu.make_async_copy(
            upg_ref.at[parts - 1, rows], final_hbm.at[r], store_sem.at[r]
        )
        item.start()
        store_final.append(item)
        own = members(0, r)
        own_low = own.astype(low)
        rest = (final - high.astype(f32)).astype(low)
        pool = matmul(own_low, high) + matmul(own_low, rest)
        pool_out[r * NSEG : (r + 1) * NSEG, :] = pool.astype(low)
        share = text_ref[r] / count_out[r * NSEG : (r + 1) * NSEG, :]
        first = share.astype(low)
        second = (share - first.astype(f32)).astype(low)
        third = (share - first.astype(f32) - second.astype(f32)).astype(low)
        grad = dot_tn(
            jnp.concatenate([own_low] * 3, axis=0), jnp.concatenate([first, second, third], axis=0)
        )
        back = normalize_back(grad * vec(GAIN_TWO), unit, scale)
        back_low = back.astype(low)
        acc_ref[rows, :] = back
        g_ref[rows, :] = back_low
        vector_out[GAIN_TWO : GAIN_TWO + 1, :] += column_sum(grad * unit)
        vector_out[SHIFT_TWO : SHIFT_TWO + 1, :] += column_sum(grad)
        vector_out[B_DOWN : B_DOWN + 1, :] += column_sum(back_low.astype(f32))

    pl.semaphore_wait(barrier, len(peers))

    def remote(source, target, slot, device=near):
        return pltpu.make_async_remote_copy(
            src_ref=source, dst_ref=target, send_sem=send_sem.at[slot],
            recv_sem=recv_sem.at[slot], device_id=device, device_id_type=MESH,
        )

    per_part = downg_ref.shape[0] // parts
    mine = parts // 2

    def up_send(i):
        return remote(upg_ref.at[i], up_got.at[i], i)

    def down_send(i):
        chunk = pl.ds(i * per_part, per_part)
        return remote(downg_ref.at[chunk, 1 - core], down_got.at[chunk], parts + i)

    cut = downg_ref.shape[3]

    def down_part(i, carry):
        part = matmul(g_t_ref[...], act_ref[:, units(i)]).astype(low)
        part = part.reshape((2, width // 2, width))
        for n in range(per_part):
            downg_ref[per_part * i + n] = part[:, :, n * cut : (n + 1) * cut]
        down_send(i).start()
        return carry

    g_t_ref[...] = g_ref[...].T
    lax.fori_loop(0, parts, down_part, 0)

    def backward_part(step, carry):
        i = (step + mine * (1 - core)) % parts
        back = dot_nt(g_ref[...], w_down[units(i), :])
        back = (back * slope_ref[:, units(i)].astype(f32)).astype(low)
        acc_ref[...] += dot_nt(back, w_up[:, units(i)])
        vector_out[pl.ds(B_UP + i, 1), :] = column_sum(back.astype(f32))
        upg_ref[step] = matmul(normed_t[...], back).astype(low)

        @pl.when(step < mine)
        def _():
            up_send(step).start()

        return carry

    def down_sum(i, carry):
        downg_ref[i, core] = (
            downg_ref[i, core].astype(f32) + down_got[i].astype(f32)
        ).astype(low)
        return carry

    piece = downg_ref.shape[2] // 2
    quarter = piece // 2
    rest = pl.ds(pl.multiple_of(piece + quarter * (1 - side), 16), quarter)
    kept = pl.ds(pl.multiple_of(piece + quarter * side, 16), quarter)
    down_moves = []
    if fused:
        for n in range(4):
            down_moves.append(
                remote(
                    downg_ref.at[2 * n + 1 - y, core, pl.ds(0, piece)], down_y.at[n],
                    2 * parts + 1 + n, y_dev,
                )
            )
        for n in range(8):
            down_moves.append(
                remote(
                    downg_ref.at[n, core, rest], down_x.at[n], 2 * parts + 5 + n, across_dev
                )
            )
    lax.fori_loop(0, 1, backward_part, 0)
    for i in range(parts):
        down_send(i).wait_recv()
    lax.fori_loop(0, downg_ref.shape[0], down_sum, 0)
    for item in down_moves:
        item.start()
    for item in store_final:
        item.wait()
    lax.fori_loop(1, parts, backward_part, 0)

    def first_back(r):
        rows = pl.ds(r * size, size)
        unit = unit_ref[rows, :]
        grad = acc_ref[rows, :]
        back = normalize_back(grad * vec(GAIN_ONE), unit, scale_ref[rows, :])
        back_low = back.astype(low)
        mixed_out[r] = back
        g_ref[rows, :] = back_low
        vector_out[GAIN_ONE : GAIN_ONE + 1, :] += column_sum(grad * unit)
        vector_out[SHIFT_ONE : SHIFT_ONE + 1, :] += column_sum(grad)
        vector_out[B_OUT : B_OUT + 1, :] += column_sum(back_low.astype(f32))
        grad_out[r] = dot_nt(g_ref[rows, :], w_out[...]).astype(low)

    for r in range(rows_here):
        first_back(r)

    for r in range(rows_here):
        g_t_ref[:, r * size : (r + 1) * size] = context_ref[r].T

    def out_part(h):
        columns = pl.ds(pl.multiple_of(h * half, 128), half)
        return matmul(g_t_ref[...], g_ref[:, columns])

    wo_sent[...] = out_part(1 - core).astype(low)
    wo_send = remote(wo_sent, wo_got, 2 * parts)
    wo_send.start()
    own_part = out_part(core)
    for i in range(mine):
        up_send(i).wait_recv()

    def up_sum(n, carry):
        rows = pl.ds(pl.multiple_of(n * 128, 128), 128)
        for i in range(mine):
            upg_ref[mine + i, rows, :] = (
                upg_ref[mine + i, rows, :].astype(f32) + up_got[i, rows, :].astype(f32)
            ).astype(low)
        return carry

    lax.fori_loop(0, width // 128, up_sum, 0)
    store_up = pltpu.make_async_copy(
        upg_ref.at[pl.ds(mine, mine)], up_out, store_sem.at[rows_here + 1]
    )
    store_up.start()
    wo_send.wait_recv()
    wo_out[...] = (own_part + wo_got[...].astype(f32)).astype(low)
    if fused:
        for item in down_moves:
            item.wait_recv()

        def near_sum(n, carry):
            down_y[n] = (
                downg_ref[2 * n + y, core, 0:piece, :].astype(f32) + down_y[n].astype(f32)
            ).astype(low)
            return carry

        def far_sum(n, carry):
            down_x[n] = (
                downg_ref[n, core, kept, :].astype(f32) + down_x[n].astype(f32)
            ).astype(low)
            return carry

        lax.fori_loop(0, 4, near_sum, 0)
        lax.fori_loop(0, 8, far_sum, 0)
        stores = [
            pltpu.make_async_copy(down_y, down_out, store_sem.at[rows_here]),
            pltpu.make_async_copy(down_x, far_out, store_sem.at[rows_here + 2]),
        ]
    else:
        stores = [
            pltpu.make_async_copy(downg_ref.at[:, core], down_out, store_sem.at[rows_here])
        ]
    for item in stores:
        item.start()
    for i in range(parts):
        down_send(i).wait_send()
    for i in range(mine):
        up_send(i).wait_send()
    wo_send.wait_send()
    for item in down_moves:
        item.wait_send()
    for item in stores + [store_up]:
        item.wait()


def middle(fused, x, context, ids, vectors, text_gradient, w_out, w_up, w_down, dp_size):
    rows_here, size, width = x.shape
    ff = w_up.shape[1]
    parts = ff // width
    tokens = rows_here * size
    low = jnp.bfloat16
    f32 = jnp.float32
    shape = jax.ShapeDtypeStruct
    whole = pl.BlockSpec(memory_space=pltpu.VMEM)
    outside = pl.BlockSpec(memory_space=pl.ANY)
    chunks = dp_size if fused else parts
    chunk = ff // chunks
    vec = (8 + parts + (-parts) % 8, width)
    if fused:
        down_shape, far_shape = (4, width // 4, chunk), (8, width // 8, chunk)
    else:
        down_shape, far_shape = (chunks, width // 2, chunk), (8, 16, 128)
    return pl.pallas_call(
        functools.partial(middle_kernel, fused),
        out_shape=(
            shape((rows_here * NSEG, width), low),
            shape((rows_here * NSEG, 1), f32),
            shape(vec, f32),
            shape((rows_here, size, width), low),
            shape((rows_here, size, width), f32),
            shape((width, width // 2), low),
            shape((rows_here, size, width), low),
            shape((parts // 2, width, width), low),
            shape(down_shape, low),
            shape(far_shape, low),
        ),
        in_specs=[whole] * 12 + [outside] * 2,
        out_specs=(whole,) * 6 + (outside,) * 4,
        scratch_shapes=[
            pltpu.VMEM(vec, f32),
            pltpu.VMEM((width, ff), low),
            pltpu.VMEM((ff, width), low),
            pltpu.VMEM((tokens, width), f32),
            pltpu.VMEM((tokens, 1), f32),
            pltpu.VMEM((tokens, width), low),
            pltpu.VMEM((width, tokens), low),
            pltpu.VMEM((tokens, ff), low),
            pltpu.VMEM((tokens, ff), low),
            pltpu.VMEM((tokens, width), f32),
            pltpu.VMEM((tokens, width), f32),
            pltpu.VMEM((tokens, width), f32),
            pltpu.VMEM((tokens, width), low),
            pltpu.VMEM((width, tokens), low),
            pltpu.VMEM((parts, width, width), low),
            pltpu.VMEM((parts // 2, width, width), low),
            pltpu.VMEM((chunks, 2, width // 2, chunk), low),
            pltpu.VMEM((chunks, width // 2, chunk), low),
            pltpu.VMEM((width, width // 2), low),
            pltpu.VMEM((width, width // 2), low),
            pltpu.VMEM(down_shape if fused else (16, 128), low),
            pltpu.VMEM(far_shape, low),
            pltpu.SemaphoreType.DMA((2 * parts + 13,)),
            pltpu.SemaphoreType.DMA((2 * parts + 13,)),
            pltpu.SemaphoreType.DMA((2, parts)),
            pltpu.SemaphoreType.DMA((rows_here + 3,)),
        ],
        compiler_params=pltpu.CompilerParams(
            vmem_limit_bytes=63 * 2**20, collective_id=2, has_side_effects=True
        ),
        cost_estimate=pl.CostEstimate(
            flops=2 * tokens * width * (6 * ff + 3 * width),
            bytes_accessed=2 * (5 * ff * width + 8 * tokens * width),
            transcendentals=2 * tokens * ff,
        ),
    )(x, context, ids, *vectors, text_gradient, w_out, w_up, w_down)


class Links:
    def __init__(self, send_sem, recv_sem):
        self.send_sem, self.recv_sem = send_sem, recv_sem
        self.slots, self.copies = {}, {}

    def start(self, name, source, target, device):
        slot = self.slots.setdefault(name, len(self.slots))
        copy = pltpu.make_async_remote_copy(
            src_ref=source, dst_ref=target, send_sem=self.send_sem.at[slot],
            recv_sem=self.recv_sem.at[slot], device_id=device, device_id_type=MESH,
        )
        copy.start()
        self.copies[name] = copy

    def arrived(self, *names):
        for name in names:
            self.copies[name].wait_recv()

    def finish(self):
        for copy in self.copies.values():
            copy.wait_send()


def add_into(target, others, count):
    def one(i, carry):
        total = target[i].astype(jnp.float32)
        for other in others:
            total = total + other[i].astype(jnp.float32)
        target[i] = total.astype(target.dtype)
        return carry

    lax.fori_loop(0, count, one, 0)


def add_up(parts):
    total = parts[0].astype(jnp.float32)
    for part in parts[1:]:
        total = total + part.astype(jnp.float32)
    return total


POOL, UP, DOWN_A, DOWN_B, DOWN, OUT, GROUP, DX, VECTOR = range(9)
STEP, NEAR, FAR, SIDE, LINE, GATHER = range(6)

GROUPS = ((0, 4 * PAIR), (4 * PAIR, PAIR), (5 * PAIR, PAIR))


def attend_back_kernel(
    fused, count_out, out_tree, tree,
    x_ref, ids_ref, lse_ref, w_query, w_key, w_value, pool_ref, count_ref, vector_ref,
    x_hbm, q_hbm, k_hbm, v_hbm, context_hbm, grad_hbm, mixed_hbm, up_ref, down_ref, far_ref, out_ref,
    dx_out, pool_out, vector_out, *rest,
):
    outs = types.SimpleNamespace(**jax.tree.unflatten(out_tree, rest[:count_out]))
    ref = types.SimpleNamespace(**jax.tree.unflatten(tree, rest[count_out:]))
    square_out, up_out, down_out, wo_out = outs.square, outs.up, outs.down, outs.wo
    q_ref, k_ref, v_ref, context_ref, grad_ref = ref.q, ref.k, ref.v, ref.context, ref.grad
    dq_ref, dk_ref, dv_ref, x_t, x_got = ref.dq, ref.dk, ref.dv, ref.x_t, ref.x_got
    extra_ref, penal_ref, delta_ref = ref.extra, ref.penal, ref.delta
    dx_acc, dx_sent, dx_far, dx_got, dx_far_got = (
        ref.dx_acc, ref.dx_sent, ref.dx_far, ref.dx_got, ref.dx_far_got
    )
    pool_parts, pool_got, vec_parts, vec_got = (
        ref.pool_parts, ref.pool_got, ref.vec_parts, ref.vec_got
    )
    row_sem, local_sem = ref.row_sem, ref.local_sem
    rows_here, size, width = x_ref.shape
    low = jnp.bfloat16
    me, place = lax.axis_index("ctx"), lax.axis_index("dp")
    core, side = me % 2, me // 2
    near, across = me + 1 - 2 * core, (me + 2) % 4
    near_dev, across_dev = {"ctx": near}, {"ctx": across}
    y, z = place % 2, place // 2
    y_dev = {"dp": place + 1 - 2 * y}
    z_at = (z + 1 - 2 * (z % 2), (z + 2) % 4, 3 - z)
    z_dev = [{"dp": other * 2 + y} for other in z_at]
    peers = [near_dev, across_dev] + ([y_dev] + z_dev if fused else [])

    barrier = pltpu.get_barrier_semaphore()
    for peer in peers:
        pl.semaphore_signal(barrier, inc=1, device_id=peer, device_id_type=MESH)
    pl.semaphore_wait(barrier, len(peers))
    links = Links(ref.send_sem, ref.recv_sem)

    first_cut = GROUPS[1][0]
    blocks = [(0, first_cut, r) for r in range(rows_here)]
    blocks += [(first_cut, width - first_cut, r) for r in range(rows_here)]

    def load_block(step):
        slot = step % 2
        start, count, r = blocks[step]
        columns, local = pl.ds(start, count), pl.ds(0, count)
        pairs = (
            (k_hbm, k_ref), (v_hbm, v_ref), (q_hbm, q_ref), (context_hbm, context_ref),
            (grad_hbm, grad_ref),
        )
        copies = [
            pltpu.make_async_copy(
                source.at[r, :, columns], target.at[slot, :, local], row_sem.at[slot, i]
            )
            for i, (source, target) in enumerate(pairs)
        ]
        if step < rows_here:
            copies.append(pltpu.make_async_copy(x_hbm.at[:, r], x_got.at[slot], row_sem.at[slot, 5]))
        return copies

    for item in load_block(0):
        item.start()
    load_mixed = pltpu.make_async_copy(mixed_hbm, dx_acc, local_sem.at[0])
    links.start((POOL, STEP, 0), pool_ref, pool_got.at[0], near_dev)
    if fused:
        u_ref, u_x, u_y, u_z = ref.u, ref.u_x, ref.u_y, ref.u_z
        a_z, a_s, a_x = ref.a_z, ref.a_s, ref.a_x
        b_ref, b_y, b_z = ref.b, ref.b_y, ref.b_z
        o_ref, o_y, o_z, o_s, o_x = ref.o, ref.o_y, ref.o_z, ref.o_s, ref.o_x
        half_rows = u_ref.shape[2] // 2
        links.start((UP, FAR, 0), up_ref.at[1 - side, :, :, pl.ds(0, half_rows)], u_x.at[0], across_dev)
        links.start((DOWN_B, SIDE), far_ref.at[:, 1 - y], b_y, y_dev)
        for o in range(3):
            links.start((DOWN_A, LINE, o), down_ref.at[z_at[o]], a_z.at[o], z_dev[o])
    load_mixed.start()
    vec_parts[0] = vector_ref[...]

    def pool_one():
        links.arrived((POOL, STEP, 0))
        pool_parts[...] = add_up([pool_ref[...], pool_got[0]]).astype(low)
        links.start((POOL, STEP, 1), pool_parts, pool_got.at[1], across_dev)

    def pool_two():
        links.arrived((POOL, STEP, 1))
        pool_out[...] = add_up([pool_parts[...], pool_got[1]]) / count_ref[...]

    def send_z(name, source, target):
        for o in range(3):
            links.start(name + (o,), source(z_at[o]), target(o), z_dev[o])

    def arrived_z(name):
        links.arrived(*(name + (o,) for o in range(3)))

    def out_y():
        links.start((OUT, SIDE), out_ref.at[:, 1 - y], o_y, y_dev)

    def out_z():
        links.arrived((OUT, SIDE))
        for i in range(4):
            o_ref[i] = add_up([out_ref[i, y], o_y[i]]).astype(low)
        send_z((OUT, LINE), lambda i: o_ref.at[i], lambda o: o_z.at[o])

    def out_far():
        arrived_z((OUT, LINE))
        o_s[...] = add_up([o_ref[z]] + [o_z[o] for o in range(3)]).astype(low)
        links.start((OUT, FAR), o_s, o_x, across_dev)

    def out_end():
        links.arrived((OUT, FAR))
        wo_out[core] = add_up([o_s[...], o_x[...]]).astype(low)
        links.start((OUT, GATHER), wo_out.at[core], wo_out.at[core], near_dev)

    def down_z():
        links.arrived((DOWN_B, SIDE))
        for i in range(4):
            b_ref[i] = add_up([far_ref[i, y], b_y[i]]).astype(low)
        send_z((DOWN_B, LINE), lambda i: b_ref.at[i], lambda o: b_z.at[o])

    def down_near_far():
        arrived_z((DOWN_A, LINE))
        a_s[...] = add_up([down_ref[z]] + [a_z[o] for o in range(3)]).astype(low)
        links.start((DOWN_A, FAR), a_s, a_x, across_dev)

    def down_far():
        arrived_z((DOWN_B, LINE))
        count = b_ref.shape[1]
        own = pl.ds(pl.multiple_of(2 * count + side * count, 16), count)
        down_out[core, own] = add_up([b_ref[z]] + [b_z[o] for o in range(3)]).astype(low)
        links.start((DOWN_B, FAR), down_out.at[core, own], down_out.at[core, own], across_dev)

    def down_end():
        links.arrived((DOWN_A, FAR), (DOWN_B, FAR))
        down_out[core, 0 : a_s.shape[0]] = add_up([a_s[...], a_x[...]]).astype(low)
        links.start((DOWN, GATHER), down_out.at[core], down_out.at[core], near_dev)

    def up_x():
        rows = pl.ds(half_rows, half_rows)
        links.start((UP, FAR, 1), up_ref.at[1 - side, :, :, rows], u_x.at[1], across_dev)

    def up_y(h):
        rows = pl.ds(h * half_rows, half_rows)
        links.arrived((UP, FAR, h))
        for i in range(4):
            for j in range(2):
                u_ref[i, j, rows] = add_up([up_ref[side, i, j, rows], u_x[h, i, j]]).astype(low)
        links.start((UP, SIDE, h), u_ref.at[:, 1 - y, rows], u_y.at[h], y_dev)

    def up_z(h):
        rows = pl.ds(h * half_rows, half_rows)
        links.arrived((UP, SIDE, h))
        for i in range(4):
            u_ref[i, y, rows] = add_up([u_ref[i, y, rows], u_y[h, i]]).astype(low)
        send_z((UP, LINE, h), lambda i: u_ref.at[i, y, rows], lambda o: u_z.at[o, rows])

    def up_far():
        arrived_z((UP, LINE, 0))
        arrived_z((UP, LINE, 1))
        up_out[me] = add_up([u_ref[z, y]] + [u_z[o] for o in range(3)]).astype(low)
        links.start((UP, GATHER), up_out.at[me], up_out.at[me], across_dev)

    def up_end():
        links.arrived((UP, GATHER))
        links.start((UP, NEAR, 0), up_out.at[me], up_out.at[me], near_dev)
        links.start((UP, NEAR, 1), up_out.at[across], up_out.at[across], near_dev)

    def group_core(g):
        links.start((GROUP, NEAR, g), ref.g[g].at[1 - core], ref.g_got[g], near_dev)

    def group_y(g):
        links.arrived((GROUP, NEAR, g))
        for i in range(4):
            add_into(ref.g[g].at[core, i], [ref.g_got[g].at[i]], 2)
        links.start((GROUP, SIDE, g), ref.g[g].at[core, :, 1 - y], ref.g_y[g], y_dev)

    def group_z(g):
        links.arrived((GROUP, SIDE, g))
        own = ref.g[g]
        for i in range(4):
            own[core, i, y] = add_up([own[core, i, y], ref.g_y[g][i]]).astype(low)
        send_z((GROUP, LINE, g), lambda i: own.at[core, i, y], lambda o: ref.g_z[g].at[o])

    def group_far(g):
        arrived_z((GROUP, LINE, g))
        pieces = [ref.g[g][core, z, y]] + [ref.g_z[g][o] for o in range(3)]
        ref.g_s[g][...] = add_up(pieces).astype(low)
        links.start((GROUP, FAR, g), ref.g_s[g], ref.g_x[g], across_dev)

    def group_end(g):
        links.arrived((GROUP, FAR, g))
        out = outs.squares[g]
        out[core] = add_up([ref.g_s[g][...], ref.g_x[g][...]]).astype(low)
        links.start((GROUP, GATHER, g), out.at[core], out.at[core], near_dev)

    def vector_step(i, device):
        if i:
            links.arrived((VECTOR, STEP, i - 1))
            vec_parts[i] = vec_parts[i - 1] + vec_got[i - 1]
        if device is not None:
            links.start((VECTOR, STEP, i), vec_parts.at[i], vec_got.at[i], device)

    def vector_z():
        vector_step(3, None)
        for o in range(3):
            links.start((VECTOR, LINE, o), vec_parts.at[3], vec_got.at[3 + o], z_dev[o])

    def vector_end():
        arrived_z((VECTOR, LINE))
        vector_out[...] = vec_parts[3] + (vec_got[3] + (vec_got[4] + vec_got[5]))

    row = lax.broadcasted_iota(jnp.int32, (PAIR, size), 0)

    def find_delta(step):
        slot = step % 2
        start, count, _ = blocks[step]
        lane = lax.broadcasted_iota(jnp.int32, (count, PAIR), 1)
        head = (start + lax.broadcasted_iota(jnp.int32, (count, PAIR), 0)) // HEAD_DIM
        member = jnp.where((lane % NSEG == head) & (lane >= NSEG) & (lane < 4 * NSEG), 1.0, 0.0)
        member = member.astype(low)
        local = pl.ds(0, count)
        product = grad_ref[slot, :, local].astype(jnp.float32) * context_ref[
            slot, :, local
        ].astype(jnp.float32)
        total = jnp.zeros((size, PAIR), jnp.float32)
        for _ in range(3):
            term = product.astype(low)
            total = total + matmul(term, member)
            product = product - term.astype(jnp.float32)
        delta_ref[...] = with_constants(jnp.zeros_like(total), -total)

    def attend_pairs(step, first, last):
        slot = step % 2
        start, _, r = blocks[step]

        class Pair:
            def __init__(self, n):
                self.local = pl.ds(n * PAIR, PAIR)
                self.columns = pl.ds(start + n * PAIR, PAIR)
                head = 2 * (start // PAIR + n)
                self.q_both = split_heads(q_ref[slot, :, self.local])
                self.g_both = split_heads(grad_ref[slot, :, self.local])
                q_extra = [of_head(penal_ref[r], head + h) for h in range(2)]
                g_extra = [of_head(delta_ref[...], head + h) for h in range(2)]
                q_wide = jnp.concatenate([self.q_both, jnp.concatenate(q_extra, axis=0)], axis=1)
                g_wide = jnp.concatenate([self.g_both, jnp.concatenate(g_extra, axis=0)], axis=1)
                self.q_wide, self.g_wide = q_wide.T, g_wide.T
                self.dq = jnp.zeros((PAIR, 2 * size), jnp.float32)

            def products(self, j):
                rows = pl.ds(j * size, size)
                extra = extra_ref[r, rows, :]
                keys = jnp.concatenate([k_ref[slot, rows, self.local], extra], axis=1)
                values = jnp.concatenate([v_ref[slot, rows, self.local], extra], axis=1)
                return matmul(keys, self.q_wide), matmul(values, self.g_wide)

            def block(self, j, scores, grad_p):
                rows = pl.ds(j * size, size)
                probs = jnp.exp(scores)
                grad_s = (probs * grad_p).astype(low)
                dv_ref[r, rows, self.columns] = matmul(probs.astype(low), self.g_both).astype(low)
                dk_ref[r, rows, self.columns] = matmul(grad_s, self.q_both).astype(low)
                self.dq = self.dq + matmul(k_ref[slot, rows, self.local].T, grad_s)

            def end(self):
                dq = jnp.where(row < HEAD_DIM, self.dq[:, :size], self.dq[:, size:])
                dq_ref[r, :, self.columns] = (dq * HEAD_DIM ** (-0.5)).T.astype(low)

        pairs = [Pair(n) for n in range(first, last)]
        for j in range(4):
            ready = [pair.products(j) for pair in pairs]
            for pair, (scores, grad_p) in zip(pairs, ready):
                pair.block(j, scores, grad_p)
        for pair in pairs:
            pair.end()

    def weight_group(g):
        start, count = GROUPS[g]
        if fused:
            depth = ref.g[g].shape[3]

        def keep(n, i, total):
            total = total.astype(low)
            wide = total.shape[1]
            if not fused:
                square_out[n, :, pl.ds(pl.multiple_of(start + i * PAIR, PAIR), wide)] = total
                return
            total = total.reshape(4, 2, 2, depth, wide)
            target = pl.ds(pl.multiple_of(n * count + i * PAIR, PAIR), wide)
            for h in range(2):
                ref.g[g][h, :, :, :, target] = total[:, :, h]

        def of_source(source, columns):
            keys = source.shape[1]
            return sum(
                matmul(x_t[r, :, :keys], source[r, :, columns]) for r in range(rows_here)
            )

        def one_part(i, carry):
            columns = pl.ds(pl.multiple_of(start + 2 * i * PAIR, PAIR), 2 * PAIR)
            for n, source in enumerate((dq_ref, dk_ref, dv_ref)):
                keep(n, 2 * i, of_source(source, columns))
            return carry

        if count % (2 * PAIR):
            columns = pl.ds(start, count)
            keep(0, 0, of_source(dq_ref, columns))
            both = sum(
                matmul(
                    x_t[r],
                    jnp.concatenate([dk_ref[r, :, columns], dv_ref[r, :, columns]], axis=1),
                )
                for r in range(rows_here)
            )
            keep(1, 0, both[:, :count])
            keep(2, 0, both[:, count:])
        else:
            lax.fori_loop(0, count // (2 * PAIR), one_part, 0)
        columns = pl.ds(start, count)
        for n, source in enumerate((dq_ref, dv_ref)):
            vec_parts[0, n : n + 1, columns] = sum(
                jnp.sum(source[r, :, columns].astype(jnp.float32), axis=0, keepdims=True)
                for r in range(rows_here)
            )

    def input_parts(r):
        for j in (3, 2, 1, 0):
            rows = pl.ds(j * size, size)
            total = dot_nt(dk_ref[r, rows, :], w_key[...]) + dot_nt(dv_ref[r, rows, :], w_value[...])
            if j == 0:
                dx_acc[r] = dx_acc[r] + total + dot_nt(dq_ref[r], w_query[...])
            elif j == 2:
                dx_far[r] = total.astype(low)
            else:
                n = j // 2
                dx_sent[r, n] = total.astype(low)
                links.start((DX, NEAR, r, n), dx_sent.at[r, n], dx_got.at[r, n], near_dev)

    def input_far(r):
        links.arrived((DX, NEAR, r, 1))
        dx_far[r] = add_up([dx_far[r], dx_got[r, 1]]).astype(low)
        links.start((DX, FAR, r), dx_far.at[r], dx_far_got.at[r], across_dev)

    def input_done(r):
        links.arrived((DX, NEAR, r, 0), (DX, FAR, r))
        dx_out[r] = add_up([dx_acc[r], dx_got[r, 0], dx_far_got[r]]).astype(low)

    def prepare_row(r):
        slot = r % 2
        for j in range(4):
            rows = slice(j * size, (j + 1) * size)
            texts = text_rows(ids_ref[j, r : r + 1, :], size)
            extra_ref[r, rows, :] = key_extra(texts)
            if j == 0:
                penal_ref[r] = with_constants(query_extra(texts), -lse_ref[r])
            block = x_ref[r] if j == 0 else x_got[slot, j - 1]
            x_t[r, :, rows] = block.T

    def begin(step):
        for item in load_block(step):
            item.wait()
        if step + 1 < len(blocks):
            for item in load_block(step + 1):
                item.start()
        find_delta(step)

    def do(*actions):
        if fused:
            for action, *given in actions:
                action(*given)

    most = first_cut // PAIR
    begin(0)
    prepare_row(0)
    attend_pairs(0, 0, most // 2)
    attend_pairs(0, most // 2, most)
    do((pool_one,))
    begin(1)
    prepare_row(1)
    attend_pairs(1, 0, most // 2)
    do((out_y,), (down_z,), (up_x,))
    attend_pairs(1, most // 2, most)
    do((pool_two,))
    begin(2)
    prepare_row(2)
    attend_pairs(2, 0, most // 2)
    do((up_y, 0), (out_z,))
    attend_pairs(2, most // 2, most)
    weight_group(0)
    do((group_core, 0), (down_near_far,), (up_y, 1))
    begin(3)
    attend_pairs(3, 0, 2)
    load_mixed.wait()
    input_parts(0)
    do((down_far,), (group_y, 0), (out_far,), (up_z, 1), (up_z, 0), (input_far, 0))
    begin(4)
    attend_pairs(4, 0, 2)
    input_parts(1)
    begin(5)
    attend_pairs(5, 0, 1)
    weight_group(1)
    do((group_core, 1), (input_far, 1))
    attend_pairs(5, 1, 2)
    do((group_z, 0))
    weight_group(2)
    do((group_core, 2), (vector_step, 0, near_dev))
    input_parts(2)
    if not fused:
        vector_out[...] = vec_parts[0]
        pool_one()
        for r in range(3):
            input_far(r)
        pool_two()
        for r in range(3):
            input_done(r)
        links.finish()
        return
    do((group_y, 2), (group_y, 1), (vector_step, 1, across_dev), (up_far,), (input_far, 2))
    do((group_z, 2), (down_end,), (out_end,), (vector_step, 2, y_dev), (up_end,), (group_z, 1))
    do((vector_z,), (group_far, 0), (group_far, 2), (group_far, 1), (input_done, 0))
    do((group_end, 0), (group_end, 2), (vector_end,), (group_end, 1), (input_done, 1))
    do((input_done, 2))
    links.arrived((DOWN, GATHER), (OUT, GATHER), (UP, NEAR, 0), (UP, NEAR, 1))
    links.arrived(*((GROUP, GATHER, g) for g in range(3)))
    links.finish()


def attend_back(
    fused, x, ids, lse, w_query, w_key, w_value, pool, counts, vectors,
    x_got, q, k, v, context, grad, mixed, up, down, far, out,
):
    rows_here, size, width = x.shape
    keys = size * 4
    low = jnp.bfloat16
    f32 = jnp.float32
    whole = pl.BlockSpec(memory_space=pltpu.VMEM)
    outside = pl.BlockSpec(memory_space=pl.ANY)
    shape = jax.ShapeDtypeStruct
    most = GROUPS[0][1]
    vec = vectors.shape
    small = shape((8, 128), low)
    if fused:
        depth = up.shape[3]
        outs = dict(
            squares=[shape((2, depth // 2, 3 * count), low) for _, count in GROUPS],
            up=shape((4, depth, width), low),
            down=shape((2, 2 * down.shape[1], down.shape[2]), low),
            wo=shape((2, depth, width // 2), low),
            square=small,
        )
    else:
        outs = dict(
            squares=[], up=small, down=small, wo=small, square=shape((3, width, width), low)
        )
    scratch = dict(
        x_got=pltpu.VMEM((2, 3, size, width), low),
        x_t=pltpu.VMEM((rows_here, width, keys), low),
        q=pltpu.VMEM((2, size, most), low),
        k=pltpu.VMEM((2, keys, most), low),
        v=pltpu.VMEM((2, keys, most), low),
        context=pltpu.VMEM((2, size, most), low),
        grad=pltpu.VMEM((2, size, most), low),
        extra=pltpu.VMEM((rows_here, keys, PAIR), low),
        penal=pltpu.VMEM((rows_here, size, PAIR), low),
        delta=pltpu.VMEM((size, PAIR), low),
        dq=pltpu.VMEM((rows_here, size, width), low),
        dk=pltpu.VMEM((rows_here, keys, width), low),
        dv=pltpu.VMEM((rows_here, keys, width), low),
        dx_acc=pltpu.VMEM((rows_here, size, width), f32),
        dx_sent=pltpu.VMEM((rows_here, 2, size, width), low),
        dx_far=pltpu.VMEM((rows_here, size, width), low),
        dx_got=pltpu.VMEM((rows_here, 2, size, width), low),
        dx_far_got=pltpu.VMEM((rows_here, size, width), low),
        pool_parts=pltpu.VMEM(pool.shape, low),
        pool_got=pltpu.VMEM((2,) + pool.shape, low),
        vec_parts=pltpu.VMEM((4,) + vec, f32),
        vec_got=pltpu.VMEM((6,) + vec, f32),
        send_sem=pltpu.SemaphoreType.DMA((72,)),
        recv_sem=pltpu.SemaphoreType.DMA((72,)),
        row_sem=pltpu.SemaphoreType.DMA((2, 6)),
        local_sem=pltpu.SemaphoreType.DMA((5,)),
    )
    if fused:
        tails = [(depth // 2, 3 * count) for _, count in GROUPS]
        spread = lambda *lead: [pltpu.VMEM(lead + tail, low) for tail in tails]
        b_shape = far.shape[2:]
        narrow = (depth, width // 2)
        scratch.update(
            g=spread(2, 4, 2), g_got=spread(4, 2), g_y=spread(4), g_z=spread(3),
            g_s=spread(), g_x=spread(),
            u=pltpu.VMEM((4, 2, depth, width), low),
            u_x=pltpu.VMEM((2, 4, 2, depth // 2, width), low),
            u_y=pltpu.VMEM((2, 4, depth // 2, width), low),
            u_z=pltpu.VMEM((3, depth, width), low),
            a_z=pltpu.VMEM((3,) + down.shape[1:], low),
            a_s=pltpu.VMEM(down.shape[1:], low),
            a_x=pltpu.VMEM(down.shape[1:], low),
            b=pltpu.VMEM((4,) + b_shape, low),
            b_y=pltpu.VMEM((4,) + b_shape, low),
            b_z=pltpu.VMEM((3,) + b_shape, low),
            o=pltpu.VMEM((4,) + narrow, low),
            o_y=pltpu.VMEM((4,) + narrow, low),
            o_z=pltpu.VMEM((3,) + narrow, low),
            o_s=pltpu.VMEM(narrow, low),
            o_x=pltpu.VMEM(narrow, low),
        )
    out_leaves, out_tree = jax.tree.flatten(outs)
    leaves, tree = jax.tree.flatten(scratch)
    count_out = len(out_leaves)
    got = pl.pallas_call(
        functools.partial(attend_back_kernel, fused, count_out, out_tree, tree),
        out_shape=(
            shape((rows_here, size, width), low),
            shape(pool.shape, f32),
            shape(vec, f32),
        )
        + tuple(out_leaves),
        in_specs=[whole] * 9 + [outside] * 7 + [whole] * 4,
        out_specs=(whole,) * (3 + count_out),
        scratch_shapes=leaves,
        compiler_params=pltpu.CompilerParams(
            vmem_limit_bytes=63 * 2**20, collective_id=1, has_side_effects=True
        ),
        cost_estimate=pl.CostEstimate(
            flops=rows_here
            * (4 * (size + 2 * keys) * width * width + 40 * size * keys * width),
            bytes_accessed=2 * (16 * width * width + 9 * keys * width),
            transcendentals=rows_here * HEADS * size * keys,
        ),
    )(
        x, ids, lse, w_query, w_key, w_value, pool, counts, vectors,
        x_got, q, k, v, context, grad, mixed, up, down, far, out,
    )
    return got[:3] + (types.SimpleNamespace(**jax.tree.unflatten(out_tree, got[3:])),)


def outputs_kernel(
    square0, square1, square2, wo, up, down, pool, final, dx,
    wq_out, wk_out, wv_out, wo_out, up_out, down_out, pool_out, final_out, dx_out,
):
    final_out[...] = final[...]
    dx_out[...] = dx[...]
    f32 = jnp.float32
    pool_out[...] = pool[...].reshape(pool_out.shape)
    for (start, count), square in zip(GROUPS, (square0, square1, square2)):
        rows = square.shape[1]
        for n, out in enumerate((wq_out, wk_out, wv_out)):
            for h in range(2):
                out[h * rows : (h + 1) * rows, start : start + count] = square[
                    h, :, n * count : (n + 1) * count
                ].astype(f32)
    for h in range(2):
        half = wo.shape[2]
        wo_out[:, h * half : (h + 1) * half] = wo[h].astype(f32)
        rows = down.shape[1]
        down_out[:, h * rows : (h + 1) * rows] = down[h].astype(f32).T
    for i in range(4):
        place, width = (i % 2) * 2 + i // 2, up.shape[2]
        up_out[:, place * width : (place + 1) * width] = up[i].astype(f32)


def outputs(squares, wo, up, down, pool, final, dx):
    f32 = jnp.float32
    whole = pl.BlockSpec(memory_space=pltpu.VMEM)
    shape = jax.ShapeDtypeStruct
    rows, width = up.shape[1:]
    row_count = final.shape[0]
    return pl.pallas_call(
        outputs_kernel,
        out_shape=(
            shape((rows, width), f32), shape((rows, width), f32), shape((rows, width), f32),
            shape((rows, width), f32), shape((rows, 4 * width), f32),
            shape((down.shape[2], 2 * down.shape[1]), f32),
            shape((row_count, pool.shape[0] // row_count, width), f32),
            shape(final.shape, final.dtype), shape(dx.shape, dx.dtype),
        ),
        in_specs=[whole] * 9,
        out_specs=(whole,) * 9,
        compiler_params=pltpu.CompilerParams(vmem_limit_bytes=63 * 2**20),
    )(*squares, wo, up, down, pool, final, dx)


def radices_of(count):
    if count == 8:
        return ((1, 2), (2, 4))
    digits = []
    stride = 1
    while stride < count:
        digits.append((stride, 2))
        stride *= 2
    return tuple(digits)


def exchange(piece, axis_name, stride, offset):
    count = lax.axis_size(axis_name)
    pairs = [(i, i ^ (offset * stride)) for i in range(count)]
    return lax.ppermute(piece, axis_name, pairs)


def digit_of(axis_name, stride, radix):
    return (lax.axis_index(axis_name) // stride) % radix


def scatter_digit(pieces, place, axis_name, stride, radix):
    here = digit_of(axis_name, stride, radix)
    received = [
        exchange(
            lax.dynamic_index_in_dim(pieces, here ^ offset, place, keepdims=False).astype(
                jnp.bfloat16
            ),
            axis_name, stride, offset,
        )
        for offset in range(1, radix)
    ]
    total = lax.dynamic_index_in_dim(pieces, here, place, keepdims=False).astype(jnp.float32)
    for item in received:
        total = total + item.astype(jnp.float32)
    return total.astype(jnp.bfloat16)


def halve(piece, place, axis_name, stride):
    half = piece.shape[place] // 2
    here = digit_of(axis_name, stride, 2)
    sent = lax.dynamic_slice_in_dim(piece, (1 - here) * half, half, place).astype(jnp.bfloat16)
    kept = lax.dynamic_slice_in_dim(piece, here * half, half, place).astype(jnp.float32)
    return (kept + exchange(sent, axis_name, stride, 1).astype(jnp.float32)).astype(jnp.bfloat16)


def join(piece, place, axis_name, stride):
    here = digit_of(axis_name, stride, 2)
    other = exchange(piece, axis_name, stride, 1)
    first = jnp.where(here == 0, piece, other)
    second = jnp.where(here == 0, other, piece)
    return jnp.concatenate([first, second], axis=place)


def scatter_rows(group, dp_size):
    digits = radices_of(dp_size)
    shape = tuple(r for _, r in reversed(digits))
    group = group.reshape(shape + (group.shape[0] // dp_size, group.shape[1]))
    for place, (stride, radix) in zip(range(len(digits) - 1, -1, -1), digits):
        group = scatter_digit(group, place, "dp", stride, radix)
    return group


def finish_weight(flat, dp_size, side):
    flat = scatter_rows(flat, dp_size)
    flat = flat.astype(jnp.float32) + exchange(flat, "ctx", 2, 1).astype(jnp.float32)
    return join(flat.astype(jnp.bfloat16), side, "ctx", 1).astype(jnp.float32)


def reduce_weight(gradient, dp_size, side):
    return finish_weight(halve(gradient, side, "ctx", 1), dp_size, side)


def per_device(
    hidden_in,
    seg_ids,
    valid,
    w_query,
    b_query,
    w_key,
    w_value,
    b_value,
    w_out,
    b_out,
    gain_attn,
    shift_attn,
    w_up,
    b_up,
    w_down,
    b_down,
    gain_ffn,
    shift_ffn,
    pooled_text_gradient,
):
    row_count, group_size, model_width = hidden_in.shape
    dp_size = lax.axis_size("dp")
    ff_width = w_up.shape[1]
    rows_here, ff_here = model_width // dp_size, ff_width // dp_size
    fused = dp_size == 8 and rows_here % 32 == 0 and ff_here % 128 == 0 and model_width % 128 == 0
    q_all, context, lse_all, ids_got, x_got, k_all, v_all = attend(
        hidden_in, seg_ids, valid, b_query, b_value, w_query, w_key, w_value
    )
    vectors = (b_out, gain_attn, shift_attn, b_up, b_down, gain_ffn, shift_ffn)
    pool, counts, vector_parts, grad_context, grad_mixed, out, final_out, up, down, far = middle(
        fused, hidden_in, context, ids_got, vectors, pooled_text_gradient, w_out, w_up, w_down,
        dp_size,
    )
    if fused:
        up_part = up.reshape(2, 4, 2, rows_here, -1)
        far_part = far.reshape((4, 2) + far.shape[1:])
        out_part = out.reshape(4, 2, rows_here, -1)
    else:
        up_part = far_part = out_part = jnp.zeros((16, 128), jnp.bfloat16)
    grad_input, pooled, vector_sum, sums_of = attend_back(
        fused, hidden_in, ids_got, lse_all, w_query, w_key, w_value,
        pool, counts, vector_parts, x_got, q_all, k_all, v_all, context, grad_context, grad_mixed,
        up_part, down, far_part, out_part,
    )
    if fused:
        *square_sums, up_sum, down_sum, pooled, final_out, grad_input = outputs(
            sums_of.squares, sums_of.wo, sums_of.up, sums_of.down, pooled, final_out, grad_input
        )
    else:
        squares = sums_of.square
        square_sums = [reduce_weight(squares[n], dp_size, 1) for n in range(3)]
        square_sums.append(finish_weight(out, dp_size, 1))
        up_sum = finish_weight(up.transpose(1, 0, 2).reshape(model_width, -1), dp_size, 1)
        down = down.transpose(0, 2, 1).reshape(ff_width, -1)
        down_sum = finish_weight(down, dp_size, 1)
        vector_sum = lax.psum(vector_sum, ("dp", "ctx"))
        pooled = pooled.reshape(row_count, NSEG, model_width)
    place = lax.axis_index("dp")
    sums = lax.dynamic_slice_in_dim(vector_sum[:8], place * rows_here, rows_here, 1)
    sum_bu = lax.dynamic_slice_in_dim(
        vector_sum[8 : 8 + ff_width // model_width].reshape(-1), place * ff_here, ff_here
    )
    results = (
        square_sums[0], sums[0], square_sums[1], square_sums[2], sums[1], square_sums[3],
        sums[2], sums[3], sums[4], up_sum, sum_bu, down_sum, sums[5], sums[6], sums[7],
    )
    return (
        final_out,
        pooled,
        grad_input,
    ) + tuple(results)


def solution(mesh):
    placed = (
        P("dp", "ctx", None),
        P("dp", "ctx"),
        P("dp", "ctx"),
        P(),
        P(),
        P(),
        P(),
        P(),
        P(),
        P(),
        P(),
        P(),
        P(),
        P(),
        P(),
        P(),
        P(),
        P(),
        P("dp", None, None),
    )
    return jax.shard_map(
        per_device,
        mesh=mesh,
        in_specs=placed,
        out_specs=(
            P("dp", "ctx", None),
            P("dp", None, None),
            P("dp", "ctx", None),
            P("dp", None),
            P("dp"),
            P("dp", None),
            P("dp", None),
            P("dp"),
            P("dp", None),
            P("dp"),
            P("dp"),
            P("dp"),
            P("dp", None),
            P("dp"),
            P("dp", None),
            P("dp"),
            P("dp"),
            P("dp"),
        ),
        check_vma=False,
    )
```
